32 devices in a mesh: grp: 8 (over z, y), ep: 4 (over x, core).
Axes of the slice: x: 2, y: 2, z: 4, core: 2. Of those that a mesh axis runs over, the one named last changes fastest.
Arguments:
- block_entry_states: bfloat16 [2, 2048, 2048], P(None, ('grp', 'ep')), may hold values from -6 to 6
- document_labels: int32 [2, 2048], P(None, 'grp'), may hold values from 0 to 125, as said below
- token_assignments: int32 [2, 2048, 8], P(None, ('grp', 'ep')), may hold values from 0 to 15, as said below
- worker_quota_tallies: int32 [16], replicated, may hold values from 24 to 48
- rescale_factors_both: bfloat16 [2, 2048], replicated, may hold values from 0.5 to 1.5
- triple_projection_matrix: bfloat16 [2048, 3, 2048], P(None, None, 'ep'), may hold values from -0.125 to 0.125
- probe_lookup_scalers: bfloat16 [2, 2048], P(None, 'ep'), may hold values from 0.5 to 1.5
- heads_merge_matrix: bfloat16 [2048, 2048], P('ep'), may hold values from -1 to 1
- dispatcher_matrix: bfloat16 [2048, 16], replicated, may hold values from -0.0625 to 0.0625
- specialist_widen_matrix: bfloat16 [16, 2048, 2048], P('ep'), may hold values from -0.125 to 0.125
- specialist_shrink_matrix: bfloat16 [16, 1024, 2048], P('ep'), may hold values from -2 to 2
- output_gradient: bfloat16 [2, 2048, 2048], P(None, ('grp', 'ep')), may hold values from -6 to 6
Outputs:
- output: bfloat16 [2, 2048, 2048], P(None, ('grp', 'ep'))
- grad_input: float32 [2, 2048, 2048], P(None, ('grp', 'ep'))
- grad_norm_gains: float32 [2, 2048], replicated
- grad_qkv: float32 [2048, 3, 2048], P(None, None, 'ep')
- grad_qk_gain: float32 [2, 2048], P(None, 'ep')
- grad_w_out: float32 [2048, 2048], P('ep')
- grad_router: float32 [2048, 16], replicated
- grad_w_in: float32 [16, 2048, 2048], P('ep', 'grp')
- grad_w_down: float32 [16, 1024, 2048], P('ep', 'grp')
The draws below stay inside these ranges and needn't reach their ends.
Inputs may be any that keep to these rules, and one draw needn't show every extreme that they name: `document_labels`: within each sequence of 256 tokens the numbers start at 0 and never fall. `token_assignments`: each row names 8 different experts in increasing order.
All inputs are finite; a program needn't handle non-finite values.
Results may differ from the reference program's by a relative error of at most 0.02.
Values may be sent and summed in bfloat16 or wider, within the bound.
A program may use at most 448 MiB of HBM per device.

```python
import math
import jax
import jax.numpy as jnp
from jax import lax

D = 2048
HEADS = 16
HD = 128
FF = 1024
TOP = 8
MICRO = 2
TOK_DEV = 64
SEQ = 256
TOKENS = 2048
EXPERTS = 16
PER_GROUP_CAP = 48


def expert_order(key):
    return jax.random.permutation(key, EXPERTS)


def draw_worker_quota_tallies(key, part):
    order = expert_order(key)
    key = jax.random.fold_in(key, 11)
    limits = jax.random.randint(key, (EXPERTS,), PER_GROUP_CAP // 2, PER_GROUP_CAP + 1)
    limits = limits.at[order[0]].set(PER_GROUP_CAP)
    limits = limits.at[order[1]].set(PER_GROUP_CAP // 2)
    return limits.astype(jnp.int32)


def draw_token_assignments(key, part):
    order = expert_order(key)
    key = jax.random.fold_in(key, 12)
    position = jnp.zeros((EXPERTS,), jnp.int32).at[order].set(jnp.arange(EXPERTS, dtype=jnp.int32))
    favour = (EXPERTS - position) * (4096 // EXPERTS)
    favour = jnp.where(position == 0, 1 << 20, favour)
    noise = jax.random.randint(key, (MICRO, TOKENS, EXPERTS), 0, 4096)
    scores = (noise + favour) * EXPERTS + jnp.arange(EXPERTS, dtype=jnp.int32)
    chosen = lax.top_k(scores, TOP)[1]
    return jnp.sort(chosen, axis=-1).astype(jnp.int32)


def draw_document_labels(key, part):
    key = jax.random.fold_in(key, 13)
    first_key, last_key, begin_key, pick_key = jax.random.split(key, 4)
    groups = TOKENS // SEQ
    count = MICRO * groups
    pick = jax.random.randint(pick_key, (groups,), 0, MICRO)
    seq_ids = jnp.arange(count, dtype=jnp.int32)
    full = (seq_ids // groups == pick[seq_ids % groups])[:, None]
    opening = jax.random.randint(first_key, (count, 1), 1, TOK_DEV)
    closing = SEQ - jax.random.randint(last_key, (count, 1), 0, TOK_DEV - 1)
    opening = jnp.where(full, TOK_DEV - 1, opening)
    closing = jnp.where(full, SEQ - TOK_DEV + 2, closing)
    destination_spot = jnp.arange(SEQ, dtype=jnp.int32)[None, :]
    begins = (jax.random.randint(begin_key, (count, SEQ), 0, 4) == 0) | full
    begins = begins & ((destination_spot < opening) | (destination_spot > closing))
    begins = begins | (destination_spot == 0) | (destination_spot == opening) | (destination_spot == closing)
    ids = jnp.cumsum(begins.astype(jnp.int32), axis=1) - 1
    return ids.reshape(MICRO, TOKENS).astype(jnp.int32)


def levels(key, extent, cuts, low, high):
    factor_of, own = 1.0, jax.random.fold_in(key, 6)
    for dim, blocks in cuts:
        heights = jnp.exp(jax.random.uniform(jax.random.fold_in(own, dim), (blocks,), jnp.float32, low / len(cuts), high / len(cuts)))
        factor_of = factor_of * jnp.repeat(heights, extent[dim] // blocks).reshape([-1 if axis == dim else 1 for axis in range(len(extent))])
    return factor_of


def scatter_about(stream_key, shape, deviation, limit, pieces=(), held_as=jnp.bfloat16):
    level = levels(stream_key, shape, pieces, -0.22, 0.18) if pieces else 1.0
    entries = jax.random.normal(stream_key, shape, jnp.float32) * deviation * level
    return jnp.minimum(jnp.maximum(entries, -limit), limit).astype(held_as)


def setup_inputs(seed: int = 0) -> dict:
    streams_of = jax.random.split(jax.random.key(seed), 13)
    block_entry_states = scatter_about(streams_of[0], (MICRO, TOKENS, D), 1.0, 6.0, ((1, 32),))
    document_labels = draw_document_labels(jax.random.fold_in(streams_of[12], 71), 0)
    token_assignments = draw_token_assignments(jax.random.fold_in(streams_of[12], 71), 0)
    worker_quota_tallies = draw_worker_quota_tallies(jax.random.fold_in(streams_of[12], 71), 0)
    rescale_factors_both = jnp.clip(1.0 + 0.1 * jax.random.normal(streams_of[4], (2, D), jnp.float32), 0.5, 1.5).astype(jnp.bfloat16)
    triple_projection_matrix = scatter_about(streams_of[5], (D, 3, D), D ** -0.5, 0.125, ((2, 4),))
    probe_lookup_scalers = jnp.clip(1.0 + 0.1 * jax.random.normal(streams_of[6], (2, D), jnp.float32), 0.5, 1.5).astype(jnp.bfloat16)
    heads_merge_matrix = scatter_about(streams_of[7], (D, D), (D // 64) ** -0.5, 1.0, ((0, 4),))
    dispatcher_matrix = scatter_about(streams_of[8], (D, EXPERTS), (4 * D) ** -0.5, 0.0625)
    specialist_widen_matrix = scatter_about(streams_of[9], (EXPERTS, D, 2 * FF), D ** -0.5, 0.125, ((0, 4),))
    specialist_shrink_matrix = scatter_about(streams_of[10], (EXPERTS, FF, D), (max(1, FF // 100)) ** -0.5, 2.0, ((0, 4),))
    output_gradient = scatter_about(streams_of[11], (MICRO, TOKENS, D), 1.0, 6.0, ((1, 32),))
    return {"block_entry_states": block_entry_states, "document_labels": document_labels, "token_assignments": token_assignments, "worker_quota_tallies": worker_quota_tallies, "rescale_factors_both": rescale_factors_both, "triple_projection_matrix": triple_projection_matrix, "probe_lookup_scalers": probe_lookup_scalers, "heads_merge_matrix": heads_merge_matrix, "dispatcher_matrix": dispatcher_matrix, "specialist_widen_matrix": specialist_widen_matrix, "specialist_shrink_matrix": specialist_shrink_matrix, "output_gradient": output_gradient}


EPS = 1e-05
THETA = 10000.0
NEG = -1e+30
HIGH = lax.Precision.HIGHEST

@jax.custom_vjp
def low(v):
    return lax.optimization_barrier(v.astype(jnp.bfloat16)).astype(jnp.float32)

@jax.custom_vjp
def low_back(v):
    return v

def low_keep(v):
    return (low(v), None)

def low_pass(kept, grad):
    return (grad,)

def back_keep(v):
    return (v, None)

def back_low(kept, grad):
    return (low(grad),)
low.defvjp(low_keep, low_pass)
low_back.defvjp(back_keep, back_low)

def apply_silu(content_vectors):
    return content_vectors * jax.nn.sigmoid(content_vectors)

def rms_scale(content_vectors, gain):
    return content_vectors * lax.rsqrt(lax.optimization_barrier(jnp.mean(content_vectors * content_vectors, axis=-1, keepdims=True)) + EPS) * gain

def softmax_rows(scores):
    highest = lax.optimization_barrier(jnp.max(scores, axis=-1, keepdims=True))
    exponent = jnp.exp(scores - highest)
    return exponent / lax.optimization_barrier(jnp.sum(exponent, axis=-1, keepdims=True))

def rope_tables(length, head_dim):
    half = head_dim // 2
    freq = THETA ** (-jnp.arange(half, dtype=jnp.float32) * 2.0 / head_dim)
    angle = jnp.arange(length, dtype=jnp.float32)[:, None] * freq[None, :]
    angle = jnp.concatenate([angle, angle], axis=-1)
    return (jnp.cos(angle), jnp.sin(angle))

def rotate_fwd(content_vectors, rotary_cos_values, rotary_sin_values):
    half = content_vectors.shape[-1] // 2
    turned = jnp.concatenate([-content_vectors[..., half:], content_vectors[..., :half]], axis=-1)
    return content_vectors * rotary_cos_values[:, None, :] + turned * rotary_sin_values[:, None, :]

def bin_start_shifts(pick_routed_workers, worker_quota_tallies):
    blocks = pick_routed_workers.reshape(SEQ // TOK_DEV, TOK_DEV, TOP)
    bucket_agreements = (blocks[..., None] == jnp.arange(EXPERTS, dtype=jnp.int32)).astype(jnp.int32)
    counts = lax.optimization_barrier(jnp.sum(bucket_agreements, axis=2))
    prior = jnp.cumsum(counts, axis=1) - counts
    bin_start_shift = lax.optimization_barrier(jnp.sum(bucket_agreements * prior[:, :, None, :], axis=-1))
    quota_upper_bound = lax.optimization_barrier(jnp.sum(bucket_agreements * worker_quota_tallies, axis=-1))
    return (bin_start_shift.reshape(SEQ, TOP), (bin_start_shift < quota_upper_bound).reshape(SEQ, TOP))

def transformer_block(skip_connection_sum, scaling_factors, triple_projection_matrix, probe_lookup_scalers, heads_merge_matrix, dispatcher_matrix, specialist_widen_matrix, specialist_shrink_matrix, document_label, pick_routed_workers, worker_quota_tallies, rotary_cos_values, rotary_sin_values):
    scale = 1.0 / math.sqrt(HD)
    attn_in = low(rms_scale(skip_connection_sum, scaling_factors[0]))
    projected = low_back(jnp.einsum('td,dcf->tcf', attn_in, triple_projection_matrix, precision=HIGH))
    shape_heads = (SEQ, HEADS, HD)
    queries = low(rotate_fwd(rms_scale(projected[:, 0], probe_lookup_scalers[0]).reshape(shape_heads), rotary_cos_values, rotary_sin_values))
    keys = low(rotate_fwd(rms_scale(projected[:, 1], probe_lookup_scalers[1]).reshape(shape_heads), rotary_cos_values, rotary_sin_values))
    values = low(projected[:, 2].reshape(shape_heads))
    place_ids = jnp.arange(SEQ, dtype=jnp.int32)
    allowed = (document_label[:, None] == document_label[None, :]) & (place_ids[None, :] <= place_ids[:, None])

    def one_head(operands):
        query_head, key_head, value_head = operands
        scores = low_back(jnp.dot(query_head, key_head.T, precision=HIGH) * scale)
        weights = softmax_rows(jnp.where(allowed, scores, NEG))
        return jnp.dot(low(weights), value_head, precision=HIGH)
    heads_out = lax.map(jax.checkpoint(one_head), (queries.transpose(1, 0, 2), keys.transpose(1, 0, 2), values.transpose(1, 0, 2)))
    mixed = low_back(low(heads_out.transpose(1, 0, 2).reshape(SEQ, D)))
    hidden = skip_connection_sum + low_back(jnp.dot(mixed, heads_merge_matrix, precision=HIGH))
    ffn_in = low(rms_scale(hidden, scaling_factors[1]))
    router_probs = softmax_rows(jnp.dot(ffn_in, dispatcher_matrix, precision=HIGH))
    bin_start_shift, kept_indicator_array = bin_start_shifts(pick_routed_workers, worker_quota_tallies)
    bucket_agreements = pick_routed_workers[..., None] == jnp.arange(EXPERTS, dtype=jnp.int32)
    router_coefficient = lax.optimization_barrier(jnp.sum(jnp.where(bucket_agreements, router_probs[:, None, :], 0.0), axis=-1))
    mixing_coefficient = jnp.where(kept_indicator_array, router_coefficient, 0.0)
    group_holding = (jnp.arange(SEQ, dtype=jnp.int32) // TOK_DEV)[:, None]
    seat_breadth = SEQ // TOK_DEV * PER_GROUP_CAP
    destination_spot = jnp.where(kept_indicator_array, group_holding * PER_GROUP_CAP + bin_start_shift, seat_breadth)
    spread_rows = jnp.broadcast_to(ffn_in[:, None, :], (SEQ, TOP, D))
    filled = jnp.zeros((EXPERTS, seat_breadth + 1, D), jnp.float32).at[pick_routed_workers, destination_spot].set(spread_rows)
    filled = low_back(filled[:, :seat_breadth])
    gate_up = low_back(jnp.einsum('erd,edf->erf', filled, specialist_widen_matrix, precision=HIGH))
    act = low(apply_silu(gate_up[..., :FF]) * gate_up[..., FF:])
    result = low_back(low(jnp.einsum('erf,efd->erd', act, specialist_shrink_matrix, precision=HIGH)))
    returned_lines = result[pick_routed_workers, jnp.minimum(destination_spot, seat_breadth - 1)]
    return hidden + lax.optimization_barrier(jnp.sum(mixing_coefficient[..., None] * returned_lines, axis=1))

def reference(block_entry_states, document_labels, token_assignments, worker_quota_tallies, rescale_factors_both, triple_projection_matrix, probe_lookup_scalers, heads_merge_matrix, dispatcher_matrix, specialist_widen_matrix, specialist_shrink_matrix, output_gradient):
    weights = tuple((w.astype(jnp.float32) for w in (rescale_factors_both, triple_projection_matrix, probe_lookup_scalers, heads_merge_matrix, dispatcher_matrix, specialist_widen_matrix, specialist_shrink_matrix)))
    count = block_entry_states.shape[0] * block_entry_states.shape[1] // SEQ
    inputs = block_entry_states.astype(jnp.float32).reshape(count, SEQ, D)
    incoming = output_gradient.astype(jnp.float32).reshape(count, SEQ, D)
    seg_all = document_labels.reshape(count, SEQ)
    route_all = token_assignments.reshape(count, SEQ, TOP)
    rotary_cos_values, rotary_sin_values = rope_tables(SEQ, HD)

    def one_sequence(totals, operands):
        skip_connection_sum, grad_out, document_label, pick_routed_workers = operands

        def forward(content_vectors, *block_arguments):
            return transformer_block(content_vectors, *block_arguments, document_label, pick_routed_workers, worker_quota_tallies, rotary_cos_values, rotary_sin_values)
        result, pull = jax.vjp(forward, skip_connection_sum, *weights)
        pulled = pull(grad_out)
        totals = tuple((total + derivative for total, derivative in zip(totals, pulled[1:])))
        return (totals, (result.astype(jnp.bfloat16), pulled[0]))
    start = tuple((jnp.zeros_like(w) for w in weights))
    totals, (results, grad_rows) = lax.scan(one_sequence, start, (inputs, incoming, seg_all, route_all))
    return (results.reshape(block_entry_states.shape), grad_rows.reshape(block_entry_states.shape), totals[0], totals[1], totals[2], totals[3], totals[4], totals[5], totals[6])
```

```python
import functools
import math

import jax
import jax.numpy as jnp
from jax import lax
from jax.experimental import pallas as pl
from jax.experimental.pallas import tpu as pltpu
from jax.sharding import PartitionSpec as P

HD = 128
TOP = 8
EPS = 1e-05
THETA = 10000.0
NEG = -1e30
HIGH = lax.Precision.HIGHEST
ALL = ("grp", "ep")
MESH = pl.DeviceIdType.MESH
ROWS = 16
BF = jnp.bfloat16
F32 = jnp.float32


def apply_silu(v):
    return v * jax.nn.sigmoid(v)


def rope_tables(length, head_dim):
    half = head_dim // 2
    freq = THETA ** (-jnp.arange(half, dtype=F32) * 2.0 / head_dim)
    angle = jnp.arange(length, dtype=F32)[:, None] * freq[None, :]
    angle = jnp.concatenate([angle, angle], axis=-1)
    return (jnp.cos(angle), jnp.sin(angle))


def swap_halves(v):
    half = v.shape[-1] // 2
    return jnp.concatenate([v[..., half:], v[..., :half]], axis=-1)


def mesh_sizes(groups, parts):
    major = 4 if groups % 4 == 0 else groups
    return major, groups // major, parts // 2


class Line:
    def __init__(self, size, place, step):
        self.size, self.place, self.step = size, place, step

    def at(self, hops):
        return (
            lax.axis_index("grp") + hops * self.step[0],
            lax.axis_index("ep") + hops * self.step[1],
        )


def lines(groups, parts):
    major, minor, xs = mesh_sizes(groups, parts)
    g, e = lax.axis_index("grp"), lax.axis_index("ep")
    core = lax.rem(e, 2)
    x_pos, minor_pos = lax.div(e, 2), lax.rem(g, minor)
    if xs == minor:
        first = Line(xs, jnp.where(core == 0, x_pos, minor_pos), (core, 2 - 2 * core))
        second = Line(xs, jnp.where(core == 0, minor_pos, x_pos), (1 - core, 2 * core))
    else:
        first = Line(xs, x_pos, (0, 2))
        second = Line(minor, minor_pos, (1, 0))
    return Line(2, core, (0, 1)), first, second, Line(major, lax.div(g, minor), (minor, 0))


def greet(some):
    barrier = pltpu.get_barrier_semaphore()
    peers = 0
    for line in some:
        if line.size == 2:
            pl.semaphore_signal(barrier, inc=1, device_id=line.at(1 - 2 * line.place), device_id_type=MESH)
            peers = peers + 1
        else:
            for way, there in ((1, line.place < line.size - 1), (-1, line.place > 0)):

                @pl.when(there)
                def _(line=line, way=way):
                    pl.semaphore_signal(barrier, inc=1, device_id=line.at(way), device_id_type=MESH)

                peers = peers + there.astype(jnp.int32)
    pl.semaphore_wait(barrier, peers)


def remote(src, dst, send, recv, target):
    return pltpu.make_async_remote_copy(
        src_ref=src, dst_ref=dst, send_sem=send, recv_sem=recv, device_id=target, device_id_type=MESH
    )


class Hop:
    def __init__(self, legs, after=None):
        self.legs, self.after = legs, after

    def _each(self, which, act):
        for leg in self.legs:
            if leg[which] is None:
                act(leg)
            else:
                pl.when(leg[which])(functools.partial(act, leg))

    def start(self):
        self._each(0, lambda leg: leg[2]().start())

    def arrive(self):
        def act(leg):
            leg[3]().wait_recv()
            if leg[4] is not None:
                leg[4]()

        self._each(1, act)

    def sent(self):
        self._each(0, lambda leg: leg[2]().wait_send())


def gather_hops(line, at, send, recv):
    n, a = line.size, line.place
    if n == 2:
        mine, theirs, peer = at(a), at(1 - a), line.at(1 - 2 * a)
        return [
            Hop([(None, None, lambda: remote(mine, mine, send(0), recv(0), peer),
                  lambda: remote(theirs, theirs, send(0), recv(0), peer), None)])
        ]
    hops = []
    for s in range(1, n):
        legs = []
        for d, way in enumerate((1, -1)):
            k = (s - 1) * 2 + d
            out = a - way * (s - 1)
            into = a - way * s
            sends = (out >= 0) & (out < n) & (a + way >= 0) & (a + way < n)
            gets = (into >= 0) & (into < n)
            out, into = jnp.clip(out, 0, n - 1), jnp.clip(into, 0, n - 1)
            legs.append((
                sends, gets,
                lambda out=out, way=way, k=k: remote(at(out), at(out), send(k), recv(k), line.at(way)),
                lambda into=into, way=way, k=k: remote(at(into), at(into), send(k), recv(k), line.at(-way)),
                None,
            ))
        hops.append(Hop(legs))
    return hops


def reduce_hops(line, acc, land, add, send, recv):
    n, a = line.size, line.place
    if n == 2:
        peer = line.at(1 - 2 * a)
        return [
            Hop([(None, None, lambda: remote(acc(1 - a), land(0), send(0), recv(0), peer),
                  lambda: remote(land(0), land(0), send(0), recv(0), peer),
                  lambda: add(acc(a), land(0)))])
        ]
    hops = []
    for s in range(n - 1):
        legs = []
        for d, way in enumerate((1, -1)):
            k = s * 2 + d
            b = a if way == 1 else n - 1 - a
            sends = (b <= s) & (b < n - 1)
            gets = (b - 1 <= s) & (b >= 1)
            out = b + n - 1 - s
            into = b + n - 2 - s
            out, into = jnp.clip(out, 0, n - 1), jnp.clip(into, 0, n - 1)
            if way == -1:
                out, into = n - 1 - out, n - 1 - into
            legs.append((
                sends, gets,
                lambda out=out, way=way, k=k: remote(acc(out), land(k), send(k), recv(k), line.at(way)),
                lambda way=way, k=k: remote(land(k), land(k), send(k), recv(k), line.at(-way)),
                lambda into=into, k=k: add(acc(into), land(k)),
            ))
        hops.append(Hop(legs))
    return hops


def hop_count(n):
    return 1 if n == 2 else n - 1


def leg_count(n):
    return 1 if n == 2 else 2 * (n - 1)


def flow(chains):
    depth, count = max(len(c) for c in chains), len(chains)
    for t in range(count + depth):
        for k in range(count):
            i = t - k
            if 1 <= i <= len(chains[k]):
                chains[k][i - 1].arrive()
            if 0 <= i < len(chains[k]):
                chains[k][i].start()
    for chain in chains:
        for hop in chain:
            hop.sent()


def add(acc, land):
    lead = acc.shape[:-2]

    def one(i):
        where = []
        for size in reversed(lead):
            where.insert(0, lax.rem(i, size))
            i = lax.div(i, size)
        where = tuple(where) + (slice(None), slice(None))
        acc[where] = (acc[where].astype(F32) + land[where].astype(F32)).astype(acc.dtype)

    if lead:
        pl.loop(0, math.prod(lead))(one)
    else:
        one(0)


def gather_kernel(groups, parts, x, out, local, send, recv):
    core, first, second, long = lines(groups, parts)
    c, p, q, z = core.place, first.place, second.place, long.place
    greet([core, first, second, long])
    chunks = x.shape[0]
    own = [pltpu.make_async_copy(x.at[k], out.at[k, c, p, q, z], local.at[k]) for k in range(chunks)]
    for copy in own:
        copy.start()
    chains = []
    for k in range(chunks):
        base = [0]

        def sems(n, k=k, base=base):
            b = base[0]
            base[0] += leg_count(n)
            return (lambda i: send.at[k, b + i]), (lambda i: recv.at[k, b + i])

        chain = []
        chain += gather_hops(long, lambda i, k=k: out.at[k, c, p, q, i], *sems(long.size))
        chain += gather_hops(second, lambda i, k=k: out.at[k, c, p, i], *sems(second.size))
        chain += gather_hops(first, lambda i, k=k: out.at[k, c, i], *sems(first.size))
        chain += gather_hops(core, lambda i, k=k: out.at[k, i], *sems(2))
        chains.append(chain)
    for copy in own:
        copy.wait()
    flow(chains)


def gather_all(x, collective_id):
    groups, parts = lax.axis_size("grp"), lax.axis_size("ep")
    major, minor, xs = mesh_sizes(groups, parts)
    width = x.shape[-1]
    x = x.reshape(-1, ROWS, width)
    legs = sum(leg_count(n) for n in (2, xs, minor, major))
    chunks = x.shape[0]
    return pl.pallas_call(
        functools.partial(gather_kernel, groups, parts),
        out_shape=jax.ShapeDtypeStruct((chunks, 2, xs, minor, major, ROWS, width), x.dtype),
        in_specs=[pl.BlockSpec(memory_space=pl.ANY)],
        out_specs=pl.BlockSpec(memory_space=pl.ANY),
        scratch_shapes=[
            pltpu.SemaphoreType.DMA((chunks,)),
            pltpu.SemaphoreType.DMA((chunks, legs)),
            pltpu.SemaphoreType.DMA((chunks, legs)),
        ],
        compiler_params=pltpu.CompilerParams(collective_id=collective_id, has_side_effects=True),
    )(x)


def scatter_kernel(groups, parts, part, out, acc, land_c, land_p, land_q, land_z, local, send, recv):
    core, first, second, long = lines(groups, parts)
    c, p, q, z = core.place, first.place, second.place, long.place
    chunks = part.shape[0]
    own = [pltpu.make_async_copy(part.at[k, c], acc.at[k], local.at[k]) for k in range(chunks)]
    for copy in own:
        copy.start()
    greet([core, first, second, long])
    chains = []
    for k in range(chunks):
        base = [0]

        def sems(n, k=k, base=base):
            b = base[0]
            base[0] += leg_count(n)
            return (lambda i: send.at[k, b + i]), (lambda i: recv.at[k, b + i])

        def add_own(acc_ref, land_ref, k=k):
            own[k].wait()
            add(acc_ref, land_ref)

        s, r = sems(2)
        peer = core.at(1 - 2 * c)
        other = part.at[k, 1 - c]
        chain = [Hop([(
            None, None,
            lambda other=other, s=s, r=r, k=k: remote(other, land_c.at[k], s(0), r(0), peer),
            lambda s=s, r=r, k=k: remote(land_c.at[k], land_c.at[k], s(0), r(0), peer),
            lambda k=k, add_own=add_own: add_own(acc.at[k], land_c.at[k]),
        )])]
        chain += reduce_hops(first, lambda i, k=k: acc.at[k, i], lambda i, k=k: land_p.at[k, i], add, *sems(first.size))
        chain += reduce_hops(second, lambda i, k=k: acc.at[k, p, i], lambda i, k=k: land_q.at[k, i], add, *sems(second.size))
        chain += reduce_hops(long, lambda i, k=k: acc.at[k, p, q, i], lambda i, k=k: land_z.at[k, i], add, *sems(long.size))
        chains.append(chain)
    flow(chains)
    for k in range(chunks):
        out[k] = acc[k, p, q, z]


def scatter_all(part, collective_id):
    groups, parts = lax.axis_size("grp"), lax.axis_size("ep")
    major, minor, xs = mesh_sizes(groups, parts)
    legs = sum(leg_count(n) for n in (2, xs, minor, major))
    chunks, width = part.shape[0], part.shape[-1]
    unit = 2 * ROWS * width
    need = unit * (2 * xs * minor * major + leg_count(xs) * minor * major + leg_count(minor) * major + leg_count(major) + 2)
    per = chunks
    while per > 1 and per * need > 44 * 2**20:
        per //= 2
    call = pl.pallas_call(
        functools.partial(scatter_kernel, groups, parts),
        out_shape=jax.ShapeDtypeStruct((per, ROWS, width), BF),
        in_specs=[pl.BlockSpec(memory_space=pl.ANY)],
        out_specs=pl.BlockSpec(memory_space=pltpu.VMEM),
        scratch_shapes=[
            pltpu.VMEM((per, xs, minor, major, ROWS, width), BF),
            pltpu.VMEM((per, xs, minor, major, ROWS, width), BF),
            pltpu.VMEM((per, leg_count(xs), minor, major, ROWS, width), BF),
            pltpu.VMEM((per, leg_count(minor), major, ROWS, width), BF),
            pltpu.VMEM((per, leg_count(major), ROWS, width), BF),
            pltpu.SemaphoreType.DMA((per,)),
            pltpu.SemaphoreType.DMA((per, legs)),
            pltpu.SemaphoreType.DMA((per, legs)),
        ],
        compiler_params=pltpu.CompilerParams(
            collective_id=collective_id, has_side_effects=True, vmem_limit_bytes=56 * 2**20
        ),
    )
    return jnp.concatenate([call(part[i:i + per]) for i in range(0, chunks, per)]) if per < chunks else call(part)


def total_kernel(groups, parts, spans, *refs):
    count = len(spans)
    ins, outs = refs[:count], refs[count:2 * count]
    acc, land_y, land_z = refs[2 * count:3 * count], refs[3 * count:4 * count], refs[4 * count:5 * count]
    local, stored, send, recv = refs[5 * count:]
    major, minor, _ = mesh_sizes(groups, parts)
    g = lax.axis_index("grp")
    short = Line(minor, lax.rem(g, minor), (1, 0))
    long = Line(major, lax.div(g, minor), (minor, 0))
    y, z = short.place, long.place
    loads, chains, number = [], [], 0
    for j in range(count):
        for k in range(spans[j]):
            load = pltpu.make_async_copy(ins[j].at[k], acc[j].at[k], local.at[number])
            load.start()
            loads.append(load)
            store = pltpu.make_async_copy(acc[j].at[k, y, z], outs[j].at[k, y, z], stored.at[number])
            base = [0]

            def sems(n, number=number, base=base):
                b = base[0]
                base[0] += leg_count(n)
                return (lambda i: send.at[number, b + i]), (lambda i: recv.at[number, b + i])

            down = reduce_hops(short, lambda i, j=j, k=k: acc[j].at[k, i], lambda i, j=j, k=k: land_y[j].at[k, i], add, *sems(minor))
            down += reduce_hops(long, lambda i, j=j, k=k: acc[j].at[k, y, i], lambda i, j=j, k=k: land_z[j].at[k, i], add, *sems(major))
            up = gather_hops(long, lambda i, j=j, k=k: outs[j].at[k, y, i], *sems(major))
            up += gather_hops(short, lambda i, j=j, k=k: outs[j].at[k, i], *sems(minor))
            chains.append((load, down, store, up))
            number += 1
    greet([short, long])
    whole = []
    for load, down, store, up in chains:
        hops = down + up
        turn = len(down)

        class Loaded:
            def __init__(self, hop, before):
                self.hop, self.before = hop, before

            def start(self):
                self.before()
                self.hop.start()

            def arrive(self):
                self.hop.arrive()

            def sent(self):
                self.hop.sent()

        def put(store=store):
            store.start()
            store.wait()

        hops[0] = Loaded(hops[0], load.wait)
        hops[turn] = Loaded(hops[turn], put)
        whole.append(hops)
    flow(whole)


def total_over_groups(arrays, spans, collective_id):
    groups, parts = lax.axis_size("grp"), lax.axis_size("ep")
    major, minor, _ = mesh_sizes(groups, parts)
    legs = 2 * (leg_count(minor) + leg_count(major))
    total = sum(spans)
    any_spec = pl.BlockSpec(memory_space=pl.ANY)
    scratch = [pltpu.VMEM(a.shape, BF) for a in arrays]
    scratch += [pltpu.VMEM((a.shape[0], leg_count(minor)) + a.shape[2:], BF) for a in arrays]
    scratch += [pltpu.VMEM((a.shape[0], leg_count(major)) + a.shape[3:], BF) for a in arrays]
    return pl.pallas_call(
        functools.partial(total_kernel, groups, parts, spans),
        out_shape=[jax.ShapeDtypeStruct(a.shape, BF) for a in arrays],
        in_specs=[any_spec] * len(arrays),
        out_specs=[any_spec] * len(arrays),
        scratch_shapes=scratch + [
            pltpu.SemaphoreType.DMA((total,)),
            pltpu.SemaphoreType.DMA((total,)),
            pltpu.SemaphoreType.DMA((total, legs)),
            pltpu.SemaphoreType.DMA((total, legs)),
        ],
        compiler_params=pltpu.CompilerParams(
            collective_id=collective_id, has_side_effects=True, vmem_limit_bytes=48 * 2**20
        ),
    )(*arrays)


def per_device(
    block_entry_states,
    document_labels,
    token_assignments,
    worker_quota_tallies,
    rescale_factors_both,
    triple_projection_matrix,
    probe_lookup_scalers,
    heads_merge_matrix,
    dispatcher_matrix,
    specialist_widen_matrix,
    specialist_shrink_matrix,
    output_gradient,
):
    micro, local_rows, width = block_entry_states.shape
    groups, parts = lax.axis_size("grp"), lax.axis_size("ep")
    major, minor, xs = mesh_sizes(groups, parts)
    group = lax.axis_index("grp")
    part = lax.axis_index("ep")
    seq_len = document_labels.shape[1]
    experts = dispatcher_matrix.shape[1]
    local_exp = specialist_widen_matrix.shape[0]
    inner = specialist_shrink_matrix.shape[1]
    share = inner // groups
    local_width = triple_projection_matrix.shape[2]
    heads = local_width // HD
    scale = 1.0 / math.sqrt(HD)
    gains = rescale_factors_both.astype(F32)
    head_gains = probe_lookup_scalers.astype(F32)
    cos, sin = rope_tables(seq_len, HD)
    signed_sin = jnp.concatenate([-sin[:, : HD // 2], sin[:, HD // 2:]], axis=-1)
    expert_ids = jnp.arange(experts, dtype=jnp.int32)

    hits = (token_assignments[..., None] == expert_ids).astype(jnp.int32)
    counts = jnp.sum(hits, axis=2)
    prior = jnp.cumsum(counts, axis=1) - counts
    keep = jnp.where((counts > 0) & (prior < worker_quota_tallies), 1.0, 0.0).astype(F32)
    keep_all = lax.all_gather(keep.astype(BF), ALL, axis=1, tiled=True).astype(F32)
    keep_all = keep_all.reshape(micro, major, minor, xs, 2, local_rows // ROWS, ROWS, experts)
    one = keep_all[:, :, :, :, 0].transpose(0, 4, 3, 2, 1, 5, 6)
    two = keep_all[:, :, :, :, 1].transpose(0, 4, 3, 2, 1, 5, 6)
    if xs == minor:
        two = keep_all[:, :, :, :, 1].transpose(0, 4, 2, 3, 1, 5, 6)
    keep_all = jnp.stack([one, two], axis=2).reshape(-1, experts)

    widen = specialist_widen_matrix.reshape(local_exp, width, 2, groups, share)
    widen = lax.dynamic_index_in_dim(widen, group, 3, keepdims=False)
    widen = widen.transpose(1, 2, 0, 3).reshape(width, 2 * local_exp * share)
    shrink = specialist_shrink_matrix.reshape(local_exp, groups, share, width)
    shrink = lax.dynamic_index_in_dim(shrink, group, 1, keepdims=False).reshape(local_exp * share, width)

    dy_all = gather_all(output_gradient, 0)
    chunk_shape = dy_all.shape[:-1]
    dy_all = dy_all.reshape(-1, width)

    skip = block_entry_states.astype(F32)
    inv_first = lax.rsqrt(jnp.mean(skip * skip, axis=-1, keepdims=True) + EPS)
    hat_first = skip * inv_first
    attn_in = (hat_first * gains[0]).astype(BF)
    gathered = lax.all_gather(attn_in, "ep", axis=1, tiled=True)
    projected = jnp.einsum("mtd,dcf->cmtf", gathered, triple_projection_matrix, preferred_element_type=F32)
    qk_raw = projected[:2]
    squares = lax.psum(jnp.sum(qk_raw * qk_raw, axis=-1), "ep")
    qk_inv = lax.rsqrt(squares / width + EPS)[..., None]
    qk_hat = qk_raw * qk_inv
    qk_n = (qk_hat * head_gains[:, None, None, :]).reshape(2, micro, seq_len, heads, HD).transpose(0, 1, 3, 2, 4)
    qk = (qk_n * cos + swap_halves(qk_n) * signed_sin).astype(BF)
    queries, keys = qk[0], qk[1]
    values = projected[2].astype(BF).reshape(micro, seq_len, heads, HD).transpose(0, 2, 1, 3)
    places = jnp.arange(seq_len, dtype=jnp.int32)
    allowed = (document_labels[:, :, None] == document_labels[:, None, :]) & (places[None, :] <= places[:, None])
    scores = jnp.einsum("mhsd,mhtd->mhst", queries, keys, preferred_element_type=F32) * scale
    scores = jnp.where(allowed[:, None], scores, NEG)
    exponent = jnp.exp(scores - jnp.max(scores, axis=-1, keepdims=True))
    weights = exponent / jnp.sum(exponent, axis=-1, keepdims=True)
    weights_low = weights.astype(BF)
    mixed = jnp.einsum("mhst,mhtd->mshd", weights_low, values, preferred_element_type=F32)
    mixed = mixed.astype(BF).reshape(micro, seq_len, local_width)
    attention = lax.psum_scatter(
        jnp.einsum("msf,fd->msd", mixed, heads_merge_matrix, preferred_element_type=F32).astype(BF),
        "ep", scatter_dimension=1, tiled=True,
    ).astype(F32)

    hidden = skip + attention
    inv_second = lax.rsqrt(jnp.mean(hidden * hidden, axis=-1, keepdims=True) + EPS)
    hat_second = hidden * inv_second
    ffn_in = (hat_second * gains[1]).astype(BF)
    x_all = gather_all(ffn_in, 1).reshape(-1, width)
    router = jax.nn.softmax(jnp.dot(x_all, dispatcher_matrix, preferred_element_type=F32), axis=-1)
    gate = lax.dynamic_slice_in_dim(router * keep_all, part * local_exp, local_exp, axis=1)
    gate = jnp.repeat(gate, share, axis=1)
    gate_up = jnp.dot(x_all, widen, preferred_element_type=F32)
    g, u = gate_up[:, : local_exp * share], gate_up[:, local_exp * share:]
    sigma = jax.nn.sigmoid(g)
    act = g * sigma * u
    gated = (gate * act).astype(BF)
    moe_part = jnp.dot(gated, shrink, preferred_element_type=F32).astype(BF)
    d_raw = lax.dot_general(dy_all, shrink, (((1,), (1,)), ((), ())), preferred_element_type=F32)
    d_gate = jnp.sum((act * d_raw).reshape(-1, local_exp, share), axis=-1)
    d_act = gate * d_raw
    d_gu = jnp.concatenate([d_act * u * sigma * (1.0 + g * (1.0 - sigma)), d_act * (g * sigma)], axis=1).astype(BF)
    dx_part = lax.dot_general(d_gu, widen, (((1,), (1,)), ((), ())), preferred_element_type=F32).astype(BF)
    lanes = jnp.arange(128, dtype=jnp.int32)
    place = (lanes[None, :] == part * local_exp + jnp.arange(local_exp, dtype=jnp.int32)[:, None])
    d_gate = jnp.sum(jnp.where(place[None], d_gate[:, :, None], 0.0), axis=1)
    dx_part = jnp.concatenate([dx_part, d_gate.astype(BF)], axis=1)
    dx_sum = scatter_all(dx_part.reshape(chunk_shape + (width + 128,)), 2).astype(F32)
    dx_sum = dx_sum.reshape(micro, local_rows, width + 128)
    grad_widen = lax.dot_general(x_all, d_gu, (((0,), (0,)), ((), ())), preferred_element_type=F32)
    grad_shrink = lax.dot_general(gated, dy_all, (((0,), (0,)), ((), ())), preferred_element_type=F32)
    grad_widen = grad_widen.astype(BF).reshape(groups, width // groups, 2, local_exp, share)
    grad_widen = lax.all_to_all(grad_widen, "grp", 0, 0, tiled=True)
    grad_widen = grad_widen.transpose(3, 1, 2, 0, 4).reshape(local_exp, width // groups, 2 * inner).astype(F32)
    grad_shrink = grad_shrink.reshape(local_exp, share, width)
    moe = scatter_all(moe_part.reshape(chunk_shape + (width,)), 3).astype(F32).reshape(micro, local_rows, width)
    output = (hidden + moe).astype(BF)

    probs = jax.nn.softmax(jnp.einsum("mtd,de->mte", ffn_in, dispatcher_matrix, preferred_element_type=F32), axis=-1)
    d_probs = dx_sum[..., width: width + experts] * keep
    d_logits = probs * (d_probs - jnp.sum(probs * d_probs, axis=-1, keepdims=True))
    d_ffn = dx_sum[..., :width] + jnp.einsum("mte,de->mtd", d_logits, dispatcher_matrix.astype(F32), precision=HIGH)
    grad_router = jnp.einsum("mtd,mte->ed", ffn_in.astype(F32), d_logits, precision=HIGH)
    scaled = d_ffn * gains[1]
    adjoint = output_gradient.astype(F32)
    d_hidden = adjoint + inv_second * (scaled - hat_second * jnp.mean(scaled * hat_second, axis=-1, keepdims=True))
    grad_second = jnp.sum(d_ffn * hat_second, axis=(0, 1))

    branch = lax.all_gather(d_hidden.astype(BF), "ep", axis=1, tiled=True)
    grad_out = jnp.einsum("msf,msd->fd", mixed, branch, preferred_element_type=F32)
    d_mixed = jnp.einsum("msd,fd->msf", branch, heads_merge_matrix, preferred_element_type=F32).astype(BF)
    d_mixed = d_mixed.reshape(micro, seq_len, heads, HD).transpose(0, 2, 1, 3)
    d_weights = jnp.einsum("mhsd,mhtd->mhst", d_mixed, values, preferred_element_type=F32)
    d_scores = (weights * (d_weights - jnp.sum(weights * d_weights, axis=-1, keepdims=True))).astype(BF)
    d_values = jnp.einsum("mhst,mhsd->mthd", weights_low, d_mixed, preferred_element_type=F32)
    d_queries = jnp.einsum("mhst,mhtd->mshd", d_scores, keys, preferred_element_type=F32) * scale
    d_keys = jnp.einsum("mhst,mhsd->mthd", d_scores, queries, preferred_element_type=F32) * scale
    d_qk = jnp.stack([d_queries, d_keys])
    d_qk = d_qk * cos[:, None] - swap_halves(d_qk) * signed_sin[:, None]
    d_qk = d_qk.reshape(2, micro, seq_len, local_width)
    scaled = d_qk * head_gains[:, None, None, :]
    inner_sums = lax.psum(jnp.sum(scaled * qk_hat, axis=-1), "ep")
    d_qk_raw = qk_inv * (scaled - qk_hat * (inner_sums / width)[..., None])
    grad_heads = jnp.sum(d_qk * qk_hat, axis=(1, 2))
    d_proj = jnp.concatenate([d_qk_raw, d_values.reshape(1, micro, seq_len, local_width)]).astype(BF)
    grad_qkv = jnp.einsum("mtd,cmtf->dcf", gathered, d_proj, preferred_element_type=F32)
    d_attn_in = lax.psum_scatter(
        jnp.einsum("cmtf,dcf->mtd", d_proj, triple_projection_matrix, preferred_element_type=F32).astype(BF),
        "ep", scatter_dimension=1, tiled=True,
    ).astype(F32)
    scaled = d_attn_in * gains[0]
    grad_input = d_hidden + inv_first * (scaled - hat_first * jnp.mean(scaled * hat_first, axis=-1, keepdims=True))
    grad_first = jnp.sum(d_attn_in * hat_first, axis=(0, 1))

    misc = jnp.concatenate([grad_first[None], grad_second[None], grad_router])
    misc = lax.psum(misc, "ep").reshape(-1)
    misc = jnp.concatenate([misc, grad_heads.reshape(-1)])
    small = major * minor * ROWS * 128
    misc_size = misc.shape[0]
    misc = jnp.pad(misc, (0, -misc_size % small)).reshape(1, minor, major, ROWS, -1).astype(BF)
    spans = 4
    qkv_cut = grad_qkv.astype(BF).reshape(spans, minor, major, -1, 3 * local_width)
    out_cut = grad_out.astype(BF).reshape(1, minor, major, -1, width)
    qkv_sum, out_sum, misc_sum = total_over_groups([qkv_cut, out_cut, misc], (spans, 1, 1), 4)
    qkv_sum = qkv_sum.reshape(grad_qkv.shape).astype(F32)
    out_sum = out_sum.reshape(grad_out.shape).astype(F32)
    misc_sum = misc_sum.reshape(-1)[:misc_size].astype(F32)
    rows = misc_sum[: (2 + experts) * width].reshape(2 + experts, width)
    return (
        output,
        grad_input,
        rows[:2],
        qkv_sum,
        misc_sum[(2 + experts) * width:].reshape(2, local_width),
        out_sum,
        rows[2:].T,
        grad_widen,
        grad_shrink,
    )


def solution(mesh):
    return jax.shard_map(
        per_device,
        mesh=mesh,
        in_specs=(
            P(None, ALL, None),
            P(None, "grp"),
            P(None, ALL, None),
            P(),
            P(),
            P(None, None, "ep"),
            P(None, "ep"),
            P("ep", None),
            P(),
            P("ep", None, None),
            P("ep", None, None),
            P(None, ALL, None),
        ),
        out_specs=(
            P(None, ALL, None),
            P(None, ALL, None),
            P(),
            P(None, None, "ep"),
            P(None, "ep"),
            P("ep", None),
            P(),
            P("ep", "grp", None),
            P("ep", "grp", None),
        ),
        check_vma=False,
    )
```

```python
import functools
import math

import jax
import jax.numpy as jnp
from jax import lax
from jax.experimental import pallas as pl
from jax.experimental.pallas import tpu as pltpu
from jax.sharding import PartitionSpec as P

HD = 128
TOP = 8
EPS = 1e-05
THETA = 10000.0
NEG = -1e30
HIGH = lax.Precision.HIGHEST
ALL = ("grp", "ep")
MESH = pl.DeviceIdType.MESH
ROWS = 16
BF = jnp.bfloat16
F32 = jnp.float32


def apply_silu(v):
    return v * jax.nn.sigmoid(v)


def rope_tables(length, head_dim):
    half = head_dim // 2
    freq = THETA ** (-jnp.arange(half, dtype=F32) * 2.0 / head_dim)
    angle = jnp.arange(length, dtype=F32)[:, None] * freq[None, :]
    angle = jnp.concatenate([angle, angle], axis=-1)
    return (jnp.cos(angle), jnp.sin(angle))


def swap_halves(v):
    half = v.shape[-1] // 2
    return jnp.concatenate([v[..., half:], v[..., :half]], axis=-1)


def mesh_sizes(groups, parts):
    major = 4 if groups % 4 == 0 else groups
    return major, groups // major, parts // 2


class Line:
    def __init__(self, size, place, step):
        self.size, self.place, self.step = size, place, step

    def at(self, hops):
        return (
            lax.axis_index("grp") + hops * self.step[0],
            lax.axis_index("ep") + hops * self.step[1],
        )


def lines(groups, parts):
    major, minor, xs = mesh_sizes(groups, parts)
    g, e = lax.axis_index("grp"), lax.axis_index("ep")
    core = lax.rem(e, 2)
    x_pos, minor_pos = lax.div(e, 2), lax.rem(g, minor)
    if xs == minor:
        first = Line(xs, jnp.where(core == 0, x_pos, minor_pos), (core, 2 - 2 * core))
        second = Line(xs, jnp.where(core == 0, minor_pos, x_pos), (1 - core, 2 * core))
    else:
        first = Line(xs, x_pos, (0, 2))
        second = Line(minor, minor_pos, (1, 0))
    return Line(2, core, (0, 1)), first, second, Line(major, lax.div(g, minor), (minor, 0))


def greet(some):
    barrier = pltpu.get_barrier_semaphore()
    peers = 0
    for line in some:
        if line.size == 2:
            pl.semaphore_signal(barrier, inc=1, device_id=line.at(1 - 2 * line.place), device_id_type=MESH)
            peers = peers + 1
        else:
            for way, there in ((1, line.place < line.size - 1), (-1, line.place > 0)):

                @pl.when(there)
                def _(line=line, way=way):
                    pl.semaphore_signal(barrier, inc=1, device_id=line.at(way), device_id_type=MESH)

                peers = peers + there.astype(jnp.int32)
    pl.semaphore_wait(barrier, peers)


def greet_lines(some):
    barrier = pltpu.get_barrier_semaphore()
    for line in some:
        for j in range(1, line.size):
            to = lax.rem(line.place + j, line.size)
            pl.semaphore_signal(barrier, inc=1, device_id=line.at(to - line.place), device_id_type=MESH)
    pl.semaphore_wait(barrier, sum(line.size - 1 for line in some))


def remote(src, dst, send, recv, target):
    return pltpu.make_async_remote_copy(
        src_ref=src, dst_ref=dst, send_sem=send, recv_sem=recv, device_id=target, device_id_type=MESH
    )


class Hop:
    def __init__(self, legs, after=None):
        self.legs, self.after = legs, after

    def _each(self, which, act):
        for leg in self.legs:
            if leg[which] is None:
                act(leg)
            else:
                pl.when(leg[which])(functools.partial(act, leg))

    def start(self):
        self._each(0, lambda leg: leg[2]().start())

    def arrive(self):
        def act(leg):
            leg[3]().wait_recv()
            if leg[4] is not None:
                leg[4]()

        self._each(1, act)

    def sent(self):
        self._each(0, lambda leg: leg[2]().wait_send())


def gather_hops(line, at, send, recv):
    n, a = line.size, line.place
    if n == 2:
        mine, theirs, peer = at(a), at(1 - a), line.at(1 - 2 * a)
        return [
            Hop([(None, None, lambda: remote(mine, mine, send(0), recv(0), peer),
                  lambda: remote(theirs, theirs, send(0), recv(0), peer), None)])
        ]
    hops = []
    for s in range(1, n):
        legs = []
        for d, way in enumerate((1, -1)):
            k = (s - 1) * 2 + d
            out = a - way * (s - 1)
            into = a - way * s
            sends = (out >= 0) & (out < n) & (a + way >= 0) & (a + way < n)
            gets = (into >= 0) & (into < n)
            out, into = jnp.clip(out, 0, n - 1), jnp.clip(into, 0, n - 1)
            legs.append((
                sends, gets,
                lambda out=out, way=way, k=k: remote(at(out), at(out), send(k), recv(k), line.at(way)),
                lambda into=into, way=way, k=k: remote(at(into), at(into), send(k), recv(k), line.at(-way)),
                None,
            ))
        hops.append(Hop(legs))
    return hops


def reduce_hops(line, acc, land, add, send, recv):
    n, a = line.size, line.place
    if n == 2:
        peer = line.at(1 - 2 * a)
        return [
            Hop([(None, None, lambda: remote(acc(1 - a), land(0), send(0), recv(0), peer),
                  lambda: remote(land(0), land(0), send(0), recv(0), peer),
                  lambda: add(acc(a), land(0)))])
        ]
    hops = []
    for s in range(n - 1):
        legs = []
        for d, way in enumerate((1, -1)):
            k = s * 2 + d
            b = a if way == 1 else n - 1 - a
            sends = (b <= s) & (b < n - 1)
            gets = (b - 1 <= s) & (b >= 1)
            out = b + n - 1 - s
            into = b + n - 2 - s
            out, into = jnp.clip(out, 0, n - 1), jnp.clip(into, 0, n - 1)
            if way == -1:
                out, into = n - 1 - out, n - 1 - into
            legs.append((
                sends, gets,
                lambda out=out, way=way, k=k: remote(acc(out), land(k), send(k), recv(k), line.at(way)),
                lambda way=way, k=k: remote(land(k), land(k), send(k), recv(k), line.at(-way)),
                lambda into=into, k=k: add(acc(into), land(k)),
            ))
        hops.append(Hop(legs))
    return hops


def hop_count(n):
    return 1 if n == 2 else n - 1


def leg_count(n):
    return 1 if n == 2 else 2 * (n - 1)


def flow(chains):
    depth, count = max(len(c) for c in chains), len(chains)
    for t in range(count + depth):
        for k in range(count):
            i = t - k
            if 1 <= i <= len(chains[k]):
                chains[k][i - 1].arrive()
            if 0 <= i < len(chains[k]):
                chains[k][i].start()
    for chain in chains:
        for hop in chain:
            hop.sent()


def add(acc, land):
    lead = acc.shape[:-2]

    def one(i):
        where = []
        for size in reversed(lead):
            where.insert(0, lax.rem(i, size))
            i = lax.div(i, size)
        where = tuple(where) + (slice(None), slice(None))
        acc[where] = (acc[where].astype(F32) + land[where].astype(F32)).astype(acc.dtype)

    if lead:
        pl.loop(0, math.prod(lead))(one)
    else:
        one(0)


def gather_kernel(groups, parts, x, out, local, send, recv):
    core, first, second, long = lines(groups, parts)
    c, p, q, z = core.place, first.place, second.place, long.place
    greet([core, first, second, long])
    chunks = x.shape[0]
    own = [pltpu.make_async_copy(x.at[k], out.at[k, c, p, q, z], local.at[k]) for k in range(chunks)]
    for copy in own:
        copy.start()
    chains = []
    for k in range(chunks):
        base = [0]

        def sems(n, k=k, base=base):
            b = base[0]
            base[0] += leg_count(n)
            return (lambda i: send.at[k, b + i]), (lambda i: recv.at[k, b + i])

        chain = []
        chain += gather_hops(long, lambda i, k=k: out.at[k, c, p, q, i], *sems(long.size))
        chain += gather_hops(second, lambda i, k=k: out.at[k, c, p, i], *sems(second.size))
        chain += gather_hops(first, lambda i, k=k: out.at[k, c, i], *sems(first.size))
        chain += gather_hops(core, lambda i, k=k: out.at[k, i], *sems(2))
        chains.append(chain)
    for copy in own:
        copy.wait()
    flow(chains)


def gather_all(x, collective_id):
    groups, parts = lax.axis_size("grp"), lax.axis_size("ep")
    major, minor, xs = mesh_sizes(groups, parts)
    width = x.shape[-1]
    x = x.reshape(-1, ROWS, width)
    legs = sum(leg_count(n) for n in (2, xs, minor, major))
    chunks = x.shape[0]
    return pl.pallas_call(
        functools.partial(gather_kernel, groups, parts),
        out_shape=jax.ShapeDtypeStruct((chunks, 2, xs, minor, major, ROWS, width), x.dtype),
        in_specs=[pl.BlockSpec(memory_space=pl.ANY)],
        out_specs=pl.BlockSpec(memory_space=pl.ANY),
        scratch_shapes=[
            pltpu.SemaphoreType.DMA((chunks,)),
            pltpu.SemaphoreType.DMA((chunks, legs)),
            pltpu.SemaphoreType.DMA((chunks, legs)),
        ],
        compiler_params=pltpu.CompilerParams(collective_id=collective_id, has_side_effects=True),
    )(x)


def scatter_kernel(groups, parts, part, out, acc, land_c, land_p, land_q, land_z, local, send, recv):
    core, first, second, long = lines(groups, parts)
    c, p, q, z = core.place, first.place, second.place, long.place
    chunks = part.shape[0]
    own = [pltpu.make_async_copy(part.at[k, c], acc.at[k], local.at[k]) for k in range(chunks)]
    for copy in own:
        copy.start()
    greet([core, first, second, long])
    chains = []
    for k in range(chunks):
        base = [0]

        def sems(n, k=k, base=base):
            b = base[0]
            base[0] += leg_count(n)
            return (lambda i: send.at[k, b + i]), (lambda i: recv.at[k, b + i])

        def add_own(acc_ref, land_ref, k=k):
            own[k].wait()
            add(acc_ref, land_ref)

        s, r = sems(2)
        peer = core.at(1 - 2 * c)
        other = part.at[k, 1 - c]
        chain = [Hop([(
            None, None,
            lambda other=other, s=s, r=r, k=k: remote(other, land_c.at[k], s(0), r(0), peer),
            lambda s=s, r=r, k=k: remote(land_c.at[k], land_c.at[k], s(0), r(0), peer),
            lambda k=k, add_own=add_own: add_own(acc.at[k], land_c.at[k]),
        )])]
        chain += reduce_hops(first, lambda i, k=k: acc.at[k, i], lambda i, k=k: land_p.at[k, i], add, *sems(first.size))
        chain += reduce_hops(second, lambda i, k=k: acc.at[k, p, i], lambda i, k=k: land_q.at[k, i], add, *sems(second.size))
        chain += reduce_hops(long, lambda i, k=k: acc.at[k, p, q, i], lambda i, k=k: land_z.at[k, i], add, *sems(long.size))
        chains.append(chain)
    flow(chains)
    for k in range(chunks):
        out[k] = acc[k, p, q, z]


def scatter_all(part, collective_id):
    groups, parts = lax.axis_size("grp"), lax.axis_size("ep")
    major, minor, xs = mesh_sizes(groups, parts)
    legs = sum(leg_count(n) for n in (2, xs, minor, major))
    chunks, width = part.shape[0], part.shape[-1]
    unit = 2 * ROWS * width
    need = unit * (2 * xs * minor * major + leg_count(xs) * minor * major + leg_count(minor) * major + leg_count(major) + 2)
    per = chunks
    while per > 1 and per * need > 44 * 2**20:
        per //= 2
    call = pl.pallas_call(
        functools.partial(scatter_kernel, groups, parts),
        out_shape=jax.ShapeDtypeStruct((per, ROWS, width), BF),
        in_specs=[pl.BlockSpec(memory_space=pl.ANY)],
        out_specs=pl.BlockSpec(memory_space=pltpu.VMEM),
        scratch_shapes=[
            pltpu.VMEM((per, xs, minor, major, ROWS, width), BF),
            pltpu.VMEM((per, xs, minor, major, ROWS, width), BF),
            pltpu.VMEM((per, leg_count(xs), minor, major, ROWS, width), BF),
            pltpu.VMEM((per, leg_count(minor), major, ROWS, width), BF),
            pltpu.VMEM((per, leg_count(major), ROWS, width), BF),
            pltpu.SemaphoreType.DMA((per,)),
            pltpu.SemaphoreType.DMA((per, legs)),
            pltpu.SemaphoreType.DMA((per, legs)),
        ],
        compiler_params=pltpu.CompilerParams(
            collective_id=collective_id, has_side_effects=True, vmem_limit_bytes=56 * 2**20
        ),
    )
    return jnp.concatenate([call(part[i:i + per]) for i in range(0, chunks, per)]) if per < chunks else call(part)


def total_kernel(groups, parts, spans, *refs):
    count = len(spans)
    ins, outs = refs[:count], refs[count:2 * count]
    acc, land_y, land_z = refs[2 * count:3 * count], refs[3 * count:4 * count], refs[4 * count:5 * count]
    local, stored, send, recv = refs[5 * count:]
    major, minor, _ = mesh_sizes(groups, parts)
    g = lax.axis_index("grp")
    short = Line(minor, lax.rem(g, minor), (1, 0))
    long = Line(major, lax.div(g, minor), (minor, 0))
    y, z = short.place, long.place
    loads, chains, number = [], [], 0
    for j in range(count):
        for k in range(spans[j]):
            load = pltpu.make_async_copy(ins[j].at[k], acc[j].at[k], local.at[number])
            load.start()
            loads.append(load)
            store = pltpu.make_async_copy(acc[j].at[k, y, z], outs[j].at[k, y, z], stored.at[number])
            base = [0]

            def sems(n, number=number, base=base):
                b = base[0]
                base[0] += leg_count(n)
                return (lambda i: send.at[number, b + i]), (lambda i: recv.at[number, b + i])

            down = reduce_hops(short, lambda i, j=j, k=k: acc[j].at[k, i], lambda i, j=j, k=k: land_y[j].at[k, i], add, *sems(minor))
            down += reduce_hops(long, lambda i, j=j, k=k: acc[j].at[k, y, i], lambda i, j=j, k=k: land_z[j].at[k, i], add, *sems(major))
            up = gather_hops(long, lambda i, j=j, k=k: outs[j].at[k, y, i], *sems(major))
            up += gather_hops(short, lambda i, j=j, k=k: outs[j].at[k, i], *sems(minor))
            chains.append((load, down, store, up))
            number += 1
    greet([short, long])
    whole = []
    for load, down, store, up in chains:
        hops = down + up
        turn = len(down)

        class Loaded:
            def __init__(self, hop, before):
                self.hop, self.before = hop, before

            def start(self):
                self.before()
                self.hop.start()

            def arrive(self):
                self.hop.arrive()

            def sent(self):
                self.hop.sent()

        def put(store=store):
            store.start()
            store.wait()

        hops[0] = Loaded(hops[0], load.wait)
        hops[turn] = Loaded(hops[turn], put)
        whole.append(hops)
    flow(whole)


def total_over_groups(arrays, spans, collective_id):
    groups, parts = lax.axis_size("grp"), lax.axis_size("ep")
    major, minor, _ = mesh_sizes(groups, parts)
    legs = 2 * (leg_count(minor) + leg_count(major))
    total = sum(spans)
    any_spec = pl.BlockSpec(memory_space=pl.ANY)
    scratch = [pltpu.VMEM(a.shape, BF) for a in arrays]
    scratch += [pltpu.VMEM((a.shape[0], leg_count(minor)) + a.shape[2:], BF) for a in arrays]
    scratch += [pltpu.VMEM((a.shape[0], leg_count(major)) + a.shape[3:], BF) for a in arrays]
    return pl.pallas_call(
        functools.partial(total_kernel, groups, parts, spans),
        out_shape=[jax.ShapeDtypeStruct(a.shape, BF) for a in arrays],
        in_specs=[any_spec] * len(arrays),
        out_specs=[any_spec] * len(arrays),
        scratch_shapes=scratch + [
            pltpu.SemaphoreType.DMA((total,)),
            pltpu.SemaphoreType.DMA((total,)),
            pltpu.SemaphoreType.DMA((total, legs)),
            pltpu.SemaphoreType.DMA((total, legs)),
        ],
        compiler_params=pltpu.CompilerParams(
            collective_id=collective_id, has_side_effects=True, vmem_limit_bytes=48 * 2**20
        ),
    )(*arrays)


def swap_legs(line, source, target, send, recv):
    n, a = line.size, line.place
    legs = []
    for j in range(1, n):
        to, off = lax.rem(a + j, n), lax.rem(a + n - j, n)
        legs.append((
            lambda to=to, j=j: remote(source(to), target(j - 1, a), send(j - 1), recv(j - 1), line.at(to - a)),
            lambda off=off, j=j: remote(target(j - 1, off), target(j - 1, off), send(j - 1), recv(j - 1), line.at(off - a)),
        ))
    return legs


def start_legs(legs):
    for out, _ in legs:
        out().start()


def end_legs(legs):
    for out, into in legs:
        into().wait_recv()
    for out, into in legs:
        out().wait_send()


def add_rows(acc, first, land, rows):
    @pl.loop(0, rows // ROWS)
    def _(i):
        here = pl.ds(pl.multiple_of(first + i * ROWS, ROWS), ROWS)
        there = pl.ds(pl.multiple_of(i * ROWS, ROWS), ROWS)
        acc[here, :] = (acc[here, :].astype(F32) + land[there, :].astype(F32)).astype(acc.dtype)


def experts_kernel(
    groups, parts, local_rows, ring, acc_ring, experts,
    x, dy, widen, shrink, dispatch, keep,
    summed, moe, grad_widen, grad_shrink,
    xs, dys, wide, down, sum_wide, sum_down, stage, acc, other, land_c, land_p, land_q, land_z,
    hid, raw, gated, d_gu, gate, d_gate,
    load, dy_sem, stage_sem, g_send, g_recv, s_send, s_recv,
):
    core, first, second, long = lines(groups, parts)
    c, p, q, z = core.place, first.place, second.place, long.place
    pn, qn, zn = first.size, second.size, long.size
    chunks, _, width = x.shape
    local_exp, inner = shrink.shape[0], shrink.shape[1]
    share = inner // groups
    group, part = lax.axis_index("grp"), lax.axis_index("ep")
    rz, rq, rp, rc = ROWS, ROWS * zn, ROWS * zn * qn, ROWS * zn * qn * pn
    rows = 2 * rc
    cuts = local_rows // ROWS
    base = part * local_exp
    pairs = local_exp // 2

    loads = []
    for e in range(local_exp):
        for half in range(2):
            to = (e // 2) * 4 * share + half * 2 * share + (e % 2) * share
            loads.append(pltpu.make_async_copy(
                widen.at[e, :, pl.ds(pl.multiple_of(half * inner + group * share, share), share)],
                wide.at[:, pl.ds(to, share)], load.at[2 * e + half]))
        loads.append(pltpu.make_async_copy(
            shrink.at[e, pl.ds(pl.multiple_of(group * share, share), share), :],
            down.at[pl.ds(e * share, share), :], load.at[2 * local_exp + e]))
    for copy in loads:
        copy.start()

    def dy_start(k):
        m, r = lax.div(k, cuts), lax.rem(k, cuts)
        for cc in range(2):
            for pp in range(pn):
                for qq in range(qn):
                    for zz in range(zn):
                        xx, yy = (pp, qq) if (cc == 0 or pn != qn) else (qq, pp)
                        device = (zz * (groups // zn) + yy) * parts + xx * 2 + cc
                        pltpu.make_async_copy(
                            dy.at[m, pl.ds(pl.multiple_of(device * local_rows + r * ROWS, ROWS), ROWS), :],
                            dys.at[lax.rem(k, 2), pl.ds((((cc * pn + pp) * qn + qq) * zn + zz) * ROWS, ROWS), :],
                            dy_sem.at[lax.rem(k, 2)],
                        ).start()

    dy_start(0)
    greet_lines([core, first, second, long])
    sum_wide[...] = jnp.zeros_like(sum_wide)
    sum_down[...] = jnp.zeros_like(sum_down)

    def rows_at(start, size):
        return pl.ds(pl.multiple_of(start, ROWS), size)

    def g_long(k):
        buf = xs.at[lax.rem(k, ring)]
        return swap_legs(
            long, lambda i: x.at[k], lambda j, i: buf.at[rows_at(c * rc + p * rp + q * rq + i * rz, rz), :],
            lambda j: g_send.at[k, j], lambda j: g_recv.at[k, j])

    def g_line(k, line, at, offset):
        return swap_legs(line, lambda i: at(line.place), lambda j, i: at(i),
                         lambda j: g_send.at[k, offset + j], lambda j: g_recv.at[k, offset + j])

    def g_second(k):
        buf = xs.at[lax.rem(k, ring)]
        return g_line(k, second, lambda i: buf.at[rows_at(c * rc + p * rp + i * rq, rq), :], zn - 1)

    def g_first(k):
        buf = xs.at[lax.rem(k, ring)]
        return g_line(k, first, lambda i: buf.at[rows_at(c * rc + i * rp, rp), :], zn + qn - 2)

    def g_core(k):
        buf = xs.at[lax.rem(k, ring)]
        return g_line(k, core, lambda i: buf.at[rows_at(i * rc, rc), :], zn + qn + pn - 3)

    def s_line(k, line, at, land, offset):
        return swap_legs(line, at, lambda j, i: land.at[lax.rem(k, 2), j],
                         lambda j: s_send.at[k, offset + j], lambda j: s_recv.at[k, offset + j])

    def s_core(k):
        return s_line(k, core, lambda i: other, land_c, 0)

    def s_first(k):
        buf = acc.at[lax.rem(k, acc_ring)]
        return s_line(k, first, lambda i: buf.at[rows_at(i * rp, rp), :], land_p, 1)

    def s_second(k):
        buf = acc.at[lax.rem(k, acc_ring)]
        return s_line(k, second, lambda i: buf.at[rows_at(p * rp + i * rq, rq), :], land_q, pn)

    def s_long(k):
        buf = acc.at[lax.rem(k, acc_ring)]
        return s_line(k, long, lambda i: buf.at[rows_at(p * rp + q * rq + i * rz, rz), :], land_z, pn + qn - 1)

    def after(t, lag, act):
        k = t - lag

        @pl.when((k >= 0) & (k < chunks))
        def _():
            act(k)

    lane = lax.broadcasted_iota(jnp.int32, (1, 128), 1)

    def compute(k):
        buf, dyk = xs.at[lax.rem(k, ring)], dys.at[lax.rem(k, 2)]

        @pl.when(k == 0)
        def _():
            for copy in loads:
                copy.wait()

        pltpu.make_async_copy(moe.at[0], dyk, dy_sem.at[lax.rem(k, 2)]).wait()

        @pl.when(k + 1 < chunks)
        def _():
            dy_start(k + 1)

        hid[:, :128] = jnp.dot(buf[...], dispatch[...], preferred_element_type=F32)

        @pl.loop(0, rows // 64)
        def _(i):
            here = pl.ds(pl.multiple_of(i * 64, 64), 64)
            logits = jnp.where(lane < experts, hid[here, :128], NEG)
            grown = jnp.exp(logits - jnp.max(logits, axis=-1, keepdims=True))
            probs = grown / jnp.sum(grown, axis=-1, keepdims=True)
            gate[here, :] = probs * keep[k, here, :].astype(F32)
            d_gate[here, :] = jnp.zeros((64, 128), F32)

        @pl.loop(0, pairs)
        def _(j):
            cols = pl.ds(pl.multiple_of(j * 4 * share, 4 * share), 4 * share)
            some = pl.ds(pl.multiple_of(j * 2 * share, 2 * share), 2 * share)
            hid[...] = jnp.dot(buf[...], wide[:, cols], preferred_element_type=F32)
            raw[...] = lax.dot_general(dyk[...], down[some, :], (((1,), (1,)), ((), ())), preferred_element_type=F32)

            @pl.loop(0, rows // 32)
            def _(i):
                here = pl.ds(pl.multiple_of(i * 32, 32), 32)
                gates = gate[here, :]
                marks = d_gate[here, :]
                for e in range(2):
                    mark = lane == base + 2 * j + e
                    weight = jnp.sum(jnp.where(mark, gates, 0.0), axis=-1, keepdims=True)
                    g = hid[here, e * share: (e + 1) * share]
                    u = hid[here, (2 + e) * share: (3 + e) * share]
                    d = raw[here, e * share: (e + 1) * share]
                    sigma = jax.nn.sigmoid(g)
                    swish = g * sigma
                    act = swish * u
                    marks = marks + jnp.where(mark, jnp.sum(act * d, axis=-1, keepdims=True), 0.0)
                    d = d * weight
                    gated[here, pl.ds(pl.multiple_of(j * 2 * share + e * share, share), share)] = (act * weight).astype(BF)
                    d_gu[here, pl.ds(pl.multiple_of(j * 4 * share + e * share, share), share)] = (
                        d * u * (sigma + swish * (1.0 - sigma))).astype(BF)
                    d_gu[here, pl.ds(pl.multiple_of(j * 4 * share + (2 + e) * share, share), share)] = (d * swish).astype(BF)
                d_gate[here, :] = marks

        tiles = width // 512

        def input_grads(half, to):
            here = pl.ds(pl.multiple_of(half * rc, rc), rc)

            @pl.loop(0, tiles)
            def _(n):
                cols = pl.ds(pl.multiple_of(n * 512, 512), 512)
                to[:, cols] = lax.dot_general(
                    d_gu[here, :], wide[cols, :], (((1,), (1,)), ((), ())), preferred_element_type=F32).astype(BF)

            to[:, width:] = d_gate[here, :].astype(BF)

        input_grads(1 - c, other)
        start_legs(s_core(k))
        input_grads(c, acc.at[lax.rem(k, acc_ring)])
        slot = lax.rem(k, 2)

        @pl.when(k >= 2)
        def _():
            pltpu.make_async_copy(stage.at[slot], moe.at[k - 2], stage_sem.at[slot]).wait()

        @pl.loop(0, tiles)
        def _(n):
            cols = pl.ds(pl.multiple_of(n * 512, 512), 512)
            stage[slot, :, cols] = jnp.dot(gated[...], down[:, cols], preferred_element_type=F32).astype(BF)
            sum_wide[cols, :] += lax.dot_general(
                buf[:, cols], d_gu[...], (((0,), (0,)), ((), ())), preferred_element_type=F32)
            sum_down[:, cols] += lax.dot_general(
                gated[...], dyk[:, cols], (((0,), (0,)), ((), ())), preferred_element_type=F32)

        pltpu.make_async_copy(stage.at[slot], moe.at[k], stage_sem.at[slot]).start()

    def end_long(k):
        end_legs(s_long(k))
        buf = acc.at[lax.rem(k, acc_ring)]
        total = buf[rows_at(p * rp + q * rq + z * rz, rz), :].astype(F32)
        for j in range(zn - 1):
            total = total + land_z[lax.rem(k, 2), j].astype(F32)
        summed[k] = total.astype(BF)

    def end_second(k):
        end_legs(s_second(k))
        for j in range(qn - 1):
            add_rows(acc.at[lax.rem(k, acc_ring)], p * rp + q * rq, land_q.at[lax.rem(k, 2), j], rq)
        start_legs(s_long(k))

    def end_first(k):
        end_legs(s_first(k))
        for j in range(pn - 1):
            add_rows(acc.at[lax.rem(k, acc_ring)], p * rp, land_p.at[lax.rem(k, 2), j], rp)
        start_legs(s_second(k))

    def end_core(k):
        end_legs(s_core(k))
        add_rows(acc.at[lax.rem(k, acc_ring)], 0, land_c.at[lax.rem(k, 2), 0], rc)
        start_legs(s_first(k))

    def begin(k):
        xs[lax.rem(k, ring), rows_at(c * rc + p * rp + q * rq + z * rz, rz), :] = x[k]
        start_legs(g_long(k))

    def then(one, two):
        def act(k):
            end_legs(one(k))
            start_legs(two(k))

        return act

    @pl.loop(0, chunks + 8)
    def _(t):
        after(t, 8, end_long)
        after(t, 7, end_second)
        after(t, 6, end_first)
        after(t, 5, end_core)
        after(t, 4, lambda k: end_legs(g_core(k)))
        after(t, 3, then(g_first, g_core))
        after(t, 2, then(g_second, g_first))
        after(t, 1, then(g_long, g_second))
        after(t, 0, begin)
        after(t, 4, compute)

    out_down = pltpu.make_async_copy(sum_down, grad_shrink, load.at[0])
    out_down.start()
    for k in range(chunks - 2, chunks):
        pltpu.make_async_copy(stage.at[k % 2], moe.at[k], stage_sem.at[k % 2]).wait()
    for i in range(width // rows):
        here = pl.ds(i * rows, rows)
        if i:
            pltpu.make_async_copy(d_gu, grad_widen.at[here, :], load.at[1]).wait()
        d_gu[...] = sum_wide[here, :].astype(BF)
        pltpu.make_async_copy(d_gu, grad_widen.at[here, :], load.at[1]).start()
    pltpu.make_async_copy(d_gu, grad_widen.at[pl.ds(0, rows), :], load.at[1]).wait()
    out_down.wait()


def experts_together(x, dy, widen, shrink, dispatch, keep, collective_id):
    experts = keep.shape[-1]
    dispatch = jnp.pad(dispatch, ((0, 0), (0, 128 - experts)))
    keep = jnp.pad(keep, ((0, 0), (0, 0), (0, 128 - experts)))
    groups, parts = lax.axis_size("grp"), lax.axis_size("ep")
    major, minor, xn = mesh_sizes(groups, parts)
    micro, local_rows, width = x.shape
    x = x.reshape(-1, ROWS, width)
    chunks = x.shape[0]
    local_exp, inner = shrink.shape[:2]
    share = inner // groups
    hidden = local_exp * share
    half = ROWS * major * minor * xn
    rows, wide = 2 * half, width + 128
    ring, acc_ring = min(chunks, 6), 4
    legs = major + minor + xn - 2
    vmem = pl.BlockSpec(memory_space=pltpu.VMEM)
    hbm = pl.BlockSpec(memory_space=pl.ANY)
    flops = 2 * chunks * rows * width * hidden * 9
    return pl.pallas_call(
        functools.partial(experts_kernel, groups, parts, local_rows, ring, acc_ring, experts),
        out_shape=[
            jax.ShapeDtypeStruct((chunks, ROWS, wide), BF),
            jax.ShapeDtypeStruct((chunks, rows, width), BF),
            jax.ShapeDtypeStruct((width, 2 * hidden), BF),
            jax.ShapeDtypeStruct((hidden, width), F32),
        ],
        in_specs=[vmem, hbm, hbm, hbm, vmem, vmem],
        out_specs=[vmem, hbm, hbm, hbm],
        scratch_shapes=[
            pltpu.VMEM((ring, rows, width), BF),
            pltpu.VMEM((2, rows, width), BF),
            pltpu.VMEM((width, 2 * hidden), BF),
            pltpu.VMEM((hidden, width), BF),
            pltpu.VMEM((width, 2 * hidden), F32),
            pltpu.VMEM((hidden, width), F32),
            pltpu.VMEM((2, rows, width), BF),
            pltpu.VMEM((acc_ring, half, wide), BF),
            pltpu.VMEM((half, wide), BF),
            pltpu.VMEM((2, 1, half, wide), BF),
            pltpu.VMEM((2, xn - 1, half // xn, wide), BF),
            pltpu.VMEM((2, minor - 1, half // xn // minor, wide), BF),
            pltpu.VMEM((2, major - 1, ROWS, wide), BF),
            pltpu.VMEM((rows, 4 * share), F32),
            pltpu.VMEM((rows, 2 * share), F32),
            pltpu.VMEM((rows, hidden), BF),
            pltpu.VMEM((rows, 2 * hidden), BF),
            pltpu.VMEM((rows, 128), F32),
            pltpu.VMEM((rows, 128), F32),
            pltpu.SemaphoreType.DMA((3 * local_exp,)),
            pltpu.SemaphoreType.DMA((2,)),
            pltpu.SemaphoreType.DMA((2,)),
            pltpu.SemaphoreType.DMA((chunks, legs)),
            pltpu.SemaphoreType.DMA((chunks, legs)),
            pltpu.SemaphoreType.DMA((chunks, legs)),
            pltpu.SemaphoreType.DMA((chunks, legs)),
        ],
        compiler_params=pltpu.CompilerParams(
            collective_id=collective_id, has_side_effects=True, vmem_limit_bytes=60 * 2**20
        ),
        cost_estimate=pl.CostEstimate(flops=flops, bytes_accessed=80 * 2**20, transcendentals=chunks * rows * hidden),
    )(x, dy, widen, shrink, dispatch, keep)


def experts_apart(x, dy_all, keep_all, specialist_widen_matrix, specialist_shrink_matrix, dispatcher_matrix):
    groups, parts = lax.axis_size("grp"), lax.axis_size("ep")
    group, part = lax.axis_index("grp"), lax.axis_index("ep")
    local_exp, inner, width = specialist_shrink_matrix.shape
    share = inner // groups
    widen = specialist_widen_matrix.reshape(local_exp, width, 2, groups, share)
    widen = lax.dynamic_index_in_dim(widen, group, 3, keepdims=False)
    widen = widen.transpose(1, 2, 0, 3).reshape(width, 2 * local_exp * share)
    shrink = specialist_shrink_matrix.reshape(local_exp, groups, share, width)
    shrink = lax.dynamic_index_in_dim(shrink, group, 1, keepdims=False).reshape(local_exp * share, width)
    x_all = gather_all(x, 1)
    chunk_shape = x_all.shape[:-1]
    x_all, dy_all = x_all.reshape(-1, width), dy_all.reshape(-1, width)
    keep_all = keep_all.reshape(x_all.shape[0], -1)
    router = jax.nn.softmax(jnp.dot(x_all, dispatcher_matrix, preferred_element_type=F32), axis=-1)
    gate = lax.dynamic_slice_in_dim(router * keep_all, part * local_exp, local_exp, axis=1)
    gate = jnp.repeat(gate, share, axis=1)
    gate_up = jnp.dot(x_all, widen, preferred_element_type=F32)
    g, u = gate_up[:, : local_exp * share], gate_up[:, local_exp * share:]
    sigma = jax.nn.sigmoid(g)
    act = g * sigma * u
    gated = (gate * act).astype(BF)
    moe_part = jnp.dot(gated, shrink, preferred_element_type=F32).astype(BF)
    d_raw = lax.dot_general(dy_all, shrink, (((1,), (1,)), ((), ())), preferred_element_type=F32)
    d_gate = jnp.sum((act * d_raw).reshape(-1, local_exp, share), axis=-1)
    d_act = gate * d_raw
    d_gu = jnp.concatenate([d_act * u * sigma * (1.0 + g * (1.0 - sigma)), d_act * (g * sigma)], axis=1).astype(BF)
    dx_part = lax.dot_general(d_gu, widen, (((1,), (1,)), ((), ())), preferred_element_type=F32).astype(BF)
    lanes = jnp.arange(128, dtype=jnp.int32)
    place = (lanes[None, :] == part * local_exp + jnp.arange(local_exp, dtype=jnp.int32)[:, None])
    d_gate = jnp.sum(jnp.where(place[None], d_gate[:, :, None], 0.0), axis=1)
    dx_part = jnp.concatenate([dx_part, d_gate.astype(BF)], axis=1)
    dx_sum = scatter_all(dx_part.reshape(chunk_shape + (width + 128,)), 2)
    grad_widen = lax.dot_general(x_all, d_gu, (((0,), (0,)), ((), ())), preferred_element_type=F32)
    grad_shrink = lax.dot_general(gated, dy_all, (((0,), (0,)), ((), ())), preferred_element_type=F32)
    grad_widen = grad_widen.astype(BF).reshape(width, 2, local_exp // 2, 2, share).transpose(0, 2, 1, 3, 4)
    return dx_sum, moe_part.reshape(chunk_shape + (width,)), grad_widen, grad_shrink


def per_device(
    block_entry_states,
    document_labels,
    token_assignments,
    worker_quota_tallies,
    rescale_factors_both,
    triple_projection_matrix,
    probe_lookup_scalers,
    heads_merge_matrix,
    dispatcher_matrix,
    specialist_widen_matrix,
    specialist_shrink_matrix,
    output_gradient,
):
    micro, local_rows, width = block_entry_states.shape
    groups, parts = lax.axis_size("grp"), lax.axis_size("ep")
    major, minor, xs = mesh_sizes(groups, parts)
    group = lax.axis_index("grp")
    part = lax.axis_index("ep")
    seq_len = document_labels.shape[1]
    experts = dispatcher_matrix.shape[1]
    local_exp = specialist_widen_matrix.shape[0]
    inner = specialist_shrink_matrix.shape[1]
    share = inner // groups
    local_width = triple_projection_matrix.shape[2]
    heads = local_width // HD
    scale = 1.0 / math.sqrt(HD)
    gains = rescale_factors_both.astype(F32)
    head_gains = probe_lookup_scalers.astype(F32)
    cos, sin = rope_tables(seq_len, HD)
    signed_sin = jnp.concatenate([-sin[:, : HD // 2], sin[:, HD // 2:]], axis=-1)
    expert_ids = jnp.arange(experts, dtype=jnp.int32)

    hits = (token_assignments[..., None] == expert_ids).astype(jnp.int32)
    counts = jnp.sum(hits, axis=2)
    prior = jnp.cumsum(counts, axis=1) - counts
    keep = jnp.where((counts > 0) & (prior < worker_quota_tallies), 1.0, 0.0).astype(F32)
    keep_all = lax.all_gather(keep.astype(BF), ALL, axis=1, tiled=True).astype(F32)
    keep_all = keep_all.reshape(micro, major, minor, xs, 2, local_rows // ROWS, ROWS, experts)
    one = keep_all[:, :, :, :, 0].transpose(0, 4, 3, 2, 1, 5, 6)
    two = keep_all[:, :, :, :, 1].transpose(0, 4, 3, 2, 1, 5, 6)
    if xs == minor:
        two = keep_all[:, :, :, :, 1].transpose(0, 4, 2, 3, 1, 5, 6)
    keep_all = jnp.stack([one, two], axis=2).reshape(-1, experts)
    fused = xs == minor and share % 128 == 0 and local_exp % 2 == 0 and 2 * xs * minor * major * ROWS <= 512

    if fused:
        dy_all = lax.all_gather(output_gradient, ALL, axis=1, tiled=True)
    else:
        dy_all = gather_all(output_gradient, 0)

    skip = block_entry_states.astype(F32)
    inv_first = lax.rsqrt(jnp.mean(skip * skip, axis=-1, keepdims=True) + EPS)
    hat_first = skip * inv_first
    attn_in = (hat_first * gains[0]).astype(BF)
    gathered = lax.all_gather(attn_in, "ep", axis=1, tiled=True)
    projected = jnp.einsum("mtd,dcf->cmtf", gathered, triple_projection_matrix, preferred_element_type=F32)
    qk_raw = projected[:2]
    squares = lax.psum(jnp.sum(qk_raw * qk_raw, axis=-1), "ep")
    qk_inv = lax.rsqrt(squares / width + EPS)[..., None]
    qk_hat = qk_raw * qk_inv
    qk_n = (qk_hat * head_gains[:, None, None, :]).reshape(2, micro, seq_len, heads, HD).transpose(0, 1, 3, 2, 4)
    qk = (qk_n * cos + swap_halves(qk_n) * signed_sin).astype(BF)
    queries, keys = qk[0], qk[1]
    values = projected[2].astype(BF).reshape(micro, seq_len, heads, HD).transpose(0, 2, 1, 3)
    places = jnp.arange(seq_len, dtype=jnp.int32)
    allowed = (document_labels[:, :, None] == document_labels[:, None, :]) & (places[None, :] <= places[:, None])
    scores = jnp.einsum("mhsd,mhtd->mhst", queries, keys, preferred_element_type=F32) * scale
    scores = jnp.where(allowed[:, None], scores, NEG)
    exponent = jnp.exp(scores - jnp.max(scores, axis=-1, keepdims=True))
    weights = exponent / jnp.sum(exponent, axis=-1, keepdims=True)
    weights_low = weights.astype(BF)
    mixed = jnp.einsum("mhst,mhtd->mshd", weights_low, values, preferred_element_type=F32)
    mixed = mixed.astype(BF).reshape(micro, seq_len, local_width)
    attention = lax.psum_scatter(
        jnp.einsum("msf,fd->msd", mixed, heads_merge_matrix, preferred_element_type=F32).astype(BF),
        "ep", scatter_dimension=1, tiled=True,
    ).astype(F32)

    hidden = skip + attention
    inv_second = lax.rsqrt(jnp.mean(hidden * hidden, axis=-1, keepdims=True) + EPS)
    hat_second = hidden * inv_second
    ffn_in = (hat_second * gains[1]).astype(BF)
    chunk_shape = (micro * local_rows // ROWS, 2, xs, minor, major, ROWS)
    keep_all = keep_all.reshape(chunk_shape[0], -1, experts)
    if fused:
        dx_sum, moe_part, grad_widen, grad_shrink = experts_together(
            ffn_in, dy_all, specialist_widen_matrix, specialist_shrink_matrix, dispatcher_matrix, keep_all.astype(BF), 1)
    else:
        dx_sum, moe_part, grad_widen, grad_shrink = experts_apart(
            ffn_in, dy_all, keep_all, specialist_widen_matrix, specialist_shrink_matrix, dispatcher_matrix)
    dx_sum = dx_sum.astype(F32).reshape(micro, local_rows, width + 128)
    grad_widen = lax.all_to_all(grad_widen.reshape(groups, width // groups, -1), "grp", 0, 0, tiled=True)
    grad_widen = grad_widen.reshape(groups, width // groups, local_exp // 2, 2, 2, share)
    grad_widen = grad_widen.transpose(2, 4, 1, 3, 0, 5).reshape(local_exp, width // groups, 2 * inner).astype(F32)
    grad_shrink = grad_shrink.reshape(local_exp, share, width)
    moe = scatter_all(moe_part.reshape(chunk_shape + (width,)), 3).astype(F32).reshape(micro, local_rows, width)
    output = (hidden + moe).astype(BF)

    probs = jax.nn.softmax(jnp.einsum("mtd,de->mte", ffn_in, dispatcher_matrix, preferred_element_type=F32), axis=-1)
    d_probs = dx_sum[..., width: width + experts] * keep
    d_logits = probs * (d_probs - jnp.sum(probs * d_probs, axis=-1, keepdims=True))
    d_ffn = dx_sum[..., :width] + jnp.einsum("mte,de->mtd", d_logits, dispatcher_matrix.astype(F32), precision=HIGH)
    grad_router = jnp.einsum("mtd,mte->ed", ffn_in.astype(F32), d_logits, precision=HIGH)
    scaled = d_ffn * gains[1]
    adjoint = output_gradient.astype(F32)
    d_hidden = adjoint + inv_second * (scaled - hat_second * jnp.mean(scaled * hat_second, axis=-1, keepdims=True))
    grad_second = jnp.sum(d_ffn * hat_second, axis=(0, 1))

    branch = lax.all_gather(d_hidden.astype(BF), "ep", axis=1, tiled=True)
    grad_out = jnp.einsum("msf,msd->fd", mixed, branch, preferred_element_type=F32)
    d_mixed = jnp.einsum("msd,fd->msf", branch, heads_merge_matrix, preferred_element_type=F32).astype(BF)
    d_mixed = d_mixed.reshape(micro, seq_len, heads, HD).transpose(0, 2, 1, 3)
    d_weights = jnp.einsum("mhsd,mhtd->mhst", d_mixed, values, preferred_element_type=F32)
    d_scores = (weights * (d_weights - jnp.sum(weights * d_weights, axis=-1, keepdims=True))).astype(BF)
    d_values = jnp.einsum("mhst,mhsd->mthd", weights_low, d_mixed, preferred_element_type=F32)
    d_queries = jnp.einsum("mhst,mhtd->mshd", d_scores, keys, preferred_element_type=F32) * scale
    d_keys = jnp.einsum("mhst,mhsd->mthd", d_scores, queries, preferred_element_type=F32) * scale
    d_qk = jnp.stack([d_queries, d_keys])
    d_qk = d_qk * cos[:, None] - swap_halves(d_qk) * signed_sin[:, None]
    d_qk = d_qk.reshape(2, micro, seq_len, local_width)
    scaled = d_qk * head_gains[:, None, None, :]
    inner_sums = lax.psum(jnp.sum(scaled * qk_hat, axis=-1), "ep")
    d_qk_raw = qk_inv * (scaled - qk_hat * (inner_sums / width)[..., None])
    grad_heads = jnp.sum(d_qk * qk_hat, axis=(1, 2))
    d_proj = jnp.concatenate([d_qk_raw, d_values.reshape(1, micro, seq_len, local_width)]).astype(BF)
    grad_qkv = jnp.einsum("mtd,cmtf->dcf", gathered, d_proj, preferred_element_type=F32)
    d_attn_in = lax.psum_scatter(
        jnp.einsum("cmtf,dcf->mtd", d_proj, triple_projection_matrix, preferred_element_type=F32).astype(BF),
        "ep", scatter_dimension=1, tiled=True,
    ).astype(F32)
    scaled = d_attn_in * gains[0]
    grad_input = d_hidden + inv_first * (scaled - hat_first * jnp.mean(scaled * hat_first, axis=-1, keepdims=True))
    grad_first = jnp.sum(d_attn_in * hat_first, axis=(0, 1))

    misc = jnp.concatenate([grad_first[None], grad_second[None], grad_router])
    misc = lax.psum(misc, "ep").reshape(-1)
    misc = jnp.concatenate([misc, grad_heads.reshape(-1)])
    small = major * minor * ROWS * 128
    misc_size = misc.shape[0]
    misc = jnp.pad(misc, (0, -misc_size % small)).reshape(1, minor, major, ROWS, -1).astype(BF)
    spans = 4
    qkv_cut = grad_qkv.astype(BF).reshape(spans, minor, major, -1, 3 * local_width)
    out_cut = grad_out.astype(BF).reshape(1, minor, major, -1, width)
    qkv_sum, out_sum, misc_sum = total_over_groups([qkv_cut, out_cut, misc], (spans, 1, 1), 4)
    qkv_sum = qkv_sum.reshape(grad_qkv.shape).astype(F32)
    out_sum = out_sum.reshape(grad_out.shape).astype(F32)
    misc_sum = misc_sum.reshape(-1)[:misc_size].astype(F32)
    rows = misc_sum[: (2 + experts) * width].reshape(2 + experts, width)
    return (
        output,
        grad_input,
        rows[:2],
        qkv_sum,
        misc_sum[(2 + experts) * width:].reshape(2, local_width),
        out_sum,
        rows[2:].T,
        grad_widen,
        grad_shrink,
    )


def solution(mesh):
    return jax.shard_map(
        per_device,
        mesh=mesh,
        in_specs=(
            P(None, ALL, None),
            P(None, "grp"),
            P(None, ALL, None),
            P(),
            P(),
            P(None, None, "ep"),
            P(None, "ep"),
            P("ep", None),
            P(),
            P("ep", None, None),
            P("ep", None, None),
            P(None, ALL, None),
        ),
        out_specs=(
            P(None, ALL, None),
            P(None, ALL, None),
            P(),
            P(None, None, "ep"),
            P(None, "ep"),
            P("ep", None),
            P(),
            P("ep", "grp", None),
            P("ep", "grp", None),
        ),
        check_vma=False,
    )
```

```python
import functools
import math

import jax
import jax.numpy as jnp
from jax import lax
from jax.experimental import pallas as pl
from jax.experimental.pallas import tpu as pltpu
from jax.sharding import PartitionSpec as P

HD = 128
TOP = 8
EPS = 1e-05
THETA = 10000.0
NEG = -1e30
HIGH = lax.Precision.HIGHEST
ALL = ("grp", "ep")
MESH = pl.DeviceIdType.MESH
ROWS = 16
BF = jnp.bfloat16
F32 = jnp.float32


def apply_silu(v):
    return v * jax.nn.sigmoid(v)


def rope_tables(length, head_dim):
    half = head_dim // 2
    freq = THETA ** (-jnp.arange(half, dtype=F32) * 2.0 / head_dim)
    angle = jnp.arange(length, dtype=F32)[:, None] * freq[None, :]
    angle = jnp.concatenate([angle, angle], axis=-1)
    return (jnp.cos(angle), jnp.sin(angle))


def swap_halves(v):
    half = v.shape[-1] // 2
    return jnp.concatenate([v[..., half:], v[..., :half]], axis=-1)


def mesh_sizes(groups, parts):
    major = 4 if groups % 4 == 0 else groups
    return major, groups // major, parts // 2


class Line:
    def __init__(self, size, place, step):
        self.size, self.place, self.step = size, place, step

    def at(self, hops):
        return (
            lax.axis_index("grp") + hops * self.step[0],
            lax.axis_index("ep") + hops * self.step[1],
        )


def lines(groups, parts):
    major, minor, xs = mesh_sizes(groups, parts)
    g, e = lax.axis_index("grp"), lax.axis_index("ep")
    core = lax.rem(e, 2)
    x_pos, minor_pos = lax.div(e, 2), lax.rem(g, minor)
    if xs == minor:
        first = Line(xs, jnp.where(core == 0, x_pos, minor_pos), (core, 2 - 2 * core))
        second = Line(xs, jnp.where(core == 0, minor_pos, x_pos), (1 - core, 2 * core))
    else:
        first = Line(xs, x_pos, (0, 2))
        second = Line(minor, minor_pos, (1, 0))
    return Line(2, core, (0, 1)), first, second, Line(major, lax.div(g, minor), (minor, 0))


def greet(some):
    barrier = pltpu.get_barrier_semaphore()
    peers = 0
    for line in some:
        if line.size == 2:
            pl.semaphore_signal(barrier, inc=1, device_id=line.at(1 - 2 * line.place), device_id_type=MESH)
            peers = peers + 1
        else:
            for way, there in ((1, line.place < line.size - 1), (-1, line.place > 0)):

                @pl.when(there)
                def _(line=line, way=way):
                    pl.semaphore_signal(barrier, inc=1, device_id=line.at(way), device_id_type=MESH)

                peers = peers + there.astype(jnp.int32)
    pl.semaphore_wait(barrier, peers)


def greet_lines(some):
    barrier = pltpu.get_barrier_semaphore()
    for line in some:
        for j in range(1, line.size):
            to = lax.rem(line.place + j, line.size)
            pl.semaphore_signal(barrier, inc=1, device_id=line.at(to - line.place), device_id_type=MESH)
    pl.semaphore_wait(barrier, sum(line.size - 1 for line in some))


def remote(src, dst, send, recv, target):
    return pltpu.make_async_remote_copy(
        src_ref=src, dst_ref=dst, send_sem=send, recv_sem=recv, device_id=target, device_id_type=MESH
    )


class Hop:
    def __init__(self, legs, after=None):
        self.legs, self.after = legs, after

    def _each(self, which, act):
        for leg in self.legs:
            if leg[which] is None:
                act(leg)
            else:
                pl.when(leg[which])(functools.partial(act, leg))

    def start(self):
        self._each(0, lambda leg: leg[2]().start())

    def arrive(self):
        def act(leg):
            leg[3]().wait_recv()
            if leg[4] is not None:
                leg[4]()

        self._each(1, act)

    def sent(self):
        self._each(0, lambda leg: leg[2]().wait_send())


def gather_hops(line, at, send, recv):
    n, a = line.size, line.place
    if n == 2:
        mine, theirs, peer = at(a), at(1 - a), line.at(1 - 2 * a)
        return [
            Hop([(None, None, lambda: remote(mine, mine, send(0), recv(0), peer),
                  lambda: remote(theirs, theirs, send(0), recv(0), peer), None)])
        ]
    hops = []
    for s in range(1, n):
        legs = []
        for d, way in enumerate((1, -1)):
            k = (s - 1) * 2 + d
            out = a - way * (s - 1)
            into = a - way * s
            sends = (out >= 0) & (out < n) & (a + way >= 0) & (a + way < n)
            gets = (into >= 0) & (into < n)
            out, into = jnp.clip(out, 0, n - 1), jnp.clip(into, 0, n - 1)
            legs.append((
                sends, gets,
                lambda out=out, way=way, k=k: remote(at(out), at(out), send(k), recv(k), line.at(way)),
                lambda into=into, way=way, k=k: remote(at(into), at(into), send(k), recv(k), line.at(-way)),
                None,
            ))
        hops.append(Hop(legs))
    return hops


def reduce_hops(line, acc, land, add, send, recv):
    n, a = line.size, line.place
    if n == 2:
        peer = line.at(1 - 2 * a)
        return [
            Hop([(None, None, lambda: remote(acc(1 - a), land(0), send(0), recv(0), peer),
                  lambda: remote(land(0), land(0), send(0), recv(0), peer),
                  lambda: add(acc(a), land(0)))])
        ]
    hops = []
    for s in range(n - 1):
        legs = []
        for d, way in enumerate((1, -1)):
            k = s * 2 + d
            b = a if way == 1 else n - 1 - a
            sends = (b <= s) & (b < n - 1)
            gets = (b - 1 <= s) & (b >= 1)
            out = b + n - 1 - s
            into = b + n - 2 - s
            out, into = jnp.clip(out, 0, n - 1), jnp.clip(into, 0, n - 1)
            if way == -1:
                out, into = n - 1 - out, n - 1 - into
            legs.append((
                sends, gets,
                lambda out=out, way=way, k=k: remote(acc(out), land(k), send(k), recv(k), line.at(way)),
                lambda way=way, k=k: remote(land(k), land(k), send(k), recv(k), line.at(-way)),
                lambda into=into, k=k: add(acc(into), land(k)),
            ))
        hops.append(Hop(legs))
    return hops


def hop_count(n):
    return 1 if n == 2 else n - 1


def leg_count(n):
    return 1 if n == 2 else 2 * (n - 1)


def flow(chains):
    depth, count = max(len(c) for c in chains), len(chains)
    for t in range(count + depth):
        for k in range(count):
            i = t - k
            if 1 <= i <= len(chains[k]):
                chains[k][i - 1].arrive()
            if 0 <= i < len(chains[k]):
                chains[k][i].start()
    for chain in chains:
        for hop in chain:
            hop.sent()


def add(acc, land):
    lead = acc.shape[:-2]

    def one(i):
        where = []
        for size in reversed(lead):
            where.insert(0, lax.rem(i, size))
            i = lax.div(i, size)
        where = tuple(where) + (slice(None), slice(None))
        acc[where] = (acc[where].astype(F32) + land[where].astype(F32)).astype(acc.dtype)

    if lead:
        pl.loop(0, math.prod(lead))(one)
    else:
        one(0)


def gather_kernel(groups, parts, x, out, local, send, recv):
    core, first, second, long = lines(groups, parts)
    c, p, q, z = core.place, first.place, second.place, long.place
    greet([core, first, second, long])
    chunks = x.shape[0]
    own = [pltpu.make_async_copy(x.at[k], out.at[k, c, p, q, z], local.at[k]) for k in range(chunks)]
    for copy in own:
        copy.start()
    chains = []
    for k in range(chunks):
        base = [0]

        def sems(n, k=k, base=base):
            b = base[0]
            base[0] += leg_count(n)
            return (lambda i: send.at[k, b + i]), (lambda i: recv.at[k, b + i])

        chain = []
        chain += gather_hops(long, lambda i, k=k: out.at[k, c, p, q, i], *sems(long.size))
        chain += gather_hops(second, lambda i, k=k: out.at[k, c, p, i], *sems(second.size))
        chain += gather_hops(first, lambda i, k=k: out.at[k, c, i], *sems(first.size))
        chain += gather_hops(core, lambda i, k=k: out.at[k, i], *sems(2))
        chains.append(chain)
    for copy in own:
        copy.wait()
    flow(chains)


def gather_all(x, collective_id):
    groups, parts = lax.axis_size("grp"), lax.axis_size("ep")
    major, minor, xs = mesh_sizes(groups, parts)
    width = x.shape[-1]
    x = x.reshape(-1, ROWS, width)
    legs = sum(leg_count(n) for n in (2, xs, minor, major))
    chunks = x.shape[0]
    return pl.pallas_call(
        functools.partial(gather_kernel, groups, parts),
        out_shape=jax.ShapeDtypeStruct((chunks, 2, xs, minor, major, ROWS, width), x.dtype),
        in_specs=[pl.BlockSpec(memory_space=pl.ANY)],
        out_specs=pl.BlockSpec(memory_space=pl.ANY),
        scratch_shapes=[
            pltpu.SemaphoreType.DMA((chunks,)),
            pltpu.SemaphoreType.DMA((chunks, legs)),
            pltpu.SemaphoreType.DMA((chunks, legs)),
        ],
        compiler_params=pltpu.CompilerParams(collective_id=collective_id, has_side_effects=True),
    )(x)


def scatter_kernel(groups, parts, part, out, acc, land_c, land_p, land_q, land_z, local, send, recv):
    core, first, second, long = lines(groups, parts)
    c, p, q, z = core.place, first.place, second.place, long.place
    chunks = part.shape[0]
    own = [pltpu.make_async_copy(part.at[k, c], acc.at[k], local.at[k]) for k in range(chunks)]
    for copy in own:
        copy.start()
    greet([core, first, second, long])
    chains = []
    for k in range(chunks):
        base = [0]

        def sems(n, k=k, base=base):
            b = base[0]
            base[0] += leg_count(n)
            return (lambda i: send.at[k, b + i]), (lambda i: recv.at[k, b + i])

        def add_own(acc_ref, land_ref, k=k):
            own[k].wait()
            add(acc_ref, land_ref)

        s, r = sems(2)
        peer = core.at(1 - 2 * c)
        other = part.at[k, 1 - c]
        chain = [Hop([(
            None, None,
            lambda other=other, s=s, r=r, k=k: remote(other, land_c.at[k], s(0), r(0), peer),
            lambda s=s, r=r, k=k: remote(land_c.at[k], land_c.at[k], s(0), r(0), peer),
            lambda k=k, add_own=add_own: add_own(acc.at[k], land_c.at[k]),
        )])]
        chain += reduce_hops(first, lambda i, k=k: acc.at[k, i], lambda i, k=k: land_p.at[k, i], add, *sems(first.size))
        chain += reduce_hops(second, lambda i, k=k: acc.at[k, p, i], lambda i, k=k: land_q.at[k, i], add, *sems(second.size))
        chain += reduce_hops(long, lambda i, k=k: acc.at[k, p, q, i], lambda i, k=k: land_z.at[k, i], add, *sems(long.size))
        chains.append(chain)
    flow(chains)
    for k in range(chunks):
        out[k] = acc[k, p, q, z]


def scatter_all(part, collective_id):
    groups, parts = lax.axis_size("grp"), lax.axis_size("ep")
    major, minor, xs = mesh_sizes(groups, parts)
    legs = sum(leg_count(n) for n in (2, xs, minor, major))
    chunks, width = part.shape[0], part.shape[-1]
    unit = 2 * ROWS * width
    need = unit * (2 * xs * minor * major + leg_count(xs) * minor * major + leg_count(minor) * major + leg_count(major) + 2)
    per = chunks
    while per > 1 and per * need > 44 * 2**20:
        per //= 2
    call = pl.pallas_call(
        functools.partial(scatter_kernel, groups, parts),
        out_shape=jax.ShapeDtypeStruct((per, ROWS, width), BF),
        in_specs=[pl.BlockSpec(memory_space=pl.ANY)],
        out_specs=pl.BlockSpec(memory_space=pltpu.VMEM),
        scratch_shapes=[
            pltpu.VMEM((per, xs, minor, major, ROWS, width), BF),
            pltpu.VMEM((per, xs, minor, major, ROWS, width), BF),
            pltpu.VMEM((per, leg_count(xs), minor, major, ROWS, width), BF),
            pltpu.VMEM((per, leg_count(minor), major, ROWS, width), BF),
            pltpu.VMEM((per, leg_count(major), ROWS, width), BF),
            pltpu.SemaphoreType.DMA((per,)),
            pltpu.SemaphoreType.DMA((per, legs)),
            pltpu.SemaphoreType.DMA((per, legs)),
        ],
        compiler_params=pltpu.CompilerParams(
            collective_id=collective_id, has_side_effects=True, vmem_limit_bytes=56 * 2**20
        ),
    )
    return jnp.concatenate([call(part[i:i + per]) for i in range(0, chunks, per)]) if per < chunks else call(part)


def total_kernel(groups, parts, spans, far_first, *refs):
    count = len(spans)
    ins, outs = refs[:count], refs[count:2 * count]
    acc, land_y, land_z = refs[2 * count:3 * count], refs[3 * count:4 * count], refs[4 * count:5 * count]
    local, stored, send, recv = refs[5 * count:]
    major, minor, _ = mesh_sizes(groups, parts)
    g = lax.axis_index("grp")
    short = Line(minor, lax.rem(g, minor), (1, 0))
    long = Line(major, lax.div(g, minor), (minor, 0))
    loads, chains, number = [], [], 0
    for j in range(count):
        one, two = (long, short) if far_first[j] else (short, long)
        y, z = one.place, two.place
        for k in range(spans[j]):
            load = pltpu.make_async_copy(ins[j].at[k], acc[j].at[k], local.at[number])
            load.start()
            loads.append(load)
            store = pltpu.make_async_copy(acc[j].at[k, y, z], outs[j].at[k, y, z], stored.at[number])
            base = [0]

            def sems(n, number=number, base=base):
                b = base[0]
                base[0] += leg_count(n)
                return (lambda i: send.at[number, b + i]), (lambda i: recv.at[number, b + i])

            down = reduce_hops(one, lambda i, j=j, k=k: acc[j].at[k, i], lambda i, j=j, k=k: land_y[j].at[k, i], add, *sems(one.size))
            down += reduce_hops(two, lambda i, j=j, k=k, y=y: acc[j].at[k, y, i], lambda i, j=j, k=k: land_z[j].at[k, i], add, *sems(two.size))
            up = gather_hops(two, lambda i, j=j, k=k, y=y: outs[j].at[k, y, i], *sems(two.size))
            up += gather_hops(one, lambda i, j=j, k=k: outs[j].at[k, i], *sems(one.size))
            chains.append((load, down, store, up))
            number += 1
    greet([short, long])
    whole = []
    for load, down, store, up in chains:
        hops = down + up
        turn = len(down)

        class Loaded:
            def __init__(self, hop, before):
                self.hop, self.before = hop, before

            def start(self):
                self.before()
                self.hop.start()

            def arrive(self):
                self.hop.arrive()

            def sent(self):
                self.hop.sent()

        def put(store=store):
            store.start()
            store.wait()

        hops[0] = Loaded(hops[0], load.wait)
        hops[turn] = Loaded(hops[turn], put)
        whole.append(hops)
    flow(whole)


def total_over_groups(arrays, far_first, collective_id):
    groups, parts = lax.axis_size("grp"), lax.axis_size("ep")
    major, minor, _ = mesh_sizes(groups, parts)
    legs = 2 * (leg_count(minor) + leg_count(major))
    spans = tuple(a.shape[0] for a in arrays)
    total = sum(spans)
    any_spec = pl.BlockSpec(memory_space=pl.ANY)
    scratch = [pltpu.VMEM(a.shape, BF) for a in arrays]
    scratch += [pltpu.VMEM((a.shape[0], leg_count(a.shape[1])) + a.shape[2:], BF) for a in arrays]
    scratch += [pltpu.VMEM((a.shape[0], leg_count(a.shape[2])) + a.shape[3:], BF) for a in arrays]
    return pl.pallas_call(
        functools.partial(total_kernel, groups, parts, spans, far_first),
        out_shape=[jax.ShapeDtypeStruct(a.shape, BF) for a in arrays],
        in_specs=[any_spec] * len(arrays),
        out_specs=[any_spec] * len(arrays),
        scratch_shapes=scratch + [
            pltpu.SemaphoreType.DMA((total,)),
            pltpu.SemaphoreType.DMA((total,)),
            pltpu.SemaphoreType.DMA((total, legs)),
            pltpu.SemaphoreType.DMA((total, legs)),
        ],
        compiler_params=pltpu.CompilerParams(
            collective_id=collective_id, has_side_effects=True, vmem_limit_bytes=48 * 2**20
        ),
    )(*arrays)


def swap_legs(line, source, target, send, recv):
    n, a = line.size, line.place
    legs = []
    for j in range(1, n):
        to, off = lax.rem(a + j, n), lax.rem(a + n - j, n)
        legs.append((
            lambda to=to, j=j: remote(source(to), target(j - 1, a), send(j - 1), recv(j - 1), line.at(to - a)),
            lambda off=off, j=j: remote(target(j - 1, off), target(j - 1, off), send(j - 1), recv(j - 1), line.at(off - a)),
        ))
    return legs


def start_legs(legs):
    for out, _ in legs:
        out().start()


def end_legs(legs):
    for out, into in legs:
        into().wait_recv()
    for out, into in legs:
        out().wait_send()


def add_rows(acc, first, land, rows):
    @pl.loop(0, rows // ROWS)
    def _(i):
        here = pl.ds(pl.multiple_of(first + i * ROWS, ROWS), ROWS)
        there = pl.ds(pl.multiple_of(i * ROWS, ROWS), ROWS)
        acc[here, :] = (acc[here, :].astype(F32) + land[there, :].astype(F32)).astype(acc.dtype)


def experts_kernel(
    groups, parts, local_rows, ring, acc_ring, experts,
    x, dy, widen, shrink, dispatch,
    summed, moe, grad_widen, grad_shrink,
    xs, dys, wide, down, sum_wide, sum_down, stage, acc, other, land_c, land_p, land_q, land_z,
    hid, raw, gated, d_gu, gate, d_gate,
    load, dy_sem, stage_sem, g_send, g_recv, s_send, s_recv,
):
    core, first, second, long = lines(groups, parts)
    c, p, q, z = core.place, first.place, second.place, long.place
    pn, qn, zn = first.size, second.size, long.size
    chunks, _, width = x.shape
    local_exp, inner = shrink.shape[0], shrink.shape[1]
    share = inner // groups
    group, part = lax.axis_index("grp"), lax.axis_index("ep")
    rz, rq, rp, rc = ROWS, ROWS * zn, ROWS * zn * qn, ROWS * zn * qn * pn
    rows = 2 * rc
    cuts = local_rows // ROWS
    base = part * local_exp
    pairs = local_exp // 2

    loads = []
    for e in range(local_exp):
        for half in range(2):
            to = (e // 2) * 4 * share + half * 2 * share + (e % 2) * share
            loads.append(pltpu.make_async_copy(
                widen.at[e, :, pl.ds(pl.multiple_of(half * inner + group * share, share), share)],
                wide.at[:, pl.ds(to, share)], load.at[2 * e + half]))
        loads.append(pltpu.make_async_copy(
            shrink.at[e, pl.ds(pl.multiple_of(group * share, share), share), :],
            down.at[pl.ds(e * share, share), :], load.at[2 * local_exp + e]))
    for copy in loads:
        copy.start()

    def dy_copy(k):
        return pltpu.make_async_copy(dy.at[k], dys.at[lax.rem(k, 2)], dy_sem.at[lax.rem(k, 2)])

    dy_start = lambda k: dy_copy(k).start()
    dy_start(0)
    greet_lines([core, first, second, long])
    sum_wide[...] = jnp.zeros_like(sum_wide)
    sum_down[...] = jnp.zeros_like(sum_down)

    def rows_at(start, size):
        return pl.ds(pl.multiple_of(start, ROWS), size)

    def g_long(k):
        buf = xs.at[lax.rem(k, ring)]
        return swap_legs(
            long, lambda i: x.at[k], lambda j, i: buf.at[rows_at(c * rc + p * rp + q * rq + i * rz, rz), :],
            lambda j: g_send.at[k, j], lambda j: g_recv.at[k, j])

    def g_line(k, line, at, offset):
        return swap_legs(line, lambda i: at(line.place), lambda j, i: at(i),
                         lambda j: g_send.at[k, offset + j], lambda j: g_recv.at[k, offset + j])

    def g_second(k):
        buf = xs.at[lax.rem(k, ring)]
        return g_line(k, second, lambda i: buf.at[rows_at(c * rc + p * rp + i * rq, rq), :], zn - 1)

    def g_first(k):
        buf = xs.at[lax.rem(k, ring)]
        return g_line(k, first, lambda i: buf.at[rows_at(c * rc + i * rp, rp), :], zn + qn - 2)

    def g_core(k):
        buf = xs.at[lax.rem(k, ring)]
        return g_line(k, core, lambda i: buf.at[rows_at(i * rc, rc), :], zn + qn + pn - 3)

    def s_line(k, line, at, land, offset):
        return swap_legs(line, at, lambda j, i: land.at[lax.rem(k, 2), j],
                         lambda j: s_send.at[k, offset + j], lambda j: s_recv.at[k, offset + j])

    def s_core(k):
        return s_line(k, core, lambda i: other, land_c, 0)

    def s_first(k):
        buf = acc.at[lax.rem(k, acc_ring)]
        return s_line(k, first, lambda i: buf.at[rows_at(i * rp, rp), :], land_p, 1)

    def s_second(k):
        buf = acc.at[lax.rem(k, acc_ring)]
        return s_line(k, second, lambda i: buf.at[rows_at(p * rp + i * rq, rq), :], land_q, pn)

    def s_long(k):
        buf = acc.at[lax.rem(k, acc_ring)]
        return s_line(k, long, lambda i: buf.at[rows_at(p * rp + q * rq + i * rz, rz), :], land_z, pn + qn - 1)

    def after(t, lag, act):
        k = t - lag

        @pl.when((k >= 0) & (k < chunks))
        def _():
            act(k)

    lane = lax.broadcasted_iota(jnp.int32, (1, 128), 1)

    def compute(k):
        buf, dyk = xs.at[lax.rem(k, ring)], dys.at[lax.rem(k, 2)]

        @pl.when(k == 0)
        def _():
            for copy in loads:
                copy.wait()

        dy_copy(k).wait()

        @pl.when(k + 1 < chunks)
        def _():
            dy_start(k + 1)

        hid[:, :128] = jnp.dot(buf[...], dispatch[...], preferred_element_type=F32)

        @pl.loop(0, rows // 64)
        def _(i):
            here = pl.ds(pl.multiple_of(i * 64, 64), 64)
            logits = jnp.where(lane < experts, hid[here, :128], NEG)
            grown = jnp.exp(logits - jnp.max(logits, axis=-1, keepdims=True))
            probs = grown / jnp.sum(grown, axis=-1, keepdims=True)
            gate[here, :] = probs * dyk[here, width:].astype(F32)
            d_gate[here, :] = jnp.zeros((64, 128), F32)

        @pl.loop(0, pairs)
        def _(j):
            cols = pl.ds(pl.multiple_of(j * 4 * share, 4 * share), 4 * share)
            some = pl.ds(pl.multiple_of(j * 2 * share, 2 * share), 2 * share)
            hid[...] = jnp.dot(buf[...], wide[:, cols], preferred_element_type=F32)
            raw[...] = lax.dot_general(dyk[:, :width], down[some, :], (((1,), (1,)), ((), ())), preferred_element_type=F32)

            @pl.loop(0, rows // 32)
            def _(i):
                here = pl.ds(pl.multiple_of(i * 32, 32), 32)
                gates = gate[here, :]
                marks = d_gate[here, :]
                for e in range(2):
                    mark = lane == base + 2 * j + e
                    weight = jnp.sum(jnp.where(mark, gates, 0.0), axis=-1, keepdims=True)
                    g = hid[here, e * share: (e + 1) * share]
                    u = hid[here, (2 + e) * share: (3 + e) * share]
                    d = raw[here, e * share: (e + 1) * share]
                    sigma = jax.nn.sigmoid(g)
                    swish = g * sigma
                    act = swish * u
                    marks = marks + jnp.where(mark, jnp.sum(act * d, axis=-1, keepdims=True), 0.0)
                    d = d * weight
                    gated[here, pl.ds(pl.multiple_of(j * 2 * share + e * share, share), share)] = (act * weight).astype(BF)
                    d_gu[here, pl.ds(pl.multiple_of(j * 4 * share + e * share, share), share)] = (
                        d * u * (sigma + swish * (1.0 - sigma))).astype(BF)
                    d_gu[here, pl.ds(pl.multiple_of(j * 4 * share + (2 + e) * share, share), share)] = (d * swish).astype(BF)
                d_gate[here, :] = marks

        tiles = width // 512

        def input_grads(half, to):
            here = pl.ds(pl.multiple_of(half * rc, rc), rc)

            @pl.loop(0, tiles)
            def _(n):
                cols = pl.ds(pl.multiple_of(n * 512, 512), 512)
                to[:, cols] = lax.dot_general(
                    d_gu[here, :], wide[cols, :], (((1,), (1,)), ((), ())), preferred_element_type=F32).astype(BF)

            to[:, width:] = d_gate[here, :].astype(BF)

        input_grads(1 - c, other)
        start_legs(s_core(k))
        input_grads(c, acc.at[lax.rem(k, acc_ring)])
        slot = lax.rem(k, 2)

        @pl.when(k >= 2)
        def _():
            pltpu.make_async_copy(stage.at[slot], moe.at[k - 2], stage_sem.at[slot]).wait()

        @pl.loop(0, tiles)
        def _(n):
            cols = pl.ds(pl.multiple_of(n * 512, 512), 512)
            stage[slot, :, cols] = jnp.dot(gated[...], down[:, cols], preferred_element_type=F32).astype(BF)
            sum_wide[cols, :] += lax.dot_general(
                buf[:, cols], d_gu[...], (((0,), (0,)), ((), ())), preferred_element_type=F32)
            sum_down[:, cols] += lax.dot_general(
                gated[...], dyk[:, cols], (((0,), (0,)), ((), ())), preferred_element_type=F32)

        pltpu.make_async_copy(stage.at[slot], moe.at[k], stage_sem.at[slot]).start()

    def end_long(k):
        end_legs(s_long(k))
        buf = acc.at[lax.rem(k, acc_ring)]
        total = buf[rows_at(p * rp + q * rq + z * rz, rz), :].astype(F32)
        for j in range(zn - 1):
            total = total + land_z[lax.rem(k, 2), j].astype(F32)
        summed[k] = total.astype(BF)

    def end_second(k):
        end_legs(s_second(k))
        for j in range(qn - 1):
            add_rows(acc.at[lax.rem(k, acc_ring)], p * rp + q * rq, land_q.at[lax.rem(k, 2), j], rq)
        start_legs(s_long(k))

    def end_first(k):
        end_legs(s_first(k))
        for j in range(pn - 1):
            add_rows(acc.at[lax.rem(k, acc_ring)], p * rp, land_p.at[lax.rem(k, 2), j], rp)
        start_legs(s_second(k))

    def end_core(k):
        end_legs(s_core(k))
        add_rows(acc.at[lax.rem(k, acc_ring)], 0, land_c.at[lax.rem(k, 2), 0], rc)
        start_legs(s_first(k))

    def begin(k):
        xs[lax.rem(k, ring), rows_at(c * rc + p * rp + q * rq + z * rz, rz), :] = x[k]
        start_legs(g_long(k))

    def then(one, two):
        def act(k):
            end_legs(one(k))
            start_legs(two(k))

        return act

    @pl.loop(0, chunks + 8)
    def _(t):
        after(t, 8, end_long)
        after(t, 7, end_second)
        after(t, 6, end_first)
        after(t, 5, end_core)
        after(t, 4, lambda k: end_legs(g_core(k)))
        after(t, 3, then(g_first, g_core))
        after(t, 2, then(g_second, g_first))
        after(t, 1, then(g_long, g_second))
        after(t, 0, begin)
        after(t, 4, compute)

    out_down = pltpu.make_async_copy(sum_down, grad_shrink, load.at[0])
    out_down.start()
    for k in range(chunks - 2, chunks):
        pltpu.make_async_copy(stage.at[k % 2], moe.at[k], stage_sem.at[k % 2]).wait()
    for i in range(width // rows):
        here = pl.ds(i * rows, rows)
        if i:
            pltpu.make_async_copy(d_gu, grad_widen.at[here, :], load.at[1]).wait()
        d_gu[...] = sum_wide[here, :].astype(BF)
        pltpu.make_async_copy(d_gu, grad_widen.at[here, :], load.at[1]).start()
    pltpu.make_async_copy(d_gu, grad_widen.at[pl.ds(0, rows), :], load.at[1]).wait()
    out_down.wait()


def experts_together(x, dy, widen, shrink, dispatch, collective_id):
    experts = dispatch.shape[1]
    dispatch = jnp.pad(dispatch, ((0, 0), (0, 128 - experts)))
    groups, parts = lax.axis_size("grp"), lax.axis_size("ep")
    major, minor, xn = mesh_sizes(groups, parts)
    micro, local_rows, width = x.shape
    x = x.reshape(-1, ROWS, width)
    chunks = x.shape[0]
    local_exp, inner = shrink.shape[:2]
    share = inner // groups
    hidden = local_exp * share
    half = ROWS * major * minor * xn
    rows, wide = 2 * half, width + 128
    ring, acc_ring = min(chunks, 6), 4
    legs = major + minor + xn - 2
    vmem = pl.BlockSpec(memory_space=pltpu.VMEM)
    hbm = pl.BlockSpec(memory_space=pl.ANY)
    flops = 2 * chunks * rows * width * hidden * 9
    return pl.pallas_call(
        functools.partial(experts_kernel, groups, parts, local_rows, ring, acc_ring, experts),
        out_shape=[
            jax.ShapeDtypeStruct((chunks, ROWS, wide), BF),
            jax.ShapeDtypeStruct((chunks, rows, width), BF),
            jax.ShapeDtypeStruct((width, 2 * hidden), BF),
            jax.ShapeDtypeStruct((hidden, width), F32),
        ],
        in_specs=[vmem, hbm, hbm, hbm, vmem],
        out_specs=[vmem, hbm, hbm, hbm],
        scratch_shapes=[
            pltpu.VMEM((ring, rows, width), BF),
            pltpu.VMEM((2, rows, wide), BF),
            pltpu.VMEM((width, 2 * hidden), BF),
            pltpu.VMEM((hidden, width), BF),
            pltpu.VMEM((width, 2 * hidden), F32),
            pltpu.VMEM((hidden, width), F32),
            pltpu.VMEM((2, rows, width), BF),
            pltpu.VMEM((acc_ring, half, wide), BF),
            pltpu.VMEM((half, wide), BF),
            pltpu.VMEM((2, 1, half, wide), BF),
            pltpu.VMEM((2, xn - 1, half // xn, wide), BF),
            pltpu.VMEM((2, minor - 1, half // xn // minor, wide), BF),
            pltpu.VMEM((2, major - 1, ROWS, wide), BF),
            pltpu.VMEM((rows, 4 * share), F32),
            pltpu.VMEM((rows, 2 * share), F32),
            pltpu.VMEM((rows, hidden), BF),
            pltpu.VMEM((rows, 2 * hidden), BF),
            pltpu.VMEM((rows, 128), F32),
            pltpu.VMEM((rows, 128), F32),
            pltpu.SemaphoreType.DMA((3 * local_exp,)),
            pltpu.SemaphoreType.DMA((2,)),
            pltpu.SemaphoreType.DMA((2,)),
            pltpu.SemaphoreType.DMA((chunks, legs)),
            pltpu.SemaphoreType.DMA((chunks, legs)),
            pltpu.SemaphoreType.DMA((chunks, legs)),
            pltpu.SemaphoreType.DMA((chunks, legs)),
        ],
        compiler_params=pltpu.CompilerParams(
            collective_id=collective_id, has_side_effects=True, vmem_limit_bytes=60 * 2**20
        ),
        cost_estimate=pl.CostEstimate(flops=flops, bytes_accessed=80 * 2**20, transcendentals=chunks * rows * hidden),
    )(x, dy, widen, shrink, dispatch)


def experts_apart(x, dy_all, specialist_widen_matrix, specialist_shrink_matrix, dispatcher_matrix):
    groups, parts = lax.axis_size("grp"), lax.axis_size("ep")
    group, part = lax.axis_index("grp"), lax.axis_index("ep")
    local_exp, inner, width = specialist_shrink_matrix.shape
    share = inner // groups
    widen = specialist_widen_matrix.reshape(local_exp, width, 2, groups, share)
    widen = lax.dynamic_index_in_dim(widen, group, 3, keepdims=False)
    widen = widen.transpose(1, 2, 0, 3).reshape(width, 2 * local_exp * share)
    shrink = specialist_shrink_matrix.reshape(local_exp, groups, share, width)
    shrink = lax.dynamic_index_in_dim(shrink, group, 1, keepdims=False).reshape(local_exp * share, width)
    x_all = gather_all(x, 1)
    chunk_shape = x_all.shape[:-1]
    x_all, dy_all = x_all.reshape(-1, width), dy_all.reshape(x_all.shape[0] * ROWS * math.prod(chunk_shape[1:-1]), -1)
    keep_all = dy_all[:, width: width + dispatcher_matrix.shape[1]].astype(F32)
    dy_all = dy_all[:, :width]
    router = jax.nn.softmax(jnp.dot(x_all, dispatcher_matrix, preferred_element_type=F32), axis=-1)
    gate = lax.dynamic_slice_in_dim(router * keep_all, part * local_exp, local_exp, axis=1)
    gate = jnp.repeat(gate, share, axis=1)
    gate_up = jnp.dot(x_all, widen, preferred_element_type=F32)
    g, u = gate_up[:, : local_exp * share], gate_up[:, local_exp * share:]
    sigma = jax.nn.sigmoid(g)
    act = g * sigma * u
    gated = (gate * act).astype(BF)
    moe_part = jnp.dot(gated, shrink, preferred_element_type=F32).astype(BF)
    d_raw = lax.dot_general(dy_all, shrink, (((1,), (1,)), ((), ())), preferred_element_type=F32)
    d_gate = jnp.sum((act * d_raw).reshape(-1, local_exp, share), axis=-1)
    d_act = gate * d_raw
    d_gu = jnp.concatenate([d_act * u * sigma * (1.0 + g * (1.0 - sigma)), d_act * (g * sigma)], axis=1).astype(BF)
    dx_part = lax.dot_general(d_gu, widen, (((1,), (1,)), ((), ())), preferred_element_type=F32).astype(BF)
    lanes = jnp.arange(128, dtype=jnp.int32)
    place = (lanes[None, :] == part * local_exp + jnp.arange(local_exp, dtype=jnp.int32)[:, None])
    d_gate = jnp.sum(jnp.where(place[None], d_gate[:, :, None], 0.0), axis=1)
    dx_part = jnp.concatenate([dx_part, d_gate.astype(BF)], axis=1)
    dx_sum = scatter_all(dx_part.reshape(chunk_shape + (width + 128,)), 2)
    grad_widen = lax.dot_general(x_all, d_gu, (((0,), (0,)), ((), ())), preferred_element_type=F32)
    grad_shrink = lax.dot_general(gated, dy_all, (((0,), (0,)), ((), ())), preferred_element_type=F32)
    grad_widen = grad_widen.astype(BF).reshape(width, 2, local_exp // 2, 2, share).transpose(0, 2, 1, 3, 4)
    return dx_sum, moe_part.reshape(chunk_shape + (width,)), grad_widen, grad_shrink


def spread_kernel(share, x, out):
    for i in range(x.shape[0]):
        out[0, :, i * share: (i + 1) * share] = x[i].astype(F32)


def spread(x, local_exp, share):
    groups, rows, _ = x.shape
    if share % 128:
        x = x.reshape(groups, rows, local_exp // 2, 2, 2, share).transpose(2, 4, 1, 3, 0, 5)
        return x.reshape(local_exp, rows, 2 * groups * share).astype(F32)
    return pl.pallas_call(
        functools.partial(spread_kernel, share),
        grid=(local_exp, 2),
        out_shape=jax.ShapeDtypeStruct((local_exp, rows, 2 * groups * share), F32),
        in_specs=[pl.BlockSpec((groups, rows, share), lambda e, h: (0, 0, e // 2 * 4 + h * 2 + e % 2))],
        out_specs=pl.BlockSpec((1, rows, groups * share), lambda e, h: (e, 0, h)),
    )(x)


class Backdrop:
    LAG = 4

    def __init__(self, groups, parts, part, out, acc, land_c, land_p, land_q, land_z, local, send, recv):
        self.core, self.first, self.second, self.long = lines(groups, parts)
        self.part, self.out, self.acc, self.lands = part, out, acc, (land_c, land_p, land_q, land_z)
        self.local, self.send, self.recv = local, send, recv
        self.chunks = part.shape[0]
        pn, qn, zn = self.first.size, self.second.size, self.long.size
        self.rz, self.rq, self.rp, self.rc = ROWS, ROWS * zn, ROWS * zn * qn, ROWS * zn * qn * pn

    @staticmethod
    def scratch(chunks, width):
        major, minor, xn = mesh_sizes(lax.axis_size("grp"), lax.axis_size("ep"))
        half = ROWS * major * minor * xn
        legs = major + minor + xn - 2
        return [
            pltpu.VMEM((4, half, width), BF),
            pltpu.VMEM((2, 1, half, width), BF),
            pltpu.VMEM((2, xn - 1, half // xn, width), BF),
            pltpu.VMEM((2, minor - 1, half // xn // minor, width), BF),
            pltpu.VMEM((2, major - 1, ROWS, width), BF),
            pltpu.SemaphoreType.DMA((chunks,)),
            pltpu.SemaphoreType.DMA((chunks, legs)),
            pltpu.SemaphoreType.DMA((chunks, legs)),
        ]

    def near(self):
        return [self.core, self.first, self.second, self.long]

    def buf(self, k):
        return self.acc.at[lax.rem(k, 4)]

    def own(self, k):
        here = pl.ds(pl.multiple_of(self.core.place * self.rc, self.rc), self.rc)
        return pltpu.make_async_copy(self.part.at[k, here, :], self.buf(k), self.local.at[k])

    def hop(self, k, level):
        c, p, q, z = self.core.place, self.first.place, self.second.place, self.long.place
        pn, qn = self.first.size, self.second.size
        at = lambda start, size: pl.ds(pl.multiple_of(start, ROWS), size)
        line, offset, source = [
            (self.core, 0, lambda i: self.part.at[k, at(i * self.rc, self.rc), :]),
            (self.first, 1, lambda i: self.buf(k).at[at(i * self.rp, self.rp), :]),
            (self.second, pn, lambda i: self.buf(k).at[at(p * self.rp + i * self.rq, self.rq), :]),
            (self.long, pn + qn - 1, lambda i: self.buf(k).at[at(p * self.rp + q * self.rq + i * self.rz, self.rz), :]),
        ][level]
        land = self.lands[level]
        return swap_legs(line, source, lambda j, i: land.at[lax.rem(k, 2), j],
                         lambda j: self.send.at[k, offset + j], lambda j: self.recv.at[k, offset + j])

    def end(self, k, level):
        c, p, q, z = self.core.place, self.first.place, self.second.place, self.long.place
        end_legs(self.hop(k, level))
        if level == 0:
            self.own(k).wait()
        first = [0, p * self.rp, p * self.rp + q * self.rq, p * self.rp + q * self.rq + z * self.rz][level]
        size = [self.rc, self.rp, self.rq, self.rz][level]
        land = self.lands[level]
        if level == 3:
            total = self.buf(k)[pl.ds(pl.multiple_of(first, ROWS), size), :].astype(F32)
            for j in range(land.shape[1]):
                total = total + land[lax.rem(k, 2), j].astype(F32)
            self.out[k] = total.astype(self.out.dtype)
        else:
            for j in range(land.shape[1]):
                add_rows(self.buf(k), first, land.at[lax.rem(k, 2), j], size)
            start_legs(self.hop(k, level + 1))

    def begin(self, k):
        self.own(k).start()
        start_legs(self.hop(k, 0))

    def step(self, t):
        for level in (3, 2, 1, 0):
            k = t - level - 1

            @pl.when((k >= 0) & (k < self.chunks))
            def _(k=k, level=level):
                self.end(k, level)

        @pl.when((t >= 0) & (t < self.chunks))
        def _():
            self.begin(t)


class Sequence:
    def __init__(self, parts, block, micro):
        e = lax.axis_index("ep")
        self.xn, self.block, self.micro, self.e = parts // 2, block, micro, e
        self.x, self.c = lax.div(e, 2), lax.rem(e, 2)
        self.line = Line(parts, e, (0, 1))
        self.line_x = Line(self.xn, self.x, (0, 2))
        self.line_c = Line(2, self.c, (0, 1))

    def at(self, ref, m, x, c):
        return ref.at[m, pl.ds(pl.multiple_of((x * 2 + c) * self.block, self.block), self.block), :]

    def gather_x(self, ref, send, recv):
        legs = []
        for m in range(self.micro):
            legs += swap_legs(
                self.line_x, lambda i, m=m: self.at(ref, m, self.x, self.c), lambda j, i, m=m: self.at(ref, m, i, self.c),
                lambda j, m=m: send.at[m, j], lambda j, m=m: recv.at[m, j])
        return legs

    def gather_c(self, ref, send, recv):
        legs = []
        for m in range(self.micro):
            for x in range(self.xn):
                legs += swap_legs(
                    self.line_c, lambda i, m=m, x=x: self.at(ref, m, x, self.c), lambda j, i, m=m, x=x: self.at(ref, m, x, i),
                    lambda j, m=m, x=x: send.at[m, self.xn - 1 + x], lambda j, m=m, x=x: recv.at[m, self.xn - 1 + x])
        return legs

    def reduce_c(self, ref, land, send, recv):
        legs = []
        for m in range(self.micro):
            for x in range(self.xn):
                legs += swap_legs(
                    self.line_c, lambda i, m=m, x=x: self.at(ref, m, x, i), lambda j, i, m=m, x=x: land.at[m, x],
                    lambda j, m=m, x=x: send.at[m, self.xn - 1 + x], lambda j, m=m, x=x: recv.at[m, self.xn - 1 + x])
        return legs

    def reduce_x(self, ref, land, send, recv):
        legs = []
        for m in range(self.micro):
            legs += swap_legs(
                self.line_x, lambda i, m=m: self.at(ref, m, i, self.c), lambda j, i, m=m: land.at[m, j],
                lambda j, m=m: send.at[m, j], lambda j, m=m: recv.at[m, j])
        return legs

    def add_c(self, ref, land):
        for m in range(self.micro):
            for x in range(self.xn):
                add_rows(ref.at[m], (x * 2 + self.c) * self.block, land.at[m, x], self.block)

    def total_x(self, ref, land, out):
        for m in range(self.micro):
            @pl.loop(0, self.block // ROWS)
            def _(i, m=m):
                here = pl.ds(pl.multiple_of(i * ROWS, ROWS), ROWS)
                total = ref[m, pl.ds(pl.multiple_of(self.e * self.block + i * ROWS, ROWS), ROWS), :].astype(F32)
                for j in range(self.xn - 1):
                    total = total + land[m, j, here, :].astype(F32)
                out[m, here, :] = total


def sum_over_parts(seq, columns, sent, got, send, recv):
    flat = columns.T
    sent[...] = flat[:8]
    legs = swap_legs(seq.line, lambda i: sent, lambda j, i: got.at[j], lambda j: send.at[j], lambda j: recv.at[j])
    start_legs(legs)
    end_legs(legs)
    total = sent[...]
    for j in range(seq.line.size - 1):
        total = total + got[j]
    return jnp.concatenate([total] * 16, axis=0).T


def back_kernel(
    groups, parts, backed,
    branch, merge, triple, queries, keys, values, mixed, probs, hat, inv, gains, cos, sin, part,
    d_proj, d_in, grad_heads, grad_out, summed,
    rows_all, merge_v, triple_v, q_v, k_v, v_v, mixed_v, probs_v, hat_v, d_mixed, d_qk, sums, partial, land_c, land_x, sent, got,
    load, g_send, g_recv, s_send, s_recv, t_send, t_recv, *behind
):
    micro, block, width = branch.shape
    seq = Sequence(parts, block, micro)
    length = queries.shape[1]
    tokens = micro * length
    heads = queries.shape[2] // HD
    scale = 1.0 / math.sqrt(HD)
    loads = [pltpu.make_async_copy(a, b, load.at[i]) for i, (a, b) in enumerate((
        (merge, merge_v), (mixed, mixed_v), (queries, q_v), (keys, k_v), (values, v_v), (probs, probs_v), (hat, hat_v), (triple, triple_v)))]
    for copy in loads:
        copy.start()
    if backed:
        back = Backdrop(groups, parts, part, summed, *behind)
        greet_lines([seq.line] + back.near())
        steps = back.chunks + back.LAG
        step = back.step
    else:
        greet_lines([seq.line])
        steps, step = 0, lambda t: None
        summed[...] = jnp.zeros_like(summed)
    for m in range(micro):
        rows_all[m, pl.ds(pl.multiple_of(seq.e * block, block), block), :] = branch[m]
    gather_x = seq.gather_x(rows_all, g_send, g_recv)
    start_legs(gather_x)
    step(0)
    step(1)
    end_legs(gather_x)
    gather_c = seq.gather_c(rows_all, g_send, g_recv)
    start_legs(gather_c)
    step(2)
    sums[...] = jnp.zeros_like(sums)
    grad_heads[...] = jnp.zeros_like(grad_heads)
    end_legs(gather_c)
    for copy in loads[:2]:
        copy.wait()
    for m in range(micro):
        d_mixed[m] = lax.dot_general(rows_all[m], merge_v[...], (((1,), (1,)), ((), ())), preferred_element_type=F32).astype(BF)

    @pl.loop(0, width // 512)
    def _(n):
        cols = pl.ds(pl.multiple_of(n * 512, 512), 512)
        total = lax.dot_general(mixed_v[0], rows_all[0, :, cols], (((0,), (0,)), ((), ())), preferred_element_type=F32)
        for m in range(1, micro):
            total = total + lax.dot_general(
                mixed_v[m], rows_all[m, :, cols], (((0,), (0,)), ((), ())), preferred_element_type=F32)
        grad_out[:, cols] = total.astype(BF)

    for copy in loads[2:7]:
        copy.wait()
    lane = lax.broadcasted_iota(jnp.int32, (1, 128), 1)

    def one_head(i):
        m, h = lax.div(i, heads), lax.rem(i, heads)
        cols = pl.ds(pl.multiple_of(h * HD, HD), HD)
        here = pl.ds(pl.multiple_of(m * length, length), length)
        d_m = d_mixed[m, :, cols]
        weights = probs_v[m, h]
        low = weights.astype(BF)
        d_proj[2, here, cols] = lax.dot_general(low, d_m, (((0,), (0,)), ((), ())), preferred_element_type=F32).astype(BF)
        d_w = lax.dot_general(d_m, v_v[m, :, cols], (((1,), (1,)), ((), ())), preferred_element_type=F32)
        d_s = (weights * (d_w - jnp.sum(weights * d_w, axis=-1, keepdims=True))).astype(BF)
        d_q = jnp.dot(d_s, k_v[m, :, cols], preferred_element_type=F32) * scale
        d_k = lax.dot_general(d_s, q_v[m, :, cols], (((0,), (0,)), ((), ())), preferred_element_type=F32) * scale
        marks = sums[here, :]
        for c, d in enumerate((d_q, d_k)):
            d = d * cos[...] - pltpu.roll(d, HD // 2, 1) * sin[...]
            d_qk[c, here, cols] = d
            product = d * hat_v[c, here, cols]
            grad_heads[c: c + 1, cols] += jnp.sum(product, axis=0, keepdims=True)
            marks = marks + jnp.where(lane == c, jnp.sum(product * gains[c: c + 1, cols], axis=-1, keepdims=True), 0.0)
        sums[here, :] = marks

    @pl.loop(0, micro * heads)
    def _(i):
        one_head(i)
        step(i + 3)

    done = 3 + micro * heads
    sums[...] = sum_over_parts(seq, sums[...], sent, got, t_send, t_recv)

    @pl.loop(0, tokens // 64)
    def _(i):
        here = pl.ds(pl.multiple_of(i * 64, 64), 64)
        for c in range(2):
            inner = sums[here, c: c + 1] * (1.0 / width)
            d_proj[c, here, :] = (inv[here, c: c + 1] * (
                d_qk[c, here, :] * gains[c: c + 1, :] - hat_v[c, here, :] * inner)).astype(BF)

    loads[7].wait()

    @pl.loop(0, width // 512)
    def _(n):
        cols = pl.ds(pl.multiple_of(n * 512, 512), 512)
        for m in range(micro):
            here = pl.ds(m * length, length)
            total = lax.dot_general(d_proj[0, here, :], triple_v[0, cols, :], (((1,), (1,)), ((), ())), preferred_element_type=F32)
            for c in (1, 2):
                total = total + lax.dot_general(
                    d_proj[c, here, :], triple_v[c, cols, :], (((1,), (1,)), ((), ())), preferred_element_type=F32)
            partial[m, :, cols] = total.astype(BF)

    reduce_c = seq.reduce_c(partial, land_c, s_send, s_recv)
    start_legs(reduce_c)
    end_legs(reduce_c)
    seq.add_c(partial, land_c)
    reduce_x = seq.reduce_x(partial, land_x, s_send, s_recv)
    start_legs(reduce_x)
    for t in range(done, max(done, steps - 1)):
        step(t)
    end_legs(reduce_x)
    seq.total_x(partial, land_x, d_in)
    if steps > done:
        step(steps - 1)


def attention_back(branch, merge, triple, queries, keys, values, mixed, probs, hat, inv, gains, cos, sin, part, collective_id):
    groups, parts = lax.axis_size("grp"), lax.axis_size("ep")
    micro, block, width = branch.shape
    length, local_width = queries.shape[1:]
    tokens = micro * length
    backed = part is not None
    behind = Backdrop.scratch(part.shape[0], width) if backed else []
    summed = (part.shape[0], ROWS, width) if backed else (8, 128)
    vmem = pl.BlockSpec(memory_space=pltpu.VMEM)
    hbm = pl.BlockSpec(memory_space=pl.ANY)
    xn = parts // 2
    return pl.pallas_call(
        functools.partial(back_kernel, groups, parts, backed),
        out_shape=[
            jax.ShapeDtypeStruct((3, tokens, local_width), BF),
            jax.ShapeDtypeStruct((micro, block, width), F32),
            jax.ShapeDtypeStruct((8, local_width), F32),
            jax.ShapeDtypeStruct((local_width, width), BF),
            jax.ShapeDtypeStruct(summed, BF if backed else F32),
        ],
        in_specs=[vmem] + [hbm] * 8 + [vmem] * 4 + [hbm],
        out_specs=[vmem] * 5,
        scratch_shapes=[
            pltpu.VMEM((micro, length, width), BF),
            pltpu.VMEM(merge.shape, BF),
            pltpu.VMEM(triple.shape, BF),
            pltpu.VMEM(queries.shape, BF),
            pltpu.VMEM(queries.shape, BF),
            pltpu.VMEM(queries.shape, BF),
            pltpu.VMEM(queries.shape, BF),
            pltpu.VMEM(probs.shape, F32),
            pltpu.VMEM(hat.shape, F32),
            pltpu.VMEM(queries.shape, BF),
            pltpu.VMEM((2, tokens, local_width), F32),
            pltpu.VMEM((tokens, 128), F32),
            pltpu.VMEM((micro, length, width), BF),
            pltpu.VMEM((micro, xn, block, width), BF),
            pltpu.VMEM((micro, xn - 1, block, width), BF),
            pltpu.VMEM((8, tokens), F32),
            pltpu.VMEM((parts - 1, 8, tokens), F32),
            pltpu.SemaphoreType.DMA((8,)),
            pltpu.SemaphoreType.DMA((micro, 2 * xn - 1)),
            pltpu.SemaphoreType.DMA((micro, 2 * xn - 1)),
            pltpu.SemaphoreType.DMA((micro, 2 * xn - 1)),
            pltpu.SemaphoreType.DMA((micro, 2 * xn - 1)),
            pltpu.SemaphoreType.DMA((parts - 1,)),
            pltpu.SemaphoreType.DMA((parts - 1,)),
        ] + behind,
        compiler_params=pltpu.CompilerParams(
            collective_id=collective_id, has_side_effects=True, vmem_limit_bytes=58 * 2**20
        ),
        cost_estimate=pl.CostEstimate(flops=10**10, bytes_accessed=40 * 2**20, transcendentals=0),
    )(branch, merge, triple, queries, keys, values, mixed, probs, hat, inv, gains, cos, sin,
      part if backed else mixed)


class BackGather:
    LAG = 4

    def __init__(self, groups, parts, own, out, local, send, recv):
        self.core, self.first, self.second, self.long = lines(groups, parts)
        self.own, self.out, self.local, self.send, self.recv = own, out, local, send, recv
        self.chunks = own.shape[0]
        pn, qn, zn = self.first.size, self.second.size, self.long.size
        self.rz, self.rq, self.rp, self.rc = ROWS, ROWS * zn, ROWS * zn * qn, ROWS * zn * qn * pn

    @staticmethod
    def scratch(chunks):
        major, minor, xn = mesh_sizes(lax.axis_size("grp"), lax.axis_size("ep"))
        legs = major + minor + xn - 2
        return [
            pltpu.SemaphoreType.DMA((chunks,)),
            pltpu.SemaphoreType.DMA((chunks, legs)),
            pltpu.SemaphoreType.DMA((chunks, legs)),
        ]

    def near(self):
        return [self.core, self.first, self.second, self.long]

    def rows(self, k, start, size):
        return self.out.at[k, pl.ds(pl.multiple_of(start, ROWS), size), :]

    def mine(self, k):
        c, p, q, z = self.core.place, self.first.place, self.second.place, self.long.place
        return pltpu.make_async_copy(
            self.own.at[k], self.rows(k, c * self.rc + p * self.rp + q * self.rq + z * self.rz, self.rz), self.local.at[k])

    def hop(self, k, level):
        c, p, q, z = self.core.place, self.first.place, self.second.place, self.long.place
        pn, qn, zn = self.first.size, self.second.size, self.long.size
        line, offset, at = [
            (self.long, 0, lambda i: self.rows(k, c * self.rc + p * self.rp + q * self.rq + i * self.rz, self.rz)),
            (self.second, zn - 1, lambda i: self.rows(k, c * self.rc + p * self.rp + i * self.rq, self.rq)),
            (self.first, zn + qn - 2, lambda i: self.rows(k, c * self.rc + i * self.rp, self.rp)),
            (self.core, zn + qn + pn - 3, lambda i: self.rows(k, i * self.rc, self.rc)),
        ][level]
        source = (lambda i: self.own.at[k]) if level == 0 else (lambda i: at(line.place))
        return swap_legs(line, source, lambda j, i: at(i),
                         lambda j: self.send.at[k, offset + j], lambda j: self.recv.at[k, offset + j])

    def step(self, t):
        for level in (3, 2, 1, 0):
            k = t - level - 1

            @pl.when((k >= 0) & (k < self.chunks))
            def _(k=k, level=level):
                end_legs(self.hop(k, level))
                if level == 0:
                    self.mine(k).wait()
                if level < 3:
                    start_legs(self.hop(k, level + 1))

        @pl.when((t >= 0) & (t < self.chunks))
        def _():
            self.mine(t).start()
            start_legs(self.hop(t, 0))


def forward_kernel(
    groups, parts, experts,
    x, dy, routes, quota, gains, head_gains, cos, sin, docs_down, docs_across, triple, merge,
    gathered, q_out, k_out, v_out, mixed, probs, hat, inv, hidden, ffn_in, dy_all,
    dy_own, triple_v, merge_v, sums, partial, land_c, land_x, sent, got,
    load, g_send, g_recv, s_send, s_recv, t_send, t_recv, *behind
):
    micro, block, width = x.shape
    seq = Sequence(parts, block, micro)
    length = gathered.shape[1]
    tokens = micro * length
    heads = q_out.shape[2] // HD
    scale = 1.0 / math.sqrt(HD)
    cuts = block // ROWS
    loads = [pltpu.make_async_copy(triple, triple_v, load.at[0]), pltpu.make_async_copy(merge, merge_v, load.at[1])]
    for copy in loads:
        copy.start()
    back = BackGather(groups, parts, dy_own, dy_all, *behind)
    step, steps = back.step, back.chunks + back.LAG
    lane = lax.broadcasted_iota(jnp.int32, (1, 128), 1)
    earlier = (lax.broadcasted_iota(jnp.int32, (block, block), 1) < lax.broadcasted_iota(jnp.int32, (block, block), 0))
    for m in range(micro):
        @pl.loop(0, cuts)
        def _(r, m=m):
            here = pl.ds(pl.multiple_of(r * ROWS, ROWS), ROWS)
            v = x[m, here, :].astype(F32)
            v = v * lax.rsqrt(jnp.mean(v * v, axis=-1, keepdims=True) + EPS)
            gathered[m, pl.ds(pl.multiple_of(seq.e * block + r * ROWS, ROWS), ROWS), :] = (v * gains[0:1, :]).astype(BF)
    greet_lines([seq.line] + back.near())
    gather_x = seq.gather_x(gathered, g_send, g_recv)
    start_legs(gather_x)
    for m in range(micro):
        chosen = routes[m]
        counts = jnp.zeros((block, 128), F32)
        for j in range(TOP):
            counts = counts + jnp.where(chosen[:, j: j + 1] == lane, 1.0, 0.0)
        prior = jnp.dot(jnp.where(earlier, 1.0, 0.0).astype(BF), counts.astype(BF), preferred_element_type=F32)
        keep = jnp.where((counts > 0.0) & (prior < quota[0:1, :]), 1.0, 0.0).astype(BF)
        for r in range(cuts):
            dy_own[m * cuts + r, :, :width] = dy[m, r * ROWS: (r + 1) * ROWS, :]
            dy_own[m * cuts + r, :, width:] = keep[r * ROWS: (r + 1) * ROWS, :]
    step(0)
    end_legs(gather_x)
    gather_c = seq.gather_c(gathered, g_send, g_recv)
    start_legs(gather_c)
    step(1)
    loads[0].wait()
    end_legs(gather_c)

    @pl.loop(0, micro)
    def _(m):
        here = pl.ds(pl.multiple_of(m * length, length), length)
        marks = jnp.zeros((length, 128), F32)
        for c in range(2):
            raw = jnp.dot(gathered[m], triple_v[c], preferred_element_type=F32)
            hat[c, here, :] = raw
            marks = marks + jnp.where(lane == c, jnp.sum(raw * raw, axis=-1, keepdims=True), 0.0)
        sums[here, :] = marks
        v_out[m] = jnp.dot(gathered[m], triple_v[2], preferred_element_type=F32).astype(BF)
        step(m + 2)

    done = micro + 2
    inv[...] = lax.rsqrt(sum_over_parts(seq, sums[...], sent, got, t_send, t_recv) * (1.0 / width) + EPS)
    loads[1].wait()

    @pl.loop(0, micro * heads)
    def _(i):
        m, h = lax.div(i, heads), lax.rem(i, heads)
        cols = pl.ds(pl.multiple_of(h * HD, HD), HD)
        here = pl.ds(pl.multiple_of(m * length, length), length)
        for c, to in enumerate((q_out, k_out)):
            v = hat[c, here, cols] * inv[here, c: c + 1]
            hat[c, here, cols] = v
            v = v * head_gains[c: c + 1, cols]
            to[m, :, cols] = (v * cos[...] + pltpu.roll(v, HD // 2, 1) * sin[...]).astype(BF)
        scores = lax.dot_general(
            q_out[m, :, cols], k_out[m, :, cols], (((1,), (1,)), ((), ())), preferred_element_type=F32) * scale
        allowed = (docs_down[m] == docs_across[m]) & (
            lax.broadcasted_iota(jnp.int32, (length, length), 1) <= lax.broadcasted_iota(jnp.int32, (length, length), 0))
        scores = jnp.where(allowed, scores, NEG)
        grown = jnp.exp(scores - jnp.max(scores, axis=-1, keepdims=True))
        weights = grown / jnp.sum(grown, axis=-1, keepdims=True)
        probs[m, h] = weights
        mixed[m, :, cols] = jnp.dot(weights.astype(BF), v_out[m, :, cols], preferred_element_type=F32).astype(BF)

        @pl.when(lax.rem(i, 2) == 1)
        def _():
            step(done + lax.div(i, 2))

    done = done + micro * heads // 2

    @pl.loop(0, width // 512)
    def _(n):
        cols = pl.ds(pl.multiple_of(n * 512, 512), 512)
        for m in range(micro):
            partial[m, :, cols] = jnp.dot(mixed[m], merge_v[:, cols], preferred_element_type=F32).astype(BF)

    reduce_c = seq.reduce_c(partial, land_c, s_send, s_recv)
    start_legs(reduce_c)
    end_legs(reduce_c)
    seq.add_c(partial, land_c)
    reduce_x = seq.reduce_x(partial, land_x, s_send, s_recv)
    start_legs(reduce_x)
    step(done)
    end_legs(reduce_x)
    seq.total_x(partial, land_x, hidden)
    for m in range(micro):
        @pl.loop(0, cuts)
        def _(r, m=m):
            here = pl.ds(pl.multiple_of(r * ROWS, ROWS), ROWS)
            v = hidden[m, here, :] + x[m, here, :].astype(F32)
            hidden[m, here, :] = v
            v = v * lax.rsqrt(jnp.mean(v * v, axis=-1, keepdims=True) + EPS)
            ffn_in[m, here, :] = (v * gains[1:2, :]).astype(BF)
    for t in range(done + 1, steps):
        step(t)


def attention_forward(x, dy, routes, quota, gains, head_gains, cos, sin, docs, triple, merge, experts, collective_id):
    groups, parts = lax.axis_size("grp"), lax.axis_size("ep")
    major, minor, xn = mesh_sizes(groups, parts)
    micro, block, width = x.shape
    length = docs.shape[1]
    local_width = triple.shape[2]
    heads = local_width // HD
    tokens = micro * length
    chunks = micro * block // ROWS
    rows = 2 * xn * minor * major * ROWS
    vmem = pl.BlockSpec(memory_space=pltpu.VMEM)
    hbm = pl.BlockSpec(memory_space=pl.ANY)
    low = jax.ShapeDtypeStruct((micro, length, local_width), BF)
    quota = jnp.pad(quota.astype(F32), (0, 128 - experts)).reshape(1, 128)
    return pl.pallas_call(
        functools.partial(forward_kernel, groups, parts, experts),
        out_shape=[
            jax.ShapeDtypeStruct((micro, length, width), BF),
            low, low, low, low,
            jax.ShapeDtypeStruct((micro, heads, length, length), F32),
            jax.ShapeDtypeStruct((2, tokens, local_width), F32),
            jax.ShapeDtypeStruct((tokens, 128), F32),
            jax.ShapeDtypeStruct((micro, block, width), F32),
            jax.ShapeDtypeStruct((micro, block, width), BF),
            jax.ShapeDtypeStruct((chunks, rows, width + 128), BF),
        ],
        in_specs=[vmem] * 10 + [hbm] * 2,
        out_specs=[vmem] * 10 + [hbm],
        scratch_shapes=[
            pltpu.VMEM((chunks, ROWS, width + 128), BF),
            pltpu.VMEM(triple.shape, BF),
            pltpu.VMEM(merge.shape, BF),
            pltpu.VMEM((tokens, 128), F32),
            pltpu.VMEM((micro, length, width), BF),
            pltpu.VMEM((micro, xn, block, width), BF),
            pltpu.VMEM((micro, xn - 1, block, width), BF),
            pltpu.VMEM((8, tokens), F32),
            pltpu.VMEM((parts - 1, 8, tokens), F32),
            pltpu.SemaphoreType.DMA((2,)),
            pltpu.SemaphoreType.DMA((micro, 2 * xn - 1)),
            pltpu.SemaphoreType.DMA((micro, 2 * xn - 1)),
            pltpu.SemaphoreType.DMA((micro, 2 * xn - 1)),
            pltpu.SemaphoreType.DMA((micro, 2 * xn - 1)),
            pltpu.SemaphoreType.DMA((parts - 1,)),
            pltpu.SemaphoreType.DMA((parts - 1,)),
        ] + BackGather.scratch(chunks),
        compiler_params=pltpu.CompilerParams(
            collective_id=collective_id, has_side_effects=True, vmem_limit_bytes=56 * 2**20
        ),
        cost_estimate=pl.CostEstimate(flops=6 * 10**9, bytes_accessed=40 * 2**20, transcendentals=0),
    )(x, dy, routes, quota, gains, head_gains, cos, sin, docs[:, :, None], docs[:, None, :], triple, merge)


def per_device(
    block_entry_states,
    document_labels,
    token_assignments,
    worker_quota_tallies,
    rescale_factors_both,
    triple_projection_matrix,
    probe_lookup_scalers,
    heads_merge_matrix,
    dispatcher_matrix,
    specialist_widen_matrix,
    specialist_shrink_matrix,
    output_gradient,
):
    micro, local_rows, width = block_entry_states.shape
    groups, parts = lax.axis_size("grp"), lax.axis_size("ep")
    major, minor, xs = mesh_sizes(groups, parts)
    group = lax.axis_index("grp")
    part = lax.axis_index("ep")
    seq_len = document_labels.shape[1]
    experts = dispatcher_matrix.shape[1]
    local_exp = specialist_widen_matrix.shape[0]
    inner = specialist_shrink_matrix.shape[1]
    share = inner // groups
    local_width = triple_projection_matrix.shape[2]
    heads = local_width // HD
    scale = 1.0 / math.sqrt(HD)
    gains = rescale_factors_both.astype(F32)
    head_gains = probe_lookup_scalers.astype(F32)
    cos, sin = rope_tables(seq_len, HD)
    signed_sin = jnp.concatenate([-sin[:, : HD // 2], sin[:, HD // 2:]], axis=-1)
    triple = triple_projection_matrix.transpose(1, 0, 2)
    gathered, queries, keys, values, mixed, weights, qk_hat, qk_inv, hidden, ffn_in, dy_all = attention_forward(
        block_entry_states, output_gradient, token_assignments, worker_quota_tallies, gains, head_gains, cos, signed_sin,
        document_labels, triple, heads_merge_matrix, experts, 0)

    fused = xs == minor and share % 128 == 0 and local_exp % 2 == 0 and 2 * xs * minor * major * ROWS <= 512
    chunk_shape = (micro * local_rows // ROWS, 2, xs, minor, major, ROWS)
    if fused:
        dx_sum, moe_part, grad_widen, grad_shrink = experts_together(
            ffn_in, dy_all, specialist_widen_matrix, specialist_shrink_matrix, dispatcher_matrix, 1)
    else:
        dx_sum, moe_part, grad_widen, grad_shrink = experts_apart(
            ffn_in, dy_all, specialist_widen_matrix, specialist_shrink_matrix, dispatcher_matrix)
    dx_sum = dx_sum.astype(F32).reshape(micro, local_rows, width + 128)
    grad_widen = lax.all_to_all(grad_widen.reshape(groups, width // groups, -1), "grp", 0, 0, tiled=True)
    grad_widen = spread(grad_widen, local_exp, share)
    grad_shrink = grad_shrink.reshape(local_exp, share, width)

    expert_ids = jnp.arange(experts, dtype=jnp.int32)
    counts = jnp.sum((token_assignments[..., None] == expert_ids).astype(jnp.int32), axis=2)
    keep = (counts > 0) & (jnp.cumsum(counts, axis=1) - counts < worker_quota_tallies)
    inv_second = lax.rsqrt(jnp.mean(hidden * hidden, axis=-1, keepdims=True) + EPS)
    hat_second = hidden * inv_second
    probs = jax.nn.softmax(jnp.einsum("mtd,de->mte", ffn_in, dispatcher_matrix, preferred_element_type=F32), axis=-1)
    d_probs = jnp.where(keep, dx_sum[..., width: width + experts], 0.0)
    d_logits = probs * (d_probs - jnp.sum(probs * d_probs, axis=-1, keepdims=True))
    d_ffn = dx_sum[..., :width] + jnp.einsum("mte,de->mtd", d_logits, dispatcher_matrix.astype(F32), precision=HIGH)
    grad_router = jnp.einsum("mtd,mte->ed", ffn_in.astype(F32), d_logits, precision=HIGH)
    scaled = d_ffn * gains[1]
    adjoint = output_gradient.astype(F32)
    d_hidden = adjoint + inv_second * (scaled - hat_second * jnp.mean(scaled * hat_second, axis=-1, keepdims=True))
    grad_second = jnp.sum(d_ffn * hat_second, axis=(0, 1))

    d_proj, d_attn_in, grad_heads, grad_out, moe = attention_back(
        d_hidden.astype(BF), heads_merge_matrix, triple, queries, keys, values, mixed, weights,
        qk_hat, qk_inv, head_gains, cos, signed_sin, moe_part if fused else None, 5)
    if not fused:
        moe = scatter_all(moe_part.reshape(chunk_shape + (width,)), 3)
    output = (hidden + moe.astype(F32).reshape(micro, local_rows, width)).astype(BF)
    grad_heads = grad_heads[:2]
    grad_qkv = jnp.einsum("td,ctf->cdf", gathered.reshape(-1, width), d_proj, preferred_element_type=F32).astype(BF)
    skip = block_entry_states.astype(F32)
    inv_first = lax.rsqrt(jnp.mean(skip * skip, axis=-1, keepdims=True) + EPS)
    hat_first = skip * inv_first
    scaled = d_attn_in * gains[0]
    grad_input = d_hidden + inv_first * (scaled - hat_first * jnp.mean(scaled * hat_first, axis=-1, keepdims=True))
    grad_first = jnp.sum(d_attn_in * hat_first, axis=(0, 1))

    misc = jnp.concatenate([grad_first[None], grad_second[None], grad_router])
    misc = lax.psum(misc, "ep").reshape(-1)
    misc = jnp.concatenate([misc, grad_heads.reshape(-1)])
    small = major * minor * ROWS * 128
    misc_size = misc.shape[0]
    misc = jnp.pad(misc, (0, -misc_size % small)).reshape(1, minor, major, ROWS, -1).astype(BF)
    qkv_cut = grad_qkv.reshape(6, minor, major, -1, local_width)
    out_low = grad_out
    near = out_low[: local_width // 2].reshape(1, minor, major, -1, width)
    far = out_low[local_width // 2:].reshape(1, major, minor, -1, width)
    qkv_sum, near_sum, far_sum, misc_sum = total_over_groups(
        [qkv_cut, near, far, misc], (False, False, True, False), 4)
    qkv_sum = qkv_sum.reshape(3, width, local_width).astype(F32).transpose(1, 0, 2)
    out_sum = jnp.concatenate([near_sum.reshape(-1, width), far_sum.reshape(-1, width)]).astype(F32)
    misc_sum = misc_sum.reshape(-1)[:misc_size].astype(F32)
    rows = misc_sum[: (2 + experts) * width].reshape(2 + experts, width)
    return (
        output,
        grad_input,
        rows[:2],
        qkv_sum,
        misc_sum[(2 + experts) * width:].reshape(2, local_width),
        out_sum,
        rows[2:].T,
        grad_widen,
        grad_shrink,
    )


def solution(mesh):
    return jax.shard_map(
        per_device,
        mesh=mesh,
        in_specs=(
            P(None, ALL, None),
            P(None, "grp"),
            P(None, ALL, None),
            P(),
            P(),
            P(None, None, "ep"),
            P(None, "ep"),
            P("ep", None),
            P(),
            P("ep", None, None),
            P("ep", None, None),
            P(None, ALL, None),
        ),
        out_specs=(
            P(None, ALL, None),
            P(None, ALL, None),
            P(),
            P(None, None, "ep"),
            P(None, "ep"),
            P("ep", None),
            P(),
            P("ep", "grp", None),
            P("ep", "grp", None),
        ),
        check_vma=False,
    )
```

```python
import functools
import math

import jax
import jax.numpy as jnp
import numpy as np
from jax import lax
from jax.experimental import pallas as pl
from jax.experimental.pallas import tpu as pltpu
from jax.sharding import PartitionSpec as P

HD = 128
TOP = 8
EPS = 1e-05
THETA = 10000.0
NEG = -1e30
HIGH = lax.Precision.HIGHEST
ALL = ("grp", "ep")
MESH = pl.DeviceIdType.MESH
ROWS = 16
BF = jnp.bfloat16
F32 = jnp.float32


def rope_tables(length, head_dim):
    half = head_dim // 2
    angle = np.arange(length)[:, None] * THETA ** (-np.arange(half) * 2.0 / head_dim)
    cos, sin = np.cos(angle), np.sin(angle)
    return np.concatenate([cos, cos], 1).astype(np.float32), np.concatenate([-sin, sin], 1).astype(np.float32)


def mesh_sizes(groups, parts):
    major = 4 if groups % 4 == 0 else groups
    return major, groups // major, parts // 2


class Line:
    def __init__(self, size, place, step):
        self.size, self.place, self.step = size, place, step

    def at(self, hops):
        return (
            lax.axis_index("grp") + hops * self.step[0],
            lax.axis_index("ep") + hops * self.step[1],
        )


def lines(groups, parts):
    major, minor, xs = mesh_sizes(groups, parts)
    g, e = lax.axis_index("grp"), lax.axis_index("ep")
    core = lax.rem(e, 2)
    x_pos, minor_pos = lax.div(e, 2), lax.rem(g, minor)
    if xs == minor:
        first = Line(xs, jnp.where(core == 0, x_pos, minor_pos), (core, 2 - 2 * core))
        second = Line(xs, jnp.where(core == 0, minor_pos, x_pos), (1 - core, 2 * core))
    else:
        first = Line(xs, x_pos, (0, 2))
        second = Line(minor, minor_pos, (1, 0))
    return Line(2, core, (0, 1)), first, second, Line(major, lax.div(g, minor), (minor, 0))


def greet(some, whole=()):
    barrier = pltpu.get_barrier_semaphore()
    peers = sum(line.size - 1 for line in whole)
    for line in whole:
        for j in range(1, line.size):
            to = lax.rem(line.place + j, line.size)
            pl.semaphore_signal(barrier, inc=1, device_id=line.at(to - line.place), device_id_type=MESH)
    for line in some:
        if line.size == 2:
            pl.semaphore_signal(barrier, inc=1, device_id=line.at(1 - 2 * line.place), device_id_type=MESH)
            peers = peers + 1
        else:
            for way, there in ((1, line.place < line.size - 1), (-1, line.place > 0)):

                @pl.when(there)
                def _(line=line, way=way):
                    pl.semaphore_signal(barrier, inc=1, device_id=line.at(way), device_id_type=MESH)

                peers = peers + there.astype(jnp.int32)
    pl.semaphore_wait(barrier, peers)


def greet_lines(some):
    barrier = pltpu.get_barrier_semaphore()
    for line in some:
        for j in range(1, line.size):
            to = lax.rem(line.place + j, line.size)
            pl.semaphore_signal(barrier, inc=1, device_id=line.at(to - line.place), device_id_type=MESH)
    pl.semaphore_wait(barrier, sum(line.size - 1 for line in some))


def remote(src, dst, send, recv, target):
    return pltpu.make_async_remote_copy(
        src_ref=src, dst_ref=dst, send_sem=send, recv_sem=recv, device_id=target, device_id_type=MESH
    )


class Hop:
    def __init__(self, legs, after=None):
        self.legs, self.after = legs, after

    def _each(self, which, act):
        for leg in self.legs:
            if leg[which] is None:
                act(leg)
            else:
                pl.when(leg[which])(functools.partial(act, leg))

    def start(self):
        self._each(0, lambda leg: leg[2]().start())

    def arrive(self):
        def act(leg):
            leg[3]().wait_recv()
            if leg[4] is not None:
                leg[4]()

        self._each(1, act)

    def sent(self):
        self._each(0, lambda leg: leg[2]().wait_send())


def gather_hops(line, at, send, recv):
    n, a = line.size, line.place
    if n == 2:
        mine, theirs, peer = at(a), at(1 - a), line.at(1 - 2 * a)
        return [
            Hop([(None, None, lambda: remote(mine, mine, send(0), recv(0), peer),
                  lambda: remote(theirs, theirs, send(0), recv(0), peer), None)])
        ]
    hops = []
    for s in range(1, n):
        legs = []
        for d, way in enumerate((1, -1)):
            k = (s - 1) * 2 + d
            out = a - way * (s - 1)
            into = a - way * s
            sends = (out >= 0) & (out < n) & (a + way >= 0) & (a + way < n)
            gets = (into >= 0) & (into < n)
            out, into = jnp.clip(out, 0, n - 1), jnp.clip(into, 0, n - 1)
            legs.append((
                sends, gets,
                lambda out=out, way=way, k=k: remote(at(out), at(out), send(k), recv(k), line.at(way)),
                lambda into=into, way=way, k=k: remote(at(into), at(into), send(k), recv(k), line.at(-way)),
                None,
            ))
        hops.append(Hop(legs))
    return hops


def reduce_hops(line, acc, land, add, send, recv):
    n, a = line.size, line.place
    if n == 2:
        peer = line.at(1 - 2 * a)
        return [
            Hop([(None, None, lambda: remote(acc(1 - a), land(0), send(0), recv(0), peer),
                  lambda: remote(land(0), land(0), send(0), recv(0), peer),
                  lambda: add(acc(a), land(0)))])
        ]
    hops = []
    for s in range(n - 1):
        legs = []
        for d, way in enumerate((1, -1)):
            k = s * 2 + d
            b = a if way == 1 else n - 1 - a
            sends = (b <= s) & (b < n - 1)
            gets = (b - 1 <= s) & (b >= 1)
            out = b + n - 1 - s
            into = b + n - 2 - s
            out, into = jnp.clip(out, 0, n - 1), jnp.clip(into, 0, n - 1)
            if way == -1:
                out, into = n - 1 - out, n - 1 - into
            legs.append((
                sends, gets,
                lambda out=out, way=way, k=k: remote(acc(out), land(k), send(k), recv(k), line.at(way)),
                lambda way=way, k=k: remote(land(k), land(k), send(k), recv(k), line.at(-way)),
                lambda into=into, k=k: add(acc(into), land(k)),
            ))
        hops.append(Hop(legs))
    return hops


def hop_count(n):
    return 1 if n == 2 else n - 1


def leg_count(n):
    return 1 if n == 2 else 2 * (n - 1)


def flow(chains):
    depth, count = max(len(c) for c in chains), len(chains)
    for t in range(count + depth):
        for k in range(count):
            i = t - k
            if 1 <= i <= len(chains[k]):
                chains[k][i - 1].arrive()
            if 0 <= i < len(chains[k]):
                chains[k][i].start()
    for chain in chains:
        for hop in chain:
            hop.sent()


def add(acc, land):
    lead = acc.shape[:-2]

    def one(i):
        where = []
        for size in reversed(lead):
            where.insert(0, lax.rem(i, size))
            i = lax.div(i, size)
        where = tuple(where) + (slice(None), slice(None))
        acc[where] = (acc[where].astype(F32) + land[where].astype(F32)).astype(acc.dtype)

    if lead:
        pl.loop(0, math.prod(lead))(one)
    else:
        one(0)


def gather_kernel(groups, parts, x, out, local, send, recv):
    core, first, second, long = lines(groups, parts)
    c, p, q, z = core.place, first.place, second.place, long.place
    greet([core, first, second, long])
    chunks = x.shape[0]
    own = [pltpu.make_async_copy(x.at[k], out.at[k, c, p, q, z], local.at[k]) for k in range(chunks)]
    for copy in own:
        copy.start()
    chains = []
    for k in range(chunks):
        base = [0]

        def sems(n, k=k, base=base):
            b = base[0]
            base[0] += leg_count(n)
            return (lambda i: send.at[k, b + i]), (lambda i: recv.at[k, b + i])

        chain = []
        chain += gather_hops(long, lambda i, k=k: out.at[k, c, p, q, i], *sems(long.size))
        chain += gather_hops(second, lambda i, k=k: out.at[k, c, p, i], *sems(second.size))
        chain += gather_hops(first, lambda i, k=k: out.at[k, c, i], *sems(first.size))
        chain += gather_hops(core, lambda i, k=k: out.at[k, i], *sems(2))
        chains.append(chain)
    for copy in own:
        copy.wait()
    flow(chains)


def gather_all(x, collective_id):
    groups, parts = lax.axis_size("grp"), lax.axis_size("ep")
    major, minor, xs = mesh_sizes(groups, parts)
    width = x.shape[-1]
    x = x.reshape(-1, ROWS, width)
    legs = sum(leg_count(n) for n in (2, xs, minor, major))
    chunks = x.shape[0]
    return pl.pallas_call(
        functools.partial(gather_kernel, groups, parts),
        out_shape=jax.ShapeDtypeStruct((chunks, 2, xs, minor, major, ROWS, width), x.dtype),
        in_specs=[pl.BlockSpec(memory_space=pl.ANY)],
        out_specs=pl.BlockSpec(memory_space=pl.ANY),
        scratch_shapes=[
            pltpu.SemaphoreType.DMA((chunks,)),
            pltpu.SemaphoreType.DMA((chunks, legs)),
            pltpu.SemaphoreType.DMA((chunks, legs)),
        ],
        compiler_params=pltpu.CompilerParams(collective_id=collective_id, has_side_effects=True),
    )(x)


def scatter_kernel(groups, parts, part, out, acc, land_c, land_p, land_q, land_z, local, send, recv):
    core, first, second, long = lines(groups, parts)
    c, p, q, z = core.place, first.place, second.place, long.place
    chunks = part.shape[0]
    own = [pltpu.make_async_copy(part.at[k, c], acc.at[k], local.at[k]) for k in range(chunks)]
    for copy in own:
        copy.start()
    greet([core, first, second, long])
    chains = []
    for k in range(chunks):
        base = [0]

        def sems(n, k=k, base=base):
            b = base[0]
            base[0] += leg_count(n)
            return (lambda i: send.at[k, b + i]), (lambda i: recv.at[k, b + i])

        def add_own(acc_ref, land_ref, k=k):
            own[k].wait()
            add(acc_ref, land_ref)

        s, r = sems(2)
        peer = core.at(1 - 2 * c)
        other = part.at[k, 1 - c]
        chain = [Hop([(
            None, None,
            lambda other=other, s=s, r=r, k=k: remote(other, land_c.at[k], s(0), r(0), peer),
            lambda s=s, r=r, k=k: remote(land_c.at[k], land_c.at[k], s(0), r(0), peer),
            lambda k=k, add_own=add_own: add_own(acc.at[k], land_c.at[k]),
        )])]
        chain += reduce_hops(first, lambda i, k=k: acc.at[k, i], lambda i, k=k: land_p.at[k, i], add, *sems(first.size))
        chain += reduce_hops(second, lambda i, k=k: acc.at[k, p, i], lambda i, k=k: land_q.at[k, i], add, *sems(second.size))
        chain += reduce_hops(long, lambda i, k=k: acc.at[k, p, q, i], lambda i, k=k: land_z.at[k, i], add, *sems(long.size))
        chains.append(chain)
    flow(chains)
    for k in range(chunks):
        out[k] = acc[k, p, q, z]


def scatter_all(part, collective_id):
    groups, parts = lax.axis_size("grp"), lax.axis_size("ep")
    major, minor, xs = mesh_sizes(groups, parts)
    legs = sum(leg_count(n) for n in (2, xs, minor, major))
    chunks, width = part.shape[0], part.shape[-1]
    unit = 2 * ROWS * width
    need = unit * (2 * xs * minor * major + leg_count(xs) * minor * major + leg_count(minor) * major + leg_count(major) + 2)
    per = chunks
    while per > 1 and per * need > 44 * 2**20:
        per //= 2
    call = pl.pallas_call(
        functools.partial(scatter_kernel, groups, parts),
        out_shape=jax.ShapeDtypeStruct((per, ROWS, width), BF),
        in_specs=[pl.BlockSpec(memory_space=pl.ANY)],
        out_specs=pl.BlockSpec(memory_space=pltpu.VMEM),
        scratch_shapes=[
            pltpu.VMEM((per, xs, minor, major, ROWS, width), BF),
            pltpu.VMEM((per, xs, minor, major, ROWS, width), BF),
            pltpu.VMEM((per, leg_count(xs), minor, major, ROWS, width), BF),
            pltpu.VMEM((per, leg_count(minor), major, ROWS, width), BF),
            pltpu.VMEM((per, leg_count(major), ROWS, width), BF),
            pltpu.SemaphoreType.DMA((per,)),
            pltpu.SemaphoreType.DMA((per, legs)),
            pltpu.SemaphoreType.DMA((per, legs)),
        ],
        compiler_params=pltpu.CompilerParams(
            collective_id=collective_id, has_side_effects=True, vmem_limit_bytes=56 * 2**20
        ),
    )
    return jnp.concatenate([call(part[i:i + per]) for i in range(0, chunks, per)]) if per < chunks else call(part)


class Begun:
    def __init__(self, hop, before):
        self.hop, self.before = hop, before

    def start(self):
        self.before()
        self.hop.start()

    def arrive(self):
        self.hop.arrive()

    def sent(self):
        self.hop.sent()


def total_kernel(groups, parts, far_first, rows_in, d_proj, out_near, out_far, shared, own, *refs):
    count = len(far_first)
    outs, acc, land_one, land_two = (refs[i * count: (i + 1) * count] for i in range(4))
    rows_v, proj_v, shared_v, own_v, got, local, stored, send, recv, t_send, t_recv = refs[4 * count:]
    major, minor, _ = mesh_sizes(groups, parts)
    g, e = lax.axis_index("grp"), lax.axis_index("ep")
    short = Line(minor, lax.rem(g, minor), (1, 0))
    long = Line(major, lax.div(g, minor), (minor, 0))
    whole = Line(parts, e, (0, 1))
    width = rows_in.shape[1]
    load = [pltpu.make_async_copy(a, b, local.at[i]) for i, (a, b) in enumerate((
        (out_near, acc[0].at[0]), (out_far, acc[1].at[0]), (rows_in, rows_v), (d_proj, proj_v), (shared, shared_v), (own, own_v)))]
    for copy in load:
        copy.start()

    def weights(k):
        def act():
            if k == 0:
                load[2].wait()
                load[3].wait()
            halves = acc[2].shape[0] // 3
            c, half = k // halves, k % halves
            rows = math.prod(acc[2].shape[2:4])

            @pl.loop(0, acc[2].shape[1])
            def _(i):
                cols = pl.ds(pl.multiple_of(half * (width // halves) + i * rows, rows), rows)
                total = lax.dot_general(rows_v[:, cols], proj_v[c], (((0,), (0,)), ((), ())), preferred_element_type=F32)
                acc[2][k, i] = total.astype(BF).reshape(acc[2].shape[2:])

        return act

    swap = swap_legs(whole, lambda i: shared_v, lambda j, i: got.at[j], lambda j: t_send.at[j], lambda j: t_recv.at[j])

    def everyone():
        end_legs(swap)
        load[5].wait()

        @pl.loop(0, major * minor)
        def _(i):
            where = (lax.div(i, major), lax.rem(i, major))
            total = shared_v[where].astype(F32) + own_v[where].astype(F32)
            for j in range(parts - 1):
                total = total + got[(j,) + where].astype(F32)
            acc[3][(0,) + where] = total.astype(BF)

    before = {(0, 0): load[0].wait, (1, 0): load[1].wait, (3, 0): everyone}
    chains, number = [], 0
    for j in range(count):
        one, two = (long, short) if far_first[j] else (short, long)
        y, z = one.place, two.place
        for k in range(acc[j].shape[0]):
            store = pltpu.make_async_copy(acc[j].at[k, y, z], outs[j].at[k, y, z], stored.at[number])
            base = [0]

            def sems(n, number=number, base=base):
                b = base[0]
                base[0] += leg_count(n)
                return (lambda i: send.at[number, b + i]), (lambda i: recv.at[number, b + i])

            down = reduce_hops(one, lambda i, j=j, k=k: acc[j].at[k, i], lambda i, j=j, k=k: land_one[j].at[k, i], add, *sems(one.size))
            down += reduce_hops(two, lambda i, j=j, k=k, y=y: acc[j].at[k, y, i], lambda i, j=j, k=k: land_two[j].at[k, i], add, *sems(two.size))
            up = gather_hops(two, lambda i, j=j, k=k, y=y: outs[j].at[k, y, i], *sems(two.size))
            up += gather_hops(one, lambda i, j=j, k=k: outs[j].at[k, i], *sems(one.size))

            def put(store=store):
                store.start()
                store.wait()

            down[0] = Begun(down[0], before.get((j, k)) or weights(k))
            up[0] = Begun(up[0], put)
            chains.append(down + up)
            number += 1
    greet([short, long], [whole])
    load[4].wait()
    start_legs(swap)
    flow(chains)


def total_over_groups(gathered, d_proj, grad_out, shared, own, collective_id):
    groups, parts = lax.axis_size("grp"), lax.axis_size("ep")
    major, minor, _ = mesh_sizes(groups, parts)
    tokens, width = gathered.shape
    local_width = d_proj.shape[2]
    half = grad_out.shape[0] // 2
    shapes = [
        (1, minor, major, half // groups, width),
        (1, major, minor, half // groups, width),
        (6, minor, major, 3 * width // 6 // groups, local_width),
        (1,) + shared.shape,
    ]
    legs = 2 * (leg_count(minor) + leg_count(major))
    total = sum(a[0] for a in shapes)
    hbm = pl.BlockSpec(memory_space=pl.ANY)
    scratch = [pltpu.VMEM(a, BF) for a in shapes]
    scratch += [pltpu.VMEM((a[0], leg_count(a[1])) + a[2:], BF) for a in shapes]
    scratch += [pltpu.VMEM((a[0], leg_count(a[2])) + a[3:], BF) for a in shapes]
    return pl.pallas_call(
        functools.partial(total_kernel, groups, parts, (False, True, False, False)),
        out_shape=[jax.ShapeDtypeStruct(a, BF) for a in shapes],
        in_specs=[hbm] * 6,
        out_specs=[hbm] * len(shapes),
        scratch_shapes=scratch + [
            pltpu.VMEM(gathered.shape, BF),
            pltpu.VMEM(d_proj.shape, BF),
            pltpu.VMEM(shared.shape, BF),
            pltpu.VMEM(shared.shape, BF),
            pltpu.VMEM((parts - 1,) + shared.shape, BF),
            pltpu.SemaphoreType.DMA((6,)),
            pltpu.SemaphoreType.DMA((total,)),
            pltpu.SemaphoreType.DMA((total, legs)),
            pltpu.SemaphoreType.DMA((total, legs)),
            pltpu.SemaphoreType.DMA((parts - 1,)),
            pltpu.SemaphoreType.DMA((parts - 1,)),
        ],
        compiler_params=pltpu.CompilerParams(
            collective_id=collective_id, has_side_effects=True, vmem_limit_bytes=48 * 2**20
        ),
        cost_estimate=pl.CostEstimate(flops=6 * tokens * width * local_width, bytes_accessed=40 * 2**20, transcendentals=0),
    )(gathered, d_proj, grad_out[:half].reshape(shapes[0][1:]), grad_out[half:].reshape(shapes[1][1:]), shared, own)


def swap_legs(line, source, target, send, recv):
    n, a = line.size, line.place
    legs = []
    for j in range(1, n):
        to, off = lax.rem(a + j, n), lax.rem(a + n - j, n)
        legs.append((
            lambda to=to, j=j: remote(source(to), target(j - 1, a), send(j - 1), recv(j - 1), line.at(to - a)),
            lambda off=off, j=j: remote(target(j - 1, off), target(j - 1, off), send(j - 1), recv(j - 1), line.at(off - a)),
        ))
    return legs


def start_legs(legs):
    for out, _ in legs:
        out().start()


def end_legs(legs):
    for out, into in legs:
        into().wait_recv()
    for out, into in legs:
        out().wait_send()


def add_and_send(acc, first, land, rows, line, send):
    def add(place, count):
        @pl.loop(0, count * rows // line.size // ROWS)
        def _(i):
            offset = place * (rows // line.size) + i * ROWS
            here = pl.ds(pl.multiple_of(first + offset, ROWS), ROWS)
            there = pl.ds(pl.multiple_of(offset, ROWS), ROWS)
            total = acc[here, :].astype(F32)
            for j in range(land.shape[0]):
                total = total + land[j, there, :].astype(F32)
            acc[here, :] = total.astype(acc.dtype)

    if line.size == 2:
        add(1 - line.place, 1)
        send()
        add(line.place, 1)
    else:
        add(0, line.size)
        send()


def add_rows(acc, first, land, rows):
    @pl.loop(0, rows // ROWS)
    def _(i):
        here = pl.ds(pl.multiple_of(first + i * ROWS, ROWS), ROWS)
        there = pl.ds(pl.multiple_of(i * ROWS, ROWS), ROWS)
        acc[here, :] = (acc[here, :].astype(F32) + land[there, :].astype(F32)).astype(acc.dtype)


def experts_kernel(
    groups, parts, local_rows, ring, acc_ring, experts,
    x, dy, widen, shrink,
    summed, moe, grad_widen, grad_shrink,
    xs, dys, wide, down, sum_wide, sum_down, stage, acc, other, land_c, land_p, land_q, land_z,
    hid, raw, gated, d_gu, gate, product, marks,
    load, dy_sem, stage_sem, g_send, g_recv, s_send, s_recv,
):
    core, first, second, long = lines(groups, parts)
    c, p, q, z = core.place, first.place, second.place, long.place
    pn, qn, zn = first.size, second.size, long.size
    chunks, width = x.shape[0], shrink.shape[2]
    local_exp, inner = shrink.shape[0], shrink.shape[1]
    share = inner // groups
    group, part = lax.axis_index("grp"), lax.axis_index("ep")
    rz, rq, rp, rc = ROWS, ROWS * zn, ROWS * zn * qn, ROWS * zn * qn * pn
    rows = 2 * rc
    cuts = local_rows // ROWS
    base = part * local_exp
    pairs = local_exp // 2

    loads = []
    for e in range(local_exp):
        for half in range(2):
            to = (e // 2) * 4 * share + half * 2 * share + (e % 2) * share
            loads.append(pltpu.make_async_copy(
                widen.at[e, :, pl.ds(pl.multiple_of(half * inner + group * share, share), share)],
                wide.at[:, pl.ds(to, share)], load.at[2 * e + half]))
        loads.append(pltpu.make_async_copy(
            shrink.at[e, pl.ds(pl.multiple_of(group * share, share), share), :],
            down.at[pl.ds(e * share, share), :], load.at[2 * local_exp + e]))
    for copy in loads:
        copy.start()

    def dy_copy(k):
        return pltpu.make_async_copy(dy.at[k], dys.at[lax.rem(k, 2)], dy_sem.at[lax.rem(k, 2)])

    dy_start = lambda k: dy_copy(k).start()
    dy_start(0)
    greet_lines([core, first, second, long])

    def rows_at(start, size):
        return pl.ds(pl.multiple_of(start, ROWS), size)

    def g_long(k):
        buf = xs.at[lax.rem(k, ring)]
        return swap_legs(
            long, lambda i: x.at[k], lambda j, i: buf.at[rows_at(c * rc + p * rp + q * rq + i * rz, rz), :],
            lambda j: g_send.at[k, j], lambda j: g_recv.at[k, j])

    def g_line(k, line, at, offset):
        return swap_legs(line, lambda i: at(line.place), lambda j, i: at(i),
                         lambda j: g_send.at[k, offset + j], lambda j: g_recv.at[k, offset + j])

    def g_second(k):
        buf = xs.at[lax.rem(k, ring)]
        return g_line(k, second, lambda i: buf.at[rows_at(c * rc + p * rp + i * rq, rq), :], zn - 1)

    def g_first(k):
        buf = xs.at[lax.rem(k, ring)]
        return g_line(k, first, lambda i: buf.at[rows_at(c * rc + i * rp, rp), :], zn + qn - 2)

    def g_core(k):
        buf = xs.at[lax.rem(k, ring)]
        return g_line(k, core, lambda i: buf.at[rows_at(i * rc, rc), :], zn + qn + pn - 3)

    def s_line(k, line, at, land, offset):
        return swap_legs(line, at, lambda j, i: land.at[lax.rem(k, 2), j],
                         lambda j: s_send.at[k, offset + j], lambda j: s_recv.at[k, offset + j])

    def s_core(k):
        return s_line(k, core, lambda i: other, land_c, 0)

    def s_first(k):
        buf = acc.at[lax.rem(k, acc_ring)]
        return s_line(k, first, lambda i: buf.at[rows_at(i * rp, rp), :], land_p, 1)

    def s_second(k):
        buf = acc.at[lax.rem(k, acc_ring)]
        return s_line(k, second, lambda i: buf.at[rows_at(p * rp + i * rq, rq), :], land_q, pn)

    def s_long(k):
        buf = acc.at[lax.rem(k, acc_ring)]
        return s_line(k, long, lambda i: buf.at[rows_at(p * rp + q * rq + i * rz, rz), :], land_z, pn + qn - 1)

    def after(t, lag, act):
        k = t - lag

        @pl.when((k >= 0) & (k < chunks))
        def _():
            act(k)

    tiles = width // 512

    def compute(k):
        buf, dyk = xs.at[lax.rem(k, ring)], dys.at[lax.rem(k, 2)]

        @pl.when(k == 0)
        def _():
            for copy in loads:
                copy.wait()

        dy_copy(k).wait()

        @pl.when(k + 1 < chunks)
        def _():
            dy_start(k + 1)

        @pl.loop(0, pairs)
        def _(j):
            cols = pl.ds(pl.multiple_of(j * 4 * share, 4 * share), 4 * share)
            some = pl.ds(pl.multiple_of(j * 2 * share, 2 * share), 2 * share)
            to_up = pl.ds(pl.multiple_of(j * 4 * share + 2 * share, share), 2 * share)
            to_gate = pl.ds(pl.multiple_of(j * 4 * share, share), 2 * share)
            hid[...] = jnp.dot(buf[:, :width], wide[:, cols], preferred_element_type=F32)
            raw[...] = lax.dot_general(dyk[...], down[some, :], (((1,), (1,)), ((), ())), preferred_element_type=F32)
            gate[...] = jnp.dot(buf[:, width:], marks[:, some], preferred_element_type=F32)

            @pl.loop(0, rows // 32)
            def _(i):
                here = pl.ds(pl.multiple_of(i * 32, 32), 32)
                g, u = hid[here, : 2 * share], hid[here, 2 * share:]
                d, weight = raw[here, :], gate[here, :]
                sigma = 0.5 * jnp.tanh(0.5 * g) + 0.5
                swish = g * sigma
                act = swish * u
                product[here, some] = (act * d).astype(BF)
                gated[here, some] = (act * weight).astype(BF)
                d = d * weight
                d_gu[here, to_gate] = (d * u * (sigma + swish * (1.0 - sigma))).astype(BF)
                d_gu[here, to_up] = (d * swish).astype(BF)

        mine = acc.at[lax.rem(k, acc_ring)]

        def split(cols, total):
            @pl.when(c == 0)
            def _():
                mine[:, cols] = total[:rc].astype(BF)
                other[:, cols] = total[rc:].astype(BF)

            @pl.when(c == 1)
            def _():
                other[:, cols] = total[:rc].astype(BF)
                mine[:, cols] = total[rc:].astype(BF)

        @pl.loop(0, tiles)
        def _(n):
            cols = pl.ds(pl.multiple_of(n * 512, 512), 512)
            split(cols, lax.dot_general(
                d_gu[...], wide[cols, :], (((1,), (1,)), ((), ())), preferred_element_type=F32))

        split(pl.ds(width, 128), lax.dot_general(
            product[...], marks[...], (((1,), (1,)), ((), ())), preferred_element_type=F32))
        start_legs(s_core(k))
        slot = lax.rem(k, 2)

        @pl.when(k >= 2)
        def _():
            pltpu.make_async_copy(stage.at[slot], moe.at[k - 2], stage_sem.at[slot]).wait()

        @pl.loop(0, tiles)
        def _(n):
            cols = pl.ds(pl.multiple_of(n * 512, 512), 512)
            stage[slot, :, cols] = jnp.dot(gated[...], down[:, cols], preferred_element_type=F32).astype(BF)
            sum_wide[cols, :] += lax.dot_general(
                buf[:, cols], d_gu[...], (((0,), (0,)), ((), ())), preferred_element_type=F32)
            sum_down[:, cols] += lax.dot_general(
                gated[...], dyk[:, cols], (((0,), (0,)), ((), ())), preferred_element_type=F32)

        pltpu.make_async_copy(stage.at[slot], moe.at[k], stage_sem.at[slot]).start()

    def end_long(k):
        end_legs(s_long(k))
        buf = acc.at[lax.rem(k, acc_ring)]
        total = buf[rows_at(p * rp + q * rq + z * rz, rz), :].astype(F32)
        for j in range(zn - 1):
            total = total + land_z[lax.rem(k, 2), j].astype(F32)
        summed[k] = total.astype(BF)

    def end_second(k):
        end_legs(s_second(k))
        add_and_send(acc.at[lax.rem(k, acc_ring)], p * rp + q * rq, land_q.at[lax.rem(k, 2)], rq, long, lambda: start_legs(s_long(k)))

    def end_first(k):
        end_legs(s_first(k))
        add_and_send(acc.at[lax.rem(k, acc_ring)], p * rp, land_p.at[lax.rem(k, 2)], rp, second, lambda: start_legs(s_second(k)))

    def end_core(k):
        end_legs(s_core(k))
        add_and_send(acc.at[lax.rem(k, acc_ring)], 0, land_c.at[lax.rem(k, 2)], rc, first, lambda: start_legs(s_first(k)))

    def begin(k):
        xs[lax.rem(k, ring), rows_at(c * rc + p * rp + q * rq + z * rz, rz), :] = x[k]
        start_legs(g_long(k))

        @pl.when(k == 0)
        def _():
            sum_wide[...] = jnp.zeros_like(sum_wide)
            sum_down[...] = jnp.zeros_like(sum_down)
            lanes = lax.broadcasted_iota(jnp.int32, marks.shape, 0)
            owner = base + lax.div(lax.broadcasted_iota(jnp.int32, marks.shape, 1), share)
            marks[...] = jnp.where((lanes == owner) | (lanes == owner + experts), 1.0, 0.0).astype(BF)

    def then(one, two):
        def act(k):
            end_legs(one(k))
            start_legs(two(k))

        return act

    def wide_out(i):
        here = pl.ds(pl.multiple_of(i * rows, rows), rows)
        return pltpu.make_async_copy(d_gu, grad_widen.at[here, :], load.at[1])

    out_down = pltpu.make_async_copy(sum_down, grad_shrink, load.at[0])

    def store(i):
        @pl.when(i == 0)
        def _():
            out_down.start()

        @pl.when(i > 0)
        def _():
            wide_out(i - 1).wait()

        d_gu[...] = sum_wide[pl.ds(pl.multiple_of(i * rows, rows), rows), :].astype(BF)
        wide_out(i).start()

    @pl.loop(0, chunks + 8)
    def _(t):
        after(t, 4, lambda k: end_legs(g_core(k)))
        after(t, 3, then(g_first, g_core))
        after(t, 2, then(g_second, g_first))
        after(t, 1, then(g_long, g_second))
        after(t, 0, begin)
        after(t, 8, end_long)
        after(t, 7, end_second)
        after(t, 6, end_first)
        after(t, 5, end_core)
        after(t, 4, compute)

        @pl.when((t >= chunks + 4) & (t < chunks + 4 + width // rows))
        def _():
            store(t - chunks - 4)

    for i in range(4, width // rows):
        store(i)
    for k in range(chunks - 2, chunks):
        pltpu.make_async_copy(stage.at[k % 2], moe.at[k], stage_sem.at[k % 2]).wait()
    wide_out(width // rows - 1).wait()
    out_down.wait()


def experts_together(x, dy, widen, shrink, experts, collective_id):
    groups, parts = lax.axis_size("grp"), lax.axis_size("ep")
    major, minor, xn = mesh_sizes(groups, parts)
    micro, local_rows, wide = x.shape
    x = x.reshape(-1, ROWS, wide)
    chunks = x.shape[0]
    local_exp, inner, width = shrink.shape
    share = inner // groups
    hidden = local_exp * share
    half = ROWS * major * minor * xn
    rows = 2 * half
    ring, acc_ring = min(chunks, 6), 4
    legs = major + minor + xn - 2
    vmem = pl.BlockSpec(memory_space=pltpu.VMEM)
    hbm = pl.BlockSpec(memory_space=pl.ANY)
    flops = 2 * chunks * rows * width * hidden * 9
    return pl.pallas_call(
        functools.partial(experts_kernel, groups, parts, local_rows, ring, acc_ring, experts),
        out_shape=[
            jax.ShapeDtypeStruct((chunks, ROWS, wide), BF),
            jax.ShapeDtypeStruct((chunks, rows, width), BF),
            jax.ShapeDtypeStruct((width, 2 * hidden), BF),
            jax.ShapeDtypeStruct((hidden, width), F32),
        ],
        in_specs=[vmem, hbm, hbm, hbm],
        out_specs=[vmem, hbm, hbm, hbm],
        scratch_shapes=[
            pltpu.VMEM((ring, rows, wide), BF),
            pltpu.VMEM((2, rows, width), BF),
            pltpu.VMEM((width, 2 * hidden), BF),
            pltpu.VMEM((hidden, width), BF),
            pltpu.VMEM((width, 2 * hidden), F32),
            pltpu.VMEM((hidden, width), F32),
            pltpu.VMEM((2, rows, width), BF),
            pltpu.VMEM((acc_ring, half, wide), BF),
            pltpu.VMEM((half, wide), BF),
            pltpu.VMEM((2, 1, half, wide), BF),
            pltpu.VMEM((2, xn - 1, half // xn, wide), BF),
            pltpu.VMEM((2, minor - 1, half // xn // minor, wide), BF),
            pltpu.VMEM((2, major - 1, ROWS, wide), BF),
            pltpu.VMEM((rows, 4 * share), F32),
            pltpu.VMEM((rows, 2 * share), F32),
            pltpu.VMEM((rows, hidden), BF),
            pltpu.VMEM((rows, 2 * hidden), BF),
            pltpu.VMEM((rows, 2 * share), F32),
            pltpu.VMEM((rows, hidden), BF),
            pltpu.VMEM((128, hidden), BF),
            pltpu.SemaphoreType.DMA((3 * local_exp,)),
            pltpu.SemaphoreType.DMA((2,)),
            pltpu.SemaphoreType.DMA((2,)),
            pltpu.SemaphoreType.DMA((chunks, legs)),
            pltpu.SemaphoreType.DMA((chunks, legs)),
            pltpu.SemaphoreType.DMA((chunks, legs)),
            pltpu.SemaphoreType.DMA((chunks, legs)),
        ],
        compiler_params=pltpu.CompilerParams(
            collective_id=collective_id, has_side_effects=True, vmem_limit_bytes=60 * 2**20
        ),
        cost_estimate=pl.CostEstimate(flops=flops, bytes_accessed=80 * 2**20, transcendentals=chunks * rows * hidden),
    )(x, dy, widen, shrink)


def experts_apart(x, dy_all, specialist_widen_matrix, specialist_shrink_matrix, experts):
    groups, parts = lax.axis_size("grp"), lax.axis_size("ep")
    group, part = lax.axis_index("grp"), lax.axis_index("ep")
    local_exp, inner, width = specialist_shrink_matrix.shape
    share = inner // groups
    widen = specialist_widen_matrix.reshape(local_exp, width, 2, groups, share)
    widen = lax.dynamic_index_in_dim(widen, group, 3, keepdims=False)
    widen = widen.transpose(1, 2, 0, 3).reshape(width, 2 * local_exp * share)
    shrink = specialist_shrink_matrix.reshape(local_exp, groups, share, width)
    shrink = lax.dynamic_index_in_dim(shrink, group, 1, keepdims=False).reshape(local_exp * share, width)
    x_all = gather_all(x, 1)
    chunk_shape = x_all.shape[:-1]
    x_all, dy_all = x_all.reshape(-1, width + 128), dy_all.reshape(-1, width)
    gate = x_all[:, width: width + experts].astype(F32) + x_all[:, width + experts: width + 2 * experts].astype(F32)
    x_all = x_all[:, :width]
    gate = lax.dynamic_slice_in_dim(gate, part * local_exp, local_exp, axis=1)
    gate = jnp.repeat(gate, share, axis=1)
    gate_up = jnp.dot(x_all, widen, preferred_element_type=F32)
    g, u = gate_up[:, : local_exp * share], gate_up[:, local_exp * share:]
    sigma = jax.nn.sigmoid(g)
    act = g * sigma * u
    gated = (gate * act).astype(BF)
    moe_part = jnp.dot(gated, shrink, preferred_element_type=F32).astype(BF)
    d_raw = lax.dot_general(dy_all, shrink, (((1,), (1,)), ((), ())), preferred_element_type=F32)
    d_gate = jnp.sum((act * d_raw).reshape(-1, local_exp, share), axis=-1)
    d_act = gate * d_raw
    d_gu = jnp.concatenate([d_act * u * sigma * (1.0 + g * (1.0 - sigma)), d_act * (g * sigma)], axis=1).astype(BF)
    dx_part = lax.dot_general(d_gu, widen, (((1,), (1,)), ((), ())), preferred_element_type=F32).astype(BF)
    lanes = jnp.arange(128, dtype=jnp.int32)
    place = (lanes[None, :] == part * local_exp + jnp.arange(local_exp, dtype=jnp.int32)[:, None])
    d_gate = jnp.sum(jnp.where(place[None], d_gate[:, :, None], 0.0), axis=1)
    dx_part = jnp.concatenate([dx_part, d_gate.astype(BF)], axis=1)
    dx_sum = scatter_all(dx_part.reshape(chunk_shape + (width + 128,)), 2)
    grad_widen = lax.dot_general(x_all, d_gu, (((0,), (0,)), ((), ())), preferred_element_type=F32)
    grad_shrink = lax.dot_general(gated, dy_all, (((0,), (0,)), ((), ())), preferred_element_type=F32)
    grad_widen = grad_widen.astype(BF).reshape(width, 2, local_exp // 2, 2, share).transpose(0, 2, 1, 3, 4)
    return dx_sum, moe_part.reshape(chunk_shape + (width,)), grad_widen, grad_shrink


def spread_kernel(share, x, out):
    for i in range(x.shape[0]):
        out[0, :, i * share: (i + 1) * share] = x[i].astype(F32)


def spread(x, local_exp, share):
    groups, rows, _ = x.shape
    if share % 128:
        x = x.reshape(groups, rows, local_exp // 2, 2, 2, share).transpose(2, 4, 1, 3, 0, 5)
        return x.reshape(local_exp, rows, 2 * groups * share).astype(F32)
    return pl.pallas_call(
        functools.partial(spread_kernel, share),
        grid=(local_exp, 2),
        out_shape=jax.ShapeDtypeStruct((local_exp, rows, 2 * groups * share), F32),
        in_specs=[pl.BlockSpec((groups, rows, share), lambda e, h: (0, 0, e // 2 * 4 + h * 2 + e % 2))],
        out_specs=pl.BlockSpec((1, rows, groups * share), lambda e, h: (e, 0, h)),
    )(x)


class Backdrop:
    LAG = 8

    def __init__(self, groups, parts, part, out, acc, land_c, land_p, land_q, land_z, local, send, recv):
        self.core, self.first, self.second, self.long = lines(groups, parts)
        self.part, self.out, self.acc, self.lands = part, out, acc, (land_c, land_p, land_q, land_z)
        self.local, self.send, self.recv = local, send, recv
        self.chunks = part.shape[0]
        pn, qn, zn = self.first.size, self.second.size, self.long.size
        self.rz, self.rq, self.rp, self.rc = ROWS, ROWS * zn, ROWS * zn * qn, ROWS * zn * qn * pn

    @staticmethod
    def scratch(chunks, width):
        major, minor, xn = mesh_sizes(lax.axis_size("grp"), lax.axis_size("ep"))
        half = ROWS * major * minor * xn
        legs = major + minor + xn - 2
        return [
            pltpu.VMEM((8, half, width), BF),
            pltpu.VMEM((4, 1, half, width), BF),
            pltpu.VMEM((4, xn - 1, half // xn, width), BF),
            pltpu.VMEM((4, minor - 1, half // xn // minor, width), BF),
            pltpu.VMEM((4, major - 1, ROWS, width), BF),
            pltpu.SemaphoreType.DMA((chunks,)),
            pltpu.SemaphoreType.DMA((chunks, legs)),
            pltpu.SemaphoreType.DMA((chunks, legs)),
        ]

    def near(self):
        return [self.core, self.first, self.second, self.long]

    def buf(self, k):
        return self.acc.at[lax.rem(k, 8)]

    def own(self, k):
        here = pl.ds(pl.multiple_of(self.core.place * self.rc, self.rc), self.rc)
        return pltpu.make_async_copy(self.part.at[k, here, :], self.buf(k), self.local.at[k])

    def hop(self, k, level):
        c, p, q, z = self.core.place, self.first.place, self.second.place, self.long.place
        pn, qn = self.first.size, self.second.size
        at = lambda start, size: pl.ds(pl.multiple_of(start, ROWS), size)
        line, offset, source = [
            (self.core, 0, lambda i: self.part.at[k, at(i * self.rc, self.rc), :]),
            (self.first, 1, lambda i: self.buf(k).at[at(i * self.rp, self.rp), :]),
            (self.second, pn, lambda i: self.buf(k).at[at(p * self.rp + i * self.rq, self.rq), :]),
            (self.long, pn + qn - 1, lambda i: self.buf(k).at[at(p * self.rp + q * self.rq + i * self.rz, self.rz), :]),
        ][level]
        land = self.lands[level]
        return swap_legs(line, source, lambda j, i: land.at[lax.rem(k, 4), j],
                         lambda j: self.send.at[k, offset + j], lambda j: self.recv.at[k, offset + j])

    def end(self, k, level):
        c, p, q, z = self.core.place, self.first.place, self.second.place, self.long.place
        end_legs(self.hop(k, level))
        if level == 0:
            self.own(k).wait()
        first = [0, p * self.rp, p * self.rp + q * self.rq, p * self.rp + q * self.rq + z * self.rz][level]
        size = [self.rc, self.rp, self.rq, self.rz][level]
        land = self.lands[level]
        if level == 3:
            total = self.buf(k)[pl.ds(pl.multiple_of(first, ROWS), size), :].astype(F32)
            for j in range(land.shape[1]):
                total = total + land[lax.rem(k, 4), j].astype(F32)
            self.out[k] = total.astype(self.out.dtype)
        else:
            add_and_send(self.buf(k), first, land.at[lax.rem(k, 4)], size, (self.first, self.second, self.long)[level],
                         lambda: start_legs(self.hop(k, level + 1)))

    def begin(self, k):
        start_legs(self.hop(k, 0))
        self.own(k).start()

    def step(self, t):
        for level in (3, 2, 1, 0):
            k = t - 2 * level - 2

            @pl.when((k >= 0) & (k < self.chunks))
            def _(k=k, level=level):
                self.end(k, level)

        @pl.when((t >= 0) & (t < self.chunks))
        def _():
            self.begin(t)


class Sequence:
    def __init__(self, parts, block, micro):
        e = lax.axis_index("ep")
        self.xn, self.block, self.micro, self.e = parts // 2, block, micro, e
        self.x, self.c = lax.div(e, 2), lax.rem(e, 2)
        self.line = Line(parts, e, (0, 1))
        self.line_x = Line(self.xn, self.x, (0, 2))
        self.line_c = Line(2, self.c, (0, 1))

    def at(self, ref, m, x, c):
        return ref.at[m, pl.ds(pl.multiple_of((x * 2 + c) * self.block, self.block), self.block), :]

    def gather_x(self, ref, send, recv):
        legs = []
        for m in range(self.micro):
            legs += swap_legs(
                self.line_x, lambda i, m=m: self.at(ref, m, self.x, self.c), lambda j, i, m=m: self.at(ref, m, i, self.c),
                lambda j, m=m: send.at[m, j], lambda j, m=m: recv.at[m, j])
        return legs

    def gather_c(self, ref, send, recv):
        legs = []
        for m in range(self.micro):
            for x in range(self.xn):
                legs += swap_legs(
                    self.line_c, lambda i, m=m, x=x: self.at(ref, m, x, self.c), lambda j, i, m=m, x=x: self.at(ref, m, x, i),
                    lambda j, m=m, x=x: send.at[m, self.xn - 1 + x], lambda j, m=m, x=x: recv.at[m, self.xn - 1 + x])
        return legs

    def reduce_c(self, ref, land, send, recv):
        legs = []
        for m in range(self.micro):
            for x in range(self.xn):
                legs += swap_legs(
                    self.line_c, lambda i, m=m, x=x: self.at(ref, m, x, i), lambda j, i, m=m, x=x: land.at[m, x],
                    lambda j, m=m, x=x: send.at[m, self.xn - 1 + x], lambda j, m=m, x=x: recv.at[m, self.xn - 1 + x])
        return legs

    def reduce_x(self, ref, land, send, recv):
        legs = []
        for m in range(self.micro):
            legs += swap_legs(
                self.line_x, lambda i, m=m: self.at(ref, m, i, self.c), lambda j, i, m=m: land.at[m, j],
                lambda j, m=m: send.at[m, j], lambda j, m=m: recv.at[m, j])
        return legs

    def add_c(self, ref, land):
        for m in range(self.micro):
            for x in range(self.xn):
                add_rows(ref.at[m], (x * 2 + self.c) * self.block, land.at[m, x], self.block)

    def total_x(self, ref, land, out):
        for m in range(self.micro):
            @pl.loop(0, self.block // ROWS)
            def _(i, m=m):
                here = pl.ds(pl.multiple_of(i * ROWS, ROWS), ROWS)
                total = ref[m, pl.ds(pl.multiple_of(self.e * self.block + i * ROWS, ROWS), ROWS), :].astype(F32)
                for j in range(self.xn - 1):
                    total = total + land[m, j, here, :].astype(F32)
                out[m, here, :] = total


def sum_over_parts(seq, columns, sent, got, send, recv, meanwhile):
    flat = columns.T
    sent[...] = flat[:8]
    legs = swap_legs(seq.line, lambda i: sent, lambda j, i: got.at[j], lambda j: send.at[j], lambda j: recv.at[j])
    start_legs(legs)
    meanwhile()
    end_legs(legs)
    total = sent[...]
    for j in range(seq.line.size - 1):
        total = total + got[j]
    return jnp.concatenate([total] * 16, axis=0).T


def back_kernel(
    groups, parts, backed,
    branch, merge, triple, queries, keys, values, mixed, probs, hat, inv, gains, cos, sin, part,
    d_proj, d_in, grad_heads, grad_out, summed,
    rows_all, merge_v, triple_v, q_v, k_v, v_v, mixed_v, probs_v, hat_v, d_mixed, d_qk, sums, partial, land_c, land_x, sent, got,
    load, g_send, g_recv, s_send, s_recv, t_send, t_recv, *behind
):
    micro, block, width = branch.shape
    seq = Sequence(parts, block, micro)
    length = queries.shape[1]
    tokens = micro * length
    heads = queries.shape[2] // HD
    scale = 1.0 / math.sqrt(HD)
    loads = [pltpu.make_async_copy(a, b, load.at[i]) for i, (a, b) in enumerate((
        (merge, merge_v), (mixed, mixed_v), (queries, q_v), (keys, k_v), (values, v_v), (probs, probs_v), (hat, hat_v), (triple, triple_v)))]
    for copy in loads:
        copy.start()
    if backed:
        back = Backdrop(groups, parts, part, summed, *behind)
        greet_lines([seq.line] + back.near())
        steps = back.chunks + back.LAG
        step = back.step
    else:
        greet_lines([seq.line])
        steps, step = 0, lambda t: None
        summed[...] = jnp.zeros_like(summed)
    for m in range(micro):
        rows_all[m, pl.ds(pl.multiple_of(seq.e * block, block), block), :] = branch[m]
    gather_x = seq.gather_x(rows_all, g_send, g_recv)
    start_legs(gather_x)
    step(0)
    step(1)
    step(2)
    end_legs(gather_x)
    gather_c = seq.gather_c(rows_all, g_send, g_recv)
    start_legs(gather_c)
    step(3)
    sums[...] = jnp.zeros_like(sums)
    grad_heads[...] = jnp.zeros_like(grad_heads)
    end_legs(gather_c)
    for copy in loads[:2]:
        copy.wait()
    for m in range(micro):
        d_mixed[m] = lax.dot_general(rows_all[m], merge_v[...], (((1,), (1,)), ((), ())), preferred_element_type=F32).astype(BF)
    step(4)

    @pl.loop(0, width // 512)
    def _(n):
        cols = pl.ds(pl.multiple_of(n * 512, 512), 512)
        total = lax.dot_general(mixed_v[0], rows_all[0, :, cols], (((0,), (0,)), ((), ())), preferred_element_type=F32)
        for m in range(1, micro):
            total = total + lax.dot_general(
                mixed_v[m], rows_all[m, :, cols], (((0,), (0,)), ((), ())), preferred_element_type=F32)
        grad_out[:, cols] = total.astype(BF)

    step(5)
    for copy in loads[2:7]:
        copy.wait()
    lane = lax.broadcasted_iota(jnp.int32, (1, 128), 1)

    def one_head(i):
        m, h = lax.div(i, heads), lax.rem(i, heads)
        cols = pl.ds(pl.multiple_of(h * HD, HD), HD)
        here = pl.ds(pl.multiple_of(m * length, length), length)
        d_m = d_mixed[m, :, cols]
        weights = probs_v[m, h]
        low = weights.astype(BF)
        d_proj[2, here, cols] = lax.dot_general(low, d_m, (((0,), (0,)), ((), ())), preferred_element_type=F32).astype(BF)
        d_w = lax.dot_general(d_m, v_v[m, :, cols], (((1,), (1,)), ((), ())), preferred_element_type=F32)
        d_s = (weights * (d_w - jnp.sum(weights * d_w, axis=-1, keepdims=True))).astype(BF)
        d_q = jnp.dot(d_s, k_v[m, :, cols], preferred_element_type=F32) * scale
        d_k = lax.dot_general(d_s, q_v[m, :, cols], (((0,), (0,)), ((), ())), preferred_element_type=F32) * scale
        marks = sums[here, :]
        for c, d in enumerate((d_q, d_k)):
            d = d * cos[...] - pltpu.roll(d, HD // 2, 1) * sin[...]
            d_qk[c, here, cols] = d
            product = d * hat_v[c, here, cols]
            grad_heads[c: c + 1, cols] += jnp.sum(product, axis=0, keepdims=True)
            marks = marks + jnp.where(lane == c, jnp.sum(product * gains[c: c + 1, cols], axis=-1, keepdims=True), 0.0)
        sums[here, :] = marks

    @pl.loop(0, micro * heads)
    def _(i):
        one_head(i)
        step(i + 6)

    done = 7 + micro * heads
    sums[...] = sum_over_parts(seq, sums[...], sent, got, t_send, t_recv, lambda: step(done - 1))

    @pl.loop(0, tokens // 64)
    def _(i):
        here = pl.ds(pl.multiple_of(i * 64, 64), 64)
        for c in range(2):
            inner = sums[here, c: c + 1] * (1.0 / width)
            d_proj[c, here, :] = (inv[here, c: c + 1] * (
                d_qk[c, here, :] * gains[c: c + 1, :] - hat_v[c, here, :] * inner)).astype(BF)

    loads[7].wait()

    @pl.loop(0, width // 512)
    def _(n):
        cols = pl.ds(pl.multiple_of(n * 512, 512), 512)
        for m in range(micro):
            here = pl.ds(m * length, length)
            total = lax.dot_general(d_proj[0, here, :], triple_v[0, cols, :], (((1,), (1,)), ((), ())), preferred_element_type=F32)
            for c in (1, 2):
                total = total + lax.dot_general(
                    d_proj[c, here, :], triple_v[c, cols, :], (((1,), (1,)), ((), ())), preferred_element_type=F32)
            partial[m, :, cols] = total.astype(BF)

    reduce_c = seq.reduce_c(partial, land_c, s_send, s_recv)
    start_legs(reduce_c)
    step(done)
    end_legs(reduce_c)
    seq.add_c(partial, land_c)
    reduce_x = seq.reduce_x(partial, land_x, s_send, s_recv)
    start_legs(reduce_x)
    step(done + 1)
    end_legs(reduce_x)
    seq.total_x(partial, land_x, d_in)
    for t in range(done + 2, steps):
        step(t)


def attention_back(branch, merge, triple, queries, keys, values, mixed, probs, hat, inv, gains, cos, sin, part, collective_id):
    groups, parts = lax.axis_size("grp"), lax.axis_size("ep")
    micro, block, width = branch.shape
    length, local_width = queries.shape[1:]
    tokens = micro * length
    backed = part is not None
    behind = Backdrop.scratch(part.shape[0], width) if backed else []
    summed = (part.shape[0], ROWS, width) if backed else (8, 128)
    vmem = pl.BlockSpec(memory_space=pltpu.VMEM)
    hbm = pl.BlockSpec(memory_space=pl.ANY)
    xn = parts // 2
    return pl.pallas_call(
        functools.partial(back_kernel, groups, parts, backed),
        out_shape=[
            jax.ShapeDtypeStruct((3, tokens, local_width), BF),
            jax.ShapeDtypeStruct((micro, block, width), F32),
            jax.ShapeDtypeStruct((8, local_width), F32),
            jax.ShapeDtypeStruct((local_width, width), BF),
            jax.ShapeDtypeStruct(summed, BF if backed else F32),
        ],
        in_specs=[vmem] + [hbm] * 8 + [vmem] * 4 + [hbm],
        out_specs=[vmem] * 5,
        scratch_shapes=[
            pltpu.VMEM((micro, length, width), BF),
            pltpu.VMEM(merge.shape, BF),
            pltpu.VMEM(triple.shape, BF),
            pltpu.VMEM(queries.shape, BF),
            pltpu.VMEM(queries.shape, BF),
            pltpu.VMEM(queries.shape, BF),
            pltpu.VMEM(queries.shape, BF),
            pltpu.VMEM(probs.shape, F32),
            pltpu.VMEM(hat.shape, F32),
            pltpu.VMEM(queries.shape, BF),
            pltpu.VMEM((2, tokens, local_width), F32),
            pltpu.VMEM((tokens, 128), F32),
            pltpu.VMEM((micro, length, width), BF),
            pltpu.VMEM((micro, xn, block, width), BF),
            pltpu.VMEM((micro, xn - 1, block, width), BF),
            pltpu.VMEM((8, tokens), F32),
            pltpu.VMEM((parts - 1, 8, tokens), F32),
            pltpu.SemaphoreType.DMA((8,)),
            pltpu.SemaphoreType.DMA((micro, 2 * xn - 1)),
            pltpu.SemaphoreType.DMA((micro, 2 * xn - 1)),
            pltpu.SemaphoreType.DMA((micro, 2 * xn - 1)),
            pltpu.SemaphoreType.DMA((micro, 2 * xn - 1)),
            pltpu.SemaphoreType.DMA((parts - 1,)),
            pltpu.SemaphoreType.DMA((parts - 1,)),
        ] + behind,
        compiler_params=pltpu.CompilerParams(
            collective_id=collective_id, has_side_effects=True, vmem_limit_bytes=58 * 2**20
        ),
        cost_estimate=pl.CostEstimate(flops=10**10, bytes_accessed=40 * 2**20, transcendentals=0),
    )(branch, merge, triple, queries, keys, values, mixed, probs, hat, inv, gains, cos, sin,
      part if backed else mixed)


class BackGather:
    LAG = 8

    def __init__(self, groups, parts, own, out, local, send, recv):
        self.core, self.first, self.second, self.long = lines(groups, parts)
        self.own, self.out, self.local, self.send, self.recv = own, out, local, send, recv
        self.chunks = own.shape[0]
        pn, qn, zn = self.first.size, self.second.size, self.long.size
        self.rz, self.rq, self.rp, self.rc = ROWS, ROWS * zn, ROWS * zn * qn, ROWS * zn * qn * pn

    @staticmethod
    def scratch(chunks):
        major, minor, xn = mesh_sizes(lax.axis_size("grp"), lax.axis_size("ep"))
        legs = major + minor + xn - 2
        return [
            pltpu.SemaphoreType.DMA((chunks,)),
            pltpu.SemaphoreType.DMA((chunks, legs)),
            pltpu.SemaphoreType.DMA((chunks, legs)),
        ]

    def near(self):
        return [self.core, self.first, self.second, self.long]

    def rows(self, k, start, size):
        return self.out.at[k, pl.ds(pl.multiple_of(start, ROWS), size), :]

    def mine(self, k):
        c, p, q, z = self.core.place, self.first.place, self.second.place, self.long.place
        return pltpu.make_async_copy(
            self.own.at[k], self.rows(k, c * self.rc + p * self.rp + q * self.rq + z * self.rz, self.rz), self.local.at[k])

    def hop(self, k, level):
        c, p, q, z = self.core.place, self.first.place, self.second.place, self.long.place
        pn, qn, zn = self.first.size, self.second.size, self.long.size
        line, offset, at = [
            (self.long, 0, lambda i: self.rows(k, c * self.rc + p * self.rp + q * self.rq + i * self.rz, self.rz)),
            (self.second, zn - 1, lambda i: self.rows(k, c * self.rc + p * self.rp + i * self.rq, self.rq)),
            (self.first, zn + qn - 2, lambda i: self.rows(k, c * self.rc + i * self.rp, self.rp)),
            (self.core, zn + qn + pn - 3, lambda i: self.rows(k, i * self.rc, self.rc)),
        ][level]
        source = (lambda i: self.own.at[k]) if level == 0 else (lambda i: at(line.place))
        return swap_legs(line, source, lambda j, i: at(i),
                         lambda j: self.send.at[k, offset + j], lambda j: self.recv.at[k, offset + j])

    def step(self, t):
        for level in (3, 2, 1, 0):
            k = t - 2 * level - 2

            @pl.when((k >= 0) & (k < self.chunks))
            def _(k=k, level=level):
                end_legs(self.hop(k, level))
                if level == 0:
                    self.mine(k).wait()
                if level < 3:
                    start_legs(self.hop(k, level + 1))

        @pl.when((t >= 0) & (t < self.chunks))
        def _():
            self.mine(t).start()
            start_legs(self.hop(t, 0))


def forward_kernel(
    groups, parts, experts,
    x, dy, routes, quota, gains, head_gains, cos, sin, docs_down, docs_across, dispatch, triple, merge,
    gathered, q_out, k_out, v_out, mixed, probs, hat, inv, hidden, ffn_in, router, dy_all,
    kept, triple_v, merge_v, sums, partial, land_c, land_x, sent, got,
    load, g_send, g_recv, s_send, s_recv, t_send, t_recv, *behind
):
    micro, block, width = x.shape
    seq = Sequence(parts, block, micro)
    length = gathered.shape[1]
    tokens = micro * length
    heads = q_out.shape[2] // HD
    scale = 1.0 / math.sqrt(HD)
    cuts = block // ROWS
    loads = [pltpu.make_async_copy(triple, triple_v, load.at[0]), pltpu.make_async_copy(merge, merge_v, load.at[1])]
    for copy in loads:
        copy.start()
    back = BackGather(groups, parts, dy, dy_all, *behind)
    step, steps = back.step, back.chunks + back.LAG
    lane = lax.broadcasted_iota(jnp.int32, (1, 128), 1)
    earlier = (lax.broadcasted_iota(jnp.int32, (block, block), 1) < lax.broadcasted_iota(jnp.int32, (block, block), 0))
    for m in range(micro):
        @pl.loop(0, cuts)
        def _(r, m=m):
            here = pl.ds(pl.multiple_of(r * ROWS, ROWS), ROWS)
            v = x[m, here, :].astype(F32)
            v = v * lax.rsqrt(jnp.mean(v * v, axis=-1, keepdims=True) + EPS)
            gathered[m, pl.ds(pl.multiple_of(seq.e * block + r * ROWS, ROWS), ROWS), :] = (v * gains[0:1, :]).astype(BF)
    greet_lines([seq.line] + back.near())
    gather_x = seq.gather_x(gathered, g_send, g_recv)
    start_legs(gather_x)
    step(0)
    for m in range(micro):
        chosen = routes[m]
        counts = jnp.zeros((block, 128), F32)
        for j in range(TOP):
            counts = counts + jnp.where(chosen[:, j: j + 1] == lane, 1.0, 0.0)
        prior = jnp.dot(jnp.where(earlier, 1.0, 0.0).astype(BF), counts.astype(BF), preferred_element_type=F32)
        kept[m] = jnp.where((counts > 0.0) & (prior < quota[0:1, :]), 1.0, 0.0)
    step(1)
    step(2)
    end_legs(gather_x)
    gather_c = seq.gather_c(gathered, g_send, g_recv)
    start_legs(gather_c)
    step(3)
    loads[0].wait()
    end_legs(gather_c)

    @pl.loop(0, micro)
    def _(m):
        here = pl.ds(pl.multiple_of(m * length, length), length)
        marks = jnp.zeros((length, 128), F32)
        for c in range(2):
            raw = jnp.dot(gathered[m], triple_v[c], preferred_element_type=F32)
            hat[c, here, :] = raw
            marks = marks + jnp.where(lane == c, jnp.sum(raw * raw, axis=-1, keepdims=True), 0.0)
        sums[here, :] = marks
        v_out[m] = jnp.dot(gathered[m], triple_v[2], preferred_element_type=F32).astype(BF)
        step(m + 4)

    done = micro + 5
    squares = sum_over_parts(seq, sums[...], sent, got, t_send, t_recv, lambda: step(done - 1))
    inv[...] = lax.rsqrt(squares * (1.0 / width) + EPS)
    loads[1].wait()

    @pl.loop(0, micro * heads)
    def _(i):
        m, h = lax.div(i, heads), lax.rem(i, heads)
        cols = pl.ds(pl.multiple_of(h * HD, HD), HD)
        here = pl.ds(pl.multiple_of(m * length, length), length)
        for c, to in enumerate((q_out, k_out)):
            v = hat[c, here, cols] * inv[here, c: c + 1]
            hat[c, here, cols] = v
            v = v * head_gains[c: c + 1, cols]
            to[m, :, cols] = (v * cos[...] + pltpu.roll(v, HD // 2, 1) * sin[...]).astype(BF)
        scores = lax.dot_general(
            q_out[m, :, cols], k_out[m, :, cols], (((1,), (1,)), ((), ())), preferred_element_type=F32) * scale
        allowed = (docs_down[m] == docs_across[m]) & (
            lax.broadcasted_iota(jnp.int32, (length, length), 1) <= lax.broadcasted_iota(jnp.int32, (length, length), 0))
        scores = jnp.where(allowed, scores, NEG)
        grown = jnp.exp(scores - jnp.max(scores, axis=-1, keepdims=True))
        weights = grown / jnp.sum(grown, axis=-1, keepdims=True)
        probs[m, h] = weights
        mixed[m, :, cols] = jnp.dot(weights.astype(BF), v_out[m, :, cols], preferred_element_type=F32).astype(BF)
        step(done + i)

    done = done + micro * heads

    @pl.loop(0, width // 512)
    def _(n):
        cols = pl.ds(pl.multiple_of(n * 512, 512), 512)
        for m in range(micro):
            partial[m, :, cols] = jnp.dot(mixed[m], merge_v[:, cols], preferred_element_type=F32).astype(BF)

    reduce_c = seq.reduce_c(partial, land_c, s_send, s_recv)
    start_legs(reduce_c)
    step(done)
    end_legs(reduce_c)
    seq.add_c(partial, land_c)
    reduce_x = seq.reduce_x(partial, land_x, s_send, s_recv)
    start_legs(reduce_x)
    step(done + 1)
    end_legs(reduce_x)
    seq.total_x(partial, land_x, hidden)
    for m in range(micro):
        @pl.loop(0, cuts)
        def _(r, m=m):
            here = pl.ds(pl.multiple_of(r * ROWS, ROWS), ROWS)
            v = hidden[m, here, :] + x[m, here, :].astype(F32)
            hidden[m, here, :] = v
            v = v * lax.rsqrt(jnp.mean(v * v, axis=-1, keepdims=True) + EPS)
            ffn_in[m, here, :width] = (v * gains[1:2, :]).astype(BF)
        logits = jnp.dot(ffn_in[m, :, :width], dispatch[...], preferred_element_type=F32)
        logits = jnp.where(lane < experts, logits, NEG)
        grown = jnp.exp(logits - jnp.max(logits, axis=-1, keepdims=True))
        grown = grown / jnp.sum(grown, axis=-1, keepdims=True)
        gate = grown * kept[m]
        router[m] = grown + pltpu.roll(kept[m], experts, 1)
        head = gate.astype(BF).astype(F32)
        ffn_in[m, :, width:] = (head + pltpu.roll(gate - head, experts, 1)).astype(BF)
    for t in range(done + 2, steps):
        step(t)


def attention_forward(x, dy, routes, quota, gains, head_gains, cos, sin, docs, dispatch, triple, merge, collective_id):
    groups, parts = lax.axis_size("grp"), lax.axis_size("ep")
    major, minor, xn = mesh_sizes(groups, parts)
    micro, block, width = x.shape
    length = docs.shape[1]
    local_width = triple.shape[2]
    heads = local_width // HD
    tokens = micro * length
    chunks = micro * block // ROWS
    rows = 2 * xn * minor * major * ROWS
    vmem = pl.BlockSpec(memory_space=pltpu.VMEM)
    hbm = pl.BlockSpec(memory_space=pl.ANY)
    low = jax.ShapeDtypeStruct((micro, length, local_width), BF)
    experts = dispatch.shape[1]
    dispatch = jnp.pad(dispatch, ((0, 0), (0, 128 - experts)))
    quota = jnp.pad(quota.astype(F32), (0, 128 - experts)).reshape(1, 128)
    return pl.pallas_call(
        functools.partial(forward_kernel, groups, parts, experts),
        out_shape=[
            jax.ShapeDtypeStruct((micro, length, width), BF),
            low, low, low, low,
            jax.ShapeDtypeStruct((micro, heads, length, length), F32),
            jax.ShapeDtypeStruct((2, tokens, local_width), F32),
            jax.ShapeDtypeStruct((tokens, 128), F32),
            jax.ShapeDtypeStruct((micro, block, width), F32),
            jax.ShapeDtypeStruct((micro, block, width + 128), BF),
            jax.ShapeDtypeStruct((micro, block, 128), F32),
            jax.ShapeDtypeStruct((chunks, rows, width), BF),
        ],
        in_specs=[vmem] * 11 + [hbm] * 2,
        out_specs=[vmem] * 11 + [hbm],
        scratch_shapes=[
            pltpu.VMEM((micro, block, 128), F32),
            pltpu.VMEM(triple.shape, BF),
            pltpu.VMEM(merge.shape, BF),
            pltpu.VMEM((tokens, 128), F32),
            pltpu.VMEM((micro, length, width), BF),
            pltpu.VMEM((micro, xn, block, width), BF),
            pltpu.VMEM((micro, xn - 1, block, width), BF),
            pltpu.VMEM((8, tokens), F32),
            pltpu.VMEM((parts - 1, 8, tokens), F32),
            pltpu.SemaphoreType.DMA((2,)),
            pltpu.SemaphoreType.DMA((micro, 2 * xn - 1)),
            pltpu.SemaphoreType.DMA((micro, 2 * xn - 1)),
            pltpu.SemaphoreType.DMA((micro, 2 * xn - 1)),
            pltpu.SemaphoreType.DMA((micro, 2 * xn - 1)),
            pltpu.SemaphoreType.DMA((parts - 1,)),
            pltpu.SemaphoreType.DMA((parts - 1,)),
        ] + BackGather.scratch(chunks),
        compiler_params=pltpu.CompilerParams(
            collective_id=collective_id, has_side_effects=True, vmem_limit_bytes=56 * 2**20
        ),
        cost_estimate=pl.CostEstimate(flops=6 * 10**9, bytes_accessed=40 * 2**20, transcendentals=0),
    )(x, dy.reshape(chunks, ROWS, width), routes, quota, gains, head_gains, cos, sin, docs[:, :, None], docs[:, None, :],
      dispatch, triple, merge)


def per_device(
    block_entry_states,
    document_labels,
    token_assignments,
    worker_quota_tallies,
    rescale_factors_both,
    triple_projection_matrix,
    probe_lookup_scalers,
    heads_merge_matrix,
    dispatcher_matrix,
    specialist_widen_matrix,
    specialist_shrink_matrix,
    output_gradient,
):
    micro, local_rows, width = block_entry_states.shape
    groups, parts = lax.axis_size("grp"), lax.axis_size("ep")
    major, minor, xs = mesh_sizes(groups, parts)
    group = lax.axis_index("grp")
    part = lax.axis_index("ep")
    seq_len = document_labels.shape[1]
    experts = dispatcher_matrix.shape[1]
    local_exp = specialist_widen_matrix.shape[0]
    inner = specialist_shrink_matrix.shape[1]
    share = inner // groups
    local_width = triple_projection_matrix.shape[2]
    heads = local_width // HD
    scale = 1.0 / math.sqrt(HD)
    gains = rescale_factors_both.astype(F32)
    head_gains = probe_lookup_scalers.astype(F32)
    cos, signed_sin = rope_tables(seq_len, HD)
    triple = triple_projection_matrix.transpose(1, 0, 2)
    gathered, queries, keys, values, mixed, weights, qk_hat, qk_inv, hidden, ffn_ext, probs, dy_all = attention_forward(
        block_entry_states, output_gradient, token_assignments, worker_quota_tallies, gains, head_gains, cos, signed_sin,
        document_labels, dispatcher_matrix, triple, heads_merge_matrix, 0)
    ffn_in = ffn_ext[..., :width]

    fused = xs == minor and share % 128 == 0 and local_exp % 2 == 0 and 2 * xs * minor * major * ROWS <= 512
    chunk_shape = (micro * local_rows // ROWS, 2, xs, minor, major, ROWS)
    if fused:
        dx_sum, moe_part, grad_widen, grad_shrink = experts_together(
            ffn_ext, dy_all, specialist_widen_matrix, specialist_shrink_matrix, experts, 1)
    else:
        dx_sum, moe_part, grad_widen, grad_shrink = experts_apart(
            ffn_ext, dy_all, specialist_widen_matrix, specialist_shrink_matrix, experts)
    dx_sum = dx_sum.astype(F32).reshape(micro, local_rows, width + 128)
    grad_widen = lax.all_to_all(grad_widen.reshape(groups, width // groups, -1), "grp", 0, 0, tiled=True)
    grad_widen = spread(grad_widen, local_exp, share)
    grad_shrink = grad_shrink.reshape(local_exp, share, width)

    inv_second = lax.rsqrt(jnp.mean(hidden * hidden, axis=-1, keepdims=True) + EPS)
    hat_second = hidden * inv_second
    probs, keep = probs[..., :experts], probs[..., experts: 2 * experts]
    d_probs = dx_sum[..., width: width + experts] * keep
    d_logits = probs * (d_probs - jnp.sum(probs * d_probs, axis=-1, keepdims=True))
    d_ffn = dx_sum[..., :width] + jnp.einsum("mte,de->mtd", d_logits, dispatcher_matrix.astype(F32), precision=HIGH)
    grad_router = jnp.einsum("mtd,mte->ed", ffn_in.astype(F32), d_logits, precision=HIGH)
    scaled = d_ffn * gains[1]
    adjoint = output_gradient.astype(F32)
    d_hidden = adjoint + inv_second * (scaled - hat_second * jnp.mean(scaled * hat_second, axis=-1, keepdims=True))
    grad_second = jnp.sum(d_ffn * hat_second, axis=(0, 1))

    d_proj, d_attn_in, grad_heads, grad_out, moe = attention_back(
        d_hidden.astype(BF), heads_merge_matrix, triple, queries, keys, values, mixed, weights,
        qk_hat, qk_inv, head_gains, cos, signed_sin, moe_part if fused else None, 5)
    if not fused:
        moe = scatter_all(moe_part.reshape(chunk_shape + (width,)), 3)
    output = (hidden + moe.astype(F32).reshape(micro, local_rows, width)).astype(BF)
    skip = block_entry_states.astype(F32)
    inv_first = lax.rsqrt(jnp.mean(skip * skip, axis=-1, keepdims=True) + EPS)
    hat_first = skip * inv_first
    scaled = d_attn_in * gains[0]
    grad_input = d_hidden + inv_first * (scaled - hat_first * jnp.mean(scaled * hat_first, axis=-1, keepdims=True))
    grad_first = jnp.sum(d_attn_in * hat_first, axis=(0, 1))

    shared = jnp.concatenate([grad_first[None], grad_second[None], grad_router]).reshape(-1).astype(BF)
    own = grad_heads[:2].reshape(-1).astype(BF)
    gap, size = shared.shape[0], shared.shape[0] + own.shape[0]
    block = (minor, major, ROWS, -(-size // (groups * ROWS * 128)) * 128)
    room = math.prod(block)
    shared = jnp.pad(shared, (0, room - gap)).reshape(block)
    own = jnp.pad(own, (gap, room - size)).reshape(block)
    near_sum, far_sum, qkv_sum, misc_sum = total_over_groups(
        gathered.reshape(-1, width), d_proj, grad_out, shared, own, 4)
    qkv_sum = qkv_sum.reshape(3, width, local_width).astype(F32).transpose(1, 0, 2)
    out_sum = jnp.concatenate([near_sum.reshape(-1, width), far_sum.reshape(-1, width)]).astype(F32)
    misc_sum = misc_sum.reshape(-1)[:size].astype(F32)
    rows = misc_sum[: (2 + experts) * width].reshape(2 + experts, width)
    return (
        output,
        grad_input,
        rows[:2],
        qkv_sum,
        misc_sum[(2 + experts) * width:].reshape(2, local_width),
        out_sum,
        rows[2:].T,
        grad_widen,
        grad_shrink,
    )


def solution(mesh):
    return jax.shard_map(
        per_device,
        mesh=mesh,
        in_specs=(
            P(None, ALL, None),
            P(None, "grp"),
            P(None, ALL, None),
            P(),
            P(),
            P(None, None, "ep"),
            P(None, "ep"),
            P("ep", None),
            P(),
            P("ep", None, None),
            P("ep", None, None),
            P(None, ALL, None),
        ),
        out_specs=(
            P(None, ALL, None),
            P(None, ALL, None),
            P(),
            P(None, None, "ep"),
            P(None, "ep"),
            P("ep", None),
            P(),
            P("ep", "grp", None),
            P("ep", "grp", None),
        ),
        check_vma=False,
    )
```

```python
import functools
import math

import jax
import jax.numpy as jnp
import numpy as np
from jax import lax
from jax.experimental import pallas as pl
from jax.experimental.pallas import tpu as pltpu
from jax.sharding import PartitionSpec as P

HD = 128
TOP = 8
EPS = 1e-05
THETA = 10000.0
NEG = -1e30
HIGH = lax.Precision.HIGHEST
ALL = ("grp", "ep")
MESH = pl.DeviceIdType.MESH
ROWS = 16
BF = jnp.bfloat16
F32 = jnp.float32


def rope_tables(length, head_dim):
    half = head_dim // 2
    angle = np.arange(length)[:, None] * THETA ** (-np.arange(half) * 2.0 / head_dim)
    cos, sin = np.cos(angle), np.sin(angle)
    return np.concatenate([cos, cos], 1).astype(np.float32), np.concatenate([-sin, sin], 1).astype(np.float32)


def mesh_sizes(groups, parts):
    major = 4 if groups % 4 == 0 else groups
    return major, groups // major, parts // 2


class Line:
    def __init__(self, size, place, step):
        self.size, self.place, self.step = size, place, step

    def at(self, hops):
        return (
            lax.axis_index("grp") + hops * self.step[0],
            lax.axis_index("ep") + hops * self.step[1],
        )


def lines(groups, parts):
    major, minor, xs = mesh_sizes(groups, parts)
    g, e = lax.axis_index("grp"), lax.axis_index("ep")
    core = lax.rem(e, 2)
    x_pos, minor_pos = lax.div(e, 2), lax.rem(g, minor)
    if xs == minor:
        first = Line(xs, jnp.where(core == 0, x_pos, minor_pos), (core, 2 - 2 * core))
        second = Line(xs, jnp.where(core == 0, minor_pos, x_pos), (1 - core, 2 * core))
    else:
        first = Line(xs, x_pos, (0, 2))
        second = Line(minor, minor_pos, (1, 0))
    return Line(2, core, (0, 1)), first, second, Line(major, lax.div(g, minor), (minor, 0))


def greet(some, whole=()):
    barrier = pltpu.get_barrier_semaphore()
    peers = sum(line.size - 1 for line in whole)
    for line in whole:
        for j in range(1, line.size):
            to = lax.rem(line.place + j, line.size)
            pl.semaphore_signal(barrier, inc=1, device_id=line.at(to - line.place), device_id_type=MESH)
    for line in some:
        if line.size == 2:
            pl.semaphore_signal(barrier, inc=1, device_id=line.at(1 - 2 * line.place), device_id_type=MESH)
            peers = peers + 1
        else:
            for way, there in ((1, line.place < line.size - 1), (-1, line.place > 0)):

                @pl.when(there)
                def _(line=line, way=way):
                    pl.semaphore_signal(barrier, inc=1, device_id=line.at(way), device_id_type=MESH)

                peers = peers + there.astype(jnp.int32)
    pl.semaphore_wait(barrier, peers)


def greet_lines(some):
    barrier = pltpu.get_barrier_semaphore()
    for line in some:
        for j in range(1, line.size):
            to = lax.rem(line.place + j, line.size)
            pl.semaphore_signal(barrier, inc=1, device_id=line.at(to - line.place), device_id_type=MESH)
    pl.semaphore_wait(barrier, sum(line.size - 1 for line in some))


def remote(src, dst, send, recv, target):
    return pltpu.make_async_remote_copy(
        src_ref=src, dst_ref=dst, send_sem=send, recv_sem=recv, device_id=target, device_id_type=MESH
    )


class Hop:
    def __init__(self, legs, after=None):
        self.legs, self.after = legs, after

    def _each(self, which, act):
        for leg in self.legs:
            if leg[which] is None:
                act(leg)
            else:
                pl.when(leg[which])(functools.partial(act, leg))

    def start(self):
        self._each(0, lambda leg: leg[2]().start())

    def arrive(self):
        def act(leg):
            leg[3]().wait_recv()
            if leg[4] is not None:
                leg[4]()

        self._each(1, act)

    def sent(self):
        self._each(0, lambda leg: leg[2]().wait_send())


def gather_hops(line, at, send, recv):
    n, a = line.size, line.place
    if n == 2:
        mine, theirs, peer = at(a), at(1 - a), line.at(1 - 2 * a)
        return [
            Hop([(None, None, lambda: remote(mine, mine, send(0), recv(0), peer),
                  lambda: remote(theirs, theirs, send(0), recv(0), peer), None)])
        ]
    hops = []
    for s in range(1, n):
        legs = []
        for d, way in enumerate((1, -1)):
            k = (s - 1) * 2 + d
            out = a - way * (s - 1)
            into = a - way * s
            sends = (out >= 0) & (out < n) & (a + way >= 0) & (a + way < n)
            gets = (into >= 0) & (into < n)
            out, into = jnp.clip(out, 0, n - 1), jnp.clip(into, 0, n - 1)
            legs.append((
                sends, gets,
                lambda out=out, way=way, k=k: remote(at(out), at(out), send(k), recv(k), line.at(way)),
                lambda into=into, way=way, k=k: remote(at(into), at(into), send(k), recv(k), line.at(-way)),
                None,
            ))
        hops.append(Hop(legs))
    return hops


def reduce_hops(line, acc, land, add, send, recv):
    n, a = line.size, line.place
    if n == 2:
        peer = line.at(1 - 2 * a)
        return [
            Hop([(None, None, lambda: remote(acc(1 - a), land(0), send(0), recv(0), peer),
                  lambda: remote(land(0), land(0), send(0), recv(0), peer),
                  lambda: add(acc(a), land(0)))])
        ]
    hops = []
    for s in range(n - 1):
        legs = []
        for d, way in enumerate((1, -1)):
            k = s * 2 + d
            b = a if way == 1 else n - 1 - a
            sends = (b <= s) & (b < n - 1)
            gets = (b - 1 <= s) & (b >= 1)
            out = b + n - 1 - s
            into = b + n - 2 - s
            out, into = jnp.clip(out, 0, n - 1), jnp.clip(into, 0, n - 1)
            if way == -1:
                out, into = n - 1 - out, n - 1 - into
            legs.append((
                sends, gets,
                lambda out=out, way=way, k=k: remote(acc(out), land(k), send(k), recv(k), line.at(way)),
                lambda way=way, k=k: remote(land(k), land(k), send(k), recv(k), line.at(-way)),
                lambda into=into, k=k: add(acc(into), land(k)),
            ))
        hops.append(Hop(legs))
    return hops


def hop_count(n):
    return 1 if n == 2 else n - 1


def leg_count(n):
    return 1 if n == 2 else 2 * (n - 1)


def flow(chains, pace=1):
    depth, count = max(len(c) for c in chains), len(chains)
    for t in range(count + pace * depth):
        for k in range(count):
            i, rest = divmod(t - k, pace)
            if rest:
                continue
            if 1 <= i <= len(chains[k]):
                chains[k][i - 1].arrive()
            if 0 <= i < len(chains[k]):
                chains[k][i].start()
    for chain in chains:
        for hop in chain:
            hop.sent()


def add(acc, land):
    lead = acc.shape[:-2]

    def one(i):
        where = []
        for size in reversed(lead):
            where.insert(0, lax.rem(i, size))
            i = lax.div(i, size)
        where = tuple(where) + (slice(None), slice(None))
        acc[where] = (acc[where].astype(F32) + land[where].astype(F32)).astype(acc.dtype)

    if lead:
        pl.loop(0, math.prod(lead))(one)
    else:
        one(0)


def gather_kernel(groups, parts, x, out, local, send, recv):
    core, first, second, long = lines(groups, parts)
    c, p, q, z = core.place, first.place, second.place, long.place
    greet([core, first, second, long])
    chunks = x.shape[0]
    own = [pltpu.make_async_copy(x.at[k], out.at[k, c, p, q, z], local.at[k]) for k in range(chunks)]
    for copy in own:
        copy.start()
    chains = []
    for k in range(chunks):
        base = [0]

        def sems(n, k=k, base=base):
            b = base[0]
            base[0] += leg_count(n)
            return (lambda i: send.at[k, b + i]), (lambda i: recv.at[k, b + i])

        chain = []
        chain += gather_hops(long, lambda i, k=k: out.at[k, c, p, q, i], *sems(long.size))
        chain += gather_hops(second, lambda i, k=k: out.at[k, c, p, i], *sems(second.size))
        chain += gather_hops(first, lambda i, k=k: out.at[k, c, i], *sems(first.size))
        chain += gather_hops(core, lambda i, k=k: out.at[k, i], *sems(2))
        chains.append(chain)
    for copy in own:
        copy.wait()
    flow(chains)


def gather_all(x, collective_id):
    groups, parts = lax.axis_size("grp"), lax.axis_size("ep")
    major, minor, xs = mesh_sizes(groups, parts)
    width = x.shape[-1]
    x = x.reshape(-1, ROWS, width)
    legs = sum(leg_count(n) for n in (2, xs, minor, major))
    chunks = x.shape[0]
    return pl.pallas_call(
        functools.partial(gather_kernel, groups, parts),
        out_shape=jax.ShapeDtypeStruct((chunks, 2, xs, minor, major, ROWS, width), x.dtype),
        in_specs=[pl.BlockSpec(memory_space=pl.ANY)],
        out_specs=pl.BlockSpec(memory_space=pl.ANY),
        scratch_shapes=[
            pltpu.SemaphoreType.DMA((chunks,)),
            pltpu.SemaphoreType.DMA((chunks, legs)),
            pltpu.SemaphoreType.DMA((chunks, legs)),
        ],
        compiler_params=pltpu.CompilerParams(collective_id=collective_id, has_side_effects=True),
    )(x)


def scatter_kernel(groups, parts, part, out, acc, land_c, land_p, land_q, land_z, local, send, recv):
    core, first, second, long = lines(groups, parts)
    c, p, q, z = core.place, first.place, second.place, long.place
    chunks = part.shape[0]
    own = [pltpu.make_async_copy(part.at[k, c], acc.at[k], local.at[k]) for k in range(chunks)]
    for copy in own:
        copy.start()
    greet([core, first, second, long])
    chains = []
    for k in range(chunks):
        base = [0]

        def sems(n, k=k, base=base):
            b = base[0]
            base[0] += leg_count(n)
            return (lambda i: send.at[k, b + i]), (lambda i: recv.at[k, b + i])

        def add_own(acc_ref, land_ref, k=k):
            own[k].wait()
            add(acc_ref, land_ref)

        s, r = sems(2)
        peer = core.at(1 - 2 * c)
        other = part.at[k, 1 - c]
        chain = [Hop([(
            None, None,
            lambda other=other, s=s, r=r, k=k: remote(other, land_c.at[k], s(0), r(0), peer),
            lambda s=s, r=r, k=k: remote(land_c.at[k], land_c.at[k], s(0), r(0), peer),
            lambda k=k, add_own=add_own: add_own(acc.at[k], land_c.at[k]),
        )])]
        chain += reduce_hops(first, lambda i, k=k: acc.at[k, i], lambda i, k=k: land_p.at[k, i], add, *sems(first.size))
        chain += reduce_hops(second, lambda i, k=k: acc.at[k, p, i], lambda i, k=k: land_q.at[k, i], add, *sems(second.size))
        chain += reduce_hops(long, lambda i, k=k: acc.at[k, p, q, i], lambda i, k=k: land_z.at[k, i], add, *sems(long.size))
        chains.append(chain)
    flow(chains)
    for k in range(chunks):
        out[k] = acc[k, p, q, z]


def scatter_all(part, collective_id):
    groups, parts = lax.axis_size("grp"), lax.axis_size("ep")
    major, minor, xs = mesh_sizes(groups, parts)
    legs = sum(leg_count(n) for n in (2, xs, minor, major))
    chunks, width = part.shape[0], part.shape[-1]
    unit = 2 * ROWS * width
    need = unit * (2 * xs * minor * major + leg_count(xs) * minor * major + leg_count(minor) * major + leg_count(major) + 2)
    per = chunks
    while per > 1 and per * need > 44 * 2**20:
        per //= 2
    call = pl.pallas_call(
        functools.partial(scatter_kernel, groups, parts),
        out_shape=jax.ShapeDtypeStruct((per, ROWS, width), BF),
        in_specs=[pl.BlockSpec(memory_space=pl.ANY)],
        out_specs=pl.BlockSpec(memory_space=pltpu.VMEM),
        scratch_shapes=[
            pltpu.VMEM((per, xs, minor, major, ROWS, width), BF),
            pltpu.VMEM((per, xs, minor, major, ROWS, width), BF),
            pltpu.VMEM((per, leg_count(xs), minor, major, ROWS, width), BF),
            pltpu.VMEM((per, leg_count(minor), major, ROWS, width), BF),
            pltpu.VMEM((per, leg_count(major), ROWS, width), BF),
            pltpu.SemaphoreType.DMA((per,)),
            pltpu.SemaphoreType.DMA((per, legs)),
            pltpu.SemaphoreType.DMA((per, legs)),
        ],
        compiler_params=pltpu.CompilerParams(
            collective_id=collective_id, has_side_effects=True, vmem_limit_bytes=56 * 2**20
        ),
    )
    return jnp.concatenate([call(part[i:i + per]) for i in range(0, chunks, per)]) if per < chunks else call(part)


class Begun:
    def __init__(self, hop, before):
        self.hop, self.before = hop, before

    def start(self):
        self.before()
        self.hop.start()

    def arrive(self):
        self.hop.arrive()

    def sent(self):
        self.hop.sent()


def total_kernel(groups, parts, plan, rows_in, d_proj, grad_out, shared, own, *refs):
    count = 3
    outs, acc, land = (refs[i * count: (i + 1) * count] for i in range(3))
    rows_v, proj_v, shared_v, own_v, got, local, stored, send, recv, t_send, t_recv = refs[3 * count:]
    major, minor, _ = mesh_sizes(groups, parts)
    g, e = lax.axis_index("grp"), lax.axis_index("ep")
    short = Line(minor, lax.rem(g, minor), (1, 0))
    long = Line(major, lax.div(g, minor), (minor, 0))
    whole = Line(parts, e, (0, 1))
    width = rows_in.shape[1]
    load = [pltpu.make_async_copy(a, b, local.at[i]) for i, (a, b) in enumerate((
        (grad_out, acc[0]), (rows_in, rows_v), (d_proj, proj_v), (shared, shared_v), (own, own_v)))]
    for copy in load:
        copy.start()

    def weights(k):
        def act():
            if k == 0:
                load[1].wait()
                load[2].wait()
            cuts = acc[1].shape[0] // 3
            c, cut = k // cuts, k % cuts
            blocks = max(1, 256 // acc[1].shape[2])
            rows = blocks * acc[1].shape[2]

            @pl.loop(0, groups // blocks)
            def _(i):
                cols = pl.ds(pl.multiple_of(cut * (width // cuts) + i * rows, 128), rows)
                total = lax.dot_general(rows_v[:, cols], proj_v[c], (((0,), (0,)), ((), ())), preferred_element_type=F32)
                acc[1][k, pl.ds(i * blocks, blocks)] = total.astype(BF).reshape((blocks,) + acc[1].shape[2:])

        return act

    swap = swap_legs(whole, lambda i: shared_v, lambda j, i: got.at[j], lambda j: t_send.at[j], lambda j: t_recv.at[j])

    def everyone():
        end_legs(swap)
        load[4].wait()

        @pl.loop(0, groups)
        def _(i):
            total = shared_v[i].astype(F32) + own_v[i].astype(F32)
            for j in range(parts - 1):
                total = total + got[j, i].astype(F32)
            acc[2][0, i] = total.astype(BF)

    before = {(0, 0): load[0].wait, (2, 0): everyone}
    chains = []
    for number, (j, k, far) in enumerate(plan):
        one, two = (long, short) if far else (short, long)
        y, z = one.place, two.place
        n = two.size

        def level_one(ref, k, n=n):
            return lambda i: ref.at[k, pl.ds(i * n, n)]

        def level_two(ref, k, y=y, n=n):
            return lambda i: ref.at[k, y * n + i]

        store = pltpu.make_async_copy(acc[j].at[k, y * n + z], outs[j].at[k, y * n + z], stored.at[number])
        base = [0]

        def sems(size, number=number, base=base):
            b = base[0]
            base[0] += leg_count(size)
            return (lambda i: send.at[number, b + i]), (lambda i: recv.at[number, b + i])

        first_land = leg_count(one.size) * n
        down = reduce_hops(one, level_one(acc[j], k), lambda i, j=j, k=k, n=n: land[j].at[k, pl.ds(i * n, n)], add, *sems(one.size))
        down += reduce_hops(two, level_two(acc[j], k), lambda i, j=j, k=k, f=first_land: land[j].at[k, f + i], add, *sems(two.size))
        up = gather_hops(two, level_two(outs[j], k), *sems(two.size))
        up += gather_hops(one, level_one(outs[j], k), *sems(one.size))

        def put(store=store):
            store.start()
            store.wait()

        down[0] = Begun(down[0], before.get((j, k)) or (weights(k) if j == 1 else lambda: None))
        up[0] = Begun(up[0], put)
        chains.append(down + up)
    greet([short, long], [whole])
    load[3].wait()
    start_legs(swap)
    flow(chains, 2)


def total_over_groups(gathered, d_proj, grad_out, shared, own, collective_id):
    groups, parts = lax.axis_size("grp"), lax.axis_size("ep")
    major, minor, _ = mesh_sizes(groups, parts)
    tokens, width = gathered.shape
    local_width = d_proj.shape[2]
    few = max(n for n in (4, 2, 1) if n == 1 or grad_out.shape[0] % (n * groups * ROWS) == 0)
    many = max(n for n in (12, 6, 3) if n == 3 or 3 * width % (n * groups * ROWS) == 0)
    shapes = [
        (few, groups, grad_out.shape[0] // few // groups, width),
        (many, groups, 3 * width // many // groups, local_width),
        (1,) + shared.shape,
    ]
    plan = [(0, k, k % 4 == 1) for k in range(few)] + [(1, k, k % 4 == 1) for k in range(many)] + [(2, 0, False)]
    blocks = max(leg_count(a) * b + leg_count(b) for a, b in ((minor, major), (major, minor)))
    legs = 2 * (leg_count(minor) + leg_count(major))
    total = len(plan)
    hbm = pl.BlockSpec(memory_space=pl.ANY)
    scratch = [pltpu.VMEM(a, BF) for a in shapes]
    scratch += [pltpu.VMEM((a[0], blocks) + a[2:], BF) for a in shapes]
    return pl.pallas_call(
        functools.partial(total_kernel, groups, parts, plan),
        out_shape=[jax.ShapeDtypeStruct(a, BF) for a in shapes],
        in_specs=[hbm] * 5,
        out_specs=[hbm] * len(shapes),
        scratch_shapes=scratch + [
            pltpu.VMEM(gathered.shape, BF),
            pltpu.VMEM(d_proj.shape, BF),
            pltpu.VMEM(shared.shape, BF),
            pltpu.VMEM(shared.shape, BF),
            pltpu.VMEM((parts - 1,) + shared.shape, BF),
            pltpu.SemaphoreType.DMA((5,)),
            pltpu.SemaphoreType.DMA((total,)),
            pltpu.SemaphoreType.DMA((total, legs)),
            pltpu.SemaphoreType.DMA((total, legs)),
            pltpu.SemaphoreType.DMA((parts - 1,)),
            pltpu.SemaphoreType.DMA((parts - 1,)),
        ],
        compiler_params=pltpu.CompilerParams(
            collective_id=collective_id, has_side_effects=True, vmem_limit_bytes=48 * 2**20
        ),
        cost_estimate=pl.CostEstimate(flops=6 * tokens * width * local_width, bytes_accessed=40 * 2**20, transcendentals=0),
    )(gathered, d_proj, grad_out.reshape(shapes[0]), shared, own)


def swap_legs(line, source, target, send, recv):
    n, a = line.size, line.place
    legs = []
    for j in range(1, n):
        to, off = lax.rem(a + j, n), lax.rem(a + n - j, n)
        legs.append((
            lambda to=to, j=j: remote(source(to), target(j - 1, a), send(j - 1), recv(j - 1), line.at(to - a)),
            lambda off=off, j=j: remote(target(j - 1, off), target(j - 1, off), send(j - 1), recv(j - 1), line.at(off - a)),
        ))
    return legs


def start_legs(legs):
    for out, _ in legs:
        out().start()


def end_legs(legs):
    for out, into in legs:
        into().wait_recv()
    for out, into in legs:
        out().wait_send()


def add_and_send(acc, first, land, rows, line, send):
    def add(place, count):
        @pl.loop(0, count * rows // line.size // ROWS)
        def _(i):
            offset = place * (rows // line.size) + i * ROWS
            here = pl.ds(pl.multiple_of(first + offset, ROWS), ROWS)
            there = pl.ds(pl.multiple_of(offset, ROWS), ROWS)
            total = acc[here, :].astype(F32)
            for j in range(land.shape[0]):
                total = total + land[j, there, :].astype(F32)
            acc[here, :] = total.astype(acc.dtype)

    if line.size == 2:
        add(1 - line.place, 1)
        send()
        add(line.place, 1)
    else:
        add(0, line.size)
        send()


def add_rows(acc, first, land, rows):
    @pl.loop(0, rows // ROWS)
    def _(i):
        here = pl.ds(pl.multiple_of(first + i * ROWS, ROWS), ROWS)
        there = pl.ds(pl.multiple_of(i * ROWS, ROWS), ROWS)
        acc[here, :] = (acc[here, :].astype(F32) + land[there, :].astype(F32)).astype(acc.dtype)


def experts_kernel(
    groups, parts, local_rows, ring, acc_ring, experts,
    x, dy, widen, shrink,
    summed, moe, grad_widen, grad_shrink,
    xs, dys, wide, down, sum_wide, sum_down, stage, acc, other, land_c, land_p, land_q, land_z,
    hid, raw, gated, d_gu, gate, product, marks,
    load, dy_sem, stage_sem, g_send, g_recv, s_send, s_recv,
):
    core, first, second, long = lines(groups, parts)
    c, p, q, z = core.place, first.place, second.place, long.place
    pn, qn, zn = first.size, second.size, long.size
    chunks, width = x.shape[0], shrink.shape[2]
    local_exp, inner = shrink.shape[0], shrink.shape[1]
    share = inner // groups
    group, part = lax.axis_index("grp"), lax.axis_index("ep")
    rz, rq, rp, rc = ROWS, ROWS * zn, ROWS * zn * qn, ROWS * zn * qn * pn
    rows = 2 * rc
    cuts = local_rows // ROWS
    base = part * local_exp
    pairs = local_exp // 2

    loads = []
    for e in range(local_exp):
        for half in range(2):
            to = (e // 2) * 4 * share + half * 2 * share + (e % 2) * share
            loads.append(pltpu.make_async_copy(
                widen.at[e, :, pl.ds(pl.multiple_of(half * inner + group * share, share), share)],
                wide.at[:, pl.ds(to, share)], load.at[2 * e + half]))
        loads.append(pltpu.make_async_copy(
            shrink.at[e, pl.ds(pl.multiple_of(group * share, share), share), :],
            down.at[pl.ds(e * share, share), :], load.at[2 * local_exp + e]))
    for copy in loads:
        copy.start()

    def dy_copy(k):
        return pltpu.make_async_copy(dy.at[k], dys.at[lax.rem(k, 2)], dy_sem.at[lax.rem(k, 2)])

    dy_start = lambda k: dy_copy(k).start()
    dy_start(0)
    greet_lines([core, first, second, long])

    def rows_at(start, size):
        return pl.ds(pl.multiple_of(start, ROWS), size)

    def g_long(k):
        buf = xs.at[lax.rem(k, ring)]
        return swap_legs(
            long, lambda i: x.at[k], lambda j, i: buf.at[rows_at(c * rc + p * rp + q * rq + i * rz, rz), :],
            lambda j: g_send.at[k, j], lambda j: g_recv.at[k, j])

    def g_line(k, line, at, offset):
        return swap_legs(line, lambda i: at(line.place), lambda j, i: at(i),
                         lambda j: g_send.at[k, offset + j], lambda j: g_recv.at[k, offset + j])

    def g_second(k):
        buf = xs.at[lax.rem(k, ring)]
        return g_line(k, second, lambda i: buf.at[rows_at(c * rc + p * rp + i * rq, rq), :], zn - 1)

    def g_first(k):
        buf = xs.at[lax.rem(k, ring)]
        return g_line(k, first, lambda i: buf.at[rows_at(c * rc + i * rp, rp), :], zn + qn - 2)

    def g_core(k):
        buf = xs.at[lax.rem(k, ring)]
        return g_line(k, core, lambda i: buf.at[rows_at(i * rc, rc), :], zn + qn + pn - 3)

    def s_line(k, line, at, land, offset):
        return swap_legs(line, at, lambda j, i: land.at[lax.rem(k, 2), j],
                         lambda j: s_send.at[k, offset + j], lambda j: s_recv.at[k, offset + j])

    def s_core(k):
        return s_line(k, core, lambda i: other, land_c, 0)

    def s_first(k):
        buf = acc.at[lax.rem(k, acc_ring)]
        return s_line(k, first, lambda i: buf.at[rows_at(i * rp, rp), :], land_p, 1)

    def s_second(k):
        buf = acc.at[lax.rem(k, acc_ring)]
        return s_line(k, second, lambda i: buf.at[rows_at(p * rp + i * rq, rq), :], land_q, pn)

    def s_long(k):
        buf = acc.at[lax.rem(k, acc_ring)]
        return s_line(k, long, lambda i: buf.at[rows_at(p * rp + q * rq + i * rz, rz), :], land_z, pn + qn - 1)

    def after(t, lag, act):
        k = t - lag

        @pl.when((k >= 0) & (k < chunks))
        def _():
            act(k)

    tiles = width // 512

    def compute(k):
        buf, dyk = xs.at[lax.rem(k, ring)], dys.at[lax.rem(k, 2)]

        @pl.when(k == 0)
        def _():
            for copy in loads:
                copy.wait()

        dy_copy(k).wait()

        @pl.when(k + 1 < chunks)
        def _():
            dy_start(k + 1)

        @pl.loop(0, pairs)
        def _(j):
            cols = pl.ds(pl.multiple_of(j * 4 * share, 4 * share), 4 * share)
            some = pl.ds(pl.multiple_of(j * 2 * share, 2 * share), 2 * share)
            to_up = pl.ds(pl.multiple_of(j * 4 * share + 2 * share, share), 2 * share)
            to_gate = pl.ds(pl.multiple_of(j * 4 * share, share), 2 * share)
            hid[...] = jnp.dot(buf[:, :width], wide[:, cols], preferred_element_type=F32)
            raw[...] = lax.dot_general(dyk[...], down[some, :], (((1,), (1,)), ((), ())), preferred_element_type=F32)
            gate[...] = jnp.dot(buf[:, width:], marks[:, some], preferred_element_type=F32)

            @pl.loop(0, rows // 32)
            def _(i):
                here = pl.ds(pl.multiple_of(i * 32, 32), 32)
                g, u = hid[here, : 2 * share], hid[here, 2 * share:]
                d, weight = raw[here, :], gate[here, :]
                sigma = 0.5 * jnp.tanh(0.5 * g) + 0.5
                swish = g * sigma
                act = swish * u
                product[here, some] = (act * d).astype(BF)
                gated[here, some] = (act * weight).astype(BF)
                d = d * weight
                d_gu[here, to_gate] = (d * u * (sigma + swish * (1.0 - sigma))).astype(BF)
                d_gu[here, to_up] = (d * swish).astype(BF)

        mine = acc.at[lax.rem(k, acc_ring)]

        def split(cols, total):
            @pl.when(c == 0)
            def _():
                mine[:, cols] = total[:rc].astype(BF)
                other[:, cols] = total[rc:].astype(BF)

            @pl.when(c == 1)
            def _():
                other[:, cols] = total[:rc].astype(BF)
                mine[:, cols] = total[rc:].astype(BF)

        @pl.loop(0, tiles)
        def _(n):
            cols = pl.ds(pl.multiple_of(n * 512, 512), 512)
            split(cols, lax.dot_general(
                d_gu[...], wide[cols, :], (((1,), (1,)), ((), ())), preferred_element_type=F32))

        split(pl.ds(width, 128), lax.dot_general(
            product[...], marks[...], (((1,), (1,)), ((), ())), preferred_element_type=F32))
        start_legs(s_core(k))
        slot = lax.rem(k, 2)

        @pl.when(k >= 2)
        def _():
            pltpu.make_async_copy(stage.at[slot], moe.at[k - 2], stage_sem.at[slot]).wait()

        @pl.loop(0, tiles)
        def _(n):
            cols = pl.ds(pl.multiple_of(n * 512, 512), 512)
            stage[slot, :, cols] = jnp.dot(gated[...], down[:, cols], preferred_element_type=F32).astype(BF)
            sum_wide[cols, :] += lax.dot_general(
                buf[:, cols], d_gu[...], (((0,), (0,)), ((), ())), preferred_element_type=F32)
            sum_down[:, cols] += lax.dot_general(
                gated[...], dyk[:, cols], (((0,), (0,)), ((), ())), preferred_element_type=F32)

        pltpu.make_async_copy(stage.at[slot], moe.at[k], stage_sem.at[slot]).start()

    def end_long(k):
        end_legs(s_long(k))
        buf = acc.at[lax.rem(k, acc_ring)]
        total = buf[rows_at(p * rp + q * rq + z * rz, rz), :].astype(F32)
        for j in range(zn - 1):
            total = total + land_z[lax.rem(k, 2), j].astype(F32)
        summed[k] = total.astype(BF)

    def end_second(k):
        end_legs(s_second(k))
        add_and_send(acc.at[lax.rem(k, acc_ring)], p * rp + q * rq, land_q.at[lax.rem(k, 2)], rq, long, lambda: start_legs(s_long(k)))

    def end_first(k):
        end_legs(s_first(k))
        add_and_send(acc.at[lax.rem(k, acc_ring)], p * rp, land_p.at[lax.rem(k, 2)], rp, second, lambda: start_legs(s_second(k)))

    def end_core(k):
        end_legs(s_core(k))
        add_and_send(acc.at[lax.rem(k, acc_ring)], 0, land_c.at[lax.rem(k, 2)], rc, first, lambda: start_legs(s_first(k)))

    def begin(k):
        xs[lax.rem(k, ring), rows_at(c * rc + p * rp + q * rq + z * rz, rz), :] = x[k]
        start_legs(g_long(k))

        @pl.when(k == 0)
        def _():
            sum_wide[...] = jnp.zeros_like(sum_wide)
            sum_down[...] = jnp.zeros_like(sum_down)
            lanes = lax.broadcasted_iota(jnp.int32, marks.shape, 0)
            owner = base + lax.div(lax.broadcasted_iota(jnp.int32, marks.shape, 1), share)
            marks[...] = jnp.where((lanes == owner) | (lanes == owner + experts), 1.0, 0.0).astype(BF)

    def then(one, two):
        def act(k):
            end_legs(one(k))
            start_legs(two(k))

        return act

    def wide_out(i):
        here = pl.ds(pl.multiple_of(i * rows, rows), rows)
        return pltpu.make_async_copy(d_gu, grad_widen.at[here, :], load.at[1])

    out_down = pltpu.make_async_copy(sum_down, grad_shrink, load.at[0])

    def store(i):
        @pl.when(i == 0)
        def _():
            out_down.start()

        @pl.when(i > 0)
        def _():
            wide_out(i - 1).wait()

        d_gu[...] = sum_wide[pl.ds(pl.multiple_of(i * rows, rows), rows), :].astype(BF)
        wide_out(i).start()

    @pl.loop(0, chunks + 8)
    def _(t):
        after(t, 4, lambda k: end_legs(g_core(k)))
        after(t, 3, then(g_first, g_core))
        after(t, 2, then(g_second, g_first))
        after(t, 1, then(g_long, g_second))
        after(t, 0, begin)
        after(t, 8, end_long)
        after(t, 7, end_second)
        after(t, 6, end_first)
        after(t, 5, end_core)
        after(t, 4, compute)

        @pl.when((t >= chunks + 4) & (t < chunks + 4 + width // rows))
        def _():
            store(t - chunks - 4)

    for i in range(4, width // rows):
        store(i)
    for k in range(chunks - 2, chunks):
        pltpu.make_async_copy(stage.at[k % 2], moe.at[k], stage_sem.at[k % 2]).wait()
    wide_out(width // rows - 1).wait()
    out_down.wait()


def experts_together(x, dy, widen, shrink, experts, collective_id):
    groups, parts = lax.axis_size("grp"), lax.axis_size("ep")
    major, minor, xn = mesh_sizes(groups, parts)
    micro, local_rows, wide = x.shape
    x = x.reshape(-1, ROWS, wide)
    chunks = x.shape[0]
    local_exp, inner, width = shrink.shape
    share = inner // groups
    hidden = local_exp * share
    half = ROWS * major * minor * xn
    rows = 2 * half
    ring, acc_ring = min(chunks, 6), 4
    legs = major + minor + xn - 2
    vmem = pl.BlockSpec(memory_space=pltpu.VMEM)
    hbm = pl.BlockSpec(memory_space=pl.ANY)
    flops = 2 * chunks * rows * width * hidden * 9
    return pl.pallas_call(
        functools.partial(experts_kernel, groups, parts, local_rows, ring, acc_ring, experts),
        out_shape=[
            jax.ShapeDtypeStruct((chunks, ROWS, wide), BF),
            jax.ShapeDtypeStruct((chunks, rows, width), BF),
            jax.ShapeDtypeStruct((width, 2 * hidden), BF),
            jax.ShapeDtypeStruct((hidden, width), F32),
        ],
        in_specs=[vmem, hbm, hbm, hbm],
        out_specs=[vmem, hbm, hbm, hbm],
        scratch_shapes=[
            pltpu.VMEM((ring, rows, wide), BF),
            pltpu.VMEM((2, rows, width), BF),
            pltpu.VMEM((width, 2 * hidden), BF),
            pltpu.VMEM((hidden, width), BF),
            pltpu.VMEM((width, 2 * hidden), F32),
            pltpu.VMEM((hidden, width), F32),
            pltpu.VMEM((2, rows, width), BF),
            pltpu.VMEM((acc_ring, half, wide), BF),
            pltpu.VMEM((half, wide), BF),
            pltpu.VMEM((2, 1, half, wide), BF),
            pltpu.VMEM((2, xn - 1, half // xn, wide), BF),
            pltpu.VMEM((2, minor - 1, half // xn // minor, wide), BF),
            pltpu.VMEM((2, major - 1, ROWS, wide), BF),
            pltpu.VMEM((rows, 4 * share), F32),
            pltpu.VMEM((rows, 2 * share), F32),
            pltpu.VMEM((rows, hidden), BF),
            pltpu.VMEM((rows, 2 * hidden), BF),
            pltpu.VMEM((rows, 2 * share), F32),
            pltpu.VMEM((rows, hidden), BF),
            pltpu.VMEM((128, hidden), BF),
            pltpu.SemaphoreType.DMA((3 * local_exp,)),
            pltpu.SemaphoreType.DMA((2,)),
            pltpu.SemaphoreType.DMA((2,)),
            pltpu.SemaphoreType.DMA((chunks, legs)),
            pltpu.SemaphoreType.DMA((chunks, legs)),
            pltpu.SemaphoreType.DMA((chunks, legs)),
            pltpu.SemaphoreType.DMA((chunks, legs)),
        ],
        compiler_params=pltpu.CompilerParams(
            collective_id=collective_id, has_side_effects=True, vmem_limit_bytes=60 * 2**20
        ),
        cost_estimate=pl.CostEstimate(flops=flops, bytes_accessed=80 * 2**20, transcendentals=chunks * rows * hidden),
    )(x, dy, widen, shrink)


def experts_apart(x, dy_all, specialist_widen_matrix, specialist_shrink_matrix, experts):
    groups, parts = lax.axis_size("grp"), lax.axis_size("ep")
    group, part = lax.axis_index("grp"), lax.axis_index("ep")
    local_exp, inner, width = specialist_shrink_matrix.shape
    share = inner // groups
    widen = specialist_widen_matrix.reshape(local_exp, width, 2, groups, share)
    widen = lax.dynamic_index_in_dim(widen, group, 3, keepdims=False)
    widen = widen.transpose(1, 2, 0, 3).reshape(width, 2 * local_exp * share)
    shrink = specialist_shrink_matrix.reshape(local_exp, groups, share, width)
    shrink = lax.dynamic_index_in_dim(shrink, group, 1, keepdims=False).reshape(local_exp * share, width)
    x_all = gather_all(x, 1)
    chunk_shape = x_all.shape[:-1]
    x_all, dy_all = x_all.reshape(-1, width + 128), dy_all.reshape(-1, width)
    gate = x_all[:, width: width + experts].astype(F32) + x_all[:, width + experts: width + 2 * experts].astype(F32)
    x_all = x_all[:, :width]
    gate = lax.dynamic_slice_in_dim(gate, part * local_exp, local_exp, axis=1)
    gate = jnp.repeat(gate, share, axis=1)
    gate_up = jnp.dot(x_all, widen, preferred_element_type=F32)
    g, u = gate_up[:, : local_exp * share], gate_up[:, local_exp * share:]
    sigma = jax.nn.sigmoid(g)
    act = g * sigma * u
    gated = (gate * act).astype(BF)
    moe_part = jnp.dot(gated, shrink, preferred_element_type=F32).astype(BF)
    d_raw = lax.dot_general(dy_all, shrink, (((1,), (1,)), ((), ())), preferred_element_type=F32)
    d_gate = jnp.sum((act * d_raw).reshape(-1, local_exp, share), axis=-1)
    d_act = gate * d_raw
    d_gu = jnp.concatenate([d_act * u * sigma * (1.0 + g * (1.0 - sigma)), d_act * (g * sigma)], axis=1).astype(BF)
    dx_part = lax.dot_general(d_gu, widen, (((1,), (1,)), ((), ())), preferred_element_type=F32).astype(BF)
    lanes = jnp.arange(128, dtype=jnp.int32)
    place = (lanes[None, :] == part * local_exp + jnp.arange(local_exp, dtype=jnp.int32)[:, None])
    d_gate = jnp.sum(jnp.where(place[None], d_gate[:, :, None], 0.0), axis=1)
    dx_part = jnp.concatenate([dx_part, d_gate.astype(BF)], axis=1)
    dx_sum = scatter_all(dx_part.reshape(chunk_shape + (width + 128,)), 2)
    grad_widen = lax.dot_general(x_all, d_gu, (((0,), (0,)), ((), ())), preferred_element_type=F32)
    grad_shrink = lax.dot_general(gated, dy_all, (((0,), (0,)), ((), ())), preferred_element_type=F32)
    grad_widen = grad_widen.astype(BF).reshape(width, 2, local_exp // 2, 2, share).transpose(0, 2, 1, 3, 4)
    return dx_sum, moe_part.reshape(chunk_shape + (width,)), grad_widen, grad_shrink


def finish_kernel(share, qkv, out, wide, shrink, qkv_to, out_to, wide_to, shrink_to):
    qkv_to[...] = qkv[...].astype(F32)
    out_to[...] = out[...].astype(F32)
    shrink_to[...] = shrink[...]
    for i in range(wide.shape[0]):
        wide_to[0, :, i * share: (i + 1) * share] = wide[i].astype(F32)


def finish(qkv, out, wide, shrink, local_exp, share):
    groups, rows, _ = wide.shape
    whole = (local_exp, rows, 2 * groups * share)
    if share % 128:
        wide = wide.reshape(groups, rows, local_exp // 2, 2, 2, share).transpose(2, 4, 1, 3, 0, 5)
        return qkv.astype(F32), out.astype(F32), wide.reshape(whole).astype(F32), shrink
    steps = 2 * local_exp
    cut = lambda a: pl.BlockSpec((a.shape[0] // (2 * steps), a.shape[1]), lambda i, j: (2 * i + j, 0))
    outs = [jax.ShapeDtypeStruct(a.shape, F32) for a in (qkv, out)] + [
        jax.ShapeDtypeStruct(whole, F32), jax.ShapeDtypeStruct(shrink.shape, F32)]
    return pl.pallas_call(
        functools.partial(finish_kernel, share),
        grid=(steps, 2),
        out_shape=outs,
        in_specs=[cut(qkv), cut(out),
                  pl.BlockSpec((groups, rows // 2, share), lambda i, j: (0, j, i // 4 * 4 + i % 2 * 2 + i // 2 % 2)), cut(shrink)],
        out_specs=[cut(qkv), cut(out),
                   pl.BlockSpec((1, rows // 2, groups * share), lambda i, j: (i // 2, j, i % 2)), cut(shrink)],
        compiler_params=pltpu.CompilerParams(vmem_limit_bytes=40 * 2**20),
    )(qkv, out, wide, shrink)


class Backdrop:
    PACE = 2

    def __init__(self, groups, parts, part, out, acc, land_c, land_p, land_q, land_z, local, send, recv):
        self.core, self.first, self.second, self.long = lines(groups, parts)
        self.part, self.out, self.acc, self.lands = part, out, acc, (land_c, land_p, land_q, land_z)
        self.local, self.send, self.recv = local, send, recv
        self.chunks = part.shape[0]
        pn, qn, zn = self.first.size, self.second.size, self.long.size
        self.rz, self.rq, self.rp, self.rc = ROWS, ROWS * zn, ROWS * zn * qn, ROWS * zn * qn * pn
        self.levels = 3 + hop_count(zn)
        self.lag = self.PACE * self.levels

    @staticmethod
    def scratch(chunks, width):
        major, minor, xn = mesh_sizes(lax.axis_size("grp"), lax.axis_size("ep"))
        half = ROWS * major * minor * xn
        legs = minor + xn - 1 + leg_count(major)
        return [
            pltpu.VMEM((min(chunks, 12), half, width), BF),
            pltpu.VMEM((4, 1, half, width), BF),
            pltpu.VMEM((4, xn - 1, half // xn, width), BF),
            pltpu.VMEM((4, minor - 1, half // xn // minor, width), BF),
            pltpu.VMEM((chunks, leg_count(major), ROWS, width), BF),
            pltpu.SemaphoreType.DMA((chunks,)),
            pltpu.SemaphoreType.DMA((chunks, legs)),
            pltpu.SemaphoreType.DMA((chunks, legs)),
        ]

    def near(self):
        return [self.core, self.first, self.second, self.long]

    def buf(self, k):
        return self.acc.at[lax.rem(k, self.acc.shape[0])]

    def own(self, k):
        here = pl.ds(pl.multiple_of(self.core.place * self.rc, self.rc), self.rc)
        return pltpu.make_async_copy(self.part.at[k, here, :], self.buf(k), self.local.at[k])

    def hop(self, k, level):
        c, p, q, z = self.core.place, self.first.place, self.second.place, self.long.place
        pn, qn = self.first.size, self.second.size
        at = lambda start, size: pl.ds(pl.multiple_of(start, ROWS), size)
        line, offset, source = [
            (self.core, 0, lambda i: self.part.at[k, at(i * self.rc, self.rc), :]),
            (self.first, 1, lambda i: self.buf(k).at[at(i * self.rp, self.rp), :]),
            (self.second, pn, lambda i: self.buf(k).at[at(p * self.rp + i * self.rq, self.rq), :]),
        ][level]
        land = self.lands[level]
        return swap_legs(line, source, lambda j, i: land.at[lax.rem(k, 4), j],
                         lambda j: self.send.at[k, offset + j], lambda j: self.recv.at[k, offset + j])

    def long_hop(self, k, number):
        base = self.first.place * self.rp + self.second.place * self.rq
        offset = self.first.size + self.second.size - 1
        at = lambda i: self.buf(k).at[pl.ds(pl.multiple_of(base + i * self.rz, ROWS), self.rz), :]
        land = self.lands[3].at[k]
        return reduce_hops(self.long, at, lambda i: land.at[i], add,
                           lambda i: self.send.at[k, offset + i], lambda i: self.recv.at[k, offset + i])[number]

    def end(self, k, level):
        p, q, z = self.first.place, self.second.place, self.long.place
        if level >= 3:
            hop = self.long_hop(k, level - 3)
            hop.arrive()
            hop.sent()
            if level + 1 < self.levels:
                self.long_hop(k, level - 2).start()
            else:
                here = pl.ds(pl.multiple_of(p * self.rp + q * self.rq + z * self.rz, ROWS), ROWS)
                self.out[k] = self.buf(k)[here, :]
            return
        end_legs(self.hop(k, level))
        if level == 0:
            self.own(k).wait()
        first = [0, p * self.rp, p * self.rp + q * self.rq][level]
        size = [self.rc, self.rp, self.rq][level]
        land = self.lands[level]
        line = (self.first, self.second, self.long)[level]
        then = (lambda: start_legs(self.hop(k, level + 1))) if level < 2 else self.long_hop(k, 0).start
        add_and_send(self.buf(k), first, land.at[lax.rem(k, 4)], size, line, then)

    def begin(self, k):
        start_legs(self.hop(k, 0))
        self.own(k).start()

    def step(self, t):
        for level in reversed(range(self.levels)):
            k = t - self.PACE * (level + 1)

            @pl.when((k >= 0) & (k < self.chunks))
            def _(k=k, level=level):
                self.end(k, level)

        @pl.when((t >= 0) & (t < self.chunks))
        def _():
            self.begin(t)


class Sequence:
    def __init__(self, parts, block, micro):
        e = lax.axis_index("ep")
        self.xn, self.block, self.micro, self.e = parts // 2, block, micro, e
        self.x, self.c = lax.div(e, 2), lax.rem(e, 2)
        self.line = Line(parts, e, (0, 1))
        self.line_x = Line(self.xn, self.x, (0, 2))
        self.line_c = Line(2, self.c, (0, 1))

    def at(self, ref, m, x, c):
        return ref.at[m, pl.ds(pl.multiple_of((x * 2 + c) * self.block, self.block), self.block), :]

    def gather_x(self, ref, send, recv):
        legs = []
        for m in range(self.micro):
            legs += swap_legs(
                self.line_x, lambda i, m=m: self.at(ref, m, self.x, self.c), lambda j, i, m=m: self.at(ref, m, i, self.c),
                lambda j, m=m: send.at[m, j], lambda j, m=m: recv.at[m, j])
        return legs

    def gather_c(self, ref, send, recv):
        legs = []
        for m in range(self.micro):
            for x in range(self.xn):
                legs += swap_legs(
                    self.line_c, lambda i, m=m, x=x: self.at(ref, m, x, self.c), lambda j, i, m=m, x=x: self.at(ref, m, x, i),
                    lambda j, m=m, x=x: send.at[m, self.xn - 1 + x], lambda j, m=m, x=x: recv.at[m, self.xn - 1 + x])
        return legs

    def reduce_c(self, ref, land, send, recv):
        legs = []
        for m in range(self.micro):
            for x in range(self.xn):
                legs += swap_legs(
                    self.line_c, lambda i, m=m, x=x: self.at(ref, m, x, i), lambda j, i, m=m, x=x: land.at[m, x],
                    lambda j, m=m, x=x: send.at[m, self.xn - 1 + x], lambda j, m=m, x=x: recv.at[m, self.xn - 1 + x])
        return legs

    def reduce_x(self, ref, land, send, recv):
        legs = []
        for m in range(self.micro):
            legs += swap_legs(
                self.line_x, lambda i, m=m: self.at(ref, m, i, self.c), lambda j, i, m=m: land.at[m, j],
                lambda j, m=m: send.at[m, j], lambda j, m=m: recv.at[m, j])
        return legs

    def add_c(self, ref, land):
        for m in range(self.micro):
            for x in range(self.xn):
                add_rows(ref.at[m], (x * 2 + self.c) * self.block, land.at[m, x], self.block)

    def total_x(self, ref, land, out):
        for m in range(self.micro):
            @pl.loop(0, self.block // ROWS)
            def _(i, m=m):
                here = pl.ds(pl.multiple_of(i * ROWS, ROWS), ROWS)
                total = ref[m, pl.ds(pl.multiple_of(self.e * self.block + i * ROWS, ROWS), ROWS), :].astype(F32)
                for j in range(self.xn - 1):
                    total = total + land[m, j, here, :].astype(F32)
                out[m, here, :] = total


def sum_over_parts(seq, columns, sent, got, send, recv, meanwhile):
    flat = columns.T
    sent[...] = flat[:8]
    legs = swap_legs(seq.line, lambda i: sent, lambda j, i: got.at[j], lambda j: send.at[j], lambda j: recv.at[j])
    start_legs(legs)
    meanwhile()
    end_legs(legs)
    total = sent[...]
    for j in range(seq.line.size - 1):
        total = total + got[j]
    return jnp.concatenate([total] * 16, axis=0).T


def back_kernel(
    groups, parts, backed,
    branch, merge, triple, queries, keys, values, mixed, probs, hat, inv, gains_in, cos, sin, wide, part,
    d_proj, d_in, grad_heads, grad_out, wide_all, summed,
    gains, rows_all, merge_v, triple_v, q_v, k_v, v_v, mixed_v, probs_v, hat_v, d_mixed, d_qk, sums, partial, land_c, land_x, sent, got,
    load, g_send, g_recv, s_send, s_recv, t_send, t_recv, w_send, w_recv, *behind
):
    micro, block, width = branch.shape
    seq = Sequence(parts, block, micro)
    length = queries.shape[1]
    tokens = micro * length
    heads = queries.shape[2] // HD
    scale = 1.0 / math.sqrt(HD)
    loads = [pltpu.make_async_copy(a, b, load.at[i]) for i, (a, b) in enumerate((
        (merge, merge_v), (mixed, mixed_v), (queries, q_v), (keys, k_v), (values, v_v), (probs, probs_v), (hat, hat_v), (triple, triple_v)))]
    for copy in loads:
        copy.start()
    gains[...] = gains_in[...].astype(F32)
    over = Line(groups, lax.axis_index("grp"), (1, 0))
    if backed:
        back = Backdrop(groups, parts, part, summed, *behind)
        greet_lines([seq.line, over] + back.near())
        steps = back.chunks + back.lag
        step = back.step
    else:
        greet_lines([seq.line, over])
        steps, step = 0, lambda t: None
        summed[...] = jnp.zeros_like(summed)
    for m in range(micro):
        rows_all[m, pl.ds(pl.multiple_of(seq.e * block, block), block), :] = branch[m]
    gather_x = seq.gather_x(rows_all, g_send, g_recv)
    start_legs(gather_x)
    g = over.place
    own_wide = pltpu.make_async_copy(wide.at[g], wide_all.at[g], load.at[8])
    own_wide.start()
    turn = swap_legs(over, lambda i: wide.at[i], lambda j, i: wide_all.at[i], lambda j: w_send.at[j], lambda j: w_recv.at[j])
    start_legs(turn)
    step(0)
    step(1)
    step(2)
    end_legs(gather_x)
    gather_c = seq.gather_c(rows_all, g_send, g_recv)
    start_legs(gather_c)
    step(3)
    sums[...] = jnp.zeros_like(sums)
    grad_heads[...] = jnp.zeros_like(grad_heads)
    end_legs(gather_c)
    for copy in loads[:2]:
        copy.wait()
    for m in range(micro):
        d_mixed[m] = lax.dot_general(rows_all[m], merge_v[...], (((1,), (1,)), ((), ())), preferred_element_type=F32).astype(BF)
    step(4)

    @pl.loop(0, width // 512)
    def _(n):
        cols = pl.ds(pl.multiple_of(n * 512, 512), 512)
        total = lax.dot_general(mixed_v[0], rows_all[0, :, cols], (((0,), (0,)), ((), ())), preferred_element_type=F32)
        for m in range(1, micro):
            total = total + lax.dot_general(
                mixed_v[m], rows_all[m, :, cols], (((0,), (0,)), ((), ())), preferred_element_type=F32)
        grad_out[:, cols] = total.astype(BF)

    step(5)
    for copy in loads[2:7]:
        copy.wait()
    lane = lax.broadcasted_iota(jnp.int32, (1, 128), 1)

    def one_head(i):
        m, h = lax.div(i, heads), lax.rem(i, heads)
        cols = pl.ds(pl.multiple_of(h * HD, HD), HD)
        here = pl.ds(pl.multiple_of(m * length, length), length)
        d_m = d_mixed[m, :, cols]
        weights = probs_v[m, h]
        low = weights.astype(BF)
        d_proj[2, here, cols] = lax.dot_general(low, d_m, (((0,), (0,)), ((), ())), preferred_element_type=F32).astype(BF)
        d_w = lax.dot_general(d_m, v_v[m, :, cols], (((1,), (1,)), ((), ())), preferred_element_type=F32)
        d_s = (weights * (d_w - jnp.sum(weights * d_w, axis=-1, keepdims=True))).astype(BF)
        d_q = jnp.dot(d_s, k_v[m, :, cols], preferred_element_type=F32) * scale
        d_k = lax.dot_general(d_s, q_v[m, :, cols], (((0,), (0,)), ((), ())), preferred_element_type=F32) * scale
        marks = sums[here, :]
        for c, d in enumerate((d_q, d_k)):
            d = d * cos[...] - pltpu.roll(d, HD // 2, 1) * sin[...]
            d_qk[c, here, cols] = d
            product = d * hat_v[c, here, cols]
            grad_heads[c: c + 1, cols] += jnp.sum(product, axis=0, keepdims=True)
            marks = marks + jnp.where(lane == c, jnp.sum(product * gains[c: c + 1, cols], axis=-1, keepdims=True), 0.0)
        sums[here, :] = marks

    @pl.loop(0, micro * heads)
    def _(i):
        one_head(i)
        step(i + 6)

    done = 7 + micro * heads
    sums[...] = sum_over_parts(seq, sums[...], sent, got, t_send, t_recv, lambda: step(done - 1))

    @pl.loop(0, tokens // 64)
    def _(i):
        here = pl.ds(pl.multiple_of(i * 64, 64), 64)
        for c in range(2):
            inner = sums[here, c: c + 1] * (1.0 / width)
            d_proj[c, here, :] = (inv[here, c: c + 1] * (
                d_qk[c, here, :] * gains[c: c + 1, :] - hat_v[c, here, :] * inner)).astype(BF)

    loads[7].wait()

    @pl.loop(0, width // 512)
    def _(n):
        cols = pl.ds(pl.multiple_of(n * 512, 512), 512)
        for m in range(micro):
            here = pl.ds(m * length, length)
            total = lax.dot_general(d_proj[0, here, :], triple_v[0, cols, :], (((1,), (1,)), ((), ())), preferred_element_type=F32)
            for c in (1, 2):
                total = total + lax.dot_general(
                    d_proj[c, here, :], triple_v[c, cols, :], (((1,), (1,)), ((), ())), preferred_element_type=F32)
            partial[m, :, cols] = total.astype(BF)

    reduce_c = seq.reduce_c(partial, land_c, s_send, s_recv)
    start_legs(reduce_c)
    step(done)
    end_legs(reduce_c)
    seq.add_c(partial, land_c)
    reduce_x = seq.reduce_x(partial, land_x, s_send, s_recv)
    start_legs(reduce_x)
    step(done + 1)
    end_legs(reduce_x)
    seq.total_x(partial, land_x, d_in)
    for t in range(done + 2, steps):
        step(t)
    end_legs(turn)
    own_wide.wait()


def attention_back(branch, merge, triple, queries, keys, values, mixed, probs, hat, inv, gains, cos, sin, wide, part, collective_id):
    groups, parts = lax.axis_size("grp"), lax.axis_size("ep")
    micro, block, width = branch.shape
    length, local_width = queries.shape[1:]
    tokens = micro * length
    backed = part is not None
    behind = Backdrop.scratch(part.shape[0], width) if backed else []
    summed = (part.shape[0], ROWS, width) if backed else (8, 128)
    vmem = pl.BlockSpec(memory_space=pltpu.VMEM)
    hbm = pl.BlockSpec(memory_space=pl.ANY)
    xn = parts // 2
    return pl.pallas_call(
        functools.partial(back_kernel, groups, parts, backed),
        out_shape=[
            jax.ShapeDtypeStruct((3, tokens, local_width), BF),
            jax.ShapeDtypeStruct((micro, block, width), F32),
            jax.ShapeDtypeStruct((8, local_width), F32),
            jax.ShapeDtypeStruct((local_width, width), BF),
            jax.ShapeDtypeStruct(wide.shape, BF),
            jax.ShapeDtypeStruct(summed, BF if backed else F32),
        ],
        in_specs=[vmem] + [hbm] * 8 + [vmem] * 4 + [hbm] * 2,
        out_specs=[vmem] * 4 + [hbm, vmem],
        scratch_shapes=[
            pltpu.VMEM(gains.shape, F32),
            pltpu.VMEM((micro, length, width), BF),
            pltpu.VMEM(merge.shape, BF),
            pltpu.VMEM(triple.shape, BF),
            pltpu.VMEM(queries.shape, BF),
            pltpu.VMEM(queries.shape, BF),
            pltpu.VMEM(queries.shape, BF),
            pltpu.VMEM(queries.shape, BF),
            pltpu.VMEM(probs.shape, F32),
            pltpu.VMEM(hat.shape, F32),
            pltpu.VMEM(queries.shape, BF),
            pltpu.VMEM((2, tokens, local_width), F32),
            pltpu.VMEM((tokens, 128), F32),
            pltpu.VMEM((micro, length, width), BF),
            pltpu.VMEM((micro, xn, block, width), BF),
            pltpu.VMEM((micro, xn - 1, block, width), BF),
            pltpu.VMEM((8, tokens), F32),
            pltpu.VMEM((parts - 1, 8, tokens), F32),
            pltpu.SemaphoreType.DMA((9,)),
            pltpu.SemaphoreType.DMA((micro, 2 * xn - 1)),
            pltpu.SemaphoreType.DMA((micro, 2 * xn - 1)),
            pltpu.SemaphoreType.DMA((micro, 2 * xn - 1)),
            pltpu.SemaphoreType.DMA((micro, 2 * xn - 1)),
            pltpu.SemaphoreType.DMA((parts - 1,)),
            pltpu.SemaphoreType.DMA((parts - 1,)),
            pltpu.SemaphoreType.DMA((groups - 1,)),
            pltpu.SemaphoreType.DMA((groups - 1,)),
        ] + behind,
        compiler_params=pltpu.CompilerParams(
            collective_id=collective_id, has_side_effects=True, vmem_limit_bytes=58 * 2**20
        ),
        cost_estimate=pl.CostEstimate(flops=10**10, bytes_accessed=40 * 2**20, transcendentals=0),
    )(branch, merge, triple, queries, keys, values, mixed, probs, hat, inv, gains, cos, sin, wide,
      part if backed else mixed)


class BackGather:
    PACE = 3
    LAG = 4 * PACE

    def __init__(self, groups, parts, own, out, local, send, recv):
        self.core, self.first, self.second, self.long = lines(groups, parts)
        self.own, self.out, self.local, self.send, self.recv = own, out, local, send, recv
        self.chunks = own.shape[0]
        pn, qn, zn = self.first.size, self.second.size, self.long.size
        self.rz, self.rq, self.rp, self.rc = ROWS, ROWS * zn, ROWS * zn * qn, ROWS * zn * qn * pn

    @staticmethod
    def scratch(chunks):
        major, minor, xn = mesh_sizes(lax.axis_size("grp"), lax.axis_size("ep"))
        legs = major + minor + xn - 2
        return [
            pltpu.SemaphoreType.DMA((chunks,)),
            pltpu.SemaphoreType.DMA((chunks, legs)),
            pltpu.SemaphoreType.DMA((chunks, legs)),
        ]

    def near(self):
        return [self.core, self.first, self.second, self.long]

    def rows(self, k, start, size):
        return self.out.at[k, pl.ds(pl.multiple_of(start, ROWS), size), :]

    def mine(self, k):
        c, p, q, z = self.core.place, self.first.place, self.second.place, self.long.place
        return pltpu.make_async_copy(
            self.own.at[k], self.rows(k, c * self.rc + p * self.rp + q * self.rq + z * self.rz, self.rz), self.local.at[k])

    def hop(self, k, level):
        c, p, q, z = self.core.place, self.first.place, self.second.place, self.long.place
        pn, qn, zn = self.first.size, self.second.size, self.long.size
        line, offset, at = [
            (self.long, 0, lambda i: self.rows(k, c * self.rc + p * self.rp + q * self.rq + i * self.rz, self.rz)),
            (self.second, zn - 1, lambda i: self.rows(k, c * self.rc + p * self.rp + i * self.rq, self.rq)),
            (self.first, zn + qn - 2, lambda i: self.rows(k, c * self.rc + i * self.rp, self.rp)),
            (self.core, zn + qn + pn - 3, lambda i: self.rows(k, i * self.rc, self.rc)),
        ][level]
        source = (lambda i: self.own.at[k]) if level == 0 else (lambda i: at(line.place))
        return swap_legs(line, source, lambda j, i: at(i),
                         lambda j: self.send.at[k, offset + j], lambda j: self.recv.at[k, offset + j])

    def step(self, t):
        for level in (3, 2, 1, 0):
            k = t - self.PACE * (level + 1)

            @pl.when((k >= 0) & (k < self.chunks))
            def _(k=k, level=level):
                end_legs(self.hop(k, level))
                if level == 0:
                    self.mine(k).wait()
                if level < 3:
                    start_legs(self.hop(k, level + 1))

        @pl.when((t >= 0) & (t < self.chunks))
        def _():
            self.mine(t).start()
            start_legs(self.hop(t, 0))


def forward_kernel(
    groups, parts, experts,
    x, dy, routes, quota, gains_in, head_gains_in, cos, sin, docs, dispatch_in, triple, merge,
    gathered, q_out, k_out, v_out, mixed, probs, hat, inv, hidden, ffn_in, router, dy_all,
    kept, gains, head_gains, docs_down, dispatch, triple_v, merge_v, sums, partial, land_c, land_x, sent, got,
    load, g_send, g_recv, s_send, s_recv, t_send, t_recv, *behind
):
    micro, block, width = x.shape
    seq = Sequence(parts, block, micro)
    length = gathered.shape[1]
    tokens = micro * length
    heads = q_out.shape[2] // HD
    scale = 1.0 / math.sqrt(HD)
    cuts = block // ROWS
    loads = [pltpu.make_async_copy(triple, triple_v, load.at[0]), pltpu.make_async_copy(merge, merge_v, load.at[1])]
    for copy in loads:
        copy.start()
    back = BackGather(groups, parts, dy, dy_all, *behind)
    step, steps = back.step, back.chunks + back.LAG
    gains[...] = gains_in[...].astype(F32)
    head_gains[...] = head_gains_in[...].astype(F32)
    lane = lax.broadcasted_iota(jnp.int32, (1, 128), 1)
    earlier = (lax.broadcasted_iota(jnp.int32, (block, block), 1) < lax.broadcasted_iota(jnp.int32, (block, block), 0))
    for m in range(micro):
        @pl.loop(0, cuts)
        def _(r, m=m):
            here = pl.ds(pl.multiple_of(r * ROWS, ROWS), ROWS)
            v = x[m, here, :].astype(F32)
            v = v * lax.rsqrt(jnp.mean(v * v, axis=-1, keepdims=True) + EPS)
            gathered[m, pl.ds(pl.multiple_of(seq.e * block + r * ROWS, ROWS), ROWS), :] = (v * gains[0:1, :]).astype(BF)
    greet_lines([seq.line] + back.near())
    gather_x = seq.gather_x(gathered, g_send, g_recv)
    start_legs(gather_x)
    step(0)
    limits = jnp.concatenate([quota[...], jnp.zeros((1, 128 - experts), jnp.int32)], axis=1).astype(F32)
    dispatch[...] = jnp.zeros_like(dispatch)
    dispatch[:experts, :] = dispatch_in[...]
    for m in range(micro):
        chosen = jnp.zeros((128, block), F32)
        for j in range(TOP):
            chosen = chosen + jnp.where(routes[m, j: j + 1, :] == lax.broadcasted_iota(jnp.int32, (128, 1), 0), 1.0, 0.0)
        counts = chosen.T
        prior = jnp.dot(jnp.where(earlier, 1.0, 0.0).astype(BF), counts.astype(BF), preferred_element_type=F32)
        kept[m] = jnp.where((counts > 0.0) & (prior < limits), 1.0, 0.0)
        docs_down[m] = jnp.broadcast_to(docs[m: m + 1, :], (128, length)).astype(F32).T
    step(1)
    step(2)
    end_legs(gather_x)
    gather_c = seq.gather_c(gathered, g_send, g_recv)
    start_legs(gather_c)
    step(3)
    loads[0].wait()
    end_legs(gather_c)

    @pl.loop(0, micro)
    def _(m):
        here = pl.ds(pl.multiple_of(m * length, length), length)
        marks = jnp.zeros((length, 128), F32)
        for c in range(2):
            raw = jnp.dot(gathered[m], triple_v[c], preferred_element_type=F32)
            hat[c, here, :] = raw
            marks = marks + jnp.where(lane == c, jnp.sum(raw * raw, axis=-1, keepdims=True), 0.0)
        sums[here, :] = marks
        v_out[m] = jnp.dot(gathered[m], triple_v[2], preferred_element_type=F32).astype(BF)
        step(m + 4)

    done = micro + 5
    squares = sum_over_parts(seq, sums[...], sent, got, t_send, t_recv, lambda: step(done - 1))
    inv[...] = lax.rsqrt(squares * (1.0 / width) + EPS)
    loads[1].wait()

    @pl.loop(0, micro * heads)
    def _(i):
        m, h = lax.div(i, heads), lax.rem(i, heads)
        cols = pl.ds(pl.multiple_of(h * HD, HD), HD)
        here = pl.ds(pl.multiple_of(m * length, length), length)
        for c, to in enumerate((q_out, k_out)):
            v = hat[c, here, cols] * inv[here, c: c + 1]
            hat[c, here, cols] = v
            v = v * head_gains[c: c + 1, cols]
            to[m, :, cols] = (v * cos[...] + pltpu.roll(v, HD // 2, 1) * sin[...]).astype(BF)
        scores = lax.dot_general(
            q_out[m, :, cols], k_out[m, :, cols], (((1,), (1,)), ((), ())), preferred_element_type=F32) * scale
        allowed = (docs_down[m][:, :1] == docs[pl.ds(m, 1), :].astype(F32)) & (
            lax.broadcasted_iota(jnp.int32, (length, length), 1) <= lax.broadcasted_iota(jnp.int32, (length, length), 0))
        scores = jnp.where(allowed, scores, NEG)
        grown = jnp.exp(scores - jnp.max(scores, axis=-1, keepdims=True))
        weights = grown / jnp.sum(grown, axis=-1, keepdims=True)
        probs[m, h] = weights
        mixed[m, :, cols] = jnp.dot(weights.astype(BF), v_out[m, :, cols], preferred_element_type=F32).astype(BF)
        step(done + i)

    done = done + micro * heads

    @pl.loop(0, width // 512)
    def _(n):
        cols = pl.ds(pl.multiple_of(n * 512, 512), 512)
        for m in range(micro):
            partial[m, :, cols] = jnp.dot(mixed[m], merge_v[:, cols], preferred_element_type=F32).astype(BF)

    reduce_c = seq.reduce_c(partial, land_c, s_send, s_recv)
    start_legs(reduce_c)
    step(done)
    end_legs(reduce_c)
    seq.add_c(partial, land_c)
    reduce_x = seq.reduce_x(partial, land_x, s_send, s_recv)
    start_legs(reduce_x)
    step(done + 1)
    end_legs(reduce_x)
    seq.total_x(partial, land_x, hidden)
    for m in range(micro):
        @pl.loop(0, cuts)
        def _(r, m=m):
            here = pl.ds(pl.multiple_of(r * ROWS, ROWS), ROWS)
            v = hidden[m, here, :] + x[m, here, :].astype(F32)
            hidden[m, here, :] = v
            v = v * lax.rsqrt(jnp.mean(v * v, axis=-1, keepdims=True) + EPS)
            ffn_in[m, here, :width] = (v * gains[1:2, :]).astype(BF)
        logits = lax.dot_general(
            ffn_in[m, :, :width], dispatch[...], (((1,), (1,)), ((), ())), preferred_element_type=F32)
        logits = jnp.where(lane < experts, logits, NEG)
        grown = jnp.exp(logits - jnp.max(logits, axis=-1, keepdims=True))
        grown = grown / jnp.sum(grown, axis=-1, keepdims=True)
        gate = grown * kept[m]
        router[m] = grown + pltpu.roll(kept[m], experts, 1)
        head = gate.astype(BF).astype(F32)
        ffn_in[m, :, width:] = (head + pltpu.roll(gate - head, experts, 1)).astype(BF)
    for t in range(done + 2, steps):
        step(t)


def attention_forward(x, dy, routes, quota, gains, head_gains, cos, sin, docs, dispatch, triple, merge, collective_id):
    groups, parts = lax.axis_size("grp"), lax.axis_size("ep")
    major, minor, xn = mesh_sizes(groups, parts)
    micro, block, width = x.shape
    length = docs.shape[1]
    local_width = triple.shape[2]
    heads = local_width // HD
    tokens = micro * length
    chunks = micro * block // ROWS
    rows = 2 * xn * minor * major * ROWS
    vmem = pl.BlockSpec(memory_space=pltpu.VMEM)
    hbm = pl.BlockSpec(memory_space=pl.ANY)
    low = jax.ShapeDtypeStruct((micro, length, local_width), BF)
    experts = dispatch.shape[1]
    return pl.pallas_call(
        functools.partial(forward_kernel, groups, parts, experts),
        out_shape=[
            jax.ShapeDtypeStruct((micro, length, width), BF),
            low, low, low, low,
            jax.ShapeDtypeStruct((micro, heads, length, length), F32),
            jax.ShapeDtypeStruct((2, tokens, local_width), F32),
            jax.ShapeDtypeStruct((tokens, 128), F32),
            jax.ShapeDtypeStruct((micro, block, width), F32),
            jax.ShapeDtypeStruct((micro, block, width + 128), BF),
            jax.ShapeDtypeStruct((micro, block, 128), F32),
            jax.ShapeDtypeStruct((chunks, rows, width), BF),
        ],
        in_specs=[vmem] * 10 + [hbm] * 2,
        out_specs=[vmem] * 11 + [hbm],
        scratch_shapes=[
            pltpu.VMEM((micro, block, 128), F32),
            pltpu.VMEM(gains.shape, F32),
            pltpu.VMEM(head_gains.shape, F32),
            pltpu.VMEM((micro, length, 128), F32),
            pltpu.VMEM((128, width), BF),
            pltpu.VMEM(triple.shape, BF),
            pltpu.VMEM(merge.shape, BF),
            pltpu.VMEM((tokens, 128), F32),
            pltpu.VMEM((micro, length, width), BF),
            pltpu.VMEM((micro, xn, block, width), BF),
            pltpu.VMEM((micro, xn - 1, block, width), BF),
            pltpu.VMEM((8, tokens), F32),
            pltpu.VMEM((parts - 1, 8, tokens), F32),
            pltpu.SemaphoreType.DMA((2,)),
            pltpu.SemaphoreType.DMA((micro, 2 * xn - 1)),
            pltpu.SemaphoreType.DMA((micro, 2 * xn - 1)),
            pltpu.SemaphoreType.DMA((micro, 2 * xn - 1)),
            pltpu.SemaphoreType.DMA((micro, 2 * xn - 1)),
            pltpu.SemaphoreType.DMA((parts - 1,)),
            pltpu.SemaphoreType.DMA((parts - 1,)),
        ] + BackGather.scratch(chunks),
        compiler_params=pltpu.CompilerParams(
            collective_id=collective_id, has_side_effects=True, vmem_limit_bytes=56 * 2**20
        ),
        cost_estimate=pl.CostEstimate(flops=6 * 10**9, bytes_accessed=40 * 2**20, transcendentals=0),
    )(x, dy.reshape(chunks, ROWS, width), routes.transpose(0, 2, 1), quota.reshape(1, -1), gains, head_gains, cos, sin, docs,
      dispatch.T, triple, merge)


def per_device(
    block_entry_states,
    document_labels,
    token_assignments,
    worker_quota_tallies,
    rescale_factors_both,
    triple_projection_matrix,
    probe_lookup_scalers,
    heads_merge_matrix,
    dispatcher_matrix,
    specialist_widen_matrix,
    specialist_shrink_matrix,
    output_gradient,
):
    micro, local_rows, width = block_entry_states.shape
    groups, parts = lax.axis_size("grp"), lax.axis_size("ep")
    major, minor, xs = mesh_sizes(groups, parts)
    group = lax.axis_index("grp")
    part = lax.axis_index("ep")
    seq_len = document_labels.shape[1]
    experts = dispatcher_matrix.shape[1]
    local_exp = specialist_widen_matrix.shape[0]
    inner = specialist_shrink_matrix.shape[1]
    share = inner // groups
    local_width = triple_projection_matrix.shape[2]
    heads = local_width // HD
    scale = 1.0 / math.sqrt(HD)
    gains = rescale_factors_both.astype(F32)
    cos, signed_sin = rope_tables(seq_len, HD)
    triple = triple_projection_matrix.transpose(1, 0, 2)
    gathered, queries, keys, values, mixed, weights, qk_hat, qk_inv, hidden, ffn_ext, probs, dy_all = attention_forward(
        block_entry_states, output_gradient, token_assignments, worker_quota_tallies, rescale_factors_both,
        probe_lookup_scalers, cos, signed_sin,
        document_labels, dispatcher_matrix, triple, heads_merge_matrix, 0)
    ffn_in = ffn_ext[..., :width]

    fused = xs == minor and share % 128 == 0 and local_exp % 2 == 0 and 2 * xs * minor * major * ROWS <= 512
    chunk_shape = (micro * local_rows // ROWS, 2, xs, minor, major, ROWS)
    if fused:
        dx_sum, moe_part, grad_widen, grad_shrink = experts_together(
            ffn_ext, dy_all, specialist_widen_matrix, specialist_shrink_matrix, experts, 1)
    else:
        dx_sum, moe_part, grad_widen, grad_shrink = experts_apart(
            ffn_ext, dy_all, specialist_widen_matrix, specialist_shrink_matrix, experts)
    dx_sum = dx_sum.astype(F32).reshape(micro, local_rows, width + 128)
    grad_widen = grad_widen.reshape(groups, width // groups, -1)

    inv_second = lax.rsqrt(jnp.mean(hidden * hidden, axis=-1, keepdims=True) + EPS)
    hat_second = hidden * inv_second
    probs, keep = probs[..., :experts], probs[..., experts: 2 * experts]
    d_probs = dx_sum[..., width: width + experts] * keep
    d_logits = probs * (d_probs - jnp.sum(probs * d_probs, axis=-1, keepdims=True))
    d_ffn = dx_sum[..., :width] + jnp.einsum("mte,de->mtd", d_logits, dispatcher_matrix.astype(F32), precision=HIGH)
    grad_router = jnp.einsum("mtd,mte->ed", ffn_in.astype(F32), d_logits, precision=HIGH)
    scaled = d_ffn * gains[1]
    adjoint = output_gradient.astype(F32)
    d_hidden = adjoint + inv_second * (scaled - hat_second * jnp.mean(scaled * hat_second, axis=-1, keepdims=True))
    grad_second = jnp.sum(d_ffn * hat_second, axis=(0, 1))

    d_proj, d_attn_in, grad_heads, grad_out, grad_widen, moe = attention_back(
        d_hidden.astype(BF), heads_merge_matrix, triple, queries, keys, values, mixed, weights,
        qk_hat, qk_inv, probe_lookup_scalers, cos, signed_sin, grad_widen,
        moe_part if fused else None, 5)
    if not fused:
        moe = scatter_all(moe_part.reshape(chunk_shape + (width,)), 3)
    output = (hidden + moe.astype(F32).reshape(micro, local_rows, width)).astype(BF)
    skip = block_entry_states.astype(F32)
    inv_first = lax.rsqrt(jnp.mean(skip * skip, axis=-1, keepdims=True) + EPS)
    hat_first = skip * inv_first
    scaled = d_attn_in * gains[0]
    grad_input = d_hidden + inv_first * (scaled - hat_first * jnp.mean(scaled * hat_first, axis=-1, keepdims=True))
    grad_first = jnp.sum(d_attn_in * hat_first, axis=(0, 1))

    shared = jnp.concatenate([grad_first[None], grad_second[None], grad_router]).reshape(-1).astype(BF)
    own = grad_heads[:2].reshape(-1).astype(BF)
    gap, size = shared.shape[0], shared.shape[0] + own.shape[0]
    block = (groups, ROWS, -(-size // (groups * ROWS * 128)) * 128)
    room = math.prod(block)
    shared = jnp.pad(shared, (0, room - gap)).reshape(block)
    own = jnp.pad(own, (gap, room - size)).reshape(block)
    out_sum, qkv_sum, misc_sum = total_over_groups(
        gathered.reshape(-1, width), d_proj, grad_out, shared, own, 4)
    qkv_sum, out_sum, grad_widen, grad_shrink = finish(
        qkv_sum.reshape(-1, local_width), out_sum.reshape(-1, width), grad_widen, grad_shrink, local_exp, share)
    qkv_sum = qkv_sum.reshape(3, width, local_width).transpose(1, 0, 2)
    grad_shrink = grad_shrink.reshape(local_exp, share, width)
    misc_sum = misc_sum.reshape(-1)[:size].astype(F32)
    rows = misc_sum[: (2 + experts) * width].reshape(2 + experts, width)
    return (
        output,
        grad_input,
        rows[:2],
        qkv_sum,
        misc_sum[(2 + experts) * width:].reshape(2, local_width),
        out_sum,
        rows[2:].T,
        grad_widen,
        grad_shrink,
    )


def solution(mesh):
    return jax.shard_map(
        per_device,
        mesh=mesh,
        in_specs=(
            P(None, ALL, None),
            P(None, "grp"),
            P(None, ALL, None),
            P(),
            P(),
            P(None, None, "ep"),
            P(None, "ep"),
            P("ep", None),
            P(),
            P("ep", None, None),
            P("ep", None, None),
            P(None, ALL, None),
        ),
        out_specs=(
            P(None, ALL, None),
            P(None, ALL, None),
            P(),
            P(None, None, "ep"),
            P(None, "ep"),
            P("ep", None),
            P(),
            P("ep", "grp", None),
            P("ep", "grp", None),
        ),
        check_vma=False,
    )
```

```python
import functools
import math

import jax
import jax.numpy as jnp
import numpy as np
from jax import lax
from jax.experimental import pallas as pl
from jax.experimental.pallas import tpu as pltpu
from jax.sharding import PartitionSpec as P

HD = 128
TOP = 8
EPS = 1e-05
THETA = 10000.0
NEG = -1e30
HIGH = lax.Precision.HIGHEST
ALL = ("grp", "ep")
MESH = pl.DeviceIdType.MESH
ROWS = 16
BF = jnp.bfloat16
F32 = jnp.float32


def rope_tables(length, head_dim):
    half = head_dim // 2
    angle = np.arange(length)[:, None] * THETA ** (-np.arange(half) * 2.0 / head_dim)
    cos, sin = np.cos(angle), np.sin(angle)
    return np.concatenate([cos, cos], 1).astype(np.float32), np.concatenate([-sin, sin], 1).astype(np.float32)


def mesh_sizes(groups, parts):
    major = 4 if groups % 4 == 0 else groups
    return major, groups // major, parts // 2


class Line:
    def __init__(self, size, place, step):
        self.size, self.place, self.step = size, place, step

    def at(self, hops):
        return (
            lax.axis_index("grp") + hops * self.step[0],
            lax.axis_index("ep") + hops * self.step[1],
        )


def lines(groups, parts):
    major, minor, xs = mesh_sizes(groups, parts)
    g, e = lax.axis_index("grp"), lax.axis_index("ep")
    core = lax.rem(e, 2)
    x_pos, minor_pos = lax.div(e, 2), lax.rem(g, minor)
    if xs == minor:
        first = Line(xs, jnp.where(core == 0, x_pos, minor_pos), (core, 2 - 2 * core))
        second = Line(xs, jnp.where(core == 0, minor_pos, x_pos), (1 - core, 2 * core))
    else:
        first = Line(xs, x_pos, (0, 2))
        second = Line(minor, minor_pos, (1, 0))
    return Line(2, core, (0, 1)), first, Line(major, lax.div(g, minor), (minor, 0)), second


def greet(some, whole=()):
    barrier = pltpu.get_barrier_semaphore()
    peers = sum(line.size - 1 for line in whole)
    for line in whole:
        for j in range(1, line.size):
            to = lax.rem(line.place + j, line.size)
            pl.semaphore_signal(barrier, inc=1, device_id=line.at(to - line.place), device_id_type=MESH)
    for line in some:
        if line.size == 2:
            pl.semaphore_signal(barrier, inc=1, device_id=line.at(1 - 2 * line.place), device_id_type=MESH)
            peers = peers + 1
        else:
            for way, there in ((1, line.place < line.size - 1), (-1, line.place > 0)):

                @pl.when(there)
                def _(line=line, way=way):
                    pl.semaphore_signal(barrier, inc=1, device_id=line.at(way), device_id_type=MESH)

                peers = peers + there.astype(jnp.int32)
    pl.semaphore_wait(barrier, peers)


def greet_lines(some):
    barrier = pltpu.get_barrier_semaphore()
    for line in some:
        for j in range(1, line.size):
            to = lax.rem(line.place + j, line.size)
            pl.semaphore_signal(barrier, inc=1, device_id=line.at(to - line.place), device_id_type=MESH)
    pl.semaphore_wait(barrier, sum(line.size - 1 for line in some))


def remote(src, dst, send, recv, target):
    return pltpu.make_async_remote_copy(
        src_ref=src, dst_ref=dst, send_sem=send, recv_sem=recv, device_id=target, device_id_type=MESH
    )


class Hop:
    def __init__(self, legs, after=None):
        self.legs, self.after = legs, after

    def _each(self, which, act):
        for leg in self.legs:
            if leg[which] is None:
                act(leg)
            else:
                pl.when(leg[which])(functools.partial(act, leg))

    def start(self):
        self._each(0, lambda leg: leg[2]().start())

    def arrive(self):
        def act(leg):
            leg[3]().wait_recv()
            if leg[4] is not None:
                leg[4]()

        self._each(1, act)

    def sent(self):
        self._each(0, lambda leg: leg[2]().wait_send())

    def finish(self):
        self.arrive()
        self.sent()


def spread_hops(core, first, third, fourth, at, own, send, recv):
    c, p, z, q = core.place, first.place, third.place, fourth.place
    r4 = ROWS
    r3 = r4 * fourth.size
    r2 = r3 * third.size
    rc = r2 * first.size
    base = [0]

    def sems(n):
        b = base[0]
        base[0] += n
        return (lambda i: send(b + i)), (lambda i: recv(b + i))

    def swap(line, place, first_source=None):
        source = first_source or (lambda i: place(line.place))
        return Swap(line, source, lambda j, i: place(i), *sems(line.size - 1))

    hops = [swap(fourth, lambda i: at(c * rc + p * r2 + z * r3 + i * r4, r4), lambda i: own)]
    hops += gather_hops(third, lambda i: at(c * rc + p * r2 + i * r3, r3), *sems(leg_count(third.size)))
    hops.append(swap(first, lambda i: at(c * rc + i * r2, r2)))
    hops.append(swap(core, lambda i: at(i * rc, rc)))
    return hops


def gather_hops(line, at, send, recv, own=None):
    n, a = line.size, line.place
    if n == 2:
        mine, theirs, peer = at(a), at(1 - a), line.at(1 - 2 * a)
        return [
            Hop([(None, None, lambda: remote(mine if own is None else own, mine, send(0), recv(0), peer),
                  lambda: remote(theirs, theirs, send(0), recv(0), peer), None)])
        ]
    hops = []
    for s in range(1, n):
        legs = []
        for d, way in enumerate((1, -1)):
            k = (s - 1) * 2 + d
            out = a - way * (s - 1)
            into = a - way * s
            sends = (out >= 0) & (out < n) & (a + way >= 0) & (a + way < n)
            gets = (into >= 0) & (into < n)
            out, into = jnp.clip(out, 0, n - 1), jnp.clip(into, 0, n - 1)
            legs.append((
                sends, gets,
                lambda out=out, way=way, k=k, s=s: remote(
                    own if s == 1 and own is not None else at(out), at(out), send(k), recv(k), line.at(way)),
                lambda into=into, way=way, k=k: remote(at(into), at(into), send(k), recv(k), line.at(-way)),
                None,
            ))
        hops.append(Hop(legs))
    return hops


def reduce_hops(line, acc, land, add, send, recv):
    n, a = line.size, line.place
    if n == 2:
        peer = line.at(1 - 2 * a)
        return [
            Hop([(None, None, lambda: remote(acc(1 - a), land(0), send(0), recv(0), peer),
                  lambda: remote(land(0), land(0), send(0), recv(0), peer),
                  lambda: add(acc(a), land(0)))])
        ]
    hops = []
    for s in range(n - 1):
        legs = []
        for d, way in enumerate((1, -1)):
            k = s * 2 + d
            b = a if way == 1 else n - 1 - a
            sends = (b <= s) & (b < n - 1)
            gets = (b - 1 <= s) & (b >= 1)
            out = b + n - 1 - s
            into = b + n - 2 - s
            out, into = jnp.clip(out, 0, n - 1), jnp.clip(into, 0, n - 1)
            if way == -1:
                out, into = n - 1 - out, n - 1 - into
            legs.append((
                sends, gets,
                lambda out=out, way=way, k=k: remote(acc(out), land(k), send(k), recv(k), line.at(way)),
                lambda way=way, k=k: remote(land(k), land(k), send(k), recv(k), line.at(-way)),
                lambda into=into, k=k: add(acc(into), land(k)),
            ))
        hops.append(Hop(legs))
    return hops


def hop_count(n):
    return 1 if n == 2 else n - 1


def leg_count(n):
    return 1 if n == 2 else 2 * (n - 1)


def flow(chains, pace=1):
    depth, count = max(len(c) for c in chains), len(chains)
    for t in range(count + pace * depth):
        for k in range(count):
            i, rest = divmod(t - k, pace)
            if rest:
                continue
            if 1 <= i <= len(chains[k]):
                chains[k][i - 1].arrive()
            if 0 <= i < len(chains[k]):
                chains[k][i].start()
    for chain in chains:
        for hop in chain:
            hop.sent()


def add(acc, land):
    lead = acc.shape[:-2]

    def one(i):
        where = []
        for size in reversed(lead):
            where.insert(0, lax.rem(i, size))
            i = lax.div(i, size)
        where = tuple(where) + (slice(None), slice(None))
        acc[where] = (acc[where].astype(F32) + land[where].astype(F32)).astype(acc.dtype)

    if lead:
        pl.loop(0, math.prod(lead))(one)
    else:
        one(0)


def gather_kernel(groups, parts, x, out, local, send, recv):
    core, first, second, long = lines(groups, parts)
    c, p, q, z = core.place, first.place, second.place, long.place
    greet([core, first, second, long])
    chunks = x.shape[0]
    own = [pltpu.make_async_copy(x.at[k], out.at[k, c, p, q, z], local.at[k]) for k in range(chunks)]
    for copy in own:
        copy.start()
    chains = []
    for k in range(chunks):
        base = [0]

        def sems(n, k=k, base=base):
            b = base[0]
            base[0] += leg_count(n)
            return (lambda i: send.at[k, b + i]), (lambda i: recv.at[k, b + i])

        chain = []
        chain += gather_hops(long, lambda i, k=k: out.at[k, c, p, q, i], *sems(long.size))
        chain += gather_hops(second, lambda i, k=k: out.at[k, c, p, i], *sems(second.size))
        chain += gather_hops(first, lambda i, k=k: out.at[k, c, i], *sems(first.size))
        chain += gather_hops(core, lambda i, k=k: out.at[k, i], *sems(2))
        chains.append(chain)
    for copy in own:
        copy.wait()
    flow(chains)


def gather_all(x, collective_id):
    groups, parts = lax.axis_size("grp"), lax.axis_size("ep")
    major, minor, xs = mesh_sizes(groups, parts)
    width = x.shape[-1]
    x = x.reshape(-1, ROWS, width)
    legs = sum(leg_count(n) for n in (2, xs, minor, major))
    chunks = x.shape[0]
    return pl.pallas_call(
        functools.partial(gather_kernel, groups, parts),
        out_shape=jax.ShapeDtypeStruct((chunks, 2, xs, major, minor, ROWS, width), x.dtype),
        in_specs=[pl.BlockSpec(memory_space=pl.ANY)],
        out_specs=pl.BlockSpec(memory_space=pl.ANY),
        scratch_shapes=[
            pltpu.SemaphoreType.DMA((chunks,)),
            pltpu.SemaphoreType.DMA((chunks, legs)),
            pltpu.SemaphoreType.DMA((chunks, legs)),
        ],
        compiler_params=pltpu.CompilerParams(collective_id=collective_id, has_side_effects=True),
    )(x)


def scatter_kernel(groups, parts, part, out, acc, land_c, land_p, land_q, land_z, local, send, recv):
    core, first, second, long = lines(groups, parts)
    c, p, q, z = core.place, first.place, second.place, long.place
    chunks = part.shape[0]
    own = [pltpu.make_async_copy(part.at[k, c], acc.at[k], local.at[k]) for k in range(chunks)]
    for copy in own:
        copy.start()
    greet([core, first, second, long])
    chains = []
    for k in range(chunks):
        base = [0]

        def sems(n, k=k, base=base):
            b = base[0]
            base[0] += leg_count(n)
            return (lambda i: send.at[k, b + i]), (lambda i: recv.at[k, b + i])

        def add_own(acc_ref, land_ref, k=k):
            own[k].wait()
            add(acc_ref, land_ref)

        s, r = sems(2)
        peer = core.at(1 - 2 * c)
        other = part.at[k, 1 - c]
        chain = [Hop([(
            None, None,
            lambda other=other, s=s, r=r, k=k: remote(other, land_c.at[k], s(0), r(0), peer),
            lambda s=s, r=r, k=k: remote(land_c.at[k], land_c.at[k], s(0), r(0), peer),
            lambda k=k, add_own=add_own: add_own(acc.at[k], land_c.at[k]),
        )])]
        chain += reduce_hops(first, lambda i, k=k: acc.at[k, i], lambda i, k=k: land_p.at[k, i], add, *sems(first.size))
        chain += reduce_hops(second, lambda i, k=k: acc.at[k, p, i], lambda i, k=k: land_q.at[k, i], add, *sems(second.size))
        chain += reduce_hops(long, lambda i, k=k: acc.at[k, p, q, i], lambda i, k=k: land_z.at[k, i], add, *sems(long.size))
        chains.append(chain)
    flow(chains)
    for k in range(chunks):
        out[k] = acc[k, p, q, z]


def scatter_all(part, collective_id):
    groups, parts = lax.axis_size("grp"), lax.axis_size("ep")
    major, minor, xs = mesh_sizes(groups, parts)
    legs = sum(leg_count(n) for n in (2, xs, minor, major))
    chunks, width = part.shape[0], part.shape[-1]
    unit = 2 * ROWS * width
    need = unit * (2 * xs * minor * major + leg_count(xs) * minor * major + leg_count(major) * minor + leg_count(minor) + 2)
    per = chunks
    while per > 1 and per * need > 44 * 2**20:
        per //= 2
    call = pl.pallas_call(
        functools.partial(scatter_kernel, groups, parts),
        out_shape=jax.ShapeDtypeStruct((per, ROWS, width), BF),
        in_specs=[pl.BlockSpec(memory_space=pl.ANY)],
        out_specs=pl.BlockSpec(memory_space=pltpu.VMEM),
        scratch_shapes=[
            pltpu.VMEM((per, xs, major, minor, ROWS, width), BF),
            pltpu.VMEM((per, xs, major, minor, ROWS, width), BF),
            pltpu.VMEM((per, leg_count(xs), major, minor, ROWS, width), BF),
            pltpu.VMEM((per, leg_count(major), minor, ROWS, width), BF),
            pltpu.VMEM((per, leg_count(minor), ROWS, width), BF),
            pltpu.SemaphoreType.DMA((per,)),
            pltpu.SemaphoreType.DMA((per, legs)),
            pltpu.SemaphoreType.DMA((per, legs)),
        ],
        compiler_params=pltpu.CompilerParams(
            collective_id=collective_id, has_side_effects=True, vmem_limit_bytes=56 * 2**20
        ),
    )
    return jnp.concatenate([call(part[i:i + per]) for i in range(0, chunks, per)]) if per < chunks else call(part)


class Begun:
    def __init__(self, hop, before):
        self.hop, self.before = hop, before

    def start(self):
        self.before()
        self.hop.start()

    def arrive(self):
        self.hop.arrive()

    def sent(self):
        self.hop.sent()


def total_kernel(groups, parts, plan, rows_in, d_proj, grad_out, shared, own, *refs):
    count = 3
    outs, acc, land = (refs[i * count: (i + 1) * count] for i in range(3))
    rows_v, proj_v, shared_v, own_v, got, local, stored, send, recv, t_send, t_recv = refs[3 * count:]
    major, minor, _ = mesh_sizes(groups, parts)
    g, e = lax.axis_index("grp"), lax.axis_index("ep")
    short = Line(minor, lax.rem(g, minor), (1, 0))
    long = Line(major, lax.div(g, minor), (minor, 0))
    whole = Line(parts, e, (0, 1))
    width = rows_in.shape[1]
    load = [pltpu.make_async_copy(a, b, local.at[i]) for i, (a, b) in enumerate((
        (grad_out, acc[0]), (rows_in, rows_v), (d_proj, proj_v), (shared, shared_v), (own, own_v)))]
    for copy in load:
        copy.start()

    def weights(k):
        def act():
            if k == 0:
                load[1].wait()
                load[2].wait()
            cuts = acc[1].shape[0] // 3
            c, cut = k // cuts, k % cuts
            blocks = max(1, 256 // acc[1].shape[2])
            rows = blocks * acc[1].shape[2]

            @pl.loop(0, groups // blocks)
            def _(i):
                cols = pl.ds(pl.multiple_of(cut * (width // cuts) + i * rows, 128), rows)
                total = lax.dot_general(rows_v[:, cols], proj_v[c], (((0,), (0,)), ((), ())), preferred_element_type=F32)
                acc[1][k, pl.ds(i * blocks, blocks)] = total.astype(BF).reshape((blocks,) + acc[1].shape[2:])

        return act

    swap = swap_legs(whole, lambda i: shared_v, lambda j, i: got.at[j], lambda j: t_send.at[j], lambda j: t_recv.at[j])

    def everyone():
        end_legs(swap)
        load[4].wait()

        @pl.loop(0, groups)
        def _(i):
            total = shared_v[i].astype(F32) + own_v[i].astype(F32)
            for j in range(parts - 1):
                total = total + got[j, i].astype(F32)
            acc[2][0, i] = total.astype(BF)

    before = {(0, 0): load[0].wait, (2, 0): everyone}
    chains = []
    for number, (j, k, far) in enumerate(plan):
        one, two = (long, short) if far else (short, long)
        y, z = one.place, two.place
        n = two.size

        def level_one(ref, k, n=n):
            return lambda i: ref.at[k, pl.ds(i * n, n)]

        def level_two(ref, k, y=y, n=n):
            return lambda i: ref.at[k, y * n + i]

        store = pltpu.make_async_copy(acc[j].at[k, y * n + z], outs[j].at[k, y * n + z], stored.at[number])
        base = [0]

        def sems(size, number=number, base=base):
            b = base[0]
            base[0] += leg_count(size)
            return (lambda i: send.at[number, b + i]), (lambda i: recv.at[number, b + i])

        first_land = leg_count(one.size) * n
        down = reduce_hops(one, level_one(acc[j], k), lambda i, j=j, k=k, n=n: land[j].at[k, pl.ds(i * n, n)], add, *sems(one.size))
        down += reduce_hops(two, level_two(acc[j], k), lambda i, j=j, k=k, f=first_land: land[j].at[k, f + i], add, *sems(two.size))
        up = gather_hops(two, level_two(outs[j], k), *sems(two.size), own=acc[j].at[k, y * n + z])
        turn = len(up)
        up += gather_hops(one, level_one(outs[j], k), *sems(one.size))

        down[0] = Begun(down[0], before.get((j, k)) or (weights(k) if j == 1 else lambda: None))
        up[0] = Begun(up[0], store.start)
        up[turn] = Begun(up[turn], store.wait)
        chains.append(down + up)
    greet([short, long], [whole])
    load[3].wait()
    start_legs(swap)
    flow(chains, 2)


def total_over_groups(gathered, d_proj, grad_out, shared, own, collective_id):
    groups, parts = lax.axis_size("grp"), lax.axis_size("ep")
    major, minor, _ = mesh_sizes(groups, parts)
    tokens, width = gathered.shape
    local_width = d_proj.shape[2]
    few = max(n for n in (4, 2, 1) if n == 1 or grad_out.shape[0] % (n * groups * ROWS) == 0)
    many = max(n for n in (12, 6, 3) if n == 3 or 3 * width % (n * groups * ROWS) == 0)
    shapes = [
        (few, groups, grad_out.shape[0] // few // groups, width),
        (many, groups, 3 * width // many // groups, local_width),
        (1,) + shared.shape,
    ]
    plan = [(0, k, k % 4 == 1) for k in range(few)] + [(1, k, k % 4 == 1) for k in range(many)] + [(2, 0, False)]
    blocks = max(leg_count(a) * b + leg_count(b) for a, b in ((minor, major), (major, minor)))
    legs = 2 * (leg_count(minor) + leg_count(major))
    total = len(plan)
    hbm = pl.BlockSpec(memory_space=pl.ANY)
    scratch = [pltpu.VMEM(a, BF) for a in shapes]
    scratch += [pltpu.VMEM((a[0], blocks) + a[2:], BF) for a in shapes]
    return pl.pallas_call(
        functools.partial(total_kernel, groups, parts, plan),
        out_shape=[jax.ShapeDtypeStruct(a, BF) for a in shapes],
        in_specs=[hbm] * 5,
        out_specs=[hbm] * len(shapes),
        scratch_shapes=scratch + [
            pltpu.VMEM(gathered.shape, BF),
            pltpu.VMEM(d_proj.shape, BF),
            pltpu.VMEM(shared.shape, BF),
            pltpu.VMEM(shared.shape, BF),
            pltpu.VMEM((parts - 1,) + shared.shape, BF),
            pltpu.SemaphoreType.DMA((5,)),
            pltpu.SemaphoreType.DMA((total,)),
            pltpu.SemaphoreType.DMA((total, legs)),
            pltpu.SemaphoreType.DMA((total, legs)),
            pltpu.SemaphoreType.DMA((parts - 1,)),
            pltpu.SemaphoreType.DMA((parts - 1,)),
        ],
        compiler_params=pltpu.CompilerParams(
            collective_id=collective_id, has_side_effects=True, vmem_limit_bytes=48 * 2**20
        ),
        cost_estimate=pl.CostEstimate(flops=6 * tokens * width * local_width, bytes_accessed=40 * 2**20, transcendentals=0),
    )(gathered, d_proj, grad_out.reshape(shapes[0]), shared, own)


def swap_legs(line, source, target, send, recv):
    n, a = line.size, line.place
    legs = []
    for j in range(1, n):
        to, off = lax.rem(a + j, n), lax.rem(a + n - j, n)
        legs.append((
            lambda to=to, j=j: remote(source(to), target(j - 1, a), send(j - 1), recv(j - 1), line.at(to - a)),
            lambda off=off, j=j: remote(target(j - 1, off), target(j - 1, off), send(j - 1), recv(j - 1), line.at(off - a)),
        ))
    return legs


def start_legs(legs):
    for out, _ in legs:
        out().start()


def end_legs(legs):
    for out, into in legs:
        into().wait_recv()
    for out, into in legs:
        out().wait_send()


class Swap:
    def __init__(self, *how):
        self.legs = swap_legs(*how)

    def start(self):
        start_legs(self.legs)

    def finish(self):
        end_legs(self.legs)


def add_rows(acc, first, land, rows):
    @pl.loop(0, rows // ROWS)
    def _(i):
        here = pl.ds(pl.multiple_of(first + i * ROWS, ROWS), ROWS)
        there = pl.ds(pl.multiple_of(i * ROWS, ROWS), ROWS)
        acc[here, :] = (acc[here, :].astype(F32) + land[there, :].astype(F32)).astype(acc.dtype)


def experts_kernel(
    groups, parts, local_rows, acc_ring, experts,
    x, dy, widen, shrink,
    summed, moe, grad_widen, grad_shrink,
    xs, dys, wide, down, sum_wide, sum_down, stage, acc, other, land_c, land_p, land_q, land_z,
    hid, raw, gated, d_gu, gate, product, marks,
    load, dy_sem, stage_sem, g_send, g_recv, s_send, s_recv,
):
    core, first, third, fourth = lines(groups, parts)
    c, p, z, q = core.place, first.place, third.place, fourth.place
    pn, zn, qn = first.size, third.size, fourth.size
    chunks, width = x.shape[0], shrink.shape[2]
    local_exp, inner = shrink.shape[0], shrink.shape[1]
    share = inner // groups
    group, part = lax.axis_index("grp"), lax.axis_index("ep")
    rq, rz, rp, rc = ROWS, ROWS * qn, ROWS * qn * zn, ROWS * qn * zn * pn
    rows = 2 * rc
    levels = 3 + hop_count(zn)
    cuts = local_rows // ROWS
    base = part * local_exp
    pairs = local_exp // 2

    loads = []
    for e in range(local_exp):
        for half in range(2):
            to = (e // 2) * 4 * share + half * 2 * share + (e % 2) * share
            loads.append(pltpu.make_async_copy(
                widen.at[e, :, pl.ds(pl.multiple_of(half * inner + group * share, share), share)],
                wide.at[:, pl.ds(to, share)], load.at[2 * e + half]))
        loads.append(pltpu.make_async_copy(
            shrink.at[e, pl.ds(pl.multiple_of(group * share, share), share), :],
            down.at[pl.ds(e * share, share), :], load.at[2 * local_exp + e]))
    for copy in loads:
        copy.start()

    def dy_copy(k):
        return pltpu.make_async_copy(dy.at[k], dys.at[lax.rem(k, 2)], dy_sem.at[lax.rem(k, 2)])

    dy_start = lambda k: dy_copy(k).start()
    dy_start(0)
    greet_lines([core, first, third, fourth])

    def rows_at(start, size):
        return pl.ds(pl.multiple_of(start, ROWS), size)

    def g_hop(k, level):
        buf = xs.at[k]
        return spread_hops(core, first, third, fourth, lambda start, size: buf.at[rows_at(start, size), :], x.at[k],
                           lambda i: g_send.at[k, i], lambda i: g_recv.at[k, i])[level]

    def s_line(k, line, at, land, offset):
        return Swap(line, at, lambda j, i: land.at[lax.rem(k, 2), j],
                    lambda j: s_send.at[k, offset + j], lambda j: s_recv.at[k, offset + j])

    def mine(k):
        return acc.at[lax.rem(k, acc_ring)]

    def s_hop(k, level):
        if level == 0:
            return s_line(k, core, lambda i: other, land_c, 0)
        if level == 1:
            return s_line(k, first, lambda i: mine(k).at[i], land_p, 1)
        if level == 2:
            return s_line(k, fourth, lambda i: mine(k).at[p, :, i], land_q, pn)
        return s_line(k, third, lambda i: mine(k).at[p, i, q], land_z, pn + qn - 1)

    def s_end(k, level):
        s_hop(k, level).finish()
        slot = lax.rem(k, 2)
        if level == 3:
            total = mine(k)[p, z, q].astype(F32)
            for j in range(zn - 1):
                total = total + land_z[slot, j].astype(F32)
            summed[k] = total.astype(BF)
            return
        if level == 0 and pn == 2:
            add(mine(k).at[1 - p], land_c.at[slot, 0, 1 - p])
            s_hop(k, 1).start()
            add(mine(k).at[p], land_c.at[slot, 0, p])
            return
        to = (mine(k), mine(k).at[p], mine(k).at[p, :, q])[level]
        land = (land_c, land_p, land_q)[level]
        for j in range(land.shape[1]):
            add(to, land.at[slot, j])
        s_hop(k, level + 1).start()

    def after(t, lag, act):
        k = t - lag

        @pl.when((k >= 0) & (k < chunks))
        def _():
            act(k)

    tiles = width // 512

    def compute(k):
        buf, dyk = xs.at[k], dys.at[lax.rem(k, 2)]

        @pl.when(k == 0)
        def _():
            for copy in loads:
                copy.wait()

        dy_copy(k).wait()

        @pl.when(k + 1 < chunks)
        def _():
            dy_start(k + 1)

        @pl.loop(0, pairs)
        def _(j):
            cols = pl.ds(pl.multiple_of(j * 4 * share, 4 * share), 4 * share)
            some = pl.ds(pl.multiple_of(j * 2 * share, 2 * share), 2 * share)
            to_up = pl.ds(pl.multiple_of(j * 4 * share + 2 * share, share), 2 * share)
            to_gate = pl.ds(pl.multiple_of(j * 4 * share, share), 2 * share)
            hid[...] = jnp.dot(buf[:, :width], wide[:, cols], preferred_element_type=F32)
            raw[...] = lax.dot_general(dyk[...], down[some, :], (((1,), (1,)), ((), ())), preferred_element_type=F32)
            gate[...] = jnp.dot(buf[:, width:], marks[:, some], preferred_element_type=F32)

            @pl.loop(0, rows // 32)
            def _(i):
                here = pl.ds(pl.multiple_of(i * 32, 32), 32)
                g, u = hid[here, : 2 * share], hid[here, 2 * share:]
                d, weight = raw[here, :], gate[here, :]
                sigma = 0.5 * jnp.tanh(0.5 * g) + 0.5
                swish = g * sigma
                act = swish * u
                product[here, some] = (act * d).astype(BF)
                gated[here, some] = (act * weight).astype(BF)
                d = d * weight
                d_gu[here, to_gate] = (d * u * (sigma + swish * (1.0 - sigma))).astype(BF)
                d_gu[here, to_up] = (d * swish).astype(BF)

        kept = mine(k)

        def split(cols, total):
            total = total.astype(BF).reshape((2,) + other.shape[:-1] + total.shape[1:])

            @pl.when(c == 0)
            def _():
                kept[..., cols] = total[0]
                other[..., cols] = total[1]

            @pl.when(c == 1)
            def _():
                other[..., cols] = total[0]
                kept[..., cols] = total[1]

        @pl.loop(0, tiles)
        def _(n):
            cols = pl.ds(pl.multiple_of(n * 512, 512), 512)
            split(cols, lax.dot_general(
                d_gu[...], wide[cols, :], (((1,), (1,)), ((), ())), preferred_element_type=F32))

        split(pl.ds(width, 128), lax.dot_general(
            product[...], marks[...], (((1,), (1,)), ((), ())), preferred_element_type=F32))
        s_hop(k, 0).start()

        @pl.when(k >= 1)
        def _():
            pltpu.make_async_copy(stage, moe.at[k - 1], stage_sem.at[0]).wait()

        @pl.loop(0, tiles)
        def _(n):
            cols = pl.ds(pl.multiple_of(n * 512, 512), 512)
            stage[:, cols] = jnp.dot(gated[...], down[:, cols], preferred_element_type=F32).astype(BF)
            sum_wide[cols, :] += lax.dot_general(
                buf[:, cols], d_gu[...], (((0,), (0,)), ((), ())), preferred_element_type=F32)
            sum_down[:, cols] += lax.dot_general(
                gated[...], dyk[:, cols], (((0,), (0,)), ((), ())), preferred_element_type=F32)

        pltpu.make_async_copy(stage, moe.at[k], stage_sem.at[0]).start()

    def begin(k):
        xs[k, rows_at(c * rc + p * rp + z * rz + q * rq, rq), :] = x[k]
        g_hop(k, 0).start()

        @pl.when(k == 0)
        def _():
            sum_wide[...] = jnp.zeros_like(sum_wide)
            sum_down[...] = jnp.zeros_like(sum_down)
            lanes = lax.broadcasted_iota(jnp.int32, marks.shape, 0)
            owner = base + lax.div(lax.broadcasted_iota(jnp.int32, marks.shape, 1), share)
            marks[...] = jnp.where((lanes == owner) | (lanes == owner + experts), 1.0, 0.0).astype(BF)

    def g_end(k, level):
        g_hop(k, level).finish()
        if level + 1 < levels:
            g_hop(k, level + 1).start()

    def wide_out(i):
        here = pl.ds(pl.multiple_of(i * rows, rows), rows)
        return pltpu.make_async_copy(d_gu, grad_widen.at[here, :], load.at[1])

    out_down = pltpu.make_async_copy(sum_down, grad_shrink, load.at[0])

    def store(i):
        @pl.when(i == 0)
        def _():
            out_down.start()

        @pl.when(i > 0)
        def _():
            wide_out(i - 1).wait()

        d_gu[...] = sum_wide[pl.ds(pl.multiple_of(i * rows, rows), rows), :].astype(BF)
        wide_out(i).start()

    @pl.loop(0, chunks + levels + 4)
    def _(t):
        for level in reversed(range(levels)):
            after(t, level + 1, functools.partial(g_end, level=level))
        after(t, 0, begin)
        for level in reversed(range(4)):
            after(t, levels + level + 1, functools.partial(s_end, level=level))
        after(t, levels, compute)

        @pl.when((t >= chunks + levels) & (t < chunks + levels + min(4, width // rows)))
        def _():
            store(t - chunks - levels)

    for i in range(4, width // rows):
        store(i)
    pltpu.make_async_copy(stage, moe.at[chunks - 1], stage_sem.at[0]).wait()
    wide_out(width // rows - 1).wait()
    out_down.wait()


def experts_together(x, dy, widen, shrink, experts, collective_id):
    groups, parts = lax.axis_size("grp"), lax.axis_size("ep")
    major, minor, xn = mesh_sizes(groups, parts)
    micro, local_rows, wide = x.shape
    x = x.reshape(-1, ROWS, wide)
    chunks = x.shape[0]
    local_exp, inner, width = shrink.shape
    share = inner // groups
    hidden = local_exp * share
    rows = 2 * ROWS * major * minor * xn
    acc_ring = 4
    legs = minor + xn - 1 + leg_count(major)
    vmem = pl.BlockSpec(memory_space=pltpu.VMEM)
    hbm = pl.BlockSpec(memory_space=pl.ANY)
    flops = 2 * chunks * rows * width * hidden * 9
    return pl.pallas_call(
        functools.partial(experts_kernel, groups, parts, local_rows, acc_ring, experts),
        out_shape=[
            jax.ShapeDtypeStruct((chunks, ROWS, wide), BF),
            jax.ShapeDtypeStruct((chunks, rows, width), BF),
            jax.ShapeDtypeStruct((width, 2 * hidden), BF),
            jax.ShapeDtypeStruct((hidden, width), F32),
        ],
        in_specs=[vmem, hbm, hbm, hbm],
        out_specs=[vmem, hbm, hbm, hbm],
        scratch_shapes=[
            pltpu.VMEM((chunks, rows, wide), BF),
            pltpu.VMEM((2, rows, width), BF),
            pltpu.VMEM((width, 2 * hidden), BF),
            pltpu.VMEM((hidden, width), BF),
            pltpu.VMEM((width, 2 * hidden), F32),
            pltpu.VMEM((hidden, width), F32),
            pltpu.VMEM((rows, width), BF),
            pltpu.VMEM((acc_ring, xn, major, minor, ROWS, wide), BF),
            pltpu.VMEM((xn, major, minor, ROWS, wide), BF),
            pltpu.VMEM((2, 1, xn, major, minor, ROWS, wide), BF),
            pltpu.VMEM((2, xn - 1, major, minor, ROWS, wide), BF),
            pltpu.VMEM((2, minor - 1, major, ROWS, wide), BF),
            pltpu.VMEM((2, major - 1, ROWS, wide), BF),
            pltpu.VMEM((rows, 4 * share), F32),
            pltpu.VMEM((rows, 2 * share), F32),
            pltpu.VMEM((rows, hidden), BF),
            pltpu.VMEM((rows, 2 * hidden), BF),
            pltpu.VMEM((rows, 2 * share), F32),
            pltpu.VMEM((rows, hidden), BF),
            pltpu.VMEM((128, hidden), BF),
            pltpu.SemaphoreType.DMA((3 * local_exp,)),
            pltpu.SemaphoreType.DMA((2,)),
            pltpu.SemaphoreType.DMA((2,)),
            pltpu.SemaphoreType.DMA((chunks, legs)),
            pltpu.SemaphoreType.DMA((chunks, legs)),
            pltpu.SemaphoreType.DMA((chunks, legs)),
            pltpu.SemaphoreType.DMA((chunks, legs)),
        ],
        compiler_params=pltpu.CompilerParams(
            collective_id=collective_id, has_side_effects=True, vmem_limit_bytes=63 * 2**20
        ),
        cost_estimate=pl.CostEstimate(flops=flops, bytes_accessed=80 * 2**20, transcendentals=chunks * rows * hidden),
    )(x, dy, widen, shrink)


def experts_apart(x, dy_all, specialist_widen_matrix, specialist_shrink_matrix, experts):
    groups, parts = lax.axis_size("grp"), lax.axis_size("ep")
    group, part = lax.axis_index("grp"), lax.axis_index("ep")
    local_exp, inner, width = specialist_shrink_matrix.shape
    share = inner // groups
    widen = specialist_widen_matrix.reshape(local_exp, width, 2, groups, share)
    widen = lax.dynamic_index_in_dim(widen, group, 3, keepdims=False)
    widen = widen.transpose(1, 2, 0, 3).reshape(width, 2 * local_exp * share)
    shrink = specialist_shrink_matrix.reshape(local_exp, groups, share, width)
    shrink = lax.dynamic_index_in_dim(shrink, group, 1, keepdims=False).reshape(local_exp * share, width)
    x_all = gather_all(x, 1)
    chunk_shape = x_all.shape[:-1]
    x_all, dy_all = x_all.reshape(-1, width + 128), dy_all.reshape(-1, width)
    gate = x_all[:, width: width + experts].astype(F32) + x_all[:, width + experts: width + 2 * experts].astype(F32)
    x_all = x_all[:, :width]
    gate = lax.dynamic_slice_in_dim(gate, part * local_exp, local_exp, axis=1)
    gate = jnp.repeat(gate, share, axis=1)
    gate_up = jnp.dot(x_all, widen, preferred_element_type=F32)
    g, u = gate_up[:, : local_exp * share], gate_up[:, local_exp * share:]
    sigma = jax.nn.sigmoid(g)
    act = g * sigma * u
    gated = (gate * act).astype(BF)
    moe_part = jnp.dot(gated, shrink, preferred_element_type=F32).astype(BF)
    d_raw = lax.dot_general(dy_all, shrink, (((1,), (1,)), ((), ())), preferred_element_type=F32)
    d_gate = jnp.sum((act * d_raw).reshape(-1, local_exp, share), axis=-1)
    d_act = gate * d_raw
    d_gu = jnp.concatenate([d_act * u * sigma * (1.0 + g * (1.0 - sigma)), d_act * (g * sigma)], axis=1).astype(BF)
    dx_part = lax.dot_general(d_gu, widen, (((1,), (1,)), ((), ())), preferred_element_type=F32).astype(BF)
    lanes = jnp.arange(128, dtype=jnp.int32)
    place = (lanes[None, :] == part * local_exp + jnp.arange(local_exp, dtype=jnp.int32)[:, None])
    d_gate = jnp.sum(jnp.where(place[None], d_gate[:, :, None], 0.0), axis=1)
    dx_part = jnp.concatenate([dx_part, d_gate.astype(BF)], axis=1)
    dx_sum = scatter_all(dx_part.reshape(chunk_shape + (width + 128,)), 2)
    grad_widen = lax.dot_general(x_all, d_gu, (((0,), (0,)), ((), ())), preferred_element_type=F32)
    grad_shrink = lax.dot_general(gated, dy_all, (((0,), (0,)), ((), ())), preferred_element_type=F32)
    grad_widen = grad_widen.astype(BF).reshape(width, 2, local_exp // 2, 2, share).transpose(0, 2, 1, 3, 4)
    return dx_sum, moe_part.reshape(chunk_shape + (width,)), grad_widen, grad_shrink


def finish_kernel(share, qkv, out, wide, shrink, qkv_to, out_to, wide_to, shrink_to):
    qkv_to[...] = qkv[...].astype(F32)
    out_to[...] = out[...].astype(F32)
    shrink_to[...] = shrink[...]
    for i in range(wide.shape[0]):
        wide_to[0, :, i * share: (i + 1) * share] = wide[i].astype(F32)


def finish(qkv, out, wide, shrink, local_exp, share):
    groups, rows, _ = wide.shape
    whole = (local_exp, rows, 2 * groups * share)
    if share % 128:
        wide = wide.reshape(groups, rows, local_exp // 2, 2, 2, share).transpose(2, 4, 1, 3, 0, 5)
        return qkv.astype(F32), out.astype(F32), wide.reshape(whole).astype(F32), shrink
    steps = 2 * local_exp
    cut = lambda a: pl.BlockSpec((a.shape[0] // (2 * steps), a.shape[1]), lambda i, j: (2 * i + j, 0))
    outs = [jax.ShapeDtypeStruct(a.shape, F32) for a in (qkv, out)] + [
        jax.ShapeDtypeStruct(whole, F32), jax.ShapeDtypeStruct(shrink.shape, F32)]
    return pl.pallas_call(
        functools.partial(finish_kernel, share),
        grid=(steps, 2),
        out_shape=outs,
        in_specs=[cut(qkv), cut(out),
                  pl.BlockSpec((groups, rows // 2, share), lambda i, j: (0, j, i // 4 * 4 + i % 2 * 2 + i // 2 % 2)), cut(shrink)],
        out_specs=[cut(qkv), cut(out),
                   pl.BlockSpec((1, rows // 2, groups * share), lambda i, j: (i // 2, j, i % 2)), cut(shrink)],
        compiler_params=pltpu.CompilerParams(vmem_limit_bytes=40 * 2**20),
    )(qkv, out, wide, shrink)


class Backdrop:
    PACE = 2

    def __init__(self, groups, parts, part, out, acc, land_c, land_p, land_q, land_z, local, send, recv):
        self.core, self.first, self.third, self.fourth = lines(groups, parts)
        self.part, self.out, self.acc, self.lands = part, out, acc, (land_c, land_p, land_q)
        self.land_z = land_z
        self.local, self.send, self.recv = local, send, recv
        self.chunks = part.shape[0]
        self.levels = 3 + hop_count(self.third.size)
        self.lag = self.PACE * self.levels

    @staticmethod
    def scratch(chunks, width):
        major, minor, xn = mesh_sizes(lax.axis_size("grp"), lax.axis_size("ep"))
        legs = minor + xn - 1 + leg_count(major)
        return [
            pltpu.VMEM((chunks, xn, major, minor, ROWS, width), BF),
            pltpu.VMEM((4, 1, xn, major, minor, ROWS, width), BF),
            pltpu.VMEM((4, xn - 1, major, minor, ROWS, width), BF),
            pltpu.VMEM((4, minor - 1, major, ROWS, width), BF),
            pltpu.VMEM((chunks, leg_count(major), ROWS, width), BF),
            pltpu.SemaphoreType.DMA((chunks,)),
            pltpu.SemaphoreType.DMA((chunks, legs)),
            pltpu.SemaphoreType.DMA((chunks, legs)),
        ]

    def near(self):
        return [self.core, self.first, self.third, self.fourth]

    def own(self, k):
        return pltpu.make_async_copy(self.part.at[k, self.core.place], self.acc.at[k], self.local.at[k])

    def hop(self, k, level):
        p, q = self.first.place, self.fourth.place
        pn, qn = self.first.size, self.fourth.size
        if level >= 3:
            offset = pn + qn - 1
            land = self.land_z.at[k]
            return reduce_hops(self.third, lambda i: self.acc.at[k, p, i, q], lambda i: land.at[i], add,
                               lambda i: self.send.at[k, offset + i], lambda i: self.recv.at[k, offset + i])[level - 3]
        line, offset, source = [
            (self.core, 0, lambda i: self.part.at[k, i]),
            (self.first, 1, lambda i: self.acc.at[k, i]),
            (self.fourth, pn, lambda i: self.acc.at[k, p, :, i]),
        ][level]
        land = self.lands[level]
        return Swap(line, source, lambda j, i: land.at[lax.rem(k, 4), j],
                    lambda j: self.send.at[k, offset + j], lambda j: self.recv.at[k, offset + j])

    def end(self, k, level):
        p, q, z = self.first.place, self.fourth.place, self.third.place
        self.hop(k, level).finish()
        if level + 1 == self.levels:
            self.out[k] = self.acc[k, p, z, q]
            return
        after = self.hop(k, level + 1)
        if level == 0:
            self.own(k).wait()
            if self.first.size == 2:
                add(self.acc.at[k, 1 - p], self.lands[0].at[lax.rem(k, 4), 0, 1 - p])
                after.start()
                add(self.acc.at[k, p], self.lands[0].at[lax.rem(k, 4), 0, p])
                return
            add(self.acc.at[k], self.lands[0].at[lax.rem(k, 4), 0])
        elif level < 3:
            to = self.acc.at[k, p] if level == 1 else self.acc.at[k, p, :, q]
            for j in range(self.lands[level].shape[1]):
                add(to, self.lands[level].at[lax.rem(k, 4), j])
        after.start()

    def begin(self, k):
        self.hop(k, 0).start()
        self.own(k).start()

    def step(self, t):
        for level in reversed(range(self.levels)):
            k = t - self.PACE * (level + 1)

            @pl.when((k >= 0) & (k < self.chunks))
            def _(k=k, level=level):
                self.end(k, level)

        @pl.when((t >= 0) & (t < self.chunks))
        def _():
            self.begin(t)


class Sequence:
    def __init__(self, parts, block, micro):
        e = lax.axis_index("ep")
        self.xn, self.block, self.micro, self.e = parts // 2, block, micro, e
        self.x, self.c = lax.div(e, 2), lax.rem(e, 2)
        self.line = Line(parts, e, (0, 1))
        self.line_x = Line(self.xn, self.x, (0, 2))
        self.line_c = Line(2, self.c, (0, 1))

    def at(self, ref, m, x, c):
        return ref.at[m, pl.ds(pl.multiple_of((x * 2 + c) * self.block, self.block), self.block), :]

    def gather_x(self, ref, send, recv):
        legs = []
        for m in range(self.micro):
            legs += swap_legs(
                self.line_x, lambda i, m=m: self.at(ref, m, self.x, self.c), lambda j, i, m=m: self.at(ref, m, i, self.c),
                lambda j, m=m: send.at[m, j], lambda j, m=m: recv.at[m, j])
        return legs

    def gather_c(self, ref, send, recv):
        legs = []
        for m in range(self.micro):
            for x in range(self.xn):
                legs += swap_legs(
                    self.line_c, lambda i, m=m, x=x: self.at(ref, m, x, self.c), lambda j, i, m=m, x=x: self.at(ref, m, x, i),
                    lambda j, m=m, x=x: send.at[m, self.xn - 1 + x], lambda j, m=m, x=x: recv.at[m, self.xn - 1 + x])
        return legs

    def reduce_c(self, ref, land, send, recv):
        legs = []
        for m in range(self.micro):
            for x in range(self.xn):
                legs += swap_legs(
                    self.line_c, lambda i, m=m, x=x: self.at(ref, m, x, i), lambda j, i, m=m, x=x: land.at[m, x],
                    lambda j, m=m, x=x: send.at[m, self.xn - 1 + x], lambda j, m=m, x=x: recv.at[m, self.xn - 1 + x])
        return legs

    def reduce_x(self, ref, land, send, recv):
        legs = []
        for m in range(self.micro):
            legs += swap_legs(
                self.line_x, lambda i, m=m: self.at(ref, m, i, self.c), lambda j, i, m=m: land.at[m, j],
                lambda j, m=m: send.at[m, j], lambda j, m=m: recv.at[m, j])
        return legs

    def add_c(self, ref, land):
        for m in range(self.micro):
            for x in range(self.xn):
                add_rows(ref.at[m], (x * 2 + self.c) * self.block, land.at[m, x], self.block)

    def total_x(self, ref, land, out):
        for m in range(self.micro):
            @pl.loop(0, self.block // ROWS)
            def _(i, m=m):
                here = pl.ds(pl.multiple_of(i * ROWS, ROWS), ROWS)
                total = ref[m, pl.ds(pl.multiple_of(self.e * self.block + i * ROWS, ROWS), ROWS), :].astype(F32)
                for j in range(self.xn - 1):
                    total = total + land[m, j, here, :].astype(F32)
                out[m, here, :] = total


def sum_over_parts(seq, columns, sent, got, send, recv, meanwhile):
    flat = columns.T
    sent[...] = flat[:8]
    legs = swap_legs(seq.line, lambda i: sent, lambda j, i: got.at[j], lambda j: send.at[j], lambda j: recv.at[j])
    start_legs(legs)
    meanwhile()
    end_legs(legs)
    total = sent[...]
    for j in range(seq.line.size - 1):
        total = total + got[j]
    return jnp.concatenate([total] * 16, axis=0).T


def back_kernel(
    groups, parts, backed,
    branch, merge, triple, queries, keys, values, mixed, probs, hat, inv, gains_in, cos, sin, wide, part,
    d_proj, d_in, grad_heads, grad_out, wide_all, summed,
    gains, rows_all, merge_v, triple_v, q_v, k_v, v_v, mixed_v, probs_v, hat_v, d_mixed, d_qk, sums, partial, land_c, land_x, sent, got,
    load, g_send, g_recv, s_send, s_recv, t_send, t_recv, w_send, w_recv, *behind
):
    micro, block, width = branch.shape
    seq = Sequence(parts, block, micro)
    length = queries.shape[1]
    tokens = micro * length
    heads = queries.shape[2] // HD
    scale = 1.0 / math.sqrt(HD)
    loads = [pltpu.make_async_copy(a, b, load.at[i]) for i, (a, b) in enumerate((
        (merge, merge_v), (mixed, mixed_v), (queries, q_v), (keys, k_v), (values, v_v), (probs, probs_v), (hat, hat_v), (triple, triple_v)))]
    for copy in loads:
        copy.start()
    gains[...] = gains_in[...].astype(F32)
    over = Line(groups, lax.axis_index("grp"), (1, 0))
    if backed:
        back = Backdrop(groups, parts, part, summed, *behind)
        greet_lines([seq.line, over] + back.near())
        steps = back.chunks + back.lag
        step = back.step
    else:
        greet_lines([seq.line, over])
        steps, step = 0, lambda t: None
        summed[...] = jnp.zeros_like(summed)
    for m in range(micro):
        rows_all[m, pl.ds(pl.multiple_of(seq.e * block, block), block), :] = branch[m]
    gather_x = seq.gather_x(rows_all, g_send, g_recv)
    start_legs(gather_x)
    g = over.place
    own_wide = pltpu.make_async_copy(wide.at[g], wide_all.at[g], load.at[8])
    own_wide.start()
    turn = swap_legs(over, lambda i: wide.at[i], lambda j, i: wide_all.at[i], lambda j: w_send.at[j], lambda j: w_recv.at[j])
    start_legs(turn)
    step(0)
    step(1)
    step(2)
    end_legs(gather_x)
    gather_c = seq.gather_c(rows_all, g_send, g_recv)
    start_legs(gather_c)
    step(3)
    sums[...] = jnp.zeros_like(sums)
    grad_heads[...] = jnp.zeros_like(grad_heads)
    end_legs(gather_c)
    for copy in loads[:2]:
        copy.wait()
    for m in range(micro):
        d_mixed[m] = lax.dot_general(rows_all[m], merge_v[...], (((1,), (1,)), ((), ())), preferred_element_type=F32).astype(BF)
    step(4)

    @pl.loop(0, width // 512)
    def _(n):
        cols = pl.ds(pl.multiple_of(n * 512, 512), 512)
        total = lax.dot_general(mixed_v[0], rows_all[0, :, cols], (((0,), (0,)), ((), ())), preferred_element_type=F32)
        for m in range(1, micro):
            total = total + lax.dot_general(
                mixed_v[m], rows_all[m, :, cols], (((0,), (0,)), ((), ())), preferred_element_type=F32)
        grad_out[:, cols] = total.astype(BF)

    step(5)
    for copy in loads[2:7]:
        copy.wait()
    lane = lax.broadcasted_iota(jnp.int32, (1, 128), 1)

    def one_head(i):
        m, h = lax.div(i, heads), lax.rem(i, heads)
        cols = pl.ds(pl.multiple_of(h * HD, HD), HD)
        here = pl.ds(pl.multiple_of(m * length, length), length)
        d_m = d_mixed[m, :, cols]
        weights = probs_v[m, h]
        low = weights.astype(BF)
        d_proj[2, here, cols] = lax.dot_general(low, d_m, (((0,), (0,)), ((), ())), preferred_element_type=F32).astype(BF)
        d_w = lax.dot_general(d_m, v_v[m, :, cols], (((1,), (1,)), ((), ())), preferred_element_type=F32)
        d_s = (weights * (d_w - jnp.sum(weights * d_w, axis=-1, keepdims=True))).astype(BF)
        d_q = jnp.dot(d_s, k_v[m, :, cols], preferred_element_type=F32) * scale
        d_k = lax.dot_general(d_s, q_v[m, :, cols], (((0,), (0,)), ((), ())), preferred_element_type=F32) * scale
        marks = sums[here, :]
        for c, d in enumerate((d_q, d_k)):
            d = d * cos[...] - pltpu.roll(d, HD // 2, 1) * sin[...]
            d_qk[c, here, cols] = d
            product = d * hat_v[c, here, cols]
            grad_heads[c: c + 1, cols] += jnp.sum(product, axis=0, keepdims=True)
            marks = marks + jnp.where(lane == c, jnp.sum(product * gains[c: c + 1, cols], axis=-1, keepdims=True), 0.0)
        sums[here, :] = marks

    @pl.loop(0, micro * heads)
    def _(i):
        one_head(i)
        step(i + 6)

    done = 7 + micro * heads
    sums[...] = sum_over_parts(seq, sums[...], sent, got, t_send, t_recv, lambda: step(done - 1))

    @pl.loop(0, tokens // 64)
    def _(i):
        here = pl.ds(pl.multiple_of(i * 64, 64), 64)
        for c in range(2):
            inner = sums[here, c: c + 1] * (1.0 / width)
            d_proj[c, here, :] = (inv[here, c: c + 1] * (
                d_qk[c, here, :] * gains[c: c + 1, :] - hat_v[c, here, :] * inner)).astype(BF)

    loads[7].wait()

    @pl.loop(0, width // 512)
    def _(n):
        cols = pl.ds(pl.multiple_of(n * 512, 512), 512)
        for m in range(micro):
            here = pl.ds(m * length, length)
            total = lax.dot_general(d_proj[0, here, :], triple_v[0, cols, :], (((1,), (1,)), ((), ())), preferred_element_type=F32)
            for c in (1, 2):
                total = total + lax.dot_general(
                    d_proj[c, here, :], triple_v[c, cols, :], (((1,), (1,)), ((), ())), preferred_element_type=F32)
            partial[m, :, cols] = total.astype(BF)

    reduce_c = seq.reduce_c(partial, land_c, s_send, s_recv)
    start_legs(reduce_c)
    step(done)
    end_legs(reduce_c)
    seq.add_c(partial, land_c)
    reduce_x = seq.reduce_x(partial, land_x, s_send, s_recv)
    start_legs(reduce_x)
    step(done + 1)
    end_legs(reduce_x)
    seq.total_x(partial, land_x, d_in)
    for t in range(done + 2, steps):
        step(t)
    end_legs(turn)
    own_wide.wait()


def attention_back(branch, merge, triple, queries, keys, values, mixed, probs, hat, inv, gains, cos, sin, wide, part, collective_id):
    groups, parts = lax.axis_size("grp"), lax.axis_size("ep")
    micro, block, width = branch.shape
    length, local_width = queries.shape[1:]
    tokens = micro * length
    backed = part is not None
    behind = Backdrop.scratch(part.shape[0], width) if backed else []
    summed = (part.shape[0], ROWS, width) if backed else (8, 128)
    vmem = pl.BlockSpec(memory_space=pltpu.VMEM)
    hbm = pl.BlockSpec(memory_space=pl.ANY)
    xn = parts // 2
    return pl.pallas_call(
        functools.partial(back_kernel, groups, parts, backed),
        out_shape=[
            jax.ShapeDtypeStruct((3, tokens, local_width), BF),
            jax.ShapeDtypeStruct((micro, block, width), F32),
            jax.ShapeDtypeStruct((8, local_width), F32),
            jax.ShapeDtypeStruct((local_width, width), BF),
            jax.ShapeDtypeStruct(wide.shape, BF),
            jax.ShapeDtypeStruct(summed, BF if backed else F32),
        ],
        in_specs=[vmem] + [hbm] * 8 + [vmem] * 4 + [hbm] * 2,
        out_specs=[vmem] * 4 + [hbm, vmem],
        scratch_shapes=[
            pltpu.VMEM(gains.shape, F32),
            pltpu.VMEM((micro, length, width), BF),
            pltpu.VMEM(merge.shape, BF),
            pltpu.VMEM(triple.shape, BF),
            pltpu.VMEM(queries.shape, BF),
            pltpu.VMEM(queries.shape, BF),
            pltpu.VMEM(queries.shape, BF),
            pltpu.VMEM(queries.shape, BF),
            pltpu.VMEM(probs.shape, F32),
            pltpu.VMEM(hat.shape, F32),
            pltpu.VMEM(queries.shape, BF),
            pltpu.VMEM((2, tokens, local_width), F32),
            pltpu.VMEM((tokens, 128), F32),
            pltpu.VMEM((micro, length, width), BF),
            pltpu.VMEM((micro, xn, block, width), BF),
            pltpu.VMEM((micro, xn - 1, block, width), BF),
            pltpu.VMEM((8, tokens), F32),
            pltpu.VMEM((parts - 1, 8, tokens), F32),
            pltpu.SemaphoreType.DMA((9,)),
            pltpu.SemaphoreType.DMA((micro, 2 * xn - 1)),
            pltpu.SemaphoreType.DMA((micro, 2 * xn - 1)),
            pltpu.SemaphoreType.DMA((micro, 2 * xn - 1)),
            pltpu.SemaphoreType.DMA((micro, 2 * xn - 1)),
            pltpu.SemaphoreType.DMA((parts - 1,)),
            pltpu.SemaphoreType.DMA((parts - 1,)),
            pltpu.SemaphoreType.DMA((groups - 1,)),
            pltpu.SemaphoreType.DMA((groups - 1,)),
        ] + behind,
        compiler_params=pltpu.CompilerParams(
            collective_id=collective_id, has_side_effects=True, vmem_limit_bytes=58 * 2**20
        ),
        cost_estimate=pl.CostEstimate(flops=10**10, bytes_accessed=40 * 2**20, transcendentals=0),
    )(branch, merge, triple, queries, keys, values, mixed, probs, hat, inv, gains, cos, sin, wide,
      part if backed else mixed)


class BackGather:
    PACE = 3

    def __init__(self, groups, parts, own, out, local, send, recv):
        self.lines = lines(groups, parts)
        self.own, self.out, self.local, self.send, self.recv = own, out, local, send, recv
        self.chunks = own.shape[0]
        self.levels = 4
        self.lag = self.PACE * self.levels

    @staticmethod
    def scratch(chunks):
        major, minor, xn = mesh_sizes(lax.axis_size("grp"), lax.axis_size("ep"))
        legs = minor + xn + major - 2
        return [
            pltpu.SemaphoreType.DMA((chunks,)),
            pltpu.SemaphoreType.DMA((chunks, legs)),
            pltpu.SemaphoreType.DMA((chunks, legs)),
        ]

    def near(self):
        return list(self.lines)

    def mine(self, k):
        return pltpu.make_async_copy(
            self.own.at[k], self.out.at[(k,) + tuple(line.place for line in self.lines)], self.local.at[k])

    def hop(self, k, level):
        core, first, third, fourth = self.lines
        c, p, q = core.place, first.place, fourth.place
        line, offset, at = [
            (third, 0, lambda i: self.out.at[k, c, p, i, q]),
            (fourth, third.size - 1, lambda i: self.out.at[k, c, p, :, i]),
            (first, third.size + fourth.size - 2, lambda i: self.out.at[k, c, i]),
            (core, third.size + fourth.size + first.size - 3, lambda i: self.out.at[k, i]),
        ][level]
        source = (lambda i: self.own.at[k]) if level == 0 else (lambda i: at(line.place))
        return Swap(line, source, lambda j, i: at(i),
                    lambda j: self.send.at[k, offset + j], lambda j: self.recv.at[k, offset + j])

    def step(self, t):
        for level in reversed(range(self.levels)):
            k = t - self.PACE * (level + 1)

            @pl.when((k >= 0) & (k < self.chunks))
            def _(k=k, level=level):
                self.hop(k, level).finish()
                if level == 0:
                    self.mine(k).wait()
                if level + 1 < self.levels:
                    self.hop(k, level + 1).start()

        @pl.when((t >= 0) & (t < self.chunks))
        def _():
            self.mine(t).start()
            self.hop(t, 0).start()


def forward_kernel(
    groups, parts, experts,
    x, dy, routes, quota, gains_in, head_gains_in, cos, sin, docs, dispatch_in, triple, merge,
    gathered, q_out, k_out, v_out, mixed, probs, hat, inv, hidden, ffn_in, router, dy_all,
    kept, gains, head_gains, docs_down, dispatch, triple_v, merge_v, sums, partial, land_c, land_x, sent, got,
    load, g_send, g_recv, s_send, s_recv, t_send, t_recv, *behind
):
    micro, block, width = x.shape
    seq = Sequence(parts, block, micro)
    length = gathered.shape[1]
    tokens = micro * length
    heads = q_out.shape[2] // HD
    scale = 1.0 / math.sqrt(HD)
    cuts = block // ROWS
    loads = [pltpu.make_async_copy(triple, triple_v, load.at[0]), pltpu.make_async_copy(merge, merge_v, load.at[1])]
    for copy in loads:
        copy.start()
    back = BackGather(groups, parts, dy, dy_all, *behind)
    step, steps = back.step, back.chunks + back.lag
    gains[...] = gains_in[...].astype(F32)
    head_gains[...] = head_gains_in[...].astype(F32)
    lane = lax.broadcasted_iota(jnp.int32, (1, 128), 1)
    earlier = (lax.broadcasted_iota(jnp.int32, (block, block), 1) < lax.broadcasted_iota(jnp.int32, (block, block), 0))
    for m in range(micro):
        @pl.loop(0, cuts)
        def _(r, m=m):
            here = pl.ds(pl.multiple_of(r * ROWS, ROWS), ROWS)
            v = x[m, here, :].astype(F32)
            v = v * lax.rsqrt(jnp.mean(v * v, axis=-1, keepdims=True) + EPS)
            gathered[m, pl.ds(pl.multiple_of(seq.e * block + r * ROWS, ROWS), ROWS), :] = (v * gains[0:1, :]).astype(BF)
    greet_lines([seq.line] + back.near())
    gather_x = seq.gather_x(gathered, g_send, g_recv)
    start_legs(gather_x)
    step(0)
    limits = jnp.concatenate([quota[...], jnp.zeros((1, 128 - experts), jnp.int32)], axis=1).astype(F32)
    dispatch[...] = jnp.zeros_like(dispatch)
    dispatch[:experts, :] = dispatch_in[...]
    for m in range(micro):
        chosen = jnp.zeros((128, block), F32)
        for j in range(TOP):
            chosen = chosen + jnp.where(routes[m, j: j + 1, :] == lax.broadcasted_iota(jnp.int32, (128, 1), 0), 1.0, 0.0)
        counts = chosen.T
        prior = jnp.dot(jnp.where(earlier, 1.0, 0.0).astype(BF), counts.astype(BF), preferred_element_type=F32)
        kept[m] = jnp.where((counts > 0.0) & (prior < limits), 1.0, 0.0)
        docs_down[m] = jnp.broadcast_to(docs[m: m + 1, :], (128, length)).astype(F32).T
    step(1)
    step(2)
    end_legs(gather_x)
    gather_c = seq.gather_c(gathered, g_send, g_recv)
    start_legs(gather_c)
    step(3)
    loads[0].wait()
    end_legs(gather_c)

    @pl.loop(0, micro)
    def _(m):
        here = pl.ds(pl.multiple_of(m * length, length), length)
        marks = jnp.zeros((length, 128), F32)
        for c in range(2):
            raw = jnp.dot(gathered[m], triple_v[c], preferred_element_type=F32)
            hat[c, here, :] = raw
            marks = marks + jnp.where(lane == c, jnp.sum(raw * raw, axis=-1, keepdims=True), 0.0)
        sums[here, :] = marks
        v_out[m] = jnp.dot(gathered[m], triple_v[2], preferred_element_type=F32).astype(BF)
        step(m + 4)

    done = micro + 5
    squares = sum_over_parts(seq, sums[...], sent, got, t_send, t_recv, lambda: step(done - 1))
    inv[...] = lax.rsqrt(squares * (1.0 / width) + EPS)
    loads[1].wait()

    @pl.loop(0, micro * heads)
    def _(i):
        m, h = lax.div(i, heads), lax.rem(i, heads)
        cols = pl.ds(pl.multiple_of(h * HD, HD), HD)
        here = pl.ds(pl.multiple_of(m * length, length), length)
        for c, to in enumerate((q_out, k_out)):
            v = hat[c, here, cols] * inv[here, c: c + 1]
            hat[c, here, cols] = v
            v = v * head_gains[c: c + 1, cols]
            to[m, :, cols] = (v * cos[...] + pltpu.roll(v, HD // 2, 1) * sin[...]).astype(BF)
        scores = lax.dot_general(
            q_out[m, :, cols], k_out[m, :, cols], (((1,), (1,)), ((), ())), preferred_element_type=F32) * scale
        allowed = (docs_down[m][:, :1] == docs[pl.ds(m, 1), :].astype(F32)) & (
            lax.broadcasted_iota(jnp.int32, (length, length), 1) <= lax.broadcasted_iota(jnp.int32, (length, length), 0))
        scores = jnp.where(allowed, scores, NEG)
        grown = jnp.exp(scores - jnp.max(scores, axis=-1, keepdims=True))
        weights = grown / jnp.sum(grown, axis=-1, keepdims=True)
        probs[m, h] = weights
        mixed[m, :, cols] = jnp.dot(weights.astype(BF), v_out[m, :, cols], preferred_element_type=F32).astype(BF)
        step(done + i)

    done = done + micro * heads

    @pl.loop(0, width // 512)
    def _(n):
        cols = pl.ds(pl.multiple_of(n * 512, 512), 512)
        for m in range(micro):
            partial[m, :, cols] = jnp.dot(mixed[m], merge_v[:, cols], preferred_element_type=F32).astype(BF)

    reduce_c = seq.reduce_c(partial, land_c, s_send, s_recv)
    start_legs(reduce_c)
    step(done)
    end_legs(reduce_c)
    seq.add_c(partial, land_c)
    reduce_x = seq.reduce_x(partial, land_x, s_send, s_recv)
    start_legs(reduce_x)
    step(done + 1)
    end_legs(reduce_x)
    seq.total_x(partial, land_x, hidden)
    for m in range(micro):
        @pl.loop(0, cuts)
        def _(r, m=m):
            here = pl.ds(pl.multiple_of(r * ROWS, ROWS), ROWS)
            v = hidden[m, here, :] + x[m, here, :].astype(F32)
            hidden[m, here, :] = v
            v = v * lax.rsqrt(jnp.mean(v * v, axis=-1, keepdims=True) + EPS)
            ffn_in[m, here, :width] = (v * gains[1:2, :]).astype(BF)
        logits = lax.dot_general(
            ffn_in[m, :, :width], dispatch[...], (((1,), (1,)), ((), ())), preferred_element_type=F32)
        logits = jnp.where(lane < experts, logits, NEG)
        grown = jnp.exp(logits - jnp.max(logits, axis=-1, keepdims=True))
        grown = grown / jnp.sum(grown, axis=-1, keepdims=True)
        gate = grown * kept[m]
        router[m] = grown + pltpu.roll(kept[m], experts, 1)
        head = gate.astype(BF).astype(F32)
        ffn_in[m, :, width:] = (head + pltpu.roll(gate - head, experts, 1)).astype(BF)
    for t in range(done + 2, steps):
        step(t)


def attention_forward(x, dy, routes, quota, gains, head_gains, cos, sin, docs, dispatch, triple, merge, collective_id):
    groups, parts = lax.axis_size("grp"), lax.axis_size("ep")
    major, minor, xn = mesh_sizes(groups, parts)
    micro, block, width = x.shape
    length = docs.shape[1]
    local_width = triple.shape[2]
    heads = local_width // HD
    tokens = micro * length
    chunks = micro * block // ROWS
    vmem = pl.BlockSpec(memory_space=pltpu.VMEM)
    hbm = pl.BlockSpec(memory_space=pl.ANY)
    low = jax.ShapeDtypeStruct((micro, length, local_width), BF)
    experts = dispatch.shape[1]
    return pl.pallas_call(
        functools.partial(forward_kernel, groups, parts, experts),
        out_shape=[
            jax.ShapeDtypeStruct((micro, length, width), BF),
            low, low, low, low,
            jax.ShapeDtypeStruct((micro, heads, length, length), F32),
            jax.ShapeDtypeStruct((2, tokens, local_width), F32),
            jax.ShapeDtypeStruct((tokens, 128), F32),
            jax.ShapeDtypeStruct((micro, block, width), F32),
            jax.ShapeDtypeStruct((micro, block, width + 128), BF),
            jax.ShapeDtypeStruct((micro, block, 128), F32),
            jax.ShapeDtypeStruct((chunks, 2, xn, major, minor, ROWS, width), BF),
        ],
        in_specs=[vmem] * 10 + [hbm] * 2,
        out_specs=[vmem] * 11 + [hbm],
        scratch_shapes=[
            pltpu.VMEM((micro, block, 128), F32),
            pltpu.VMEM(gains.shape, F32),
            pltpu.VMEM(head_gains.shape, F32),
            pltpu.VMEM((micro, length, 128), F32),
            pltpu.VMEM((128, width), BF),
            pltpu.VMEM(triple.shape, BF),
            pltpu.VMEM(merge.shape, BF),
            pltpu.VMEM((tokens, 128), F32),
            pltpu.VMEM((micro, length, width), BF),
            pltpu.VMEM((micro, xn, block, width), BF),
            pltpu.VMEM((micro, xn - 1, block, width), BF),
            pltpu.VMEM((8, tokens), F32),
            pltpu.VMEM((parts - 1, 8, tokens), F32),
            pltpu.SemaphoreType.DMA((2,)),
            pltpu.SemaphoreType.DMA((micro, 2 * xn - 1)),
            pltpu.SemaphoreType.DMA((micro, 2 * xn - 1)),
            pltpu.SemaphoreType.DMA((micro, 2 * xn - 1)),
            pltpu.SemaphoreType.DMA((micro, 2 * xn - 1)),
            pltpu.SemaphoreType.DMA((parts - 1,)),
            pltpu.SemaphoreType.DMA((parts - 1,)),
        ] + BackGather.scratch(chunks),
        compiler_params=pltpu.CompilerParams(
            collective_id=collective_id, has_side_effects=True, vmem_limit_bytes=56 * 2**20
        ),
        cost_estimate=pl.CostEstimate(flops=6 * 10**9, bytes_accessed=40 * 2**20, transcendentals=0),
    )(x, dy.reshape(chunks, ROWS, width), routes.transpose(0, 2, 1), quota.reshape(1, -1), gains, head_gains, cos, sin, docs,
      dispatch.T, triple, merge)


def per_device(
    block_entry_states,
    document_labels,
    token_assignments,
    worker_quota_tallies,
    rescale_factors_both,
    triple_projection_matrix,
    probe_lookup_scalers,
    heads_merge_matrix,
    dispatcher_matrix,
    specialist_widen_matrix,
    specialist_shrink_matrix,
    output_gradient,
):
    micro, local_rows, width = block_entry_states.shape
    groups, parts = lax.axis_size("grp"), lax.axis_size("ep")
    major, minor, xs = mesh_sizes(groups, parts)
    group = lax.axis_index("grp")
    part = lax.axis_index("ep")
    seq_len = document_labels.shape[1]
    experts = dispatcher_matrix.shape[1]
    local_exp = specialist_widen_matrix.shape[0]
    inner = specialist_shrink_matrix.shape[1]
    share = inner // groups
    local_width = triple_projection_matrix.shape[2]
    heads = local_width // HD
    scale = 1.0 / math.sqrt(HD)
    gains = rescale_factors_both.astype(F32)
    cos, signed_sin = rope_tables(seq_len, HD)
    triple = triple_projection_matrix.transpose(1, 0, 2)
    gathered, queries, keys, values, mixed, weights, qk_hat, qk_inv, hidden, ffn_ext, probs, dy_all = attention_forward(
        block_entry_states, output_gradient, token_assignments, worker_quota_tallies, rescale_factors_both,
        probe_lookup_scalers, cos, signed_sin,
        document_labels, dispatcher_matrix, triple, heads_merge_matrix, 0)
    ffn_in = ffn_ext[..., :width]

    fused = xs == minor and share % 128 == 0 and local_exp % 2 == 0 and 2 * xs * minor * major * ROWS <= 512
    chunk_shape = (micro * local_rows // ROWS, 2, xs, major, minor, ROWS)
    if fused:
        dx_sum, moe_part, grad_widen, grad_shrink = experts_together(
            ffn_ext, dy_all.reshape(dy_all.shape[0], -1, width), specialist_widen_matrix, specialist_shrink_matrix, experts, 1)
    else:
        dx_sum, moe_part, grad_widen, grad_shrink = experts_apart(
            ffn_ext, dy_all, specialist_widen_matrix, specialist_shrink_matrix, experts)
    dx_sum = dx_sum.astype(F32).reshape(micro, local_rows, width + 128)
    grad_widen = grad_widen.reshape(groups, width // groups, -1)

    inv_second = lax.rsqrt(jnp.mean(hidden * hidden, axis=-1, keepdims=True) + EPS)
    hat_second = hidden * inv_second
    probs, keep = probs[..., :experts], probs[..., experts: 2 * experts]
    d_probs = dx_sum[..., width: width + experts] * keep
    d_logits = probs * (d_probs - jnp.sum(probs * d_probs, axis=-1, keepdims=True))
    d_ffn = dx_sum[..., :width] + jnp.einsum("mte,de->mtd", d_logits, dispatcher_matrix.astype(F32), precision=HIGH)
    grad_router = jnp.einsum("mtd,mte->ed", ffn_in.astype(F32), d_logits, precision=HIGH)
    scaled = d_ffn * gains[1]
    adjoint = output_gradient.astype(F32)
    d_hidden = adjoint + inv_second * (scaled - hat_second * jnp.mean(scaled * hat_second, axis=-1, keepdims=True))
    grad_second = jnp.sum(d_ffn * hat_second, axis=(0, 1))

    d_proj, d_attn_in, grad_heads, grad_out, grad_widen, moe = attention_back(
        d_hidden.astype(BF), heads_merge_matrix, triple, queries, keys, values, mixed, weights,
        qk_hat, qk_inv, probe_lookup_scalers, cos, signed_sin, grad_widen,
        moe_part.reshape(chunk_shape + (width,)) if fused else None, 5)
    if not fused:
        moe = scatter_all(moe_part.reshape(chunk_shape + (width,)), 3)
    output = (hidden + moe.astype(F32).reshape(micro, local_rows, width)).astype(BF)
    skip = block_entry_states.astype(F32)
    inv_first = lax.rsqrt(jnp.mean(skip * skip, axis=-1, keepdims=True) + EPS)
    hat_first = skip * inv_first
    scaled = d_attn_in * gains[0]
    grad_input = d_hidden + inv_first * (scaled - hat_first * jnp.mean(scaled * hat_first, axis=-1, keepdims=True))
    grad_first = jnp.sum(d_attn_in * hat_first, axis=(0, 1))

    shared = jnp.concatenate([grad_first[None], grad_second[None], grad_router]).reshape(-1).astype(BF)
    own = grad_heads[:2].reshape(-1).astype(BF)
    gap, size = shared.shape[0], shared.shape[0] + own.shape[0]
    block = (groups, ROWS, -(-size // (groups * ROWS * 128)) * 128)
    room = math.prod(block)
    shared = jnp.pad(shared, (0, room - gap)).reshape(block)
    own = jnp.pad(own, (gap, room - size)).reshape(block)
    out_sum, qkv_sum, misc_sum = total_over_groups(
        gathered.reshape(-1, width), d_proj, grad_out, shared, own, 4)
    qkv_sum, out_sum, grad_widen, grad_shrink = finish(
        qkv_sum.reshape(-1, local_width), out_sum.reshape(-1, width), grad_widen, grad_shrink, local_exp, share)
    qkv_sum = qkv_sum.reshape(3, width, local_width).transpose(1, 0, 2)
    grad_shrink = grad_shrink.reshape(local_exp, share, width)
    misc_sum = misc_sum.reshape(-1)[:size].astype(F32)
    rows = misc_sum[: (2 + experts) * width].reshape(2 + experts, width)
    return (
        output,
        grad_input,
        rows[:2],
        qkv_sum,
        misc_sum[(2 + experts) * width:].reshape(2, local_width),
        out_sum,
        rows[2:].T,
        grad_widen,
        grad_shrink,
    )


def solution(mesh):
    return jax.shard_map(
        per_device,
        mesh=mesh,
        in_specs=(
            P(None, ALL, None),
            P(None, "grp"),
            P(None, ALL, None),
            P(),
            P(),
            P(None, None, "ep"),
            P(None, "ep"),
            P("ep", None),
            P(),
            P("ep", None, None),
            P("ep", None, None),
            P(None, ALL, None),
        ),
        out_specs=(
            P(None, ALL, None),
            P(None, ALL, None),
            P(),
            P(None, None, "ep"),
            P(None, "ep"),
            P("ep", None),
            P(),
            P("ep", "grp", None),
            P("ep", "grp", None),
        ),
        check_vma=False,
    )
```

```python
import functools
import math

import jax
import jax.numpy as jnp
import numpy as np
from jax import lax
from jax.experimental import pallas as pl
from jax.experimental.pallas import tpu as pltpu
from jax.sharding import PartitionSpec as P

HD = 128
TOP = 8
EPS = 1e-05
THETA = 10000.0
NEG = -1e30
HIGH = lax.Precision.HIGHEST
ALL = ("grp", "ep")
MESH = pl.DeviceIdType.MESH
ROWS = 16
CUTS = 8
PER_STEP = 4
BF = jnp.bfloat16
F32 = jnp.float32


def rope_tables(length, head_dim):
    half = head_dim // 2
    angle = np.arange(length)[:, None] * THETA ** (-np.arange(half) * 2.0 / head_dim)
    cos, sin = np.cos(angle), np.sin(angle)
    return np.concatenate([cos, cos], 1).astype(np.float32), np.concatenate([-sin, sin], 1).astype(np.float32)


def mesh_sizes(groups, parts):
    major = 4 if groups % 4 == 0 else groups
    return major, groups // major, parts // 2


class Line:
    def __init__(self, size, place, step):
        self.size, self.place, self.step = size, place, step

    def at(self, hops):
        return (
            lax.axis_index("grp") + hops * self.step[0],
            lax.axis_index("ep") + hops * self.step[1],
        )


def lines(groups, parts):
    major, minor, xs = mesh_sizes(groups, parts)
    g, e = lax.axis_index("grp"), lax.axis_index("ep")
    core = lax.rem(e, 2)
    x_pos, minor_pos = lax.div(e, 2), lax.rem(g, minor)
    if xs == minor:
        first = Line(xs, jnp.where(core == 0, x_pos, minor_pos), (core, 2 - 2 * core))
        second = Line(xs, jnp.where(core == 0, minor_pos, x_pos), (1 - core, 2 * core))
    else:
        first = Line(xs, x_pos, (0, 2))
        second = Line(minor, minor_pos, (1, 0))
    return Line(2, core, (0, 1)), first, Line(major, lax.div(g, minor), (minor, 0)), second


def greet(some, whole=()):
    barrier = pltpu.get_barrier_semaphore()
    peers = sum(line.size - 1 for line in whole)
    for line in whole:
        for j in range(1, line.size):
            to = lax.rem(line.place + j, line.size)
            pl.semaphore_signal(barrier, inc=1, device_id=line.at(to - line.place), device_id_type=MESH)
    for line in some:
        if line.size == 2:
            pl.semaphore_signal(barrier, inc=1, device_id=line.at(1 - 2 * line.place), device_id_type=MESH)
            peers = peers + 1
        else:
            for way, there in ((1, line.place < line.size - 1), (-1, line.place > 0)):

                @pl.when(there)
                def _(line=line, way=way):
                    pl.semaphore_signal(barrier, inc=1, device_id=line.at(way), device_id_type=MESH)

                peers = peers + there.astype(jnp.int32)
    pl.semaphore_wait(barrier, peers)


def greet_lines(some):
    barrier = pltpu.get_barrier_semaphore()
    for line in some:
        for j in range(1, line.size):
            to = lax.rem(line.place + j, line.size)
            pl.semaphore_signal(barrier, inc=1, device_id=line.at(to - line.place), device_id_type=MESH)
    pl.semaphore_wait(barrier, sum(line.size - 1 for line in some))


def remote(src, dst, send, recv, target):
    return pltpu.make_async_remote_copy(
        src_ref=src, dst_ref=dst, send_sem=send, recv_sem=recv, device_id=target, device_id_type=MESH
    )


class Hop:
    def __init__(self, legs, after=None):
        self.legs, self.after = legs, after

    def _each(self, which, act):
        for leg in self.legs:
            if leg[which] is None:
                act(leg)
            else:
                pl.when(leg[which])(functools.partial(act, leg))

    def start(self):
        self._each(0, lambda leg: leg[2]().start())

    def arrive(self):
        def act(leg):
            leg[3]().wait_recv()
            if leg[4] is not None:
                leg[4]()

        self._each(1, act)

    def sent(self):
        self._each(0, lambda leg: leg[2]().wait_send())

    def finish(self):
        self.arrive()
        self.sent()


def spread_hops(core, first, third, fourth, at, own, send, recv):
    c, p, z, q = core.place, first.place, third.place, fourth.place
    r4 = ROWS
    r3 = r4 * fourth.size
    r2 = r3 * third.size
    rc = r2 * first.size
    base = [0]

    def sems(n):
        b = base[0]
        base[0] += n
        return (lambda i: send(b + i)), (lambda i: recv(b + i))

    def swap(line, place, first_source=None):
        source = first_source or (lambda i: place(line.place))
        return Swap(line, source, lambda j, i: place(i), *sems(line.size - 1))

    hops = [swap(fourth, lambda i: at(c * rc + p * r2 + z * r3 + i * r4, r4), lambda i: own)]
    hops += gather_hops(third, lambda i: at(c * rc + p * r2 + i * r3, r3), *sems(leg_count(third.size)))
    hops.append(swap(first, lambda i: at(c * rc + i * r2, r2)))
    hops.append(swap(core, lambda i: at(i * rc, rc)))
    return hops


def gather_hops(line, at, send, recv, own=None):
    n, a = line.size, line.place
    if n == 2:
        mine, theirs, peer = at(a), at(1 - a), line.at(1 - 2 * a)
        return [
            Hop([(None, None, lambda: remote(mine if own is None else own, mine, send(0), recv(0), peer),
                  lambda: remote(theirs, theirs, send(0), recv(0), peer), None)])
        ]
    hops = []
    for s in range(1, n):
        legs = []
        for d, way in enumerate((1, -1)):
            k = (s - 1) * 2 + d
            out = a - way * (s - 1)
            into = a - way * s
            sends = (out >= 0) & (out < n) & (a + way >= 0) & (a + way < n)
            gets = (into >= 0) & (into < n)
            out, into = jnp.clip(out, 0, n - 1), jnp.clip(into, 0, n - 1)
            legs.append((
                sends, gets,
                lambda out=out, way=way, k=k, s=s: remote(
                    own if s == 1 and own is not None else at(out), at(out), send(k), recv(k), line.at(way)),
                lambda into=into, way=way, k=k: remote(at(into), at(into), send(k), recv(k), line.at(-way)),
                None,
            ))
        hops.append(Hop(legs))
    return hops


def reduce_hops(line, acc, land, add, send, recv):
    n, a = line.size, line.place
    if n == 2:
        peer = line.at(1 - 2 * a)
        return [
            Hop([(None, None, lambda: remote(acc(1 - a), land(0), send(0), recv(0), peer),
                  lambda: remote(land(0), land(0), send(0), recv(0), peer),
                  lambda: add(acc(a), land(0)))])
        ]
    hops = []
    for s in range(n - 1):
        legs = []
        for d, way in enumerate((1, -1)):
            k = s * 2 + d
            b = a if way == 1 else n - 1 - a
            sends = (b <= s) & (b < n - 1)
            gets = (b - 1 <= s) & (b >= 1)
            out = b + n - 1 - s
            into = b + n - 2 - s
            out, into = jnp.clip(out, 0, n - 1), jnp.clip(into, 0, n - 1)
            if way == -1:
                out, into = n - 1 - out, n - 1 - into
            legs.append((
                sends, gets,
                lambda out=out, way=way, k=k: remote(acc(out), land(k), send(k), recv(k), line.at(way)),
                lambda way=way, k=k: remote(land(k), land(k), send(k), recv(k), line.at(-way)),
                lambda into=into, k=k: add(acc(into), land(k)),
            ))
        hops.append(Hop(legs))
    return hops


def hop_count(n):
    return 1 if n == 2 else n - 1


def leg_count(n):
    return 1 if n == 2 else 2 * (n - 1)


def flow(chains, pace=1):
    depth, count = max(len(c) for c in chains), len(chains)
    for t in range(count + pace * depth):
        for k in range(count):
            i, rest = divmod(t - k, pace)
            if rest:
                continue
            if 1 <= i <= len(chains[k]):
                chains[k][i - 1].arrive()
            if 0 <= i < len(chains[k]):
                chains[k][i].start()
    for chain in chains:
        for hop in chain:
            hop.sent()


def add(acc, land):
    lead = acc.shape[:-2]

    def one(i):
        where = []
        for size in reversed(lead):
            where.insert(0, lax.rem(i, size))
            i = lax.div(i, size)
        where = tuple(where) + (slice(None), slice(None))
        acc[where] = (acc[where].astype(F32) + land[where].astype(F32)).astype(acc.dtype)

    if lead:
        pl.loop(0, math.prod(lead))(one)
    else:
        one(0)


def gather_kernel(groups, parts, x, out, local, send, recv):
    core, first, second, long = lines(groups, parts)
    c, p, q, z = core.place, first.place, second.place, long.place
    greet([core, first, second, long])
    chunks = x.shape[0]
    own = [pltpu.make_async_copy(x.at[k], out.at[k, c, p, q, z], local.at[k]) for k in range(chunks)]
    for copy in own:
        copy.start()
    chains = []
    for k in range(chunks):
        base = [0]

        def sems(n, k=k, base=base):
            b = base[0]
            base[0] += leg_count(n)
            return (lambda i: send.at[k, b + i]), (lambda i: recv.at[k, b + i])

        chain = []
        chain += gather_hops(long, lambda i, k=k: out.at[k, c, p, q, i], *sems(long.size))
        chain += gather_hops(second, lambda i, k=k: out.at[k, c, p, i], *sems(second.size))
        chain += gather_hops(first, lambda i, k=k: out.at[k, c, i], *sems(first.size))
        chain += gather_hops(core, lambda i, k=k: out.at[k, i], *sems(2))
        chains.append(chain)
    for copy in own:
        copy.wait()
    flow(chains)


def gather_all(x, collective_id):
    groups, parts = lax.axis_size("grp"), lax.axis_size("ep")
    major, minor, xs = mesh_sizes(groups, parts)
    width = x.shape[-1]
    x = x.reshape(-1, ROWS, width)
    legs = sum(leg_count(n) for n in (2, xs, minor, major))
    chunks = x.shape[0]
    return pl.pallas_call(
        functools.partial(gather_kernel, groups, parts),
        out_shape=jax.ShapeDtypeStruct((chunks, 2, xs, major, minor, ROWS, width), x.dtype),
        in_specs=[pl.BlockSpec(memory_space=pl.ANY)],
        out_specs=pl.BlockSpec(memory_space=pl.ANY),
        scratch_shapes=[
            pltpu.SemaphoreType.DMA((chunks,)),
            pltpu.SemaphoreType.DMA((chunks, legs)),
            pltpu.SemaphoreType.DMA((chunks, legs)),
        ],
        compiler_params=pltpu.CompilerParams(collective_id=collective_id, has_side_effects=True),
    )(x)


def scatter_kernel(groups, parts, part, out, acc, land_c, land_p, land_q, land_z, local, send, recv):
    core, first, second, long = lines(groups, parts)
    c, p, q, z = core.place, first.place, second.place, long.place
    chunks = part.shape[0]
    own = [pltpu.make_async_copy(part.at[k, c], acc.at[k], local.at[k]) for k in range(chunks)]
    for copy in own:
        copy.start()
    greet([core, first, second, long])
    chains = []
    for k in range(chunks):
        base = [0]

        def sems(n, k=k, base=base):
            b = base[0]
            base[0] += leg_count(n)
            return (lambda i: send.at[k, b + i]), (lambda i: recv.at[k, b + i])

        def add_own(acc_ref, land_ref, k=k):
            own[k].wait()
            add(acc_ref, land_ref)

        s, r = sems(2)
        peer = core.at(1 - 2 * c)
        other = part.at[k, 1 - c]
        chain = [Hop([(
            None, None,
            lambda other=other, s=s, r=r, k=k: remote(other, land_c.at[k], s(0), r(0), peer),
            lambda s=s, r=r, k=k: remote(land_c.at[k], land_c.at[k], s(0), r(0), peer),
            lambda k=k, add_own=add_own: add_own(acc.at[k], land_c.at[k]),
        )])]
        chain += reduce_hops(first, lambda i, k=k: acc.at[k, i], lambda i, k=k: land_p.at[k, i], add, *sems(first.size))
        chain += reduce_hops(second, lambda i, k=k: acc.at[k, p, i], lambda i, k=k: land_q.at[k, i], add, *sems(second.size))
        chain += reduce_hops(long, lambda i, k=k: acc.at[k, p, q, i], lambda i, k=k: land_z.at[k, i], add, *sems(long.size))
        chains.append(chain)
    flow(chains)
    for k in range(chunks):
        out[k] = acc[k, p, q, z]


def scatter_all(part, collective_id):
    groups, parts = lax.axis_size("grp"), lax.axis_size("ep")
    major, minor, xs = mesh_sizes(groups, parts)
    legs = sum(leg_count(n) for n in (2, xs, minor, major))
    chunks, width = part.shape[0], part.shape[-1]
    unit = 2 * ROWS * width
    need = unit * (2 * xs * minor * major + leg_count(xs) * minor * major + leg_count(major) * minor + leg_count(minor) + 2)
    per = chunks
    while per > 1 and per * need > 44 * 2**20:
        per //= 2
    call = pl.pallas_call(
        functools.partial(scatter_kernel, groups, parts),
        out_shape=jax.ShapeDtypeStruct((per, ROWS, width), BF),
        in_specs=[pl.BlockSpec(memory_space=pl.ANY)],
        out_specs=pl.BlockSpec(memory_space=pltpu.VMEM),
        scratch_shapes=[
            pltpu.VMEM((per, xs, major, minor, ROWS, width), BF),
            pltpu.VMEM((per, xs, major, minor, ROWS, width), BF),
            pltpu.VMEM((per, leg_count(xs), major, minor, ROWS, width), BF),
            pltpu.VMEM((per, leg_count(major), minor, ROWS, width), BF),
            pltpu.VMEM((per, leg_count(minor), ROWS, width), BF),
            pltpu.SemaphoreType.DMA((per,)),
            pltpu.SemaphoreType.DMA((per, legs)),
            pltpu.SemaphoreType.DMA((per, legs)),
        ],
        compiler_params=pltpu.CompilerParams(
            collective_id=collective_id, has_side_effects=True, vmem_limit_bytes=56 * 2**20
        ),
    )
    return jnp.concatenate([call(part[i:i + per]) for i in range(0, chunks, per)]) if per < chunks else call(part)


class Begun:
    def __init__(self, hop, before):
        self.hop, self.before = hop, before

    def start(self):
        self.before()
        self.hop.start()

    def arrive(self):
        self.hop.arrive()

    def sent(self):
        self.hop.sent()


def total_kernel(groups, parts, plan, rows_in, d_proj, grad_out, shared, own, *refs):
    count = 3
    outs, acc, land = (refs[i * count: (i + 1) * count] for i in range(3))
    rows_v, proj_v, shared_v, own_v, got, local, stored, send, recv, t_send, t_recv = refs[3 * count:]
    major, minor, _ = mesh_sizes(groups, parts)
    g, e = lax.axis_index("grp"), lax.axis_index("ep")
    short = Line(minor, lax.rem(g, minor), (1, 0))
    long = Line(major, lax.div(g, minor), (minor, 0))
    whole = Line(parts, e, (0, 1))
    width = rows_in.shape[1]
    load = [pltpu.make_async_copy(a, b, local.at[i]) for i, (a, b) in enumerate((
        (grad_out, acc[0]), (rows_in, rows_v), (d_proj, proj_v), (shared, shared_v), (own, own_v)))]
    for copy in load:
        copy.start()

    def weights(k):
        def act():
            if k == 0:
                load[1].wait()
                load[2].wait()
            cuts = acc[1].shape[0] // 3
            c, cut = k // cuts, k % cuts
            blocks = max(1, 256 // acc[1].shape[2])
            rows = blocks * acc[1].shape[2]

            @pl.loop(0, groups // blocks)
            def _(i):
                cols = pl.ds(pl.multiple_of(cut * (width // cuts) + i * rows, 128), rows)
                total = lax.dot_general(rows_v[:, cols], proj_v[c], (((0,), (0,)), ((), ())), preferred_element_type=F32)
                acc[1][k, pl.ds(i * blocks, blocks)] = total.astype(BF).reshape((blocks,) + acc[1].shape[2:])

        return act

    swap = swap_legs(whole, lambda i: shared_v, lambda j, i: got.at[j], lambda j: t_send.at[j], lambda j: t_recv.at[j])

    def everyone():
        end_legs(swap)
        load[4].wait()

        @pl.loop(0, groups)
        def _(i):
            total = shared_v[i].astype(F32) + own_v[i].astype(F32)
            for j in range(parts - 1):
                total = total + got[j, i].astype(F32)
            acc[2][0, i] = total.astype(BF)

    before = {(0, 0): load[0].wait, (2, 0): everyone}
    chains = []
    for number, (j, k, far) in enumerate(plan):
        one, two = (long, short) if far else (short, long)
        y, z = one.place, two.place
        n = two.size

        def level_one(ref, k, n=n):
            return lambda i: ref.at[k, pl.ds(i * n, n)]

        def level_two(ref, k, y=y, n=n):
            return lambda i: ref.at[k, y * n + i]

        store = pltpu.make_async_copy(acc[j].at[k, y * n + z], outs[j].at[k, y * n + z], stored.at[number])
        base = [0]

        def sems(size, number=number, base=base):
            b = base[0]
            base[0] += leg_count(size)
            return (lambda i: send.at[number, b + i]), (lambda i: recv.at[number, b + i])

        first_land = leg_count(one.size) * n
        down = reduce_hops(one, level_one(acc[j], k), lambda i, j=j, k=k, n=n: land[j].at[k, pl.ds(i * n, n)], add, *sems(one.size))
        down += reduce_hops(two, level_two(acc[j], k), lambda i, j=j, k=k, f=first_land: land[j].at[k, f + i], add, *sems(two.size))
        up = gather_hops(two, level_two(outs[j], k), *sems(two.size), own=acc[j].at[k, y * n + z])
        turn = len(up)
        up += gather_hops(one, level_one(outs[j], k), *sems(one.size))

        down[0] = Begun(down[0], before.get((j, k)) or (weights(k) if j == 1 else lambda: None))
        up[0] = Begun(up[0], store.start)
        up[turn] = Begun(up[turn], store.wait)
        chains.append(down + up)
    greet([short, long], [whole])
    load[3].wait()
    start_legs(swap)
    flow(chains, 2)


def total_over_groups(gathered, d_proj, grad_out, shared, own, collective_id):
    groups, parts = lax.axis_size("grp"), lax.axis_size("ep")
    major, minor, _ = mesh_sizes(groups, parts)
    tokens, width = gathered.shape
    local_width = d_proj.shape[2]
    few = max(n for n in (4, 2, 1) if n == 1 or grad_out.shape[0] % (n * groups * ROWS) == 0)
    many = max(n for n in (12, 6, 3) if n == 3 or 3 * width % (n * groups * ROWS) == 0)
    shapes = [
        (few, groups, grad_out.shape[0] // few // groups, width),
        (many, groups, 3 * width // many // groups, local_width),
        (1,) + shared.shape,
    ]
    plan = [(0, k, k % 4 == 1) for k in range(few)] + [(1, k, k % 4 == 1) for k in range(many)] + [(2, 0, False)]
    blocks = max(leg_count(a) * b + leg_count(b) for a, b in ((minor, major), (major, minor)))
    legs = 2 * (leg_count(minor) + leg_count(major))
    total = len(plan)
    hbm = pl.BlockSpec(memory_space=pl.ANY)
    scratch = [pltpu.VMEM(a, BF) for a in shapes]
    scratch += [pltpu.VMEM((a[0], blocks) + a[2:], BF) for a in shapes]
    return pl.pallas_call(
        functools.partial(total_kernel, groups, parts, plan),
        out_shape=[jax.ShapeDtypeStruct(a, BF) for a in shapes],
        in_specs=[hbm] * 5,
        out_specs=[hbm] * len(shapes),
        scratch_shapes=scratch + [
            pltpu.VMEM(gathered.shape, BF),
            pltpu.VMEM(d_proj.shape, BF),
            pltpu.VMEM(shared.shape, BF),
            pltpu.VMEM(shared.shape, BF),
            pltpu.VMEM((parts - 1,) + shared.shape, BF),
            pltpu.SemaphoreType.DMA((5,)),
            pltpu.SemaphoreType.DMA((total,)),
            pltpu.SemaphoreType.DMA((total, legs)),
            pltpu.SemaphoreType.DMA((total, legs)),
            pltpu.SemaphoreType.DMA((parts - 1,)),
            pltpu.SemaphoreType.DMA((parts - 1,)),
        ],
        compiler_params=pltpu.CompilerParams(
            collective_id=collective_id, has_side_effects=True, vmem_limit_bytes=48 * 2**20
        ),
        cost_estimate=pl.CostEstimate(flops=6 * tokens * width * local_width, bytes_accessed=40 * 2**20, transcendentals=0),
    )(gathered, d_proj, grad_out.reshape(shapes[0]), shared, own)


def swap_legs(line, source, target, send, recv):
    n, a = line.size, line.place
    legs = []
    for j in range(1, n):
        to, off = lax.rem(a + j, n), lax.rem(a + n - j, n)
        legs.append((
            lambda to=to, j=j: remote(source(to), target(j - 1, a), send(j - 1), recv(j - 1), line.at(to - a)),
            lambda off=off, j=j: remote(target(j - 1, off), target(j - 1, off), send(j - 1), recv(j - 1), line.at(off - a)),
        ))
    return legs


def start_legs(legs):
    for out, _ in legs:
        out().start()


def end_legs(legs):
    for out, into in legs:
        into().wait_recv()
    for out, into in legs:
        out().wait_send()


class Swap:
    def __init__(self, *how):
        self.legs = swap_legs(*how)

    def start(self):
        start_legs(self.legs)

    def finish(self):
        end_legs(self.legs)


def add_rows(acc, first, land, rows):
    @pl.loop(0, rows // ROWS)
    def _(i):
        here = pl.ds(pl.multiple_of(first + i * ROWS, ROWS), ROWS)
        there = pl.ds(pl.multiple_of(i * ROWS, ROWS), ROWS)
        acc[here, :] = (acc[here, :].astype(F32) + land[there, :].astype(F32)).astype(acc.dtype)


def experts_kernel(
    groups, parts, local_rows, acc_ring, experts,
    x, dy, widen, shrink,
    summed, moe, grad_widen, grad_shrink,
    xs, dys, wide, down, sum_wide, sum_down, stage, acc, other, land_c, land_p, land_q, land_z,
    hid, raw, gated, d_gu, gate, product, marks,
    load, dy_sem, stage_sem, g_send, g_recv, s_send, s_recv,
):
    core, first, third, fourth = lines(groups, parts)
    c, p, z, q = core.place, first.place, third.place, fourth.place
    pn, zn, qn = first.size, third.size, fourth.size
    chunks, width = x.shape[0], shrink.shape[2]
    local_exp, inner = shrink.shape[0], shrink.shape[1]
    share = inner // groups
    group, part = lax.axis_index("grp"), lax.axis_index("ep")
    rq, rz, rp, rc = ROWS, ROWS * qn, ROWS * qn * zn, ROWS * qn * zn * pn
    rows = 2 * rc
    levels = 3 + hop_count(zn)
    cuts = local_rows // ROWS
    base = part * local_exp
    pairs = local_exp // 2

    loads = []
    for e in range(local_exp):
        for half in range(2):
            to = (e // 2) * 4 * share + half * 2 * share + (e % 2) * share
            loads.append(pltpu.make_async_copy(
                widen.at[e, :, pl.ds(pl.multiple_of(half * inner + group * share, share), share)],
                wide.at[:, pl.ds(to, share)], load.at[2 * e + half]))
        loads.append(pltpu.make_async_copy(
            shrink.at[e, pl.ds(pl.multiple_of(group * share, share), share), :],
            down.at[pl.ds(e * share, share), :], load.at[2 * local_exp + e]))
    for copy in loads:
        copy.start()

    def dy_copy(k):
        return pltpu.make_async_copy(dy.at[k], dys.at[lax.rem(k, 2)], dy_sem.at[lax.rem(k, 2)])

    dy_start = lambda k: dy_copy(k).start()
    dy_start(0)
    greet_lines([core, first, third, fourth])

    def rows_at(start, size):
        return pl.ds(pl.multiple_of(start, ROWS), size)

    def g_hop(k, level):
        buf = xs.at[k]
        return spread_hops(core, first, third, fourth, lambda start, size: buf.at[rows_at(start, size), :], x.at[k],
                           lambda i: g_send.at[k, i], lambda i: g_recv.at[k, i])[level]

    def s_line(k, line, at, land, offset):
        return Swap(line, at, lambda j, i: land.at[lax.rem(k, 2), j],
                    lambda j: s_send.at[k, offset + j], lambda j: s_recv.at[k, offset + j])

    def mine(k):
        return acc.at[lax.rem(k, acc_ring)]

    def s_hop(k, level):
        if level == 0:
            return s_line(k, core, lambda i: other, land_c, 0)
        if level == 1:
            return s_line(k, first, lambda i: mine(k).at[i], land_p, 1)
        if level == 2:
            return s_line(k, fourth, lambda i: mine(k).at[p, :, i], land_q, pn)
        return s_line(k, third, lambda i: mine(k).at[p, i, q], land_z, pn + qn - 1)

    def s_end(k, level):
        s_hop(k, level).finish()
        slot = lax.rem(k, 2)
        if level == 3:
            total = mine(k)[p, z, q].astype(F32)
            for j in range(zn - 1):
                total = total + land_z[slot, j].astype(F32)
            summed[k] = total.astype(BF)
            return
        if level == 0 and pn == 2:
            add(mine(k).at[1 - p], land_c.at[slot, 0, 1 - p])
            s_hop(k, 1).start()
            add(mine(k).at[p], land_c.at[slot, 0, p])
            return
        to = (mine(k), mine(k).at[p], mine(k).at[p, :, q])[level]
        land = (land_c, land_p, land_q)[level]
        for j in range(land.shape[1]):
            add(to, land.at[slot, j])
        s_hop(k, level + 1).start()

    def after(t, lag, act):
        k = t - lag

        @pl.when((k >= 0) & (k < chunks))
        def _():
            act(k)

    tiles = width // 512

    def compute(k):
        buf, dyk = xs.at[k], dys.at[lax.rem(k, 2)]

        @pl.when(k == 0)
        def _():
            for copy in loads:
                copy.wait()

        dy_copy(k).wait()

        @pl.when(k + 1 < chunks)
        def _():
            dy_start(k + 1)

        @pl.loop(0, pairs)
        def _(j):
            cols = pl.ds(pl.multiple_of(j * 4 * share, 4 * share), 4 * share)
            some = pl.ds(pl.multiple_of(j * 2 * share, 2 * share), 2 * share)
            to_up = pl.ds(pl.multiple_of(j * 4 * share + 2 * share, share), 2 * share)
            to_gate = pl.ds(pl.multiple_of(j * 4 * share, share), 2 * share)
            hid[...] = jnp.dot(buf[:, :width], wide[:, cols], preferred_element_type=F32)
            raw[...] = lax.dot_general(dyk[...], down[some, :], (((1,), (1,)), ((), ())), preferred_element_type=F32)
            gate[...] = jnp.dot(buf[:, width:], marks[:, some], preferred_element_type=F32)

            @pl.loop(0, rows // 32)
            def _(i):
                here = pl.ds(pl.multiple_of(i * 32, 32), 32)
                g, u = hid[here, : 2 * share], hid[here, 2 * share:]
                d, weight = raw[here, :], gate[here, :]
                sigma = 0.5 * jnp.tanh(0.5 * g) + 0.5
                swish = g * sigma
                act = swish * u
                product[here, some] = (act * d).astype(BF)
                gated[here, some] = (act * weight).astype(BF)
                d = d * weight
                d_gu[here, to_gate] = (d * u * (sigma + swish * (1.0 - sigma))).astype(BF)
                d_gu[here, to_up] = (d * swish).astype(BF)

        kept = mine(k)

        def split(cols, total):
            total = total.astype(BF).reshape((2,) + other.shape[:-1] + total.shape[1:])

            @pl.when(c == 0)
            def _():
                kept[..., cols] = total[0]
                other[..., cols] = total[1]

            @pl.when(c == 1)
            def _():
                other[..., cols] = total[0]
                kept[..., cols] = total[1]

        @pl.loop(0, tiles)
        def _(n):
            cols = pl.ds(pl.multiple_of(n * 512, 512), 512)
            split(cols, lax.dot_general(
                d_gu[...], wide[cols, :], (((1,), (1,)), ((), ())), preferred_element_type=F32))

        split(pl.ds(width, 128), lax.dot_general(
            product[...], marks[...], (((1,), (1,)), ((), ())), preferred_element_type=F32))
        s_hop(k, 0).start()

        @pl.when(k >= 1)
        def _():
            pltpu.make_async_copy(stage, moe.at[k - 1], stage_sem.at[0]).wait()

        @pl.loop(0, tiles)
        def _(n):
            cols = pl.ds(pl.multiple_of(n * 512, 512), 512)
            stage[:, cols] = jnp.dot(gated[...], down[:, cols], preferred_element_type=F32).astype(BF)
            sum_wide[cols, :] += lax.dot_general(
                buf[:, cols], d_gu[...], (((0,), (0,)), ((), ())), preferred_element_type=F32)
            sum_down[:, cols] += lax.dot_general(
                gated[...], dyk[:, cols], (((0,), (0,)), ((), ())), preferred_element_type=F32)

        pltpu.make_async_copy(stage, moe.at[k], stage_sem.at[0]).start()

    def begin(k):
        xs[k, rows_at(c * rc + p * rp + z * rz + q * rq, rq), :] = x[k]
        g_hop(k, 0).start()

        @pl.when(k == 0)
        def _():
            sum_wide[...] = jnp.zeros_like(sum_wide)
            sum_down[...] = jnp.zeros_like(sum_down)
            lanes = lax.broadcasted_iota(jnp.int32, marks.shape, 0)
            owner = base + lax.div(lax.broadcasted_iota(jnp.int32, marks.shape, 1), share)
            marks[...] = jnp.where((lanes == owner) | (lanes == owner + experts), 1.0, 0.0).astype(BF)

    def g_end(k, level):
        g_hop(k, level).finish()
        if level + 1 < levels:
            g_hop(k, level + 1).start()

    def wide_out(i):
        here = pl.ds(pl.multiple_of(i * rows, rows), rows)
        return pltpu.make_async_copy(d_gu, grad_widen.at[here, :], load.at[1])

    out_down = pltpu.make_async_copy(sum_down, grad_shrink, load.at[0])

    def store(i):
        @pl.when(i == 0)
        def _():
            out_down.start()

        @pl.when(i > 0)
        def _():
            wide_out(i - 1).wait()

        d_gu[...] = sum_wide[pl.ds(pl.multiple_of(i * rows, rows), rows), :].astype(BF)
        wide_out(i).start()

    @pl.loop(0, chunks + levels + 4)
    def _(t):
        for level in reversed(range(levels)):
            after(t, level + 1, functools.partial(g_end, level=level))
        after(t, 0, begin)
        for level in reversed(range(4)):
            after(t, levels + level + 1, functools.partial(s_end, level=level))
        after(t, levels, compute)

        @pl.when((t >= chunks + levels) & (t < chunks + levels + min(4, width // rows)))
        def _():
            store(t - chunks - levels)

    for i in range(4, width // rows):
        store(i)
    pltpu.make_async_copy(stage, moe.at[chunks - 1], stage_sem.at[0]).wait()
    wide_out(width // rows - 1).wait()
    out_down.wait()


def experts_together(x, dy, widen, shrink, experts, collective_id):
    groups, parts = lax.axis_size("grp"), lax.axis_size("ep")
    major, minor, xn = mesh_sizes(groups, parts)
    micro, local_rows, wide = x.shape
    x = x.reshape(-1, ROWS, wide)
    chunks = x.shape[0]
    local_exp, inner, width = shrink.shape
    share = inner // groups
    hidden = local_exp * share
    rows = 2 * ROWS * major * minor * xn
    acc_ring = 4
    legs = minor + xn - 1 + leg_count(major)
    vmem = pl.BlockSpec(memory_space=pltpu.VMEM)
    hbm = pl.BlockSpec(memory_space=pl.ANY)
    flops = 2 * chunks * rows * width * hidden * 9
    return pl.pallas_call(
        functools.partial(experts_kernel, groups, parts, local_rows, acc_ring, experts),
        out_shape=[
            jax.ShapeDtypeStruct((chunks, ROWS, wide), BF),
            jax.ShapeDtypeStruct((chunks, rows, width), BF),
            jax.ShapeDtypeStruct((width, 2 * hidden), BF),
            jax.ShapeDtypeStruct((hidden, width), F32),
        ],
        in_specs=[vmem, hbm, hbm, hbm],
        out_specs=[vmem, hbm, hbm, hbm],
        scratch_shapes=[
            pltpu.VMEM((chunks, rows, wide), BF),
            pltpu.VMEM((2, rows, width), BF),
            pltpu.VMEM((width, 2 * hidden), BF),
            pltpu.VMEM((hidden, width), BF),
            pltpu.VMEM((width, 2 * hidden), F32),
            pltpu.VMEM((hidden, width), F32),
            pltpu.VMEM((rows, width), BF),
            pltpu.VMEM((acc_ring, xn, major, minor, ROWS, wide), BF),
            pltpu.VMEM((xn, major, minor, ROWS, wide), BF),
            pltpu.VMEM((2, 1, xn, major, minor, ROWS, wide), BF),
            pltpu.VMEM((2, xn - 1, major, minor, ROWS, wide), BF),
            pltpu.VMEM((2, minor - 1, major, ROWS, wide), BF),
            pltpu.VMEM((2, major - 1, ROWS, wide), BF),
            pltpu.VMEM((rows, 4 * share), F32),
            pltpu.VMEM((rows, 2 * share), F32),
            pltpu.VMEM((rows, hidden), BF),
            pltpu.VMEM((rows, 2 * hidden), BF),
            pltpu.VMEM((rows, 2 * share), F32),
            pltpu.VMEM((rows, hidden), BF),
            pltpu.VMEM((128, hidden), BF),
            pltpu.SemaphoreType.DMA((3 * local_exp,)),
            pltpu.SemaphoreType.DMA((2,)),
            pltpu.SemaphoreType.DMA((2,)),
            pltpu.SemaphoreType.DMA((chunks, legs)),
            pltpu.SemaphoreType.DMA((chunks, legs)),
            pltpu.SemaphoreType.DMA((chunks, legs)),
            pltpu.SemaphoreType.DMA((chunks, legs)),
        ],
        compiler_params=pltpu.CompilerParams(
            collective_id=collective_id, has_side_effects=True, vmem_limit_bytes=63 * 2**20
        ),
        cost_estimate=pl.CostEstimate(flops=flops, bytes_accessed=80 * 2**20, transcendentals=chunks * rows * hidden),
    )(x, dy, widen, shrink)


def experts_apart(x, dy_all, specialist_widen_matrix, specialist_shrink_matrix, experts):
    groups, parts = lax.axis_size("grp"), lax.axis_size("ep")
    group, part = lax.axis_index("grp"), lax.axis_index("ep")
    local_exp, inner, width = specialist_shrink_matrix.shape
    share = inner // groups
    widen = specialist_widen_matrix.reshape(local_exp, width, 2, groups, share)
    widen = lax.dynamic_index_in_dim(widen, group, 3, keepdims=False)
    widen = widen.transpose(1, 2, 0, 3).reshape(width, 2 * local_exp * share)
    shrink = specialist_shrink_matrix.reshape(local_exp, groups, share, width)
    shrink = lax.dynamic_index_in_dim(shrink, group, 1, keepdims=False).reshape(local_exp * share, width)
    x_all = gather_all(x, 1)
    chunk_shape = x_all.shape[:-1]
    x_all, dy_all = x_all.reshape(-1, width + 128), dy_all.reshape(-1, width)
    gate = x_all[:, width: width + experts].astype(F32) + x_all[:, width + experts: width + 2 * experts].astype(F32)
    x_all = x_all[:, :width]
    gate = lax.dynamic_slice_in_dim(gate, part * local_exp, local_exp, axis=1)
    gate = jnp.repeat(gate, share, axis=1)
    gate_up = jnp.dot(x_all, widen, preferred_element_type=F32)
    g, u = gate_up[:, : local_exp * share], gate_up[:, local_exp * share:]
    sigma = jax.nn.sigmoid(g)
    act = g * sigma * u
    gated = (gate * act).astype(BF)
    moe_part = jnp.dot(gated, shrink, preferred_element_type=F32).astype(BF)
    d_raw = lax.dot_general(dy_all, shrink, (((1,), (1,)), ((), ())), preferred_element_type=F32)
    d_gate = jnp.sum((act * d_raw).reshape(-1, local_exp, share), axis=-1)
    d_act = gate * d_raw
    d_gu = jnp.concatenate([d_act * u * sigma * (1.0 + g * (1.0 - sigma)), d_act * (g * sigma)], axis=1).astype(BF)
    dx_part = lax.dot_general(d_gu, widen, (((1,), (1,)), ((), ())), preferred_element_type=F32).astype(BF)
    lanes = jnp.arange(128, dtype=jnp.int32)
    place = (lanes[None, :] == part * local_exp + jnp.arange(local_exp, dtype=jnp.int32)[:, None])
    d_gate = jnp.sum(jnp.where(place[None], d_gate[:, :, None], 0.0), axis=1)
    dx_part = jnp.concatenate([dx_part, d_gate.astype(BF)], axis=1)
    dx_sum = scatter_all(dx_part.reshape(chunk_shape + (width + 128,)), 2)
    grad_widen = lax.dot_general(x_all, d_gu, (((0,), (0,)), ((), ())), preferred_element_type=F32)
    grad_shrink = lax.dot_general(gated, dy_all, (((0,), (0,)), ((), ())), preferred_element_type=F32)
    grad_widen = grad_widen.astype(BF).reshape(width, 2, local_exp // 2, 2, share).transpose(0, 2, 1, 3, 4)
    return dx_sum, moe_part.reshape(chunk_shape + (width,)), grad_widen, grad_shrink


def finish_kernel(share, qkv, out, wide, shrink, qkv_to, out_to, wide_to, shrink_to):
    qkv_to[...] = qkv[...].astype(F32)
    out_to[...] = out[...].astype(F32)
    shrink_to[...] = shrink[...]
    for i in range(wide.shape[0]):
        wide_to[0, :, i * share: (i + 1) * share] = wide[i].astype(F32)


def finish(qkv, out, wide, shrink, local_exp, share):
    groups, rows, _ = wide.shape
    whole = (local_exp, rows, 2 * groups * share)
    if share % 128:
        wide = wide.reshape(groups, rows, local_exp // 2, 2, 2, share).transpose(2, 4, 1, 3, 0, 5)
        return qkv.astype(F32), out.astype(F32), wide.reshape(whole).astype(F32), shrink
    steps = 2 * local_exp
    cut = lambda a: pl.BlockSpec((a.shape[0] // (2 * steps), a.shape[1]), lambda i, j: (2 * i + j, 0))
    outs = [jax.ShapeDtypeStruct(a.shape, F32) for a in (qkv, out)] + [
        jax.ShapeDtypeStruct(whole, F32), jax.ShapeDtypeStruct(shrink.shape, F32)]
    return pl.pallas_call(
        functools.partial(finish_kernel, share),
        grid=(steps, 2),
        out_shape=outs,
        in_specs=[cut(qkv), cut(out),
                  pl.BlockSpec((groups, rows // 2, share), lambda i, j: (0, j, i // 4 * 4 + i % 2 * 2 + i // 2 % 2)), cut(shrink)],
        out_specs=[cut(qkv), cut(out),
                   pl.BlockSpec((1, rows // 2, groups * share), lambda i, j: (i // 2, j, i % 2)), cut(shrink)],
        compiler_params=pltpu.CompilerParams(vmem_limit_bytes=40 * 2**20),
    )(qkv, out, wide, shrink)


class Backdrop:
    PACE = 2

    def __init__(self, groups, parts, part, out, acc, land_c, land_p, land_q, land_z, local, send, recv):
        self.core, self.first, self.third, self.fourth = lines(groups, parts)
        self.part, self.out, self.acc, self.lands = part, out, acc, (land_c, land_p, land_q)
        self.land_z = land_z
        self.local, self.send, self.recv = local, send, recv
        self.chunks = part.shape[0]
        self.levels = 3 + hop_count(self.third.size)
        self.lag = self.PACE * self.levels

    @staticmethod
    def scratch(chunks, width):
        major, minor, xn = mesh_sizes(lax.axis_size("grp"), lax.axis_size("ep"))
        legs = minor + xn - 1 + leg_count(major)
        return [
            pltpu.VMEM((chunks, xn, major, minor, ROWS, width), BF),
            pltpu.VMEM((4, 1, xn, major, minor, ROWS, width), BF),
            pltpu.VMEM((4, xn - 1, major, minor, ROWS, width), BF),
            pltpu.VMEM((4, minor - 1, major, ROWS, width), BF),
            pltpu.VMEM((chunks, leg_count(major), ROWS, width), BF),
            pltpu.SemaphoreType.DMA((chunks,)),
            pltpu.SemaphoreType.DMA((chunks, legs)),
            pltpu.SemaphoreType.DMA((chunks, legs)),
        ]

    def near(self):
        return [self.core, self.first, self.third, self.fourth]

    def own(self, k):
        return pltpu.make_async_copy(self.part.at[k, self.core.place], self.acc.at[k], self.local.at[k])

    def hop(self, k, level):
        p, q = self.first.place, self.fourth.place
        pn, qn = self.first.size, self.fourth.size
        if level >= 3:
            offset = pn + qn - 1
            land = self.land_z.at[k]
            return reduce_hops(self.third, lambda i: self.acc.at[k, p, i, q], lambda i: land.at[i], add,
                               lambda i: self.send.at[k, offset + i], lambda i: self.recv.at[k, offset + i])[level - 3]
        line, offset, source = [
            (self.core, 0, lambda i: self.part.at[k, i]),
            (self.first, 1, lambda i: self.acc.at[k, i]),
            (self.fourth, pn, lambda i: self.acc.at[k, p, :, i]),
        ][level]
        land = self.lands[level]
        return Swap(line, source, lambda j, i: land.at[lax.rem(k, 4), j],
                    lambda j: self.send.at[k, offset + j], lambda j: self.recv.at[k, offset + j])

    def end(self, k, level):
        p, q, z = self.first.place, self.fourth.place, self.third.place
        self.hop(k, level).finish()
        if level + 1 == self.levels:
            self.out[k] = self.acc[k, p, z, q]
            return
        after = self.hop(k, level + 1)
        if level == 0:
            self.own(k).wait()
            if self.first.size == 2:
                add(self.acc.at[k, 1 - p], self.lands[0].at[lax.rem(k, 4), 0, 1 - p])
                after.start()
                add(self.acc.at[k, p], self.lands[0].at[lax.rem(k, 4), 0, p])
                return
            add(self.acc.at[k], self.lands[0].at[lax.rem(k, 4), 0])
        elif level < 3:
            to = self.acc.at[k, p] if level == 1 else self.acc.at[k, p, :, q]
            for j in range(self.lands[level].shape[1]):
                add(to, self.lands[level].at[lax.rem(k, 4), j])
        after.start()

    def begin(self, k):
        self.hop(k, 0).start()
        self.own(k).start()

    def step(self, t):
        for level in reversed(range(self.levels)):
            k = t - self.PACE * (level + 1)

            @pl.when((k >= 0) & (k < self.chunks))
            def _(k=k, level=level):
                self.end(k, level)

        @pl.when((t >= 0) & (t < self.chunks))
        def _():
            self.begin(t)


class Sequence:
    def __init__(self, parts, block, micro):
        e = lax.axis_index("ep")
        self.xn, self.block, self.micro, self.e = parts // 2, block, micro, e
        self.x, self.c = lax.div(e, 2), lax.rem(e, 2)
        self.line = Line(parts, e, (0, 1))
        self.line_x = Line(self.xn, self.x, (0, 2))
        self.line_c = Line(2, self.c, (0, 1))

    def at(self, ref, m, x, c):
        return ref.at[m, pl.ds(pl.multiple_of((x * 2 + c) * self.block, self.block), self.block), :]

    def gather_x(self, ref, send, recv):
        legs = []
        for m in range(self.micro):
            legs += swap_legs(
                self.line_x, lambda i, m=m: self.at(ref, m, self.x, self.c), lambda j, i, m=m: self.at(ref, m, i, self.c),
                lambda j, m=m: send.at[m, j], lambda j, m=m: recv.at[m, j])
        return legs

    def gather_c(self, ref, send, recv):
        legs = []
        for m in range(self.micro):
            for x in range(self.xn):
                legs += swap_legs(
                    self.line_c, lambda i, m=m, x=x: self.at(ref, m, x, self.c), lambda j, i, m=m, x=x: self.at(ref, m, x, i),
                    lambda j, m=m, x=x: send.at[m, self.xn - 1 + x], lambda j, m=m, x=x: recv.at[m, self.xn - 1 + x])
        return legs

    def reduce_c(self, ref, land, send, recv):
        legs = []
        for m in range(self.micro):
            for x in range(self.xn):
                legs += swap_legs(
                    self.line_c, lambda i, m=m, x=x: self.at(ref, m, x, i), lambda j, i, m=m, x=x: land.at[m, x],
                    lambda j, m=m, x=x: send.at[m, self.xn - 1 + x], lambda j, m=m, x=x: recv.at[m, self.xn - 1 + x])
        return legs

    def reduce_x(self, ref, land, send, recv):
        legs = []
        for m in range(self.micro):
            legs += swap_legs(
                self.line_x, lambda i, m=m: self.at(ref, m, i, self.c), lambda j, i, m=m: land.at[m, j],
                lambda j, m=m: send.at[m, j], lambda j, m=m: recv.at[m, j])
        return legs

    def add_c(self, ref, land):
        for m in range(self.micro):
            for x in range(self.xn):
                add_rows(ref.at[m], (x * 2 + self.c) * self.block, land.at[m, x], self.block)

    def total_x(self, ref, land, out):
        for m in range(self.micro):
            @pl.loop(0, self.block // ROWS)
            def _(i, m=m):
                here = pl.ds(pl.multiple_of(i * ROWS, ROWS), ROWS)
                total = ref[m, pl.ds(pl.multiple_of(self.e * self.block + i * ROWS, ROWS), ROWS), :].astype(F32)
                for j in range(self.xn - 1):
                    total = total + land[m, j, here, :].astype(F32)
                out[m, here, :] = total


def sum_over_parts(seq, columns, sent, got, send, recv, meanwhile):
    flat = columns.T
    sent[...] = flat[:8]
    legs = swap_legs(seq.line, lambda i: sent, lambda j, i: got.at[j], lambda j: send.at[j], lambda j: recv.at[j])
    start_legs(legs)
    meanwhile()
    end_legs(legs)
    total = sent[...]
    for j in range(seq.line.size - 1):
        total = total + got[j]
    return jnp.concatenate([total] * 16, axis=0).T


def back_kernel(
    groups, parts, backed,
    branch, merge, triple, queries, keys, values, mixed, probs, hat, inv, gains_in, cos, sin, wide, part,
    d_proj, d_in, grad_heads, grad_out, wide_all, summed,
    gains, rows_all, merge_v, triple_v, q_v, k_v, v_v, mixed_v, probs_v, hat_v, d_mixed, d_qk, sums, partial, land_c, land_x, sent, got,
    load, g_send, g_recv, s_send, s_recv, t_send, t_recv, w_send, w_recv, *behind
):
    micro, block, width = branch.shape
    seq = Sequence(parts, block, micro)
    length = queries.shape[1]
    tokens = micro * length
    heads = queries.shape[2] // HD
    scale = 1.0 / math.sqrt(HD)
    loads = [pltpu.make_async_copy(a, b, load.at[i]) for i, (a, b) in enumerate((
        (merge, merge_v), (mixed, mixed_v), (queries, q_v), (keys, k_v), (values, v_v), (probs, probs_v), (hat, hat_v), (triple, triple_v)))]
    for copy in loads:
        copy.start()
    gains[...] = gains_in[...].astype(F32)
    over = Line(groups, lax.axis_index("grp"), (1, 0))
    if backed:
        back = Backdrop(groups, parts, part, summed, *behind)
        greet_lines([seq.line, over] + back.near())
        steps = back.chunks + back.lag
        behind_step = back.step
    else:
        greet_lines([seq.line, over])
        steps, behind_step = 0, lambda t: None
        summed[...] = jnp.zeros_like(summed)
    for m in range(micro):
        rows_all[m, pl.ds(pl.multiple_of(seq.e * block, block), block), :] = branch[m]
    gather_x = seq.gather_x(rows_all, g_send, g_recv)
    start_legs(gather_x)
    g = over.place
    own_wide = pltpu.make_async_copy(wide.at[g], wide_all.at[g], load.at[8])
    own_wide.start()
    turn = swap_legs(over, lambda i: wide.at[i], lambda j, i: wide_all.at[i], lambda j: w_send.at[j], lambda j: w_recv.at[j])
    pieces = CUTS * (groups - 1)
    tall = wide.shape[1] // CUTS

    def step(t):
        for u in range(PER_STEP):
            i = t * PER_STEP + u

            @pl.when((i >= 0) & (i < pieces))
            def _(i=i):
                j, cut = lax.rem(i, groups - 1), lax.div(i, groups - 1)
                to = lax.rem(g + 1 + j, groups)
                here = pl.ds(pl.multiple_of(cut * tall, ROWS), tall)
                remote(wide.at[to, here, :], wide_all.at[g, here, :], w_send.at[j], w_recv.at[j], over.at(to - g)).start()

        behind_step(t)

    step(0)
    step(1)
    step(2)
    end_legs(gather_x)
    gather_c = seq.gather_c(rows_all, g_send, g_recv)
    start_legs(gather_c)
    step(3)
    sums[...] = jnp.zeros_like(sums)
    grad_heads[...] = jnp.zeros_like(grad_heads)
    end_legs(gather_c)
    for copy in loads[:2]:
        copy.wait()
    for m in range(micro):
        d_mixed[m] = lax.dot_general(rows_all[m], merge_v[...], (((1,), (1,)), ((), ())), preferred_element_type=F32).astype(BF)
    step(4)

    @pl.loop(0, width // 512)
    def _(n):
        cols = pl.ds(pl.multiple_of(n * 512, 512), 512)
        total = lax.dot_general(mixed_v[0], rows_all[0, :, cols], (((0,), (0,)), ((), ())), preferred_element_type=F32)
        for m in range(1, micro):
            total = total + lax.dot_general(
                mixed_v[m], rows_all[m, :, cols], (((0,), (0,)), ((), ())), preferred_element_type=F32)
        grad_out[:, cols] = total.astype(BF)

    step(5)
    for copy in loads[2:7]:
        copy.wait()
    lane = lax.broadcasted_iota(jnp.int32, (1, 128), 1)

    def one_head(i):
        m, h = lax.div(i, heads), lax.rem(i, heads)
        cols = pl.ds(pl.multiple_of(h * HD, HD), HD)
        here = pl.ds(pl.multiple_of(m * length, length), length)
        d_m = d_mixed[m, :, cols]
        weights = probs_v[m, h]
        low = weights.astype(BF)
        d_proj[2, here, cols] = lax.dot_general(low, d_m, (((0,), (0,)), ((), ())), preferred_element_type=F32).astype(BF)
        d_w = lax.dot_general(d_m, v_v[m, :, cols], (((1,), (1,)), ((), ())), preferred_element_type=F32)
        d_s = (weights * (d_w - jnp.sum(weights * d_w, axis=-1, keepdims=True))).astype(BF)
        d_q = jnp.dot(d_s, k_v[m, :, cols], preferred_element_type=F32) * scale
        d_k = lax.dot_general(d_s, q_v[m, :, cols], (((0,), (0,)), ((), ())), preferred_element_type=F32) * scale
        marks = sums[here, :]
        for c, d in enumerate((d_q, d_k)):
            d = d * cos[...] - pltpu.roll(d, HD // 2, 1) * sin[...]
            d_qk[c, here, cols] = d
            product = d * hat_v[c, here, cols]
            grad_heads[c: c + 1, cols] += jnp.sum(product, axis=0, keepdims=True)
            marks = marks + jnp.where(lane == c, jnp.sum(product * gains[c: c + 1, cols], axis=-1, keepdims=True), 0.0)
        sums[here, :] = marks

    @pl.loop(0, micro * heads)
    def _(i):
        one_head(i)
        step(i + 6)

    done = 7 + micro * heads
    sums[...] = sum_over_parts(seq, sums[...], sent, got, t_send, t_recv, lambda: step(done - 1))

    @pl.loop(0, tokens // 64)
    def _(i):
        here = pl.ds(pl.multiple_of(i * 64, 64), 64)
        for c in range(2):
            inner = sums[here, c: c + 1] * (1.0 / width)
            d_proj[c, here, :] = (inv[here, c: c + 1] * (
                d_qk[c, here, :] * gains[c: c + 1, :] - hat_v[c, here, :] * inner)).astype(BF)

    loads[7].wait()

    @pl.loop(0, width // 512)
    def _(n):
        cols = pl.ds(pl.multiple_of(n * 512, 512), 512)
        for m in range(micro):
            here = pl.ds(m * length, length)
            total = lax.dot_general(d_proj[0, here, :], triple_v[0, cols, :], (((1,), (1,)), ((), ())), preferred_element_type=F32)
            for c in (1, 2):
                total = total + lax.dot_general(
                    d_proj[c, here, :], triple_v[c, cols, :], (((1,), (1,)), ((), ())), preferred_element_type=F32)
            partial[m, :, cols] = total.astype(BF)

    reduce_c = seq.reduce_c(partial, land_c, s_send, s_recv)
    start_legs(reduce_c)
    step(done)
    end_legs(reduce_c)
    seq.add_c(partial, land_c)
    reduce_x = seq.reduce_x(partial, land_x, s_send, s_recv)
    start_legs(reduce_x)
    step(done + 1)
    end_legs(reduce_x)
    seq.total_x(partial, land_x, d_in)
    for t in range(done + 2, max(steps, -(-pieces // PER_STEP))):
        step(t)
    end_legs(turn)
    own_wide.wait()


def attention_back(branch, merge, triple, queries, keys, values, mixed, probs, hat, inv, gains, cos, sin, wide, part, collective_id):
    groups, parts = lax.axis_size("grp"), lax.axis_size("ep")
    micro, block, width = branch.shape
    length, local_width = queries.shape[1:]
    tokens = micro * length
    backed = part is not None
    behind = Backdrop.scratch(part.shape[0], width) if backed else []
    summed = (part.shape[0], ROWS, width) if backed else (8, 128)
    vmem = pl.BlockSpec(memory_space=pltpu.VMEM)
    hbm = pl.BlockSpec(memory_space=pl.ANY)
    xn = parts // 2
    return pl.pallas_call(
        functools.partial(back_kernel, groups, parts, backed),
        out_shape=[
            jax.ShapeDtypeStruct((3, tokens, local_width), BF),
            jax.ShapeDtypeStruct((micro, block, width), F32),
            jax.ShapeDtypeStruct((8, local_width), F32),
            jax.ShapeDtypeStruct((local_width, width), BF),
            jax.ShapeDtypeStruct(wide.shape, BF),
            jax.ShapeDtypeStruct(summed, BF if backed else F32),
        ],
        in_specs=[vmem] + [hbm] * 8 + [vmem] * 4 + [hbm] * 2,
        out_specs=[vmem] * 4 + [hbm, vmem],
        scratch_shapes=[
            pltpu.VMEM(gains.shape, F32),
            pltpu.VMEM((micro, length, width), BF),
            pltpu.VMEM(merge.shape, BF),
            pltpu.VMEM(triple.shape, BF),
            pltpu.VMEM(queries.shape, BF),
            pltpu.VMEM(queries.shape, BF),
            pltpu.VMEM(queries.shape, BF),
            pltpu.VMEM(queries.shape, BF),
            pltpu.VMEM(probs.shape, F32),
            pltpu.VMEM(hat.shape, F32),
            pltpu.VMEM(queries.shape, BF),
            pltpu.VMEM((2, tokens, local_width), F32),
            pltpu.VMEM((tokens, 128), F32),
            pltpu.VMEM((micro, length, width), BF),
            pltpu.VMEM((micro, xn, block, width), BF),
            pltpu.VMEM((micro, xn - 1, block, width), BF),
            pltpu.VMEM((8, tokens), F32),
            pltpu.VMEM((parts - 1, 8, tokens), F32),
            pltpu.SemaphoreType.DMA((9,)),
            pltpu.SemaphoreType.DMA((micro, 2 * xn - 1)),
            pltpu.SemaphoreType.DMA((micro, 2 * xn - 1)),
            pltpu.SemaphoreType.DMA((micro, 2 * xn - 1)),
            pltpu.SemaphoreType.DMA((micro, 2 * xn - 1)),
            pltpu.SemaphoreType.DMA((parts - 1,)),
            pltpu.SemaphoreType.DMA((parts - 1,)),
            pltpu.SemaphoreType.DMA((groups - 1,)),
            pltpu.SemaphoreType.DMA((groups - 1,)),
        ] + behind,
        compiler_params=pltpu.CompilerParams(
            collective_id=collective_id, has_side_effects=True, vmem_limit_bytes=58 * 2**20
        ),
        cost_estimate=pl.CostEstimate(flops=10**10, bytes_accessed=40 * 2**20, transcendentals=0),
    )(branch, merge, triple, queries, keys, values, mixed, probs, hat, inv, gains, cos, sin, wide,
      part if backed else mixed)


class BackGather:
    PACE = 3

    def __init__(self, groups, parts, own, out, local, send, recv):
        self.lines = lines(groups, parts)
        self.own, self.out, self.local, self.send, self.recv = own, out, local, send, recv
        self.chunks = own.shape[0]
        self.levels = 4
        self.lag = self.PACE * self.levels

    @staticmethod
    def scratch(chunks):
        major, minor, xn = mesh_sizes(lax.axis_size("grp"), lax.axis_size("ep"))
        legs = minor + xn + major - 2
        return [
            pltpu.SemaphoreType.DMA((chunks,)),
            pltpu.SemaphoreType.DMA((chunks, legs)),
            pltpu.SemaphoreType.DMA((chunks, legs)),
        ]

    def near(self):
        return list(self.lines)

    def mine(self, k):
        return pltpu.make_async_copy(
            self.own.at[k], self.out.at[(k,) + tuple(line.place for line in self.lines)], self.local.at[k])

    def hop(self, k, level):
        core, first, third, fourth = self.lines
        c, p, q = core.place, first.place, fourth.place
        line, offset, at = [
            (third, 0, lambda i: self.out.at[k, c, p, i, q]),
            (fourth, third.size - 1, lambda i: self.out.at[k, c, p, :, i]),
            (first, third.size + fourth.size - 2, lambda i: self.out.at[k, c, i]),
            (core, third.size + fourth.size + first.size - 3, lambda i: self.out.at[k, i]),
        ][level]
        source = (lambda i: self.own.at[k]) if level == 0 else (lambda i: at(line.place))
        return Swap(line, source, lambda j, i: at(i),
                    lambda j: self.send.at[k, offset + j], lambda j: self.recv.at[k, offset + j])

    def step(self, t):
        for level in reversed(range(self.levels)):
            k = t - self.PACE * (level + 1)

            @pl.when((k >= 0) & (k < self.chunks))
            def _(k=k, level=level):
                self.hop(k, level).finish()
                if level == 0:
                    self.mine(k).wait()
                if level + 1 < self.levels:
                    self.hop(k, level + 1).start()

        @pl.when((t >= 0) & (t < self.chunks))
        def _():
            self.mine(t).start()
            self.hop(t, 0).start()


def forward_kernel(
    groups, parts, experts,
    x, dy, routes, quota, gains_in, head_gains_in, cos, sin, docs, dispatch_in, triple, merge,
    gathered, q_out, k_out, v_out, mixed, probs, hat, inv, hidden, ffn_in, router, dy_all,
    kept, gains, head_gains, docs_down, dispatch, triple_v, merge_v, sums, partial, land_c, land_x, sent, got,
    load, g_send, g_recv, s_send, s_recv, t_send, t_recv, *behind
):
    micro, block, width = x.shape
    seq = Sequence(parts, block, micro)
    length = gathered.shape[1]
    tokens = micro * length
    heads = q_out.shape[2] // HD
    scale = 1.0 / math.sqrt(HD)
    cuts = block // ROWS
    loads = [pltpu.make_async_copy(triple, triple_v, load.at[0]), pltpu.make_async_copy(merge, merge_v, load.at[1])]
    for copy in loads:
        copy.start()
    back = BackGather(groups, parts, dy, dy_all, *behind)
    step, steps = back.step, back.chunks + back.lag
    gains[...] = gains_in[...].astype(F32)
    head_gains[...] = head_gains_in[...].astype(F32)
    lane = lax.broadcasted_iota(jnp.int32, (1, 128), 1)
    earlier = (lax.broadcasted_iota(jnp.int32, (block, block), 1) < lax.broadcasted_iota(jnp.int32, (block, block), 0))
    for m in range(micro):
        @pl.loop(0, cuts)
        def _(r, m=m):
            here = pl.ds(pl.multiple_of(r * ROWS, ROWS), ROWS)
            v = x[m, here, :].astype(F32)
            v = v * lax.rsqrt(jnp.mean(v * v, axis=-1, keepdims=True) + EPS)
            gathered[m, pl.ds(pl.multiple_of(seq.e * block + r * ROWS, ROWS), ROWS), :] = (v * gains[0:1, :]).astype(BF)
    greet_lines([seq.line] + back.near())
    gather_x = seq.gather_x(gathered, g_send, g_recv)
    start_legs(gather_x)
    step(0)
    limits = jnp.concatenate([quota[...], jnp.zeros((1, 128 - experts), jnp.int32)], axis=1).astype(F32)
    dispatch[...] = jnp.zeros_like(dispatch)
    dispatch[:experts, :] = dispatch_in[...]
    for m in range(micro):
        chosen = jnp.zeros((128, block), F32)
        for j in range(TOP):
            chosen = chosen + jnp.where(routes[m, j: j + 1, :] == lax.broadcasted_iota(jnp.int32, (128, 1), 0), 1.0, 0.0)
        counts = chosen.T
        prior = jnp.dot(jnp.where(earlier, 1.0, 0.0).astype(BF), counts.astype(BF), preferred_element_type=F32)
        kept[m] = jnp.where((counts > 0.0) & (prior < limits), 1.0, 0.0)
        docs_down[m] = jnp.broadcast_to(docs[m: m + 1, :], (128, length)).astype(F32).T
    step(1)
    step(2)
    end_legs(gather_x)
    gather_c = seq.gather_c(gathered, g_send, g_recv)
    start_legs(gather_c)
    step(3)
    loads[0].wait()
    end_legs(gather_c)

    @pl.loop(0, micro)
    def _(m):
        here = pl.ds(pl.multiple_of(m * length, length), length)
        marks = jnp.zeros((length, 128), F32)
        for c in range(2):
            raw = jnp.dot(gathered[m], triple_v[c], preferred_element_type=F32)
            hat[c, here, :] = raw
            marks = marks + jnp.where(lane == c, jnp.sum(raw * raw, axis=-1, keepdims=True), 0.0)
        sums[here, :] = marks
        v_out[m] = jnp.dot(gathered[m], triple_v[2], preferred_element_type=F32).astype(BF)
        step(m + 4)

    done = micro + 5
    squares = sum_over_parts(seq, sums[...], sent, got, t_send, t_recv, lambda: step(done - 1))
    inv[...] = lax.rsqrt(squares * (1.0 / width) + EPS)
    loads[1].wait()

    @pl.loop(0, micro * heads)
    def _(i):
        m, h = lax.div(i, heads), lax.rem(i, heads)
        cols = pl.ds(pl.multiple_of(h * HD, HD), HD)
        here = pl.ds(pl.multiple_of(m * length, length), length)
        for c, to in enumerate((q_out, k_out)):
            v = hat[c, here, cols] * inv[here, c: c + 1]
            hat[c, here, cols] = v
            v = v * head_gains[c: c + 1, cols]
            to[m, :, cols] = (v * cos[...] + pltpu.roll(v, HD // 2, 1) * sin[...]).astype(BF)
        scores = lax.dot_general(
            q_out[m, :, cols], k_out[m, :, cols], (((1,), (1,)), ((), ())), preferred_element_type=F32) * scale
        allowed = (docs_down[m][:, :1] == docs[pl.ds(m, 1), :].astype(F32)) & (
            lax.broadcasted_iota(jnp.int32, (length, length), 1) <= lax.broadcasted_iota(jnp.int32, (length, length), 0))
        scores = jnp.where(allowed, scores, NEG)
        grown = jnp.exp(scores - jnp.max(scores, axis=-1, keepdims=True))
        weights = grown / jnp.sum(grown, axis=-1, keepdims=True)
        probs[m, h] = weights
        mixed[m, :, cols] = jnp.dot(weights.astype(BF), v_out[m, :, cols], preferred_element_type=F32).astype(BF)
        step(done + i)

    done = done + micro * heads

    @pl.loop(0, width // 512)
    def _(n):
        cols = pl.ds(pl.multiple_of(n * 512, 512), 512)
        for m in range(micro):
            partial[m, :, cols] = jnp.dot(mixed[m], merge_v[:, cols], preferred_element_type=F32).astype(BF)

    reduce_c = seq.reduce_c(partial, land_c, s_send, s_recv)
    start_legs(reduce_c)
    step(done)
    end_legs(reduce_c)
    seq.add_c(partial, land_c)
    reduce_x = seq.reduce_x(partial, land_x, s_send, s_recv)
    start_legs(reduce_x)
    step(done + 1)
    end_legs(reduce_x)
    seq.total_x(partial, land_x, hidden)
    for m in range(micro):
        @pl.loop(0, cuts)
        def _(r, m=m):
            here = pl.ds(pl.multiple_of(r * ROWS, ROWS), ROWS)
            v = hidden[m, here, :] + x[m, here, :].astype(F32)
            hidden[m, here, :] = v
            v = v * lax.rsqrt(jnp.mean(v * v, axis=-1, keepdims=True) + EPS)
            ffn_in[m, here, :width] = (v * gains[1:2, :]).astype(BF)
        logits = lax.dot_general(
            ffn_in[m, :, :width], dispatch[...], (((1,), (1,)), ((), ())), preferred_element_type=F32)
        logits = jnp.where(lane < experts, logits, NEG)
        grown = jnp.exp(logits - jnp.max(logits, axis=-1, keepdims=True))
        grown = grown / jnp.sum(grown, axis=-1, keepdims=True)
        gate = grown * kept[m]
        router[m] = grown + pltpu.roll(kept[m], experts, 1)
        head = gate.astype(BF).astype(F32)
        ffn_in[m, :, width:] = (head + pltpu.roll(gate - head, experts, 1)).astype(BF)
    for t in range(done + 2, steps):
        step(t)


def attention_forward(x, dy, routes, quota, gains, head_gains, cos, sin, docs, dispatch, triple, merge, collective_id):
    groups, parts = lax.axis_size("grp"), lax.axis_size("ep")
    major, minor, xn = mesh_sizes(groups, parts)
    micro, block, width = x.shape
    length = docs.shape[1]
    local_width = triple.shape[2]
    heads = local_width // HD
    tokens = micro * length
    chunks = micro * block // ROWS
    vmem = pl.BlockSpec(memory_space=pltpu.VMEM)
    hbm = pl.BlockSpec(memory_space=pl.ANY)
    low = jax.ShapeDtypeStruct((micro, length, local_width), BF)
    experts = dispatch.shape[1]
    return pl.pallas_call(
        functools.partial(forward_kernel, groups, parts, experts),
        out_shape=[
            jax.ShapeDtypeStruct((micro, length, width), BF),
            low, low, low, low,
            jax.ShapeDtypeStruct((micro, heads, length, length), F32),
            jax.ShapeDtypeStruct((2, tokens, local_width), F32),
            jax.ShapeDtypeStruct((tokens, 128), F32),
            jax.ShapeDtypeStruct((micro, block, width), F32),
            jax.ShapeDtypeStruct((micro, block, width + 128), BF),
            jax.ShapeDtypeStruct((micro, block, 128), F32),
            jax.ShapeDtypeStruct((chunks, 2, xn, major, minor, ROWS, width), BF),
        ],
        in_specs=[vmem] * 10 + [hbm] * 2,
        out_specs=[vmem] * 11 + [hbm],
        scratch_shapes=[
            pltpu.VMEM((micro, block, 128), F32),
            pltpu.VMEM(gains.shape, F32),
            pltpu.VMEM(head_gains.shape, F32),
            pltpu.VMEM((micro, length, 128), F32),
            pltpu.VMEM((128, width), BF),
            pltpu.VMEM(triple.shape, BF),
            pltpu.VMEM(merge.shape, BF),
            pltpu.VMEM((tokens, 128), F32),
            pltpu.VMEM((micro, length, width), BF),
            pltpu.VMEM((micro, xn, block, width), BF),
            pltpu.VMEM((micro, xn - 1, block, width), BF),
            pltpu.VMEM((8, tokens), F32),
            pltpu.VMEM((parts - 1, 8, tokens), F32),
            pltpu.SemaphoreType.DMA((2,)),
            pltpu.SemaphoreType.DMA((micro, 2 * xn - 1)),
            pltpu.SemaphoreType.DMA((micro, 2 * xn - 1)),
            pltpu.SemaphoreType.DMA((micro, 2 * xn - 1)),
            pltpu.SemaphoreType.DMA((micro, 2 * xn - 1)),
            pltpu.SemaphoreType.DMA((parts - 1,)),
            pltpu.SemaphoreType.DMA((parts - 1,)),
        ] + BackGather.scratch(chunks),
        compiler_params=pltpu.CompilerParams(
            collective_id=collective_id, has_side_effects=True, vmem_limit_bytes=56 * 2**20
        ),
        cost_estimate=pl.CostEstimate(flops=6 * 10**9, bytes_accessed=40 * 2**20, transcendentals=0),
    )(x, dy.reshape(chunks, ROWS, width), routes.transpose(0, 2, 1), quota.reshape(1, -1), gains, head_gains, cos, sin, docs,
      dispatch.T, triple, merge)


def per_device(
    block_entry_states,
    document_labels,
    token_assignments,
    worker_quota_tallies,
    rescale_factors_both,
    triple_projection_matrix,
    probe_lookup_scalers,
    heads_merge_matrix,
    dispatcher_matrix,
    specialist_widen_matrix,
    specialist_shrink_matrix,
    output_gradient,
):
    micro, local_rows, width = block_entry_states.shape
    groups, parts = lax.axis_size("grp"), lax.axis_size("ep")
    major, minor, xs = mesh_sizes(groups, parts)
    group = lax.axis_index("grp")
    part = lax.axis_index("ep")
    seq_len = document_labels.shape[1]
    experts = dispatcher_matrix.shape[1]
    local_exp = specialist_widen_matrix.shape[0]
    inner = specialist_shrink_matrix.shape[1]
    share = inner // groups
    local_width = triple_projection_matrix.shape[2]
    heads = local_width // HD
    scale = 1.0 / math.sqrt(HD)
    gains = rescale_factors_both.astype(F32)
    cos, signed_sin = rope_tables(seq_len, HD)
    triple = triple_projection_matrix.transpose(1, 0, 2)
    gathered, queries, keys, values, mixed, weights, qk_hat, qk_inv, hidden, ffn_ext, probs, dy_all = attention_forward(
        block_entry_states, output_gradient, token_assignments, worker_quota_tallies, rescale_factors_both,
        probe_lookup_scalers, cos, signed_sin,
        document_labels, dispatcher_matrix, triple, heads_merge_matrix, 0)
    ffn_in = ffn_ext[..., :width]

    fused = xs == minor and share % 128 == 0 and local_exp % 2 == 0 and 2 * xs * minor * major * ROWS <= 512
    chunk_shape = (micro * local_rows // ROWS, 2, xs, major, minor, ROWS)
    if fused:
        dx_sum, moe_part, grad_widen, grad_shrink = experts_together(
            ffn_ext, dy_all.reshape(dy_all.shape[0], -1, width), specialist_widen_matrix, specialist_shrink_matrix, experts, 1)
    else:
        dx_sum, moe_part, grad_widen, grad_shrink = experts_apart(
            ffn_ext, dy_all, specialist_widen_matrix, specialist_shrink_matrix, experts)
    dx_sum = dx_sum.astype(F32).reshape(micro, local_rows, width + 128)
    grad_widen = grad_widen.reshape(groups, width // groups, -1)

    inv_second = lax.rsqrt(jnp.mean(hidden * hidden, axis=-1, keepdims=True) + EPS)
    hat_second = hidden * inv_second
    probs, keep = probs[..., :experts], probs[..., experts: 2 * experts]
    d_probs = dx_sum[..., width: width + experts] * keep
    d_logits = probs * (d_probs - jnp.sum(probs * d_probs, axis=-1, keepdims=True))
    d_ffn = dx_sum[..., :width] + jnp.einsum("mte,de->mtd", d_logits, dispatcher_matrix.astype(F32), precision=HIGH)
    grad_router = jnp.einsum("mtd,mte->ed", ffn_in.astype(F32), d_logits, precision=HIGH)
    scaled = d_ffn * gains[1]
    adjoint = output_gradient.astype(F32)
    d_hidden = adjoint + inv_second * (scaled - hat_second * jnp.mean(scaled * hat_second, axis=-1, keepdims=True))
    grad_second = jnp.sum(d_ffn * hat_second, axis=(0, 1))

    d_proj, d_attn_in, grad_heads, grad_out, grad_widen, moe = attention_back(
        d_hidden.astype(BF), heads_merge_matrix, triple, queries, keys, values, mixed, weights,
        qk_hat, qk_inv, probe_lookup_scalers, cos, signed_sin, grad_widen,
        moe_part.reshape(chunk_shape + (width,)) if fused else None, 5)
    if not fused:
        moe = scatter_all(moe_part.reshape(chunk_shape + (width,)), 3)
    output = (hidden + moe.astype(F32).reshape(micro, local_rows, width)).astype(BF)
    skip = block_entry_states.astype(F32)
    inv_first = lax.rsqrt(jnp.mean(skip * skip, axis=-1, keepdims=True) + EPS)
    hat_first = skip * inv_first
    scaled = d_attn_in * gains[0]
    grad_input = d_hidden + inv_first * (scaled - hat_first * jnp.mean(scaled * hat_first, axis=-1, keepdims=True))
    grad_first = jnp.sum(d_attn_in * hat_first, axis=(0, 1))

    shared = jnp.concatenate([grad_first[None], grad_second[None], grad_router]).reshape(-1).astype(BF)
    own = grad_heads[:2].reshape(-1).astype(BF)
    gap, size = shared.shape[0], shared.shape[0] + own.shape[0]
    block = (groups, ROWS, -(-size // (groups * ROWS * 128)) * 128)
    room = math.prod(block)
    shared = jnp.pad(shared, (0, room - gap)).reshape(block)
    own = jnp.pad(own, (gap, room - size)).reshape(block)
    out_sum, qkv_sum, misc_sum = total_over_groups(
        gathered.reshape(-1, width), d_proj, grad_out, shared, own, 4)
    qkv_sum, out_sum, grad_widen, grad_shrink = finish(
        qkv_sum.reshape(-1, local_width), out_sum.reshape(-1, width), grad_widen, grad_shrink, local_exp, share)
    qkv_sum = qkv_sum.reshape(3, width, local_width).transpose(1, 0, 2)
    grad_shrink = grad_shrink.reshape(local_exp, share, width)
    misc_sum = misc_sum.reshape(-1)[:size].astype(F32)
    rows = misc_sum[: (2 + experts) * width].reshape(2 + experts, width)
    return (
        output,
        grad_input,
        rows[:2],
        qkv_sum,
        misc_sum[(2 + experts) * width:].reshape(2, local_width),
        out_sum,
        rows[2:].T,
        grad_widen,
        grad_shrink,
    )


def solution(mesh):
    return jax.shard_map(
        per_device,
        mesh=mesh,
        in_specs=(
            P(None, ALL, None),
            P(None, "grp"),
            P(None, ALL, None),
            P(),
            P(),
            P(None, None, "ep"),
            P(None, "ep"),
            P("ep", None),
            P(),
            P("ep", None, None),
            P("ep", None, None),
            P(None, ALL, None),
        ),
        out_specs=(
            P(None, ALL, None),
            P(None, ALL, None),
            P(),
            P(None, None, "ep"),
            P(None, "ep"),
            P("ep", None),
            P(),
            P("ep", "grp", None),
            P("ep", "grp", None),
        ),
        check_vma=False,
    )
```

```python
import functools
import math

import jax
import jax.numpy as jnp
import numpy as np
from jax import lax
from jax.experimental import pallas as pl
from jax.experimental.pallas import tpu as pltpu
from jax.sharding import PartitionSpec as P

HD = 128
TOP = 8
EPS = 1e-05
THETA = 10000.0
NEG = -1e30
HIGH = lax.Precision.HIGHEST
ALL = ("grp", "ep")
MESH = pl.DeviceIdType.MESH
ROWS = 16
CUTS = 8
PER_STEP = 4
BF = jnp.bfloat16
F32 = jnp.float32


def rope_tables(length, head_dim):
    half = head_dim // 2
    angle = np.arange(length)[:, None] * THETA ** (-np.arange(half) * 2.0 / head_dim)
    cos, sin = np.cos(angle), np.sin(angle)
    return np.concatenate([cos, cos], 1).astype(np.float32), np.concatenate([-sin, sin], 1).astype(np.float32)


def mesh_sizes(groups, parts):
    major = 4 if groups % 4 == 0 else groups
    return major, groups // major, parts // 2


class Line:
    def __init__(self, size, place, step):
        self.size, self.place, self.step = size, place, step

    def at(self, hops):
        return (
            lax.axis_index("grp") + hops * self.step[0],
            lax.axis_index("ep") + hops * self.step[1],
        )


def lines(groups, parts):
    major, minor, xs = mesh_sizes(groups, parts)
    g, e = lax.axis_index("grp"), lax.axis_index("ep")
    core = lax.rem(e, 2)
    x_pos, minor_pos = lax.div(e, 2), lax.rem(g, minor)
    if xs == minor:
        first = Line(xs, jnp.where(core == 0, x_pos, minor_pos), (core, 2 - 2 * core))
        second = Line(xs, jnp.where(core == 0, minor_pos, x_pos), (1 - core, 2 * core))
    else:
        first = Line(xs, x_pos, (0, 2))
        second = Line(minor, minor_pos, (1, 0))
    return Line(2, core, (0, 1)), first, Line(major, lax.div(g, minor), (minor, 0)), second


def greet(some, whole=()):
    barrier = pltpu.get_barrier_semaphore()
    peers = sum(line.size - 1 for line in whole)
    for line in whole:
        for j in range(1, line.size):
            to = lax.rem(line.place + j, line.size)
            pl.semaphore_signal(barrier, inc=1, device_id=line.at(to - line.place), device_id_type=MESH)
    for line in some:
        if line.size == 2:
            pl.semaphore_signal(barrier, inc=1, device_id=line.at(1 - 2 * line.place), device_id_type=MESH)
            peers = peers + 1
        else:
            for way, there in ((1, line.place < line.size - 1), (-1, line.place > 0)):

                @pl.when(there)
                def _(line=line, way=way):
                    pl.semaphore_signal(barrier, inc=1, device_id=line.at(way), device_id_type=MESH)

                peers = peers + there.astype(jnp.int32)
    pl.semaphore_wait(barrier, peers)


def greet_lines(some):
    barrier = pltpu.get_barrier_semaphore()
    for line in some:
        for j in range(1, line.size):
            to = lax.rem(line.place + j, line.size)
            pl.semaphore_signal(barrier, inc=1, device_id=line.at(to - line.place), device_id_type=MESH)
    pl.semaphore_wait(barrier, sum(line.size - 1 for line in some))


def remote(src, dst, send, recv, target):
    return pltpu.make_async_remote_copy(
        src_ref=src, dst_ref=dst, send_sem=send, recv_sem=recv, device_id=target, device_id_type=MESH
    )


class Hop:
    def __init__(self, legs, after=None):
        self.legs, self.after = legs, after

    def _each(self, which, act):
        for leg in self.legs:
            if leg[which] is None:
                act(leg)
            else:
                pl.when(leg[which])(functools.partial(act, leg))

    def start(self):
        self._each(0, lambda leg: leg[2]().start())

    def arrive(self):
        def act(leg):
            leg[3]().wait_recv()
            if leg[4] is not None:
                leg[4]()

        self._each(1, act)

    def sent(self):
        self._each(0, lambda leg: leg[2]().wait_send())

    def finish(self):
        self.arrive()
        self.sent()


def spread_hops(core, first, third, fourth, at, own, send, recv):
    c, p, z, q = core.place, first.place, third.place, fourth.place
    r4 = ROWS
    r3 = r4 * fourth.size
    r2 = r3 * third.size
    rc = r2 * first.size
    base = [0]

    def sems(n):
        b = base[0]
        base[0] += n
        return (lambda i: send(b + i)), (lambda i: recv(b + i))

    def swap(line, place, first_source=None):
        source = first_source or (lambda i: place(line.place))
        return Swap(line, source, lambda j, i: place(i), *sems(line.size - 1))

    hops = [swap(fourth, lambda i: at(c * rc + p * r2 + z * r3 + i * r4, r4), lambda i: own)]
    hops += gather_hops(third, lambda i: at(c * rc + p * r2 + i * r3, r3), *sems(leg_count(third.size)))
    hops.append(swap(first, lambda i: at(c * rc + i * r2, r2)))
    hops.append(swap(core, lambda i: at(i * rc, rc)))
    return hops


def gather_hops(line, at, send, recv, own=None):
    n, a = line.size, line.place
    if n == 2:
        mine, theirs, peer = at(a), at(1 - a), line.at(1 - 2 * a)
        return [
            Hop([(None, None, lambda: remote(mine if own is None else own, mine, send(0), recv(0), peer),
                  lambda: remote(theirs, theirs, send(0), recv(0), peer), None)])
        ]
    hops = []
    for s in range(1, n):
        legs = []
        for d, way in enumerate((1, -1)):
            k = (s - 1) * 2 + d
            out = a - way * (s - 1)
            into = a - way * s
            sends = (out >= 0) & (out < n) & (a + way >= 0) & (a + way < n)
            gets = (into >= 0) & (into < n)
            out, into = jnp.clip(out, 0, n - 1), jnp.clip(into, 0, n - 1)
            legs.append((
                sends, gets,
                lambda out=out, way=way, k=k, s=s: remote(
                    own if s == 1 and own is not None else at(out), at(out), send(k), recv(k), line.at(way)),
                lambda into=into, way=way, k=k: remote(at(into), at(into), send(k), recv(k), line.at(-way)),
                None,
            ))
        hops.append(Hop(legs))
    return hops


def reduce_hops(line, acc, land, add, send, recv):
    n, a = line.size, line.place
    if n == 2:
        peer = line.at(1 - 2 * a)
        return [
            Hop([(None, None, lambda: remote(acc(1 - a), land(0), send(0), recv(0), peer),
                  lambda: remote(land(0), land(0), send(0), recv(0), peer),
                  lambda: add(acc(a), land(0)))])
        ]
    hops = []
    for s in range(n - 1):
        legs = []
        for d, way in enumerate((1, -1)):
            k = s * 2 + d
            b = a if way == 1 else n - 1 - a
            sends = (b <= s) & (b < n - 1)
            gets = (b - 1 <= s) & (b >= 1)
            out = b + n - 1 - s
            into = b + n - 2 - s
            out, into = jnp.clip(out, 0, n - 1), jnp.clip(into, 0, n - 1)
            if way == -1:
                out, into = n - 1 - out, n - 1 - into
            legs.append((
                sends, gets,
                lambda out=out, way=way, k=k: remote(acc(out), land(k), send(k), recv(k), line.at(way)),
                lambda way=way, k=k: remote(land(k), land(k), send(k), recv(k), line.at(-way)),
                lambda into=into, k=k: add(acc(into), land(k)),
            ))
        hops.append(Hop(legs))
    return hops


def hop_count(n):
    return 1 if n == 2 else n - 1


def leg_count(n):
    return 1 if n == 2 else 2 * (n - 1)


def flow(chains, pace=1):
    depth, count = max(len(c) for c in chains), len(chains)
    for t in range(count + pace * depth):
        for k in range(count):
            i, rest = divmod(t - k, pace)
            if rest:
                continue
            if 1 <= i <= len(chains[k]):
                chains[k][i - 1].arrive()
            if 0 <= i < len(chains[k]):
                chains[k][i].start()
    for chain in chains:
        for hop in chain:
            hop.sent()


def add(acc, land):
    lead = acc.shape[:-2]

    def one(i):
        where = []
        for size in reversed(lead):
            where.insert(0, lax.rem(i, size))
            i = lax.div(i, size)
        where = tuple(where) + (slice(None), slice(None))
        acc[where] = (acc[where].astype(F32) + land[where].astype(F32)).astype(acc.dtype)

    if lead:
        pl.loop(0, math.prod(lead))(one)
    else:
        one(0)


def gather_kernel(groups, parts, x, out, local, send, recv):
    core, first, second, long = lines(groups, parts)
    c, p, q, z = core.place, first.place, second.place, long.place
    greet([core, first, second, long])
    chunks = x.shape[0]
    own = [pltpu.make_async_copy(x.at[k], out.at[k, c, p, q, z], local.at[k]) for k in range(chunks)]
    for copy in own:
        copy.start()
    chains = []
    for k in range(chunks):
        base = [0]

        def sems(n, k=k, base=base):
            b = base[0]
            base[0] += leg_count(n)
            return (lambda i: send.at[k, b + i]), (lambda i: recv.at[k, b + i])

        chain = []
        chain += gather_hops(long, lambda i, k=k: out.at[k, c, p, q, i], *sems(long.size))
        chain += gather_hops(second, lambda i, k=k: out.at[k, c, p, i], *sems(second.size))
        chain += gather_hops(first, lambda i, k=k: out.at[k, c, i], *sems(first.size))
        chain += gather_hops(core, lambda i, k=k: out.at[k, i], *sems(2))
        chains.append(chain)
    for copy in own:
        copy.wait()
    flow(chains)


def gather_all(x, collective_id):
    groups, parts = lax.axis_size("grp"), lax.axis_size("ep")
    major, minor, xs = mesh_sizes(groups, parts)
    width = x.shape[-1]
    x = x.reshape(-1, ROWS, width)
    legs = sum(leg_count(n) for n in (2, xs, minor, major))
    chunks = x.shape[0]
    return pl.pallas_call(
        functools.partial(gather_kernel, groups, parts),
        out_shape=jax.ShapeDtypeStruct((chunks, 2, xs, major, minor, ROWS, width), x.dtype),
        in_specs=[pl.BlockSpec(memory_space=pl.ANY)],
        out_specs=pl.BlockSpec(memory_space=pl.ANY),
        scratch_shapes=[
            pltpu.SemaphoreType.DMA((chunks,)),
            pltpu.SemaphoreType.DMA((chunks, legs)),
            pltpu.SemaphoreType.DMA((chunks, legs)),
        ],
        compiler_params=pltpu.CompilerParams(collective_id=collective_id, has_side_effects=True),
    )(x)


def scatter_kernel(groups, parts, part, out, acc, land_c, land_p, land_q, land_z, local, send, recv):
    core, first, second, long = lines(groups, parts)
    c, p, q, z = core.place, first.place, second.place, long.place
    chunks = part.shape[0]
    own = [pltpu.make_async_copy(part.at[k, c], acc.at[k], local.at[k]) for k in range(chunks)]
    for copy in own:
        copy.start()
    greet([core, first, second, long])
    chains = []
    for k in range(chunks):
        base = [0]

        def sems(n, k=k, base=base):
            b = base[0]
            base[0] += leg_count(n)
            return (lambda i: send.at[k, b + i]), (lambda i: recv.at[k, b + i])

        def add_own(acc_ref, land_ref, k=k):
            own[k].wait()
            add(acc_ref, land_ref)

        s, r = sems(2)
        peer = core.at(1 - 2 * c)
        other = part.at[k, 1 - c]
        chain = [Hop([(
            None, None,
            lambda other=other, s=s, r=r, k=k: remote(other, land_c.at[k], s(0), r(0), peer),
            lambda s=s, r=r, k=k: remote(land_c.at[k], land_c.at[k], s(0), r(0), peer),
            lambda k=k, add_own=add_own: add_own(acc.at[k], land_c.at[k]),
        )])]
        chain += reduce_hops(first, lambda i, k=k: acc.at[k, i], lambda i, k=k: land_p.at[k, i], add, *sems(first.size))
        chain += reduce_hops(second, lambda i, k=k: acc.at[k, p, i], lambda i, k=k: land_q.at[k, i], add, *sems(second.size))
        chain += reduce_hops(long, lambda i, k=k: acc.at[k, p, q, i], lambda i, k=k: land_z.at[k, i], add, *sems(long.size))
        chains.append(chain)
    flow(chains)
    for k in range(chunks):
        out[k] = acc[k, p, q, z]


def scatter_all(part, collective_id):
    groups, parts = lax.axis_size("grp"), lax.axis_size("ep")
    major, minor, xs = mesh_sizes(groups, parts)
    legs = sum(leg_count(n) for n in (2, xs, minor, major))
    chunks, width = part.shape[0], part.shape[-1]
    unit = 2 * ROWS * width
    need = unit * (2 * xs * minor * major + leg_count(xs) * minor * major + leg_count(major) * minor + leg_count(minor) + 2)
    per = chunks
    while per > 1 and per * need > 44 * 2**20:
        per //= 2
    call = pl.pallas_call(
        functools.partial(scatter_kernel, groups, parts),
        out_shape=jax.ShapeDtypeStruct((per, ROWS, width), BF),
        in_specs=[pl.BlockSpec(memory_space=pl.ANY)],
        out_specs=pl.BlockSpec(memory_space=pltpu.VMEM),
        scratch_shapes=[
            pltpu.VMEM((per, xs, major, minor, ROWS, width), BF),
            pltpu.VMEM((per, xs, major, minor, ROWS, width), BF),
            pltpu.VMEM((per, leg_count(xs), major, minor, ROWS, width), BF),
            pltpu.VMEM((per, leg_count(major), minor, ROWS, width), BF),
            pltpu.VMEM((per, leg_count(minor), ROWS, width), BF),
            pltpu.SemaphoreType.DMA((per,)),
            pltpu.SemaphoreType.DMA((per, legs)),
            pltpu.SemaphoreType.DMA((per, legs)),
        ],
        compiler_params=pltpu.CompilerParams(
            collective_id=collective_id, has_side_effects=True, vmem_limit_bytes=56 * 2**20
        ),
    )
    return jnp.concatenate([call(part[i:i + per]) for i in range(0, chunks, per)]) if per < chunks else call(part)


class Begun:
    def __init__(self, hop, before):
        self.hop, self.before = hop, before

    def start(self):
        self.before()
        self.hop.start()

    def arrive(self):
        self.hop.arrive()

    def sent(self):
        self.hop.sent()


def total_kernel(groups, parts, plan, rows_in, d_proj, grad_out, shared, own, *refs):
    count = 3
    outs, acc, land = (refs[i * count: (i + 1) * count] for i in range(3))
    rows_v, proj_v, shared_v, own_v, got, local, stored, send, recv, t_send, t_recv = refs[3 * count:]
    major, minor, _ = mesh_sizes(groups, parts)
    g, e = lax.axis_index("grp"), lax.axis_index("ep")
    short = Line(minor, lax.rem(g, minor), (1, 0))
    long = Line(major, lax.div(g, minor), (minor, 0))
    whole = Line(parts, e, (0, 1))
    width = rows_in.shape[1]
    load = [pltpu.make_async_copy(a, b, local.at[i]) for i, (a, b) in enumerate((
        (grad_out, acc[0]), (rows_in, rows_v), (d_proj, proj_v), (shared, shared_v), (own, own_v)))]
    for copy in load:
        copy.start()

    def weights(k):
        def act():
            if k == 0:
                load[1].wait()
                load[2].wait()
            cuts = acc[1].shape[0] // 3
            c, cut = k // cuts, k % cuts
            blocks = max(1, 256 // acc[1].shape[2])
            rows = blocks * acc[1].shape[2]

            @pl.loop(0, groups // blocks)
            def _(i):
                cols = pl.ds(pl.multiple_of(cut * (width // cuts) + i * rows, 128), rows)
                total = lax.dot_general(rows_v[:, cols], proj_v[c], (((0,), (0,)), ((), ())), preferred_element_type=F32)
                acc[1][k, pl.ds(i * blocks, blocks)] = total.astype(BF).reshape((blocks,) + acc[1].shape[2:])

        return act

    swap = swap_legs(whole, lambda i: shared_v, lambda j, i: got.at[j], lambda j: t_send.at[j], lambda j: t_recv.at[j])

    def everyone():
        end_legs(swap)
        load[4].wait()

        @pl.loop(0, groups)
        def _(i):
            total = shared_v[i].astype(F32) + own_v[i].astype(F32)
            for j in range(parts - 1):
                total = total + got[j, i].astype(F32)
            acc[2][0, i] = total.astype(BF)

    before = {(0, 0): load[0].wait, (2, 0): everyone}
    chains = []
    for number, (j, k, far) in enumerate(plan):
        one, two = (long, short) if far else (short, long)
        y, z = one.place, two.place
        n = two.size

        def level_one(ref, k, n=n):
            return lambda i: ref.at[k, pl.ds(i * n, n)]

        def level_two(ref, k, y=y, n=n):
            return lambda i: ref.at[k, y * n + i]

        store = pltpu.make_async_copy(acc[j].at[k, y * n + z], outs[j].at[k, y * n + z], stored.at[number])
        base = [0]

        def sems(size, number=number, base=base):
            b = base[0]
            base[0] += leg_count(size)
            return (lambda i: send.at[number, b + i]), (lambda i: recv.at[number, b + i])

        first_land = leg_count(one.size) * n
        down = reduce_hops(one, level_one(acc[j], k), lambda i, j=j, k=k, n=n: land[j].at[k, pl.ds(i * n, n)], add, *sems(one.size))
        down += reduce_hops(two, level_two(acc[j], k), lambda i, j=j, k=k, f=first_land: land[j].at[k, f + i], add, *sems(two.size))
        up = gather_hops(two, level_two(outs[j], k), *sems(two.size), own=acc[j].at[k, y * n + z])
        turn = len(up)
        up += gather_hops(one, level_one(outs[j], k), *sems(one.size))

        down[0] = Begun(down[0], before.get((j, k)) or (weights(k) if j == 1 else lambda: None))
        up[0] = Begun(up[0], store.start)
        up[turn] = Begun(up[turn], store.wait)
        chains.append(down + up)
    greet([short, long], [whole])
    load[3].wait()
    start_legs(swap)
    flow(chains, 2)


def total_over_groups(gathered, d_proj, grad_out, shared, own, collective_id):
    groups, parts = lax.axis_size("grp"), lax.axis_size("ep")
    major, minor, _ = mesh_sizes(groups, parts)
    tokens, width = gathered.shape
    local_width = d_proj.shape[2]
    few = max(n for n in (4, 2, 1) if n == 1 or grad_out.shape[0] % (n * groups * ROWS) == 0)
    many = max(n for n in (12, 6, 3) if n == 3 or 3 * width % (n * groups * ROWS) == 0)
    shapes = [
        (few, groups, grad_out.shape[0] // few // groups, width),
        (many, groups, 3 * width // many // groups, local_width),
        (1,) + shared.shape,
    ]
    plan = [(0, k, k % 4 == 1) for k in range(few)] + [(1, k, k % 4 == 1) for k in range(many)] + [(2, 0, False)]
    blocks = max(leg_count(a) * b + leg_count(b) for a, b in ((minor, major), (major, minor)))
    legs = 2 * (leg_count(minor) + leg_count(major))
    total = len(plan)
    hbm = pl.BlockSpec(memory_space=pl.ANY)
    scratch = [pltpu.VMEM(a, BF) for a in shapes]
    scratch += [pltpu.VMEM((a[0], blocks) + a[2:], BF) for a in shapes]
    return pl.pallas_call(
        functools.partial(total_kernel, groups, parts, plan),
        out_shape=[jax.ShapeDtypeStruct(a, BF) for a in shapes],
        in_specs=[hbm] * 5,
        out_specs=[hbm] * len(shapes),
        scratch_shapes=scratch + [
            pltpu.VMEM(gathered.shape, BF),
            pltpu.VMEM(d_proj.shape, BF),
            pltpu.VMEM(shared.shape, BF),
            pltpu.VMEM(shared.shape, BF),
            pltpu.VMEM((parts - 1,) + shared.shape, BF),
            pltpu.SemaphoreType.DMA((5,)),
            pltpu.SemaphoreType.DMA((total,)),
            pltpu.SemaphoreType.DMA((total, legs)),
            pltpu.SemaphoreType.DMA((total, legs)),
            pltpu.SemaphoreType.DMA((parts - 1,)),
            pltpu.SemaphoreType.DMA((parts - 1,)),
        ],
        compiler_params=pltpu.CompilerParams(
            collective_id=collective_id, has_side_effects=True, vmem_limit_bytes=48 * 2**20
        ),
        cost_estimate=pl.CostEstimate(flops=6 * tokens * width * local_width, bytes_accessed=40 * 2**20, transcendentals=0),
    )(gathered, d_proj, grad_out.reshape(shapes[0]), shared, own)


def swap_legs(line, source, target, send, recv):
    n, a = line.size, line.place
    legs = []
    for j in range(1, n):
        to, off = lax.rem(a + j, n), lax.rem(a + n - j, n)
        legs.append((
            lambda to=to, j=j: remote(source(to), target(j - 1, a), send(j - 1), recv(j - 1), line.at(to - a)),
            lambda off=off, j=j: remote(target(j - 1, off), target(j - 1, off), send(j - 1), recv(j - 1), line.at(off - a)),
        ))
    return legs


def start_legs(legs):
    for out, _ in legs:
        out().start()


def end_legs(legs):
    for out, into in legs:
        into().wait_recv()
    for out, into in legs:
        out().wait_send()


class Swap:
    def __init__(self, *how):
        self.legs = swap_legs(*how)

    def start(self):
        start_legs(self.legs)

    def finish(self):
        end_legs(self.legs)


def add_rows(acc, first, land, rows):
    @pl.loop(0, rows // ROWS)
    def _(i):
        here = pl.ds(pl.multiple_of(first + i * ROWS, ROWS), ROWS)
        there = pl.ds(pl.multiple_of(i * ROWS, ROWS), ROWS)
        acc[here, :] = (acc[here, :].astype(F32) + land[there, :].astype(F32)).astype(acc.dtype)


def experts_kernel(
    groups, parts, local_rows, acc_ring, experts,
    x, dy, widen, shrink,
    summed, moe, grad_widen, grad_shrink,
    xs, dys, wide, down, sum_wide, sum_down, stage, acc, other, land_c, land_p, land_q, land_z,
    hid, raw, gated, d_gu, gate, product, marks,
    load, dy_sem, stage_sem, g_send, g_recv, s_send, s_recv,
):
    core, first, third, fourth = lines(groups, parts)
    c, p, z, q = core.place, first.place, third.place, fourth.place
    pn, zn, qn = first.size, third.size, fourth.size
    chunks, width = x.shape[0], shrink.shape[2]
    local_exp, inner = shrink.shape[0], shrink.shape[1]
    share = inner // groups
    group, part = lax.axis_index("grp"), lax.axis_index("ep")
    rq, rz, rp, rc = ROWS, ROWS * qn, ROWS * qn * zn, ROWS * qn * zn * pn
    rows = 2 * rc
    levels = 3 + hop_count(zn)
    cuts = local_rows // ROWS
    base = part * local_exp
    pairs = local_exp // 2

    loads = []
    for e in range(local_exp):
        for half in range(2):
            to = (e // 2) * 4 * share + half * 2 * share + (e % 2) * share
            loads.append(pltpu.make_async_copy(
                widen.at[e, :, pl.ds(pl.multiple_of(half * inner + group * share, share), share)],
                wide.at[:, pl.ds(to, share)], load.at[2 * e + half]))
        loads.append(pltpu.make_async_copy(
            shrink.at[e, pl.ds(pl.multiple_of(group * share, share), share), :],
            down.at[pl.ds(e * share, share), :], load.at[2 * local_exp + e]))
    for copy in loads:
        copy.start()

    def dy_copy(k):
        return pltpu.make_async_copy(dy.at[k], dys.at[lax.rem(k, 2)], dy_sem.at[lax.rem(k, 2)])

    dy_start = lambda k: dy_copy(k).start()
    dy_start(0)
    greet_lines([core, first, third, fourth])

    def rows_at(start, size):
        return pl.ds(pl.multiple_of(start, ROWS), size)

    def g_hop(k, level):
        buf = xs.at[k]
        return spread_hops(core, first, third, fourth, lambda start, size: buf.at[rows_at(start, size), :], x.at[k],
                           lambda i: g_send.at[k, i], lambda i: g_recv.at[k, i])[level]

    def s_line(k, line, at, land, offset):
        return Swap(line, at, lambda j, i: land.at[lax.rem(k, 2), j],
                    lambda j: s_send.at[k, offset + j], lambda j: s_recv.at[k, offset + j])

    def mine(k):
        return acc.at[lax.rem(k, acc_ring)]

    def s_hop(k, level):
        if level == 0:
            return s_line(k, core, lambda i: other, land_c, 0)
        if level == 1:
            return s_line(k, first, lambda i: mine(k).at[i], land_p, 1)
        if level == 2:
            return s_line(k, fourth, lambda i: mine(k).at[p, :, i], land_q, pn)
        return s_line(k, third, lambda i: mine(k).at[p, i, q], land_z, pn + qn - 1)

    def s_end(k, level):
        s_hop(k, level).finish()
        slot = lax.rem(k, 2)
        if level == 3:
            total = mine(k)[p, z, q].astype(F32)
            for j in range(zn - 1):
                total = total + land_z[slot, j].astype(F32)
            summed[k] = total.astype(BF)
            return
        if level == 0 and pn == 2:
            add(mine(k).at[1 - p], land_c.at[slot, 0, 1 - p])
            s_hop(k, 1).start()
            add(mine(k).at[p], land_c.at[slot, 0, p])
            return
        to = (mine(k), mine(k).at[p], mine(k).at[p, :, q])[level]
        land = (land_c, land_p, land_q)[level]
        for j in range(land.shape[1]):
            add(to, land.at[slot, j])
        s_hop(k, level + 1).start()

    def after(t, lag, act):
        k = t - lag

        @pl.when((k >= 0) & (k < chunks))
        def _():
            act(k)

    tiles = width // 512

    def compute(k):
        buf, dyk = xs.at[k], dys.at[lax.rem(k, 2)]

        @pl.when(k == 0)
        def _():
            for copy in loads:
                copy.wait()

        dy_copy(k).wait()

        @pl.when(k + 1 < chunks)
        def _():
            dy_start(k + 1)

        @pl.loop(0, pairs)
        def _(j):
            cols = pl.ds(pl.multiple_of(j * 4 * share, 4 * share), 4 * share)
            some = pl.ds(pl.multiple_of(j * 2 * share, 2 * share), 2 * share)
            to_up = pl.ds(pl.multiple_of(j * 4 * share + 2 * share, share), 2 * share)
            to_gate = pl.ds(pl.multiple_of(j * 4 * share, share), 2 * share)
            hid[...] = jnp.dot(buf[:, :width], wide[:, cols], preferred_element_type=F32)
            raw[...] = lax.dot_general(dyk[...], down[some, :], (((1,), (1,)), ((), ())), preferred_element_type=F32)
            gate[...] = jnp.dot(buf[:, width:], marks[:, some], preferred_element_type=F32)

            @pl.loop(0, rows // 32)
            def _(i):
                here = pl.ds(pl.multiple_of(i * 32, 32), 32)
                g, u = hid[here, : 2 * share], hid[here, 2 * share:]
                d, weight = raw[here, :], gate[here, :]
                sigma = 0.5 * jnp.tanh(0.5 * g) + 0.5
                swish = g * sigma
                act = swish * u
                product[here, some] = (act * d).astype(BF)
                gated[here, some] = (act * weight).astype(BF)
                d = d * weight
                d_gu[here, to_gate] = (d * u * (sigma + swish * (1.0 - sigma))).astype(BF)
                d_gu[here, to_up] = (d * swish).astype(BF)

        kept = mine(k)

        def split(cols, total):
            total = total.astype(BF).reshape((2,) + other.shape[:-1] + total.shape[1:])

            @pl.when(c == 0)
            def _():
                kept[..., cols] = total[0]
                other[..., cols] = total[1]

            @pl.when(c == 1)
            def _():
                other[..., cols] = total[0]
                kept[..., cols] = total[1]

        @pl.loop(0, tiles)
        def _(n):
            cols = pl.ds(pl.multiple_of(n * 512, 512), 512)
            split(cols, lax.dot_general(
                d_gu[...], wide[cols, :], (((1,), (1,)), ((), ())), preferred_element_type=F32))

        split(pl.ds(width, 128), lax.dot_general(
            product[...], marks[...], (((1,), (1,)), ((), ())), preferred_element_type=F32))
        s_hop(k, 0).start()

        @pl.when(k >= 1)
        def _():
            pltpu.make_async_copy(stage, moe.at[k - 1], stage_sem.at[0]).wait()

        @pl.loop(0, tiles)
        def _(n):
            cols = pl.ds(pl.multiple_of(n * 512, 512), 512)
            stage[:, cols] = jnp.dot(gated[...], down[:, cols], preferred_element_type=F32).astype(BF)
            sum_wide[cols, :] += lax.dot_general(
                buf[:, cols], d_gu[...], (((0,), (0,)), ((), ())), preferred_element_type=F32)
            sum_down[:, cols] += lax.dot_general(
                gated[...], dyk[:, cols], (((0,), (0,)), ((), ())), preferred_element_type=F32)

        pltpu.make_async_copy(stage, moe.at[k], stage_sem.at[0]).start()

    def begin(k):
        xs[k, rows_at(c * rc + p * rp + z * rz + q * rq, rq), :] = x[k]
        g_hop(k, 0).start()

        @pl.when(k == 0)
        def _():
            sum_wide[...] = jnp.zeros_like(sum_wide)
            sum_down[...] = jnp.zeros_like(sum_down)
            lanes = lax.broadcasted_iota(jnp.int32, marks.shape, 0)
            owner = base + lax.div(lax.broadcasted_iota(jnp.int32, marks.shape, 1), share)
            marks[...] = jnp.where((lanes == owner) | (lanes == owner + experts), 1.0, 0.0).astype(BF)

    def g_end(k, level):
        g_hop(k, level).finish()
        if level + 1 < levels:
            g_hop(k, level + 1).start()

    def wide_out(i):
        here = pl.ds(pl.multiple_of(i * rows, rows), rows)
        return pltpu.make_async_copy(d_gu, grad_widen.at[here, :], load.at[1])

    out_down = pltpu.make_async_copy(sum_down, grad_shrink, load.at[0])

    def store(i):
        @pl.when(i == 0)
        def _():
            out_down.start()

        @pl.when(i > 0)
        def _():
            wide_out(i - 1).wait()

        d_gu[...] = sum_wide[pl.ds(pl.multiple_of(i * rows, rows), rows), :].astype(BF)
        wide_out(i).start()

    @pl.loop(0, chunks + levels + 4)
    def _(t):
        for level in reversed(range(levels)):
            after(t, level + 1, functools.partial(g_end, level=level))
        after(t, 0, begin)
        for level in reversed(range(4)):
            after(t, levels + level + 1, functools.partial(s_end, level=level))
        after(t, levels, compute)

        @pl.when((t >= chunks + levels) & (t < chunks + levels + min(4, width // rows)))
        def _():
            store(t - chunks - levels)

    for i in range(4, width // rows):
        store(i)
    pltpu.make_async_copy(stage, moe.at[chunks - 1], stage_sem.at[0]).wait()
    wide_out(width // rows - 1).wait()
    out_down.wait()


def experts_together(x, dy, widen, shrink, experts, collective_id):
    groups, parts = lax.axis_size("grp"), lax.axis_size("ep")
    major, minor, xn = mesh_sizes(groups, parts)
    micro, local_rows, wide = x.shape
    x = x.reshape(-1, ROWS, wide)
    chunks = x.shape[0]
    local_exp, inner, width = shrink.shape
    share = inner // groups
    hidden = local_exp * share
    rows = 2 * ROWS * major * minor * xn
    acc_ring = 4
    legs = minor + xn - 1 + leg_count(major)
    vmem = pl.BlockSpec(memory_space=pltpu.VMEM)
    hbm = pl.BlockSpec(memory_space=pl.ANY)
    flops = 2 * chunks * rows * width * hidden * 9
    return pl.pallas_call(
        functools.partial(experts_kernel, groups, parts, local_rows, acc_ring, experts),
        out_shape=[
            jax.ShapeDtypeStruct((chunks, ROWS, wide), BF),
            jax.ShapeDtypeStruct((chunks, rows, width), BF),
            jax.ShapeDtypeStruct((width, 2 * hidden), BF),
            jax.ShapeDtypeStruct((hidden, width), F32),
        ],
        in_specs=[vmem, hbm, hbm, hbm],
        out_specs=[vmem, hbm, hbm, hbm],
        scratch_shapes=[
            pltpu.VMEM((chunks, rows, wide), BF),
            pltpu.VMEM((2, rows, width), BF),
            pltpu.VMEM((width, 2 * hidden), BF),
            pltpu.VMEM((hidden, width), BF),
            pltpu.VMEM((width, 2 * hidden), F32),
            pltpu.VMEM((hidden, width), F32),
            pltpu.VMEM((rows, width), BF),
            pltpu.VMEM((acc_ring, xn, major, minor, ROWS, wide), BF),
            pltpu.VMEM((xn, major, minor, ROWS, wide), BF),
            pltpu.VMEM((2, 1, xn, major, minor, ROWS, wide), BF),
            pltpu.VMEM((2, xn - 1, major, minor, ROWS, wide), BF),
            pltpu.VMEM((2, minor - 1, major, ROWS, wide), BF),
            pltpu.VMEM((2, major - 1, ROWS, wide), BF),
            pltpu.VMEM((rows, 4 * share), F32),
            pltpu.VMEM((rows, 2 * share), F32),
            pltpu.VMEM((rows, hidden), BF),
            pltpu.VMEM((rows, 2 * hidden), BF),
            pltpu.VMEM((rows, 2 * share), F32),
            pltpu.VMEM((rows, hidden), BF),
            pltpu.VMEM((128, hidden), BF),
            pltpu.SemaphoreType.DMA((3 * local_exp,)),
            pltpu.SemaphoreType.DMA((2,)),
            pltpu.SemaphoreType.DMA((2,)),
            pltpu.SemaphoreType.DMA((chunks, legs)),
            pltpu.SemaphoreType.DMA((chunks, legs)),
            pltpu.SemaphoreType.DMA((chunks, legs)),
            pltpu.SemaphoreType.DMA((chunks, legs)),
        ],
        compiler_params=pltpu.CompilerParams(
            collective_id=collective_id, has_side_effects=True, vmem_limit_bytes=63 * 2**20
        ),
        cost_estimate=pl.CostEstimate(flops=flops, bytes_accessed=80 * 2**20, transcendentals=chunks * rows * hidden),
    )(x, dy, widen, shrink)


def experts_apart(x, dy_all, specialist_widen_matrix, specialist_shrink_matrix, experts):
    groups, parts = lax.axis_size("grp"), lax.axis_size("ep")
    group, part = lax.axis_index("grp"), lax.axis_index("ep")
    local_exp, inner, width = specialist_shrink_matrix.shape
    share = inner // groups
    widen = specialist_widen_matrix.reshape(local_exp, width, 2, groups, share)
    widen = lax.dynamic_index_in_dim(widen, group, 3, keepdims=False)
    widen = widen.transpose(1, 2, 0, 3).reshape(width, 2 * local_exp * share)
    shrink = specialist_shrink_matrix.reshape(local_exp, groups, share, width)
    shrink = lax.dynamic_index_in_dim(shrink, group, 1, keepdims=False).reshape(local_exp * share, width)
    x_all = gather_all(x, 1)
    chunk_shape = x_all.shape[:-1]
    x_all, dy_all = x_all.reshape(-1, width + 128), dy_all.reshape(-1, width)
    gate = x_all[:, width: width + experts].astype(F32) + x_all[:, width + experts: width + 2 * experts].astype(F32)
    x_all = x_all[:, :width]
    gate = lax.dynamic_slice_in_dim(gate, part * local_exp, local_exp, axis=1)
    gate = jnp.repeat(gate, share, axis=1)
    gate_up = jnp.dot(x_all, widen, preferred_element_type=F32)
    g, u = gate_up[:, : local_exp * share], gate_up[:, local_exp * share:]
    sigma = jax.nn.sigmoid(g)
    act = g * sigma * u
    gated = (gate * act).astype(BF)
    moe_part = jnp.dot(gated, shrink, preferred_element_type=F32).astype(BF)
    d_raw = lax.dot_general(dy_all, shrink, (((1,), (1,)), ((), ())), preferred_element_type=F32)
    d_gate = jnp.sum((act * d_raw).reshape(-1, local_exp, share), axis=-1)
    d_act = gate * d_raw
    d_gu = jnp.concatenate([d_act * u * sigma * (1.0 + g * (1.0 - sigma)), d_act * (g * sigma)], axis=1).astype(BF)
    dx_part = lax.dot_general(d_gu, widen, (((1,), (1,)), ((), ())), preferred_element_type=F32).astype(BF)
    lanes = jnp.arange(128, dtype=jnp.int32)
    place = (lanes[None, :] == part * local_exp + jnp.arange(local_exp, dtype=jnp.int32)[:, None])
    d_gate = jnp.sum(jnp.where(place[None], d_gate[:, :, None], 0.0), axis=1)
    dx_part = jnp.concatenate([dx_part, d_gate.astype(BF)], axis=1)
    dx_sum = scatter_all(dx_part.reshape(chunk_shape + (width + 128,)), 2)
    grad_widen = lax.dot_general(x_all, d_gu, (((0,), (0,)), ((), ())), preferred_element_type=F32)
    grad_shrink = lax.dot_general(gated, dy_all, (((0,), (0,)), ((), ())), preferred_element_type=F32)
    grad_widen = grad_widen.astype(BF).reshape(width, 2, local_exp // 2, 2, share).transpose(0, 2, 1, 3, 4)
    return dx_sum, moe_part.reshape(chunk_shape + (width,)), grad_widen, grad_shrink


def finish_kernel(share, qkv, out, wide, shrink, qkv_to, out_to, wide_to, shrink_to):
    qkv_to[...] = qkv[...].astype(F32)
    out_to[...] = out[...].astype(F32)
    shrink_to[...] = shrink[...]
    for i in range(wide.shape[0]):
        wide_to[0, :, i * share: (i + 1) * share] = wide[i].astype(F32)


def finish(qkv, out, wide, shrink, local_exp, share):
    groups, rows, _ = wide.shape
    whole = (local_exp, rows, 2 * groups * share)
    if share % 128:
        wide = wide.reshape(groups, rows, local_exp // 2, 2, 2, share).transpose(2, 4, 1, 3, 0, 5)
        return qkv.astype(F32), out.astype(F32), wide.reshape(whole).astype(F32), shrink
    steps = 2 * local_exp
    cut = lambda a: pl.BlockSpec((a.shape[0] // steps, a.shape[1]), lambda i: (i, 0))
    outs = [jax.ShapeDtypeStruct(a.shape, F32) for a in (qkv, out)] + [
        jax.ShapeDtypeStruct(whole, F32), jax.ShapeDtypeStruct(shrink.shape, F32)]
    return pl.pallas_call(
        functools.partial(finish_kernel, share),
        grid=(steps,),
        out_shape=outs,
        in_specs=[cut(qkv), cut(out),
                  pl.BlockSpec((groups, rows, share), lambda i: (0, 0, i // 4 * 4 + i % 2 * 2 + i // 2 % 2)), cut(shrink)],
        out_specs=[cut(qkv), cut(out),
                   pl.BlockSpec((1, rows, groups * share), lambda i: (i // 2, 0, i % 2)), cut(shrink)],
        compiler_params=pltpu.CompilerParams(vmem_limit_bytes=40 * 2**20),
    )(qkv, out, wide, shrink)


class Backdrop:
    PACE = 2

    def __init__(self, groups, parts, part, out, acc, land_c, land_p, land_q, land_z, local, send, recv):
        self.core, self.first, self.third, self.fourth = lines(groups, parts)
        self.part, self.out, self.acc, self.lands = part, out, acc, (land_c, land_p, land_q)
        self.land_z = land_z
        self.local, self.send, self.recv = local, send, recv
        self.chunks = part.shape[0]
        self.levels = 3 + hop_count(self.third.size)
        self.lag = self.PACE * self.levels

    @staticmethod
    def scratch(chunks, width):
        major, minor, xn = mesh_sizes(lax.axis_size("grp"), lax.axis_size("ep"))
        legs = minor + xn - 1 + leg_count(major)
        return [
            pltpu.VMEM((chunks, xn, major, minor, ROWS, width), BF),
            pltpu.VMEM((4, 1, xn, major, minor, ROWS, width), BF),
            pltpu.VMEM((4, xn - 1, major, minor, ROWS, width), BF),
            pltpu.VMEM((4, minor - 1, major, ROWS, width), BF),
            pltpu.VMEM((chunks, leg_count(major), ROWS, width), BF),
            pltpu.SemaphoreType.DMA((chunks,)),
            pltpu.SemaphoreType.DMA((chunks, legs)),
            pltpu.SemaphoreType.DMA((chunks, legs)),
        ]

    def near(self):
        return [self.core, self.first, self.third, self.fourth]

    def own(self, k):
        return pltpu.make_async_copy(self.part.at[k, self.core.place], self.acc.at[k], self.local.at[k])

    def hop(self, k, level):
        p, q = self.first.place, self.fourth.place
        pn, qn = self.first.size, self.fourth.size
        if level >= 3:
            offset = pn + qn - 1
            land = self.land_z.at[k]
            return reduce_hops(self.third, lambda i: self.acc.at[k, p, i, q], lambda i: land.at[i], add,
                               lambda i: self.send.at[k, offset + i], lambda i: self.recv.at[k, offset + i])[level - 3]
        line, offset, source = [
            (self.core, 0, lambda i: self.part.at[k, i]),
            (self.first, 1, lambda i: self.acc.at[k, i]),
            (self.fourth, pn, lambda i: self.acc.at[k, p, :, i]),
        ][level]
        land = self.lands[level]
        return Swap(line, source, lambda j, i: land.at[lax.rem(k, 4), j],
                    lambda j: self.send.at[k, offset + j], lambda j: self.recv.at[k, offset + j])

    def end(self, k, level):
        p, q, z = self.first.place, self.fourth.place, self.third.place
        self.hop(k, level).finish()
        if level + 1 == self.levels:
            self.out[k] = self.acc[k, p, z, q]
            return
        after = self.hop(k, level + 1)
        if level == 0:
            self.own(k).wait()
            if self.first.size == 2:
                add(self.acc.at[k, 1 - p], self.lands[0].at[lax.rem(k, 4), 0, 1 - p])
                after.start()
                add(self.acc.at[k, p], self.lands[0].at[lax.rem(k, 4), 0, p])
                return
            add(self.acc.at[k], self.lands[0].at[lax.rem(k, 4), 0])
        elif level < 3:
            to = self.acc.at[k, p] if level == 1 else self.acc.at[k, p, :, q]
            for j in range(self.lands[level].shape[1]):
                add(to, self.lands[level].at[lax.rem(k, 4), j])
        after.start()

    def begin(self, k):
        self.hop(k, 0).start()
        self.own(k).start()

    def step(self, t):
        for level in reversed(range(self.levels)):
            k = t - self.PACE * (level + 1)

            @pl.when((k >= 0) & (k < self.chunks))
            def _(k=k, level=level):
                self.end(k, level)

        @pl.when((t >= 0) & (t < self.chunks))
        def _():
            self.begin(t)


class Sequence:
    def __init__(self, parts, block, micro):
        e = lax.axis_index("ep")
        self.xn, self.block, self.micro, self.e = parts // 2, block, micro, e
        self.x, self.c = lax.div(e, 2), lax.rem(e, 2)
        self.line = Line(parts, e, (0, 1))
        self.line_x = Line(self.xn, self.x, (0, 2))
        self.line_c = Line(2, self.c, (0, 1))

    def at(self, ref, m, x, c):
        return ref.at[m, pl.ds(pl.multiple_of((x * 2 + c) * self.block, self.block), self.block), :]

    def gather_x(self, ref, send, recv):
        legs = []
        for m in range(self.micro):
            legs += swap_legs(
                self.line_x, lambda i, m=m: self.at(ref, m, self.x, self.c), lambda j, i, m=m: self.at(ref, m, i, self.c),
                lambda j, m=m: send.at[m, j], lambda j, m=m: recv.at[m, j])
        return legs

    def gather_c(self, ref, send, recv):
        legs = []
        for m in range(self.micro):
            for x in range(self.xn):
                legs += swap_legs(
                    self.line_c, lambda i, m=m, x=x: self.at(ref, m, x, self.c), lambda j, i, m=m, x=x: self.at(ref, m, x, i),
                    lambda j, m=m, x=x: send.at[m, self.xn - 1 + x], lambda j, m=m, x=x: recv.at[m, self.xn - 1 + x])
        return legs

    def reduce_c(self, ref, land, send, recv):
        legs = []
        for m in range(self.micro):
            for x in range(self.xn):
                legs += swap_legs(
                    self.line_c, lambda i, m=m, x=x: self.at(ref, m, x, i), lambda j, i, m=m, x=x: land.at[m, x],
                    lambda j, m=m, x=x: send.at[m, self.xn - 1 + x], lambda j, m=m, x=x: recv.at[m, self.xn - 1 + x])
        return legs

    def reduce_x(self, ref, land, send, recv):
        legs = []
        for m in range(self.micro):
            legs += swap_legs(
                self.line_x, lambda i, m=m: self.at(ref, m, i, self.c), lambda j, i, m=m: land.at[m, j],
                lambda j, m=m: send.at[m, j], lambda j, m=m: recv.at[m, j])
        return legs

    def add_c(self, ref, land):
        for m in range(self.micro):
            for x in range(self.xn):
                add_rows(ref.at[m], (x * 2 + self.c) * self.block, land.at[m, x], self.block)

    def total_x(self, ref, land, out):
        for m in range(self.micro):
            @pl.loop(0, self.block // ROWS)
            def _(i, m=m):
                here = pl.ds(pl.multiple_of(i * ROWS, ROWS), ROWS)
                total = ref[m, pl.ds(pl.multiple_of(self.e * self.block + i * ROWS, ROWS), ROWS), :].astype(F32)
                for j in range(self.xn - 1):
                    total = total + land[m, j, here, :].astype(F32)
                out[m, here, :] = total


def sum_over_parts(seq, columns, sent, got, send, recv, meanwhile):
    flat = columns.T
    sent[...] = flat[:8]
    legs = swap_legs(seq.line, lambda i: sent, lambda j, i: got.at[j], lambda j: send.at[j], lambda j: recv.at[j])
    start_legs(legs)
    meanwhile()
    end_legs(legs)
    total = sent[...]
    for j in range(seq.line.size - 1):
        total = total + got[j]
    return jnp.concatenate([total] * 16, axis=0).T


def back_kernel(
    groups, parts, backed,
    branch, merge, triple, queries, keys, values, mixed, probs, hat, inv, gains_in, cos, sin, wide, part,
    d_proj, d_in, grad_heads, grad_out, wide_all, summed,
    gains, rows_all, merge_v, triple_v, q_v, k_v, v_v, mixed_v, probs_v, hat_v, d_mixed, d_qk, sums, partial, land_c, land_x, sent, got,
    load, g_send, g_recv, s_send, s_recv, t_send, t_recv, w_send, w_recv, *behind
):
    micro, block, width = branch.shape
    seq = Sequence(parts, block, micro)
    length = queries.shape[1]
    tokens = micro * length
    heads = queries.shape[2] // HD
    scale = 1.0 / math.sqrt(HD)
    loads = [pltpu.make_async_copy(a, b, load.at[i]) for i, (a, b) in enumerate((
        (merge, merge_v), (mixed, mixed_v), (queries, q_v), (keys, k_v), (values, v_v), (probs, probs_v), (hat, hat_v), (triple, triple_v)))]
    for copy in loads:
        copy.start()
    gains[...] = gains_in[...].astype(F32)
    over = Line(groups, lax.axis_index("grp"), (1, 0))
    if backed:
        back = Backdrop(groups, parts, part, summed, *behind)
        greet_lines([seq.line, over] + back.near())
        steps = back.chunks + back.lag
        behind_step = back.step
    else:
        greet_lines([seq.line, over])
        steps, behind_step = 0, lambda t: None
        summed[...] = jnp.zeros_like(summed)
    for m in range(micro):
        rows_all[m, pl.ds(pl.multiple_of(seq.e * block, block), block), :] = branch[m]
    gather_x = seq.gather_x(rows_all, g_send, g_recv)
    start_legs(gather_x)
    g = over.place
    own_wide = pltpu.make_async_copy(wide.at[g], wide_all.at[g], load.at[8])
    own_wide.start()
    turn = swap_legs(over, lambda i: wide.at[i], lambda j, i: wide_all.at[i], lambda j: w_send.at[j], lambda j: w_recv.at[j])
    pieces = CUTS * (groups - 1)
    tall = wide.shape[1] // CUTS

    def step(t):
        for u in range(PER_STEP):
            i = t * PER_STEP + u

            @pl.when((i >= 0) & (i < pieces))
            def _(i=i):
                j, cut = lax.rem(i, groups - 1), lax.div(i, groups - 1)
                to = lax.rem(g + 1 + j, groups)
                here = pl.ds(pl.multiple_of(cut * tall, ROWS), tall)
                remote(wide.at[to, here, :], wide_all.at[g, here, :], w_send.at[j], w_recv.at[j], over.at(to - g)).start()

        behind_step(t)

    step(0)
    step(1)
    step(2)
    end_legs(gather_x)
    gather_c = seq.gather_c(rows_all, g_send, g_recv)
    start_legs(gather_c)
    step(3)
    sums[...] = jnp.zeros_like(sums)
    grad_heads[...] = jnp.zeros_like(grad_heads)
    end_legs(gather_c)
    for copy in loads[:2]:
        copy.wait()
    for m in range(micro):
        d_mixed[m] = lax.dot_general(rows_all[m], merge_v[...], (((1,), (1,)), ((), ())), preferred_element_type=F32).astype(BF)
    step(4)

    @pl.loop(0, width // 512)
    def _(n):
        cols = pl.ds(pl.multiple_of(n * 512, 512), 512)
        total = lax.dot_general(mixed_v[0], rows_all[0, :, cols], (((0,), (0,)), ((), ())), preferred_element_type=F32)
        for m in range(1, micro):
            total = total + lax.dot_general(
                mixed_v[m], rows_all[m, :, cols], (((0,), (0,)), ((), ())), preferred_element_type=F32)
        grad_out[:, cols] = total.astype(BF)

    step(5)
    for copy in loads[2:7]:
        copy.wait()
    lane = lax.broadcasted_iota(jnp.int32, (1, 128), 1)

    def one_head(i):
        m, h = lax.div(i, heads), lax.rem(i, heads)
        cols = pl.ds(pl.multiple_of(h * HD, HD), HD)
        here = pl.ds(pl.multiple_of(m * length, length), length)
        d_m = d_mixed[m, :, cols]
        weights = probs_v[m, h]
        low = weights.astype(BF)
        d_proj[2, here, cols] = lax.dot_general(low, d_m, (((0,), (0,)), ((), ())), preferred_element_type=F32).astype(BF)
        d_w = lax.dot_general(d_m, v_v[m, :, cols], (((1,), (1,)), ((), ())), preferred_element_type=F32)
        d_s = (weights * (d_w - jnp.sum(weights * d_w, axis=-1, keepdims=True))).astype(BF)
        d_q = jnp.dot(d_s, k_v[m, :, cols], preferred_element_type=F32) * scale
        d_k = lax.dot_general(d_s, q_v[m, :, cols], (((0,), (0,)), ((), ())), preferred_element_type=F32) * scale
        marks = sums[here, :]
        for c, d in enumerate((d_q, d_k)):
            d = d * cos[...] - pltpu.roll(d, HD // 2, 1) * sin[...]
            d_qk[c, here, cols] = d
            product = d * hat_v[c, here, cols]
            grad_heads[c: c + 1, cols] += jnp.sum(product, axis=0, keepdims=True)
            marks = marks + jnp.where(lane == c, jnp.sum(product * gains[c: c + 1, cols], axis=-1, keepdims=True), 0.0)
        sums[here, :] = marks

    @pl.loop(0, micro * heads)
    def _(i):
        one_head(i)
        step(i + 6)

    done = 7 + micro * heads
    sums[...] = sum_over_parts(seq, sums[...], sent, got, t_send, t_recv, lambda: step(done - 1))

    @pl.loop(0, tokens // 64)
    def _(i):
        here = pl.ds(pl.multiple_of(i * 64, 64), 64)
        for c in range(2):
            inner = sums[here, c: c + 1] * (1.0 / width)
            d_proj[c, here, :] = (inv[here, c: c + 1] * (
                d_qk[c, here, :] * gains[c: c + 1, :] - hat_v[c, here, :] * inner)).astype(BF)

    loads[7].wait()

    @pl.loop(0, width // 512)
    def _(n):
        cols = pl.ds(pl.multiple_of(n * 512, 512), 512)
        for m in range(micro):
            here = pl.ds(m * length, length)
            total = lax.dot_general(d_proj[0, here, :], triple_v[0, cols, :], (((1,), (1,)), ((), ())), preferred_element_type=F32)
            for c in (1, 2):
                total = total + lax.dot_general(
                    d_proj[c, here, :], triple_v[c, cols, :], (((1,), (1,)), ((), ())), preferred_element_type=F32)
            partial[m, :, cols] = total.astype(BF)

    reduce_c = seq.reduce_c(partial, land_c, s_send, s_recv)
    start_legs(reduce_c)
    step(done)
    end_legs(reduce_c)
    seq.add_c(partial, land_c)
    reduce_x = seq.reduce_x(partial, land_x, s_send, s_recv)
    start_legs(reduce_x)
    step(done + 1)
    end_legs(reduce_x)
    seq.total_x(partial, land_x, d_in)
    for t in range(done + 2, max(steps, -(-pieces // PER_STEP))):
        step(t)
    end_legs(turn)
    own_wide.wait()


def attention_back(branch, merge, triple, queries, keys, values, mixed, probs, hat, inv, gains, cos, sin, wide, part, collective_id):
    groups, parts = lax.axis_size("grp"), lax.axis_size("ep")
    micro, block, width = branch.shape
    length, local_width = queries.shape[1:]
    tokens = micro * length
    backed = part is not None
    behind = Backdrop.scratch(part.shape[0], width) if backed else []
    summed = (part.shape[0], ROWS, width) if backed else (8, 128)
    vmem = pl.BlockSpec(memory_space=pltpu.VMEM)
    hbm = pl.BlockSpec(memory_space=pl.ANY)
    xn = parts // 2
    return pl.pallas_call(
        functools.partial(back_kernel, groups, parts, backed),
        out_shape=[
            jax.ShapeDtypeStruct((3, tokens, local_width), BF),
            jax.ShapeDtypeStruct((micro, block, width), F32),
            jax.ShapeDtypeStruct((8, local_width), F32),
            jax.ShapeDtypeStruct((local_width, width), BF),
            jax.ShapeDtypeStruct(wide.shape, BF),
            jax.ShapeDtypeStruct(summed, BF if backed else F32),
        ],
        in_specs=[vmem] + [hbm] * 8 + [vmem] * 4 + [hbm] * 2,
        out_specs=[vmem] * 4 + [hbm, vmem],
        scratch_shapes=[
            pltpu.VMEM(gains.shape, F32),
            pltpu.VMEM((micro, length, width), BF),
            pltpu.VMEM(merge.shape, BF),
            pltpu.VMEM(triple.shape, BF),
            pltpu.VMEM(queries.shape, BF),
            pltpu.VMEM(queries.shape, BF),
            pltpu.VMEM(queries.shape, BF),
            pltpu.VMEM(queries.shape, BF),
            pltpu.VMEM(probs.shape, F32),
            pltpu.VMEM(hat.shape, F32),
            pltpu.VMEM(queries.shape, BF),
            pltpu.VMEM((2, tokens, local_width), F32),
            pltpu.VMEM((tokens, 128), F32),
            pltpu.VMEM((micro, length, width), BF),
            pltpu.VMEM((micro, xn, block, width), BF),
            pltpu.VMEM((micro, xn - 1, block, width), BF),
            pltpu.VMEM((8, tokens), F32),
            pltpu.VMEM((parts - 1, 8, tokens), F32),
            pltpu.SemaphoreType.DMA((9,)),
            pltpu.SemaphoreType.DMA((micro, 2 * xn - 1)),
            pltpu.SemaphoreType.DMA((micro, 2 * xn - 1)),
            pltpu.SemaphoreType.DMA((micro, 2 * xn - 1)),
            pltpu.SemaphoreType.DMA((micro, 2 * xn - 1)),
            pltpu.SemaphoreType.DMA((parts - 1,)),
            pltpu.SemaphoreType.DMA((parts - 1,)),
            pltpu.SemaphoreType.DMA((groups - 1,)),
            pltpu.SemaphoreType.DMA((groups - 1,)),
        ] + behind,
        compiler_params=pltpu.CompilerParams(
            collective_id=collective_id, has_side_effects=True, vmem_limit_bytes=58 * 2**20
        ),
        cost_estimate=pl.CostEstimate(flops=10**10, bytes_accessed=40 * 2**20, transcendentals=0),
    )(branch, merge, triple, queries, keys, values, mixed, probs, hat, inv, gains, cos, sin, wide,
      part if backed else mixed)


class BackGather:
    PACE = 3

    def __init__(self, groups, parts, own, out, local, send, recv):
        self.lines = lines(groups, parts)
        self.own, self.out, self.local, self.send, self.recv = own, out, local, send, recv
        self.chunks = own.shape[0]
        self.levels = 4
        self.lag = self.PACE * self.levels

    @staticmethod
    def scratch(chunks):
        major, minor, xn = mesh_sizes(lax.axis_size("grp"), lax.axis_size("ep"))
        legs = minor + xn + major - 2
        return [
            pltpu.SemaphoreType.DMA((chunks,)),
            pltpu.SemaphoreType.DMA((chunks, legs)),
            pltpu.SemaphoreType.DMA((chunks, legs)),
        ]

    def near(self):
        return list(self.lines)

    def mine(self, k):
        return pltpu.make_async_copy(
            self.own.at[k], self.out.at[(k,) + tuple(line.place for line in self.lines)], self.local.at[k])

    def hop(self, k, level):
        core, first, third, fourth = self.lines
        c, p, q = core.place, first.place, fourth.place
        line, offset, at = [
            (third, 0, lambda i: self.out.at[k, c, p, i, q]),
            (fourth, third.size - 1, lambda i: self.out.at[k, c, p, :, i]),
            (first, third.size + fourth.size - 2, lambda i: self.out.at[k, c, i]),
            (core, third.size + fourth.size + first.size - 3, lambda i: self.out.at[k, i]),
        ][level]
        source = (lambda i: self.own.at[k]) if level == 0 else (lambda i: at(line.place))
        return Swap(line, source, lambda j, i: at(i),
                    lambda j: self.send.at[k, offset + j], lambda j: self.recv.at[k, offset + j])

    def step(self, t):
        for level in reversed(range(self.levels)):
            k = t - self.PACE * (level + 1)

            @pl.when((k >= 0) & (k < self.chunks))
            def _(k=k, level=level):
                self.hop(k, level).finish()
                if level == 0:
                    self.mine(k).wait()
                if level + 1 < self.levels:
                    self.hop(k, level + 1).start()

        @pl.when((t >= 0) & (t < self.chunks))
        def _():
            self.mine(t).start()
            self.hop(t, 0).start()


def forward_kernel(
    groups, parts, experts,
    x, dy, routes, quota, gains_in, head_gains_in, cos, sin, docs, dispatch_in, triple, merge,
    gathered, q_out, k_out, v_out, mixed, probs, hat, inv, hidden, ffn_in, router, dy_all,
    kept, gains, head_gains, docs_down, dispatch, triple_v, merge_v, sums, partial, land_c, land_x, sent, got,
    load, g_send, g_recv, s_send, s_recv, t_send, t_recv, *behind
):
    micro, block, width = x.shape
    seq = Sequence(parts, block, micro)
    length = gathered.shape[1]
    tokens = micro * length
    heads = q_out.shape[2] // HD
    scale = 1.0 / math.sqrt(HD)
    cuts = block // ROWS
    loads = [pltpu.make_async_copy(triple, triple_v, load.at[0]), pltpu.make_async_copy(merge, merge_v, load.at[1])]
    for copy in loads:
        copy.start()
    back = BackGather(groups, parts, dy, dy_all, *behind)
    step, steps = back.step, back.chunks + back.lag
    gains[...] = gains_in[...].astype(F32)
    head_gains[...] = head_gains_in[...].astype(F32)
    lane = lax.broadcasted_iota(jnp.int32, (1, 128), 1)
    earlier = (lax.broadcasted_iota(jnp.int32, (block, block), 1) < lax.broadcasted_iota(jnp.int32, (block, block), 0))
    for m in range(micro):
        @pl.loop(0, cuts)
        def _(r, m=m):
            here = pl.ds(pl.multiple_of(r * ROWS, ROWS), ROWS)
            v = x[m, here, :].astype(F32)
            v = v * lax.rsqrt(jnp.mean(v * v, axis=-1, keepdims=True) + EPS)
            gathered[m, pl.ds(pl.multiple_of(seq.e * block + r * ROWS, ROWS), ROWS), :] = (v * gains[0:1, :]).astype(BF)
    greet_lines([seq.line] + back.near())
    gather_x = seq.gather_x(gathered, g_send, g_recv)
    start_legs(gather_x)
    step(0)
    limits = jnp.concatenate([quota[...], jnp.zeros((1, 128 - experts), jnp.int32)], axis=1).astype(F32)
    dispatch[...] = jnp.zeros_like(dispatch)
    dispatch[:experts, :] = dispatch_in[...]
    for m in range(micro):
        chosen = jnp.zeros((128, block), F32)
        for j in range(TOP):
            chosen = chosen + jnp.where(routes[m, j: j + 1, :] == lax.broadcasted_iota(jnp.int32, (128, 1), 0), 1.0, 0.0)
        counts = chosen.T
        prior = jnp.dot(jnp.where(earlier, 1.0, 0.0).astype(BF), counts.astype(BF), preferred_element_type=F32)
        kept[m] = jnp.where((counts > 0.0) & (prior < limits), 1.0, 0.0)
        docs_down[m] = jnp.broadcast_to(docs[m: m + 1, :], (128, length)).astype(F32).T
    step(1)
    step(2)
    end_legs(gather_x)
    gather_c = seq.gather_c(gathered, g_send, g_recv)
    start_legs(gather_c)
    step(3)
    loads[0].wait()
    end_legs(gather_c)

    @pl.loop(0, micro)
    def _(m):
        here = pl.ds(pl.multiple_of(m * length, length), length)
        marks = jnp.zeros((length, 128), F32)
        for c in range(2):
            raw = jnp.dot(gathered[m], triple_v[c], preferred_element_type=F32)
            hat[c, here, :] = raw
            marks = marks + jnp.where(lane == c, jnp.sum(raw * raw, axis=-1, keepdims=True), 0.0)
        sums[here, :] = marks
        v_out[m] = jnp.dot(gathered[m], triple_v[2], preferred_element_type=F32).astype(BF)
        step(m + 4)

    done = micro + 5
    squares = sum_over_parts(seq, sums[...], sent, got, t_send, t_recv, lambda: step(done - 1))
    inv[...] = lax.rsqrt(squares * (1.0 / width) + EPS)
    loads[1].wait()

    @pl.loop(0, micro * heads)
    def _(i):
        m, h = lax.div(i, heads), lax.rem(i, heads)
        cols = pl.ds(pl.multiple_of(h * HD, HD), HD)
        here = pl.ds(pl.multiple_of(m * length, length), length)
        for c, to in enumerate((q_out, k_out)):
            v = hat[c, here, cols] * inv[here, c: c + 1]
            hat[c, here, cols] = v
            v = v * head_gains[c: c + 1, cols]
            to[m, :, cols] = (v * cos[...] + pltpu.roll(v, HD // 2, 1) * sin[...]).astype(BF)
        scores = lax.dot_general(
            q_out[m, :, cols], k_out[m, :, cols], (((1,), (1,)), ((), ())), preferred_element_type=F32) * scale
        allowed = (docs_down[m][:, :1] == docs[pl.ds(m, 1), :].astype(F32)) & (
            lax.broadcasted_iota(jnp.int32, (length, length), 1) <= lax.broadcasted_iota(jnp.int32, (length, length), 0))
        scores = jnp.where(allowed, scores, NEG)
        grown = jnp.exp(scores - jnp.max(scores, axis=-1, keepdims=True))
        weights = grown / jnp.sum(grown, axis=-1, keepdims=True)
        probs[m, h] = weights
        mixed[m, :, cols] = jnp.dot(weights.astype(BF), v_out[m, :, cols], preferred_element_type=F32).astype(BF)
        step(done + i)

    done = done + micro * heads

    @pl.loop(0, width // 512)
    def _(n):
        cols = pl.ds(pl.multiple_of(n * 512, 512), 512)
        for m in range(micro):
            partial[m, :, cols] = jnp.dot(mixed[m], merge_v[:, cols], preferred_element_type=F32).astype(BF)

    reduce_c = seq.reduce_c(partial, land_c, s_send, s_recv)
    start_legs(reduce_c)
    step(done)
    end_legs(reduce_c)
    seq.add_c(partial, land_c)
    reduce_x = seq.reduce_x(partial, land_x, s_send, s_recv)
    start_legs(reduce_x)
    step(done + 1)
    end_legs(reduce_x)
    seq.total_x(partial, land_x, hidden)
    for m in range(micro):
        @pl.loop(0, cuts)
        def _(r, m=m):
            here = pl.ds(pl.multiple_of(r * ROWS, ROWS), ROWS)
            v = hidden[m, here, :] + x[m, here, :].astype(F32)
            hidden[m, here, :] = v
            v = v * lax.rsqrt(jnp.mean(v * v, axis=-1, keepdims=True) + EPS)
            ffn_in[m, here, :width] = (v * gains[1:2, :]).astype(BF)
        logits = lax.dot_general(
            ffn_in[m, :, :width], dispatch[...], (((1,), (1,)), ((), ())), preferred_element_type=F32)
        logits = jnp.where(lane < experts, logits, NEG)
        grown = jnp.exp(logits - jnp.max(logits, axis=-1, keepdims=True))
        grown = grown / jnp.sum(grown, axis=-1, keepdims=True)
        gate = grown * kept[m]
        router[m] = grown + pltpu.roll(kept[m], experts, 1)
        head = gate.astype(BF).astype(F32)
        ffn_in[m, :, width:] = (head + pltpu.roll(gate - head, experts, 1)).astype(BF)
    for t in range(done + 2, steps):
        step(t)


def attention_forward(x, dy, routes, quota, gains, head_gains, cos, sin, docs, dispatch, triple, merge, collective_id):
    groups, parts = lax.axis_size("grp"), lax.axis_size("ep")
    major, minor, xn = mesh_sizes(groups, parts)
    micro, block, width = x.shape
    length = docs.shape[1]
    local_width = triple.shape[2]
    heads = local_width // HD
    tokens = micro * length
    chunks = micro * block // ROWS
    vmem = pl.BlockSpec(memory_space=pltpu.VMEM)
    hbm = pl.BlockSpec(memory_space=pl.ANY)
    low = jax.ShapeDtypeStruct((micro, length, local_width), BF)
    experts = dispatch.shape[1]
    return pl.pallas_call(
        functools.partial(forward_kernel, groups, parts, experts),
        out_shape=[
            jax.ShapeDtypeStruct((micro, length, width), BF),
            low, low, low, low,
            jax.ShapeDtypeStruct((micro, heads, length, length), F32),
            jax.ShapeDtypeStruct((2, tokens, local_width), F32),
            jax.ShapeDtypeStruct((tokens, 128), F32),
            jax.ShapeDtypeStruct((micro, block, width), F32),
            jax.ShapeDtypeStruct((micro, block, width + 128), BF),
            jax.ShapeDtypeStruct((micro, block, 128), F32),
            jax.ShapeDtypeStruct((chunks, 2, xn, major, minor, ROWS, width), BF),
        ],
        in_specs=[vmem] * 10 + [hbm] * 2,
        out_specs=[vmem] * 11 + [hbm],
        scratch_shapes=[
            pltpu.VMEM((micro, block, 128), F32),
            pltpu.VMEM(gains.shape, F32),
            pltpu.VMEM(head_gains.shape, F32),
            pltpu.VMEM((micro, length, 128), F32),
            pltpu.VMEM((128, width), BF),
            pltpu.VMEM(triple.shape, BF),
            pltpu.VMEM(merge.shape, BF),
            pltpu.VMEM((tokens, 128), F32),
            pltpu.VMEM((micro, length, width), BF),
            pltpu.VMEM((micro, xn, block, width), BF),
            pltpu.VMEM((micro, xn - 1, block, width), BF),
            pltpu.VMEM((8, tokens), F32),
            pltpu.VMEM((parts - 1, 8, tokens), F32),
            pltpu.SemaphoreType.DMA((2,)),
            pltpu.SemaphoreType.DMA((micro, 2 * xn - 1)),
            pltpu.SemaphoreType.DMA((micro, 2 * xn - 1)),
            pltpu.SemaphoreType.DMA((micro, 2 * xn - 1)),
            pltpu.SemaphoreType.DMA((micro, 2 * xn - 1)),
            pltpu.SemaphoreType.DMA((parts - 1,)),
            pltpu.SemaphoreType.DMA((parts - 1,)),
        ] + BackGather.scratch(chunks),
        compiler_params=pltpu.CompilerParams(
            collective_id=collective_id, has_side_effects=True, vmem_limit_bytes=56 * 2**20
        ),
        cost_estimate=pl.CostEstimate(flops=6 * 10**9, bytes_accessed=40 * 2**20, transcendentals=0),
    )(x, dy.reshape(chunks, ROWS, width), routes.transpose(0, 2, 1), quota.reshape(1, -1), gains, head_gains, cos, sin, docs,
      dispatch.T, triple, merge)


def per_device(
    block_entry_states,
    document_labels,
    token_assignments,
    worker_quota_tallies,
    rescale_factors_both,
    triple_projection_matrix,
    probe_lookup_scalers,
    heads_merge_matrix,
    dispatcher_matrix,
    specialist_widen_matrix,
    specialist_shrink_matrix,
    output_gradient,
):
    micro, local_rows, width = block_entry_states.shape
    groups, parts = lax.axis_size("grp"), lax.axis_size("ep")
    major, minor, xs = mesh_sizes(groups, parts)
    group = lax.axis_index("grp")
    part = lax.axis_index("ep")
    seq_len = document_labels.shape[1]
    experts = dispatcher_matrix.shape[1]
    local_exp = specialist_widen_matrix.shape[0]
    inner = specialist_shrink_matrix.shape[1]
    share = inner // groups
    local_width = triple_projection_matrix.shape[2]
    heads = local_width // HD
    scale = 1.0 / math.sqrt(HD)
    gains = rescale_factors_both.astype(F32)
    cos, signed_sin = rope_tables(seq_len, HD)
    triple = triple_projection_matrix.transpose(1, 0, 2)
    gathered, queries, keys, values, mixed, weights, qk_hat, qk_inv, hidden, ffn_ext, probs, dy_all = attention_forward(
        block_entry_states, output_gradient, token_assignments, worker_quota_tallies, rescale_factors_both,
        probe_lookup_scalers, cos, signed_sin,
        document_labels, dispatcher_matrix, triple, heads_merge_matrix, 0)
    ffn_in = ffn_ext[..., :width]

    fused = xs == minor and share % 128 == 0 and local_exp % 2 == 0 and 2 * xs * minor * major * ROWS <= 512
    chunk_shape = (micro * local_rows // ROWS, 2, xs, major, minor, ROWS)
    if fused:
        dx_sum, moe_part, grad_widen, grad_shrink = experts_together(
            ffn_ext, dy_all.reshape(dy_all.shape[0], -1, width), specialist_widen_matrix, specialist_shrink_matrix, experts, 1)
    else:
        dx_sum, moe_part, grad_widen, grad_shrink = experts_apart(
            ffn_ext, dy_all, specialist_widen_matrix, specialist_shrink_matrix, experts)
    dx_sum = dx_sum.astype(F32).reshape(micro, local_rows, width + 128)
    grad_widen = grad_widen.reshape(groups, width // groups, -1)

    inv_second = lax.rsqrt(jnp.mean(hidden * hidden, axis=-1, keepdims=True) + EPS)
    hat_second = hidden * inv_second
    probs, keep = probs[..., :experts], probs[..., experts: 2 * experts]
    d_probs = dx_sum[..., width: width + experts] * keep
    d_logits = probs * (d_probs - jnp.sum(probs * d_probs, axis=-1, keepdims=True))
    d_ffn = dx_sum[..., :width] + jnp.einsum("mte,de->mtd", d_logits, dispatcher_matrix.astype(F32), precision=HIGH)
    grad_router = jnp.einsum("mtd,mte->ed", ffn_in.astype(F32), d_logits, precision=HIGH)
    scaled = d_ffn * gains[1]
    adjoint = output_gradient.astype(F32)
    d_hidden = adjoint + inv_second * (scaled - hat_second * jnp.mean(scaled * hat_second, axis=-1, keepdims=True))
    grad_second = jnp.sum(d_ffn * hat_second, axis=(0, 1))

    d_proj, d_attn_in, grad_heads, grad_out, grad_widen, moe = attention_back(
        d_hidden.astype(BF), heads_merge_matrix, triple, queries, keys, values, mixed, weights,
        qk_hat, qk_inv, probe_lookup_scalers, cos, signed_sin, grad_widen,
        moe_part.reshape(chunk_shape + (width,)) if fused else None, 5)
    if not fused:
        moe = scatter_all(moe_part.reshape(chunk_shape + (width,)), 3)
    output = (hidden + moe.astype(F32).reshape(micro, local_rows, width)).astype(BF)
    skip = block_entry_states.astype(F32)
    inv_first = lax.rsqrt(jnp.mean(skip * skip, axis=-1, keepdims=True) + EPS)
    hat_first = skip * inv_first
    scaled = d_attn_in * gains[0]
    grad_input = d_hidden + inv_first * (scaled - hat_first * jnp.mean(scaled * hat_first, axis=-1, keepdims=True))
    grad_first = jnp.sum(d_attn_in * hat_first, axis=(0, 1))

    shared = jnp.concatenate([grad_first[None], grad_second[None], grad_router]).reshape(-1).astype(BF)
    own = grad_heads[:2].reshape(-1).astype(BF)
    gap, size = shared.shape[0], shared.shape[0] + own.shape[0]
    block = (groups, ROWS, -(-size // (groups * ROWS * 128)) * 128)
    room = math.prod(block)
    shared = jnp.pad(shared, (0, room - gap)).reshape(block)
    own = jnp.pad(own, (gap, room - size)).reshape(block)
    out_sum, qkv_sum, misc_sum = total_over_groups(
        gathered.reshape(-1, width), d_proj, grad_out, shared, own, 4)
    qkv_sum, out_sum, grad_widen, grad_shrink = finish(
        qkv_sum.reshape(-1, local_width), out_sum.reshape(-1, width), grad_widen, grad_shrink, local_exp, share)
    qkv_sum = qkv_sum.reshape(3, width, local_width).transpose(1, 0, 2)
    grad_shrink = grad_shrink.reshape(local_exp, share, width)
    misc_sum = misc_sum.reshape(-1)[:size].astype(F32)
    rows = misc_sum[: (2 + experts) * width].reshape(2 + experts, width)
    return (
        output,
        grad_input,
        rows[:2],
        qkv_sum,
        misc_sum[(2 + experts) * width:].reshape(2, local_width),
        out_sum,
        rows[2:].T,
        grad_widen,
        grad_shrink,
    )


def solution(mesh):
    return jax.shard_map(
        per_device,
        mesh=mesh,
        in_specs=(
            P(None, ALL, None),
            P(None, "grp"),
            P(None, ALL, None),
            P(),
            P(),
            P(None, None, "ep"),
            P(None, "ep"),
            P("ep", None),
            P(),
            P("ep", None, None),
            P("ep", None, None),
            P(None, ALL, None),
        ),
        out_specs=(
            P(None, ALL, None),
            P(None, ALL, None),
            P(),
            P(None, None, "ep"),
            P(None, "ep"),
            P("ep", None),
            P(),
            P("ep", "grp", None),
            P("ep", "grp", None),
        ),
        check_vma=False,
    )
```

```python
import functools
import math

import jax
import jax.numpy as jnp
import numpy as np
from jax import lax
from jax.experimental import pallas as pl
from jax.experimental.pallas import tpu as pltpu
from jax.sharding import PartitionSpec as P

HD = 128
TOP = 8
EPS = 1e-05
THETA = 10000.0
NEG = -1e30
HIGH = lax.Precision.HIGHEST
ALL = ("grp", "ep")
MESH = pl.DeviceIdType.MESH
ROWS = 16
CUTS = 8
PER_STEP = 6
BF = jnp.bfloat16
F32 = jnp.float32


def rope_tables(length, head_dim):
    half = head_dim // 2
    angle = np.arange(length)[:, None] * THETA ** (-np.arange(half) * 2.0 / head_dim)
    cos, sin = np.cos(angle), np.sin(angle)
    return np.concatenate([cos, cos], 1).astype(np.float32), np.concatenate([-sin, sin], 1).astype(np.float32)


def mesh_sizes(groups, parts):
    major = 4 if groups % 4 == 0 else groups
    return major, groups // major, parts // 2


class Line:
    def __init__(self, size, place, step):
        self.size, self.place, self.step = size, place, step

    def at(self, hops):
        return (
            lax.axis_index("grp") + hops * self.step[0],
            lax.axis_index("ep") + hops * self.step[1],
        )


def lines(groups, parts):
    major, minor, xs = mesh_sizes(groups, parts)
    g, e = lax.axis_index("grp"), lax.axis_index("ep")
    core = lax.rem(e, 2)
    x_pos, minor_pos = lax.div(e, 2), lax.rem(g, minor)
    if xs == minor:
        first = Line(xs, jnp.where(core == 0, x_pos, minor_pos), (core, 2 - 2 * core))
        second = Line(xs, jnp.where(core == 0, minor_pos, x_pos), (1 - core, 2 * core))
    else:
        first = Line(xs, x_pos, (0, 2))
        second = Line(minor, minor_pos, (1, 0))
    return Line(2, core, (0, 1)), first, Line(major, lax.div(g, minor), (minor, 0)), second


def greet(some, whole=()):
    barrier = pltpu.get_barrier_semaphore()
    peers = sum(line.size - 1 for line in whole)
    for line in whole:
        for j in range(1, line.size):
            to = lax.rem(line.place + j, line.size)
            pl.semaphore_signal(barrier, inc=1, device_id=line.at(to - line.place), device_id_type=MESH)
    for line in some:
        if line.size == 2:
            pl.semaphore_signal(barrier, inc=1, device_id=line.at(1 - 2 * line.place), device_id_type=MESH)
            peers = peers + 1
        else:
            for way, there in ((1, line.place < line.size - 1), (-1, line.place > 0)):

                @pl.when(there)
                def _(line=line, way=way):
                    pl.semaphore_signal(barrier, inc=1, device_id=line.at(way), device_id_type=MESH)

                peers = peers + there.astype(jnp.int32)
    pl.semaphore_wait(barrier, peers)


def greet_lines(some):
    barrier = pltpu.get_barrier_semaphore()
    for line in some:
        for j in range(1, line.size):
            to = lax.rem(line.place + j, line.size)
            pl.semaphore_signal(barrier, inc=1, device_id=line.at(to - line.place), device_id_type=MESH)
    pl.semaphore_wait(barrier, sum(line.size - 1 for line in some))


def remote(src, dst, send, recv, target):
    return pltpu.make_async_remote_copy(
        src_ref=src, dst_ref=dst, send_sem=send, recv_sem=recv, device_id=target, device_id_type=MESH
    )


class Hop:
    def __init__(self, legs, after=None):
        self.legs, self.after = legs, after

    def _each(self, which, act):
        for leg in self.legs:
            if leg[which] is None:
                act(leg)
            else:
                pl.when(leg[which])(functools.partial(act, leg))

    def start(self):
        self._each(0, lambda leg: leg[2]().start())

    def arrive(self):
        def act(leg):
            leg[3]().wait_recv()
            if leg[4] is not None:
                leg[4]()

        self._each(1, act)

    def sent(self):
        self._each(0, lambda leg: leg[2]().wait_send())

    def finish(self):
        self.arrive()
        self.sent()


def spread_hops(core, first, third, fourth, at, own, send, recv):
    c, p, z, q = core.place, first.place, third.place, fourth.place
    r4 = ROWS
    r3 = r4 * fourth.size
    r2 = r3 * third.size
    rc = r2 * first.size
    base = [0]

    def sems(n):
        b = base[0]
        base[0] += n
        return (lambda i: send(b + i)), (lambda i: recv(b + i))

    def swap(line, place, first_source=None):
        source = first_source or (lambda i: place(line.place))
        return Swap(line, source, lambda j, i: place(i), *sems(line.size - 1))

    hops = [swap(fourth, lambda i: at(c * rc + p * r2 + z * r3 + i * r4, r4), lambda i: own)]
    hops += gather_hops(third, lambda i: at(c * rc + p * r2 + i * r3, r3), *sems(leg_count(third.size)))
    hops.append(swap(first, lambda i: at(c * rc + i * r2, r2)))
    hops.append(swap(core, lambda i: at(i * rc, rc)))
    return hops


def gather_hops(line, at, send, recv, own=None):
    n, a = line.size, line.place
    if n == 2:
        mine, theirs, peer = at(a), at(1 - a), line.at(1 - 2 * a)
        return [
            Hop([(None, None, lambda: remote(mine if own is None else own, mine, send(0), recv(0), peer),
                  lambda: remote(theirs, theirs, send(0), recv(0), peer), None)])
        ]
    hops = []
    for s in range(1, n):
        legs = []
        for d, way in enumerate((1, -1)):
            k = (s - 1) * 2 + d
            out = a - way * (s - 1)
            into = a - way * s
            sends = (out >= 0) & (out < n) & (a + way >= 0) & (a + way < n)
            gets = (into >= 0) & (into < n)
            out, into = jnp.clip(out, 0, n - 1), jnp.clip(into, 0, n - 1)
            legs.append((
                sends, gets,
                lambda out=out, way=way, k=k, s=s: remote(
                    own if s == 1 and own is not None else at(out), at(out), send(k), recv(k), line.at(way)),
                lambda into=into, way=way, k=k: remote(at(into), at(into), send(k), recv(k), line.at(-way)),
                None,
            ))
        hops.append(Hop(legs))
    return hops


def reduce_hops(line, acc, land, add, send, recv):
    n, a = line.size, line.place
    if n == 2:
        peer = line.at(1 - 2 * a)
        return [
            Hop([(None, None, lambda: remote(acc(1 - a), land(0), send(0), recv(0), peer),
                  lambda: remote(land(0), land(0), send(0), recv(0), peer),
                  lambda: add(acc(a), land(0)))])
        ]
    hops = []
    for s in range(n - 1):
        legs = []
        for d, way in enumerate((1, -1)):
            k = s * 2 + d
            b = a if way == 1 else n - 1 - a
            sends = (b <= s) & (b < n - 1)
            gets = (b - 1 <= s) & (b >= 1)
            out = b + n - 1 - s
            into = b + n - 2 - s
            out, into = jnp.clip(out, 0, n - 1), jnp.clip(into, 0, n - 1)
            if way == -1:
                out, into = n - 1 - out, n - 1 - into
            legs.append((
                sends, gets,
                lambda out=out, way=way, k=k: remote(acc(out), land(k), send(k), recv(k), line.at(way)),
                lambda way=way, k=k: remote(land(k), land(k), send(k), recv(k), line.at(-way)),
                lambda into=into, k=k: add(acc(into), land(k)),
            ))
        hops.append(Hop(legs))
    return hops


def hop_count(n):
    return 1 if n == 2 else n - 1


def leg_count(n):
    return 1 if n == 2 else 2 * (n - 1)


def flow(chains, pace=1):
    depth, count = max(len(c) for c in chains), len(chains)
    for t in range(count + pace * depth):
        for k in range(count):
            i, rest = divmod(t - k, pace)
            if rest:
                continue
            if 1 <= i <= len(chains[k]):
                chains[k][i - 1].arrive()
            if 0 <= i < len(chains[k]):
                chains[k][i].start()
    for chain in chains:
        for hop in chain:
            hop.sent()


def add(acc, land):
    lead = acc.shape[:-2]

    def one(i):
        where = []
        for size in reversed(lead):
            where.insert(0, lax.rem(i, size))
            i = lax.div(i, size)
        where = tuple(where) + (slice(None), slice(None))
        acc[where] = (acc[where].astype(F32) + land[where].astype(F32)).astype(acc.dtype)

    if lead:
        pl.loop(0, math.prod(lead))(one)
    else:
        one(0)


def gather_kernel(groups, parts, x, out, local, send, recv):
    core, first, second, long = lines(groups, parts)
    c, p, q, z = core.place, first.place, second.place, long.place
    greet([core, first, second, long])
    chunks = x.shape[0]
    own = [pltpu.make_async_copy(x.at[k], out.at[k, c, p, q, z], local.at[k]) for k in range(chunks)]
    for copy in own:
        copy.start()
    chains = []
    for k in range(chunks):
        base = [0]

        def sems(n, k=k, base=base):
            b = base[0]
            base[0] += leg_count(n)
            return (lambda i: send.at[k, b + i]), (lambda i: recv.at[k, b + i])

        chain = []
        chain += gather_hops(long, lambda i, k=k: out.at[k, c, p, q, i], *sems(long.size))
        chain += gather_hops(second, lambda i, k=k: out.at[k, c, p, i], *sems(second.size))
        chain += gather_hops(first, lambda i, k=k: out.at[k, c, i], *sems(first.size))
        chain += gather_hops(core, lambda i, k=k: out.at[k, i], *sems(2))
        chains.append(chain)
    for copy in own:
        copy.wait()
    flow(chains)


def gather_all(x, collective_id):
    groups, parts = lax.axis_size("grp"), lax.axis_size("ep")
    major, minor, xs = mesh_sizes(groups, parts)
    width = x.shape[-1]
    x = x.reshape(-1, ROWS, width)
    legs = sum(leg_count(n) for n in (2, xs, minor, major))
    chunks = x.shape[0]
    return pl.pallas_call(
        functools.partial(gather_kernel, groups, parts),
        out_shape=jax.ShapeDtypeStruct((chunks, 2, xs, major, minor, ROWS, width), x.dtype),
        in_specs=[pl.BlockSpec(memory_space=pl.ANY)],
        out_specs=pl.BlockSpec(memory_space=pl.ANY),
        scratch_shapes=[
            pltpu.SemaphoreType.DMA((chunks,)),
            pltpu.SemaphoreType.DMA((chunks, legs)),
            pltpu.SemaphoreType.DMA((chunks, legs)),
        ],
        compiler_params=pltpu.CompilerParams(collective_id=collective_id, has_side_effects=True),
    )(x)


def scatter_kernel(groups, parts, part, out, acc, land_c, land_p, land_q, land_z, local, send, recv):
    core, first, second, long = lines(groups, parts)
    c, p, q, z = core.place, first.place, second.place, long.place
    chunks = part.shape[0]
    own = [pltpu.make_async_copy(part.at[k, c], acc.at[k], local.at[k]) for k in range(chunks)]
    for copy in own:
        copy.start()
    greet([core, first, second, long])
    chains = []
    for k in range(chunks):
        base = [0]

        def sems(n, k=k, base=base):
            b = base[0]
            base[0] += leg_count(n)
            return (lambda i: send.at[k, b + i]), (lambda i: recv.at[k, b + i])

        def add_own(acc_ref, land_ref, k=k):
            own[k].wait()
            add(acc_ref, land_ref)

        s, r = sems(2)
        peer = core.at(1 - 2 * c)
        other = part.at[k, 1 - c]
        chain = [Hop([(
            None, None,
            lambda other=other, s=s, r=r, k=k: remote(other, land_c.at[k], s(0), r(0), peer),
            lambda s=s, r=r, k=k: remote(land_c.at[k], land_c.at[k], s(0), r(0), peer),
            lambda k=k, add_own=add_own: add_own(acc.at[k], land_c.at[k]),
        )])]
        chain += reduce_hops(first, lambda i, k=k: acc.at[k, i], lambda i, k=k: land_p.at[k, i], add, *sems(first.size))
        chain += reduce_hops(second, lambda i, k=k: acc.at[k, p, i], lambda i, k=k: land_q.at[k, i], add, *sems(second.size))
        chain += reduce_hops(long, lambda i, k=k: acc.at[k, p, q, i], lambda i, k=k: land_z.at[k, i], add, *sems(long.size))
        chains.append(chain)
    flow(chains)
    for k in range(chunks):
        out[k] = acc[k, p, q, z]


def scatter_all(part, collective_id):
    groups, parts = lax.axis_size("grp"), lax.axis_size("ep")
    major, minor, xs = mesh_sizes(groups, parts)
    legs = sum(leg_count(n) for n in (2, xs, minor, major))
    chunks, width = part.shape[0], part.shape[-1]
    unit = 2 * ROWS * width
    need = unit * (2 * xs * minor * major + leg_count(xs) * minor * major + leg_count(major) * minor + leg_count(minor) + 2)
    per = chunks
    while per > 1 and per * need > 44 * 2**20:
        per //= 2
    call = pl.pallas_call(
        functools.partial(scatter_kernel, groups, parts),
        out_shape=jax.ShapeDtypeStruct((per, ROWS, width), BF),
        in_specs=[pl.BlockSpec(memory_space=pl.ANY)],
        out_specs=pl.BlockSpec(memory_space=pltpu.VMEM),
        scratch_shapes=[
            pltpu.VMEM((per, xs, major, minor, ROWS, width), BF),
            pltpu.VMEM((per, xs, major, minor, ROWS, width), BF),
            pltpu.VMEM((per, leg_count(xs), major, minor, ROWS, width), BF),
            pltpu.VMEM((per, leg_count(major), minor, ROWS, width), BF),
            pltpu.VMEM((per, leg_count(minor), ROWS, width), BF),
            pltpu.SemaphoreType.DMA((per,)),
            pltpu.SemaphoreType.DMA((per, legs)),
            pltpu.SemaphoreType.DMA((per, legs)),
        ],
        compiler_params=pltpu.CompilerParams(
            collective_id=collective_id, has_side_effects=True, vmem_limit_bytes=56 * 2**20
        ),
    )
    return jnp.concatenate([call(part[i:i + per]) for i in range(0, chunks, per)]) if per < chunks else call(part)


class Begun:
    def __init__(self, hop, before):
        self.hop, self.before = hop, before

    def start(self):
        self.before()
        self.hop.start()

    def arrive(self):
        self.hop.arrive()

    def sent(self):
        self.hop.sent()


def total_kernel(groups, parts, plan, rows_in, d_proj, grad_out, shared, own, *refs):
    count = 3
    outs, acc, land = (refs[i * count: (i + 1) * count] for i in range(3))
    rows_v, proj_v, shared_v, own_v, got, local, stored, send, recv, t_send, t_recv = refs[3 * count:]
    major, minor, _ = mesh_sizes(groups, parts)
    g, e = lax.axis_index("grp"), lax.axis_index("ep")
    short = Line(minor, lax.rem(g, minor), (1, 0))
    long = Line(major, lax.div(g, minor), (minor, 0))
    whole = Line(parts, e, (0, 1))
    width = rows_in.shape[1]
    load = [pltpu.make_async_copy(a, b, local.at[i]) for i, (a, b) in enumerate((
        (grad_out, acc[0]), (rows_in, rows_v), (d_proj, proj_v), (shared, shared_v), (own, own_v)))]
    for copy in load:
        copy.start()

    def weights(k):
        def act():
            if k == 0:
                load[1].wait()
                load[2].wait()
            cuts = acc[1].shape[0] // 3
            c, cut = k // cuts, k % cuts
            blocks = max(1, 256 // acc[1].shape[2])
            rows = blocks * acc[1].shape[2]

            @pl.loop(0, groups // blocks)
            def _(i):
                cols = pl.ds(pl.multiple_of(cut * (width // cuts) + i * rows, 128), rows)
                total = lax.dot_general(rows_v[:, cols], proj_v[c], (((0,), (0,)), ((), ())), preferred_element_type=F32)
                acc[1][k, pl.ds(i * blocks, blocks)] = total.astype(BF).reshape((blocks,) + acc[1].shape[2:])

        return act

    swap = swap_legs(whole, lambda i: shared_v, lambda j, i: got.at[j], lambda j: t_send.at[j], lambda j: t_recv.at[j])

    def everyone():
        end_legs(swap)
        load[4].wait()

        @pl.loop(0, groups)
        def _(i):
            total = shared_v[i].astype(F32) + own_v[i].astype(F32)
            for j in range(parts - 1):
                total = total + got[j, i].astype(F32)
            acc[2][0, i] = total.astype(BF)

    before = {(0, 0): load[0].wait, (2, 0): everyone}
    chains = []
    for number, (j, k, far) in enumerate(plan):
        one, two = (long, short) if far else (short, long)
        y, z = one.place, two.place
        n = two.size

        def level_one(ref, k, n=n):
            return lambda i: ref.at[k, pl.ds(i * n, n)]

        def level_two(ref, k, y=y, n=n):
            return lambda i: ref.at[k, y * n + i]

        store = pltpu.make_async_copy(acc[j].at[k, y * n + z], outs[j].at[k, y * n + z], stored.at[number])
        base = [0]

        def sems(size, number=number, base=base):
            b = base[0]
            base[0] += leg_count(size)
            return (lambda i: send.at[number, b + i]), (lambda i: recv.at[number, b + i])

        first_land = leg_count(one.size) * n
        down = reduce_hops(one, level_one(acc[j], k), lambda i, j=j, k=k, n=n: land[j].at[k, pl.ds(i * n, n)], add, *sems(one.size))
        down += reduce_hops(two, level_two(acc[j], k), lambda i, j=j, k=k, f=first_land: land[j].at[k, f + i], add, *sems(two.size))
        up = gather_hops(two, level_two(outs[j], k), *sems(two.size), own=acc[j].at[k, y * n + z])
        turn = len(up)
        up += gather_hops(one, level_one(outs[j], k), *sems(one.size))

        down[0] = Begun(down[0], before.get((j, k)) or (weights(k) if j == 1 else lambda: None))
        up[0] = Begun(up[0], store.start)
        up[turn] = Begun(up[turn], store.wait)
        chains.append(down + up)
    greet([short, long], [whole])
    load[3].wait()
    start_legs(swap)
    flow(chains, 2)


def total_over_groups(gathered, d_proj, grad_out, shared, own, collective_id):
    groups, parts = lax.axis_size("grp"), lax.axis_size("ep")
    major, minor, _ = mesh_sizes(groups, parts)
    tokens, width = gathered.shape
    local_width = d_proj.shape[2]
    few = max(n for n in (4, 2, 1) if n == 1 or grad_out.shape[0] % (n * groups * ROWS) == 0)
    many = max(n for n in (12, 6, 3) if n == 3 or 3 * width % (n * groups * ROWS) == 0)
    shapes = [
        (few, groups, grad_out.shape[0] // few // groups, width),
        (many, groups, 3 * width // many // groups, local_width),
        (1,) + shared.shape,
    ]
    plan = [(0, k, k % 4 == 1) for k in range(few)] + [(1, k, k % 4 == 1) for k in range(many)] + [(2, 0, False)]
    blocks = max(leg_count(a) * b + leg_count(b) for a, b in ((minor, major), (major, minor)))
    legs = 2 * (leg_count(minor) + leg_count(major))
    total = len(plan)
    hbm = pl.BlockSpec(memory_space=pl.ANY)
    scratch = [pltpu.VMEM(a, BF) for a in shapes]
    scratch += [pltpu.VMEM((a[0], blocks) + a[2:], BF) for a in shapes]
    return pl.pallas_call(
        functools.partial(total_kernel, groups, parts, plan),
        out_shape=[jax.ShapeDtypeStruct(a, BF) for a in shapes],
        in_specs=[hbm] * 5,
        out_specs=[hbm] * len(shapes),
        scratch_shapes=scratch + [
            pltpu.VMEM(gathered.shape, BF),
            pltpu.VMEM(d_proj.shape, BF),
            pltpu.VMEM(shared.shape, BF),
            pltpu.VMEM(shared.shape, BF),
            pltpu.VMEM((parts - 1,) + shared.shape, BF),
            pltpu.SemaphoreType.DMA((5,)),
            pltpu.SemaphoreType.DMA((total,)),
            pltpu.SemaphoreType.DMA((total, legs)),
            pltpu.SemaphoreType.DMA((total, legs)),
            pltpu.SemaphoreType.DMA((parts - 1,)),
            pltpu.SemaphoreType.DMA((parts - 1,)),
        ],
        compiler_params=pltpu.CompilerParams(
            collective_id=collective_id, has_side_effects=True, vmem_limit_bytes=48 * 2**20
        ),
        cost_estimate=pl.CostEstimate(flops=6 * tokens * width * local_width, bytes_accessed=40 * 2**20, transcendentals=0),
    )(gathered, d_proj, grad_out.reshape(shapes[0]), shared, own)


def swap_legs(line, source, target, send, recv):
    n, a = line.size, line.place
    legs = []
    for j in range(1, n):
        to, off = lax.rem(a + j, n), lax.rem(a + n - j, n)
        legs.append((
            lambda to=to, j=j: remote(source(to), target(j - 1, a), send(j - 1), recv(j - 1), line.at(to - a)),
            lambda off=off, j=j: remote(target(j - 1, off), target(j - 1, off), send(j - 1), recv(j - 1), line.at(off - a)),
        ))
    return legs


def start_legs(legs):
    for out, _ in legs:
        out().start()


def end_legs(legs):
    for out, into in legs:
        into().wait_recv()
    for out, into in legs:
        out().wait_send()


class Swap:
    def __init__(self, *how):
        self.legs = swap_legs(*how)

    def start(self):
        start_legs(self.legs)

    def finish(self):
        end_legs(self.legs)


def add_rows(acc, first, land, rows):
    @pl.loop(0, rows // ROWS)
    def _(i):
        here = pl.ds(pl.multiple_of(first + i * ROWS, ROWS), ROWS)
        there = pl.ds(pl.multiple_of(i * ROWS, ROWS), ROWS)
        acc[here, :] = (acc[here, :].astype(F32) + land[there, :].astype(F32)).astype(acc.dtype)


def experts_kernel(
    groups, parts, local_rows, acc_ring, experts,
    x, dy, widen, shrink,
    summed, moe, grad_widen, grad_shrink,
    xs, dys, wide, down, sum_wide, sum_down, stage, acc, other, land_c, land_p, land_q, land_z,
    hid, raw, gated, d_gu, gate, product, marks,
    load, dy_sem, stage_sem, g_send, g_recv, s_send, s_recv,
):
    core, first, third, fourth = lines(groups, parts)
    c, p, z, q = core.place, first.place, third.place, fourth.place
    pn, zn, qn = first.size, third.size, fourth.size
    chunks, width = x.shape[0], shrink.shape[2]
    local_exp, inner = shrink.shape[0], shrink.shape[1]
    share = inner // groups
    group, part = lax.axis_index("grp"), lax.axis_index("ep")
    rq, rz, rp, rc = ROWS, ROWS * qn, ROWS * qn * zn, ROWS * qn * zn * pn
    rows = 2 * rc
    levels = 3 + hop_count(zn)
    cuts = local_rows // ROWS
    base = part * local_exp
    pairs = local_exp // 2

    loads = []
    for e in range(local_exp):
        for half in range(2):
            to = (e // 2) * 4 * share + half * 2 * share + (e % 2) * share
            loads.append(pltpu.make_async_copy(
                widen.at[e, :, pl.ds(pl.multiple_of(half * inner + group * share, share), share)],
                wide.at[:, pl.ds(to, share)], load.at[2 * e + half]))
        loads.append(pltpu.make_async_copy(
            shrink.at[e, pl.ds(pl.multiple_of(group * share, share), share), :],
            down.at[pl.ds(e * share, share), :], load.at[2 * local_exp + e]))
    for copy in loads:
        copy.start()

    def dy_copy(k):
        return pltpu.make_async_copy(dy.at[k], dys.at[lax.rem(k, 2)], dy_sem.at[lax.rem(k, 2)])

    dy_start = lambda k: dy_copy(k).start()
    dy_start(0)
    greet_lines([core, first, third, fourth])

    def rows_at(start, size):
        return pl.ds(pl.multiple_of(start, ROWS), size)

    def g_hop(k, level):
        buf = xs.at[k]
        return spread_hops(core, first, third, fourth, lambda start, size: buf.at[rows_at(start, size), :], x.at[k],
                           lambda i: g_send.at[k, i], lambda i: g_recv.at[k, i])[level]

    def s_line(k, line, at, land, offset):
        return Swap(line, at, lambda j, i: land.at[lax.rem(k, 2), j],
                    lambda j: s_send.at[k, offset + j], lambda j: s_recv.at[k, offset + j])

    def mine(k):
        return acc.at[lax.rem(k, acc_ring)]

    def s_hop(k, level):
        if level == 0:
            return s_line(k, core, lambda i: other, land_c, 0)
        if level == 1:
            return s_line(k, first, lambda i: mine(k).at[i], land_p, 1)
        if level == 2:
            return s_line(k, fourth, lambda i: mine(k).at[p, :, i], land_q, pn)
        return s_line(k, third, lambda i: mine(k).at[p, i, q], land_z, pn + qn - 1)

    def s_end(k, level):
        s_hop(k, level).finish()
        slot = lax.rem(k, 2)
        if level == 3:
            total = mine(k)[p, z, q].astype(F32)
            for j in range(zn - 1):
                total = total + land_z[slot, j].astype(F32)
            summed[k] = total.astype(BF)
            return
        if level == 0 and pn == 2:
            add(mine(k).at[1 - p], land_c.at[slot, 0, 1 - p])
            s_hop(k, 1).start()
            add(mine(k).at[p], land_c.at[slot, 0, p])
            return
        to = (mine(k), mine(k).at[p], mine(k).at[p, :, q])[level]
        land = (land_c, land_p, land_q)[level]
        for j in range(land.shape[1]):
            add(to, land.at[slot, j])
        s_hop(k, level + 1).start()

    def after(t, lag, act):
        k = t - lag

        @pl.when((k >= 0) & (k < chunks))
        def _():
            act(k)

    tiles = width // 512

    def compute(k):
        buf, dyk = xs.at[k], dys.at[lax.rem(k, 2)]

        @pl.when(k == 0)
        def _():
            for copy in loads:
                copy.wait()

        dy_copy(k).wait()

        @pl.when(k + 1 < chunks)
        def _():
            dy_start(k + 1)

        @pl.loop(0, pairs)
        def _(j):
            cols = pl.ds(pl.multiple_of(j * 4 * share, 4 * share), 4 * share)
            some = pl.ds(pl.multiple_of(j * 2 * share, 2 * share), 2 * share)
            to_up = pl.ds(pl.multiple_of(j * 4 * share + 2 * share, share), 2 * share)
            to_gate = pl.ds(pl.multiple_of(j * 4 * share, share), 2 * share)
            hid[...] = jnp.dot(buf[:, :width], wide[:, cols], preferred_element_type=F32)
            raw[...] = lax.dot_general(dyk[...], down[some, :], (((1,), (1,)), ((), ())), preferred_element_type=F32)
            gate[...] = jnp.dot(buf[:, width:], marks[:, some], preferred_element_type=F32)

            @pl.loop(0, rows // 32)
            def _(i):
                here = pl.ds(pl.multiple_of(i * 32, 32), 32)
                g, u = hid[here, : 2 * share], hid[here, 2 * share:]
                d, weight = raw[here, :], gate[here, :]
                sigma = 0.5 * jnp.tanh(0.5 * g) + 0.5
                swish = g * sigma
                act = swish * u
                product[here, some] = (act * d).astype(BF)
                gated[here, some] = (act * weight).astype(BF)
                d = d * weight
                d_gu[here, to_gate] = (d * u * (sigma + swish * (1.0 - sigma))).astype(BF)
                d_gu[here, to_up] = (d * swish).astype(BF)

        kept = mine(k)

        def split(cols, total):
            total = total.astype(BF).reshape((2,) + other.shape[:-1] + total.shape[1:])

            @pl.when(c == 0)
            def _():
                kept[..., cols] = total[0]
                other[..., cols] = total[1]

            @pl.when(c == 1)
            def _():
                other[..., cols] = total[0]
                kept[..., cols] = total[1]

        @pl.loop(0, tiles)
        def _(n):
            cols = pl.ds(pl.multiple_of(n * 512, 512), 512)
            split(cols, lax.dot_general(
                d_gu[...], wide[cols, :], (((1,), (1,)), ((), ())), preferred_element_type=F32))

        split(pl.ds(width, 128), lax.dot_general(
            product[...], marks[...], (((1,), (1,)), ((), ())), preferred_element_type=F32))
        s_hop(k, 0).start()

        @pl.when(k >= 1)
        def _():
            pltpu.make_async_copy(stage, moe.at[k - 1], stage_sem.at[0]).wait()

        @pl.loop(0, tiles)
        def _(n):
            cols = pl.ds(pl.multiple_of(n * 512, 512), 512)
            stage[:, cols] = jnp.dot(gated[...], down[:, cols], preferred_element_type=F32).astype(BF)
            sum_wide[cols, :] += lax.dot_general(
                buf[:, cols], d_gu[...], (((0,), (0,)), ((), ())), preferred_element_type=F32)
            sum_down[:, cols] += lax.dot_general(
                gated[...], dyk[:, cols], (((0,), (0,)), ((), ())), preferred_element_type=F32)

        pltpu.make_async_copy(stage, moe.at[k], stage_sem.at[0]).start()

    def begin(k):
        xs[k, rows_at(c * rc + p * rp + z * rz + q * rq, rq), :] = x[k]
        g_hop(k, 0).start()

        @pl.when(k == 0)
        def _():
            sum_wide[...] = jnp.zeros_like(sum_wide)
            sum_down[...] = jnp.zeros_like(sum_down)
            lanes = lax.broadcasted_iota(jnp.int32, marks.shape, 0)
            owner = base + lax.div(lax.broadcasted_iota(jnp.int32, marks.shape, 1), share)
            marks[...] = jnp.where((lanes == owner) | (lanes == owner + experts), 1.0, 0.0).astype(BF)

    def g_end(k, level):
        g_hop(k, level).finish()
        if level + 1 < levels:
            g_hop(k, level + 1).start()

    def wide_out(i):
        here = pl.ds(pl.multiple_of(i * rows, rows), rows)
        return pltpu.make_async_copy(d_gu, grad_widen.at[here, :], load.at[1])

    out_down = pltpu.make_async_copy(sum_down, grad_shrink, load.at[0])

    def store(i):
        @pl.when(i == 0)
        def _():
            out_down.start()

        @pl.when(i > 0)
        def _():
            wide_out(i - 1).wait()

        d_gu[...] = sum_wide[pl.ds(pl.multiple_of(i * rows, rows), rows), :].astype(BF)
        wide_out(i).start()

    @pl.loop(0, chunks + levels + 4)
    def _(t):
        for level in reversed(range(levels)):
            after(t, level + 1, functools.partial(g_end, level=level))
        after(t, 0, begin)
        for level in reversed(range(4)):
            after(t, levels + level + 1, functools.partial(s_end, level=level))
        after(t, levels, compute)

        @pl.when((t >= chunks + levels) & (t < chunks + levels + min(4, width // rows)))
        def _():
            store(t - chunks - levels)

    for i in range(4, width // rows):
        store(i)
    pltpu.make_async_copy(stage, moe.at[chunks - 1], stage_sem.at[0]).wait()
    wide_out(width // rows - 1).wait()
    out_down.wait()


def experts_together(x, dy, widen, shrink, experts, collective_id):
    groups, parts = lax.axis_size("grp"), lax.axis_size("ep")
    major, minor, xn = mesh_sizes(groups, parts)
    micro, local_rows, wide = x.shape
    x = x.reshape(-1, ROWS, wide)
    chunks = x.shape[0]
    local_exp, inner, width = shrink.shape
    share = inner // groups
    hidden = local_exp * share
    rows = 2 * ROWS * major * minor * xn
    acc_ring = 4
    legs = minor + xn - 1 + leg_count(major)
    vmem = pl.BlockSpec(memory_space=pltpu.VMEM)
    hbm = pl.BlockSpec(memory_space=pl.ANY)
    flops = 2 * chunks * rows * width * hidden * 9
    return pl.pallas_call(
        functools.partial(experts_kernel, groups, parts, local_rows, acc_ring, experts),
        out_shape=[
            jax.ShapeDtypeStruct((chunks, ROWS, wide), BF),
            jax.ShapeDtypeStruct((chunks, rows, width), BF),
            jax.ShapeDtypeStruct((width, 2 * hidden), BF),
            jax.ShapeDtypeStruct((hidden, width), F32),
        ],
        in_specs=[vmem, hbm, hbm, hbm],
        out_specs=[vmem, hbm, hbm, hbm],
        scratch_shapes=[
            pltpu.VMEM((chunks, rows, wide), BF),
            pltpu.VMEM((2, rows, width), BF),
            pltpu.VMEM((width, 2 * hidden), BF),
            pltpu.VMEM((hidden, width), BF),
            pltpu.VMEM((width, 2 * hidden), F32),
            pltpu.VMEM((hidden, width), F32),
            pltpu.VMEM((rows, width), BF),
            pltpu.VMEM((acc_ring, xn, major, minor, ROWS, wide), BF),
            pltpu.VMEM((xn, major, minor, ROWS, wide), BF),
            pltpu.VMEM((2, 1, xn, major, minor, ROWS, wide), BF),
            pltpu.VMEM((2, xn - 1, major, minor, ROWS, wide), BF),
            pltpu.VMEM((2, minor - 1, major, ROWS, wide), BF),
            pltpu.VMEM((2, major - 1, ROWS, wide), BF),
            pltpu.VMEM((rows, 4 * share), F32),
            pltpu.VMEM((rows, 2 * share), F32),
            pltpu.VMEM((rows, hidden), BF),
            pltpu.VMEM((rows, 2 * hidden), BF),
            pltpu.VMEM((rows, 2 * share), F32),
            pltpu.VMEM((rows, hidden), BF),
            pltpu.VMEM((128, hidden), BF),
            pltpu.SemaphoreType.DMA((3 * local_exp,)),
            pltpu.SemaphoreType.DMA((2,)),
            pltpu.SemaphoreType.DMA((2,)),
            pltpu.SemaphoreType.DMA((chunks, legs)),
            pltpu.SemaphoreType.DMA((chunks, legs)),
            pltpu.SemaphoreType.DMA((chunks, legs)),
            pltpu.SemaphoreType.DMA((chunks, legs)),
        ],
        compiler_params=pltpu.CompilerParams(
            collective_id=collective_id, has_side_effects=True, vmem_limit_bytes=63 * 2**20
        ),
        cost_estimate=pl.CostEstimate(flops=flops, bytes_accessed=80 * 2**20, transcendentals=chunks * rows * hidden),
    )(x, dy, widen, shrink)


def experts_apart(x, dy_all, specialist_widen_matrix, specialist_shrink_matrix, experts):
    groups, parts = lax.axis_size("grp"), lax.axis_size("ep")
    group, part = lax.axis_index("grp"), lax.axis_index("ep")
    local_exp, inner, width = specialist_shrink_matrix.shape
    share = inner // groups
    widen = specialist_widen_matrix.reshape(local_exp, width, 2, groups, share)
    widen = lax.dynamic_index_in_dim(widen, group, 3, keepdims=False)
    widen = widen.transpose(1, 2, 0, 3).reshape(width, 2 * local_exp * share)
    shrink = specialist_shrink_matrix.reshape(local_exp, groups, share, width)
    shrink = lax.dynamic_index_in_dim(shrink, group, 1, keepdims=False).reshape(local_exp * share, width)
    x_all = gather_all(x, 1)
    chunk_shape = x_all.shape[:-1]
    x_all, dy_all = x_all.reshape(-1, width + 128), dy_all.reshape(-1, width)
    gate = x_all[:, width: width + experts].astype(F32) + x_all[:, width + experts: width + 2 * experts].astype(F32)
    x_all = x_all[:, :width]
    gate = lax.dynamic_slice_in_dim(gate, part * local_exp, local_exp, axis=1)
    gate = jnp.repeat(gate, share, axis=1)
    gate_up = jnp.dot(x_all, widen, preferred_element_type=F32)
    g, u = gate_up[:, : local_exp * share], gate_up[:, local_exp * share:]
    sigma = jax.nn.sigmoid(g)
    act = g * sigma * u
    gated = (gate * act).astype(BF)
    moe_part = jnp.dot(gated, shrink, preferred_element_type=F32).astype(BF)
    d_raw = lax.dot_general(dy_all, shrink, (((1,), (1,)), ((), ())), preferred_element_type=F32)
    d_gate = jnp.sum((act * d_raw).reshape(-1, local_exp, share), axis=-1)
    d_act = gate * d_raw
    d_gu = jnp.concatenate([d_act * u * sigma * (1.0 + g * (1.0 - sigma)), d_act * (g * sigma)], axis=1).astype(BF)
    dx_part = lax.dot_general(d_gu, widen, (((1,), (1,)), ((), ())), preferred_element_type=F32).astype(BF)
    lanes = jnp.arange(128, dtype=jnp.int32)
    place = (lanes[None, :] == part * local_exp + jnp.arange(local_exp, dtype=jnp.int32)[:, None])
    d_gate = jnp.sum(jnp.where(place[None], d_gate[:, :, None], 0.0), axis=1)
    dx_part = jnp.concatenate([dx_part, d_gate.astype(BF)], axis=1)
    dx_sum = scatter_all(dx_part.reshape(chunk_shape + (width + 128,)), 2)
    grad_widen = lax.dot_general(x_all, d_gu, (((0,), (0,)), ((), ())), preferred_element_type=F32)
    grad_shrink = lax.dot_general(gated, dy_all, (((0,), (0,)), ((), ())), preferred_element_type=F32)
    grad_widen = grad_widen.astype(BF).reshape(width, 2, local_exp // 2, 2, share).transpose(0, 2, 1, 3, 4)
    return dx_sum, moe_part.reshape(chunk_shape + (width,)), grad_widen, grad_shrink


def finish_kernel(share, qkv, out, wide, shrink, qkv_to, out_to, wide_to, shrink_to):
    qkv_to[...] = qkv[...].astype(F32)
    out_to[...] = out[...].astype(F32)
    shrink_to[...] = shrink[...]
    for i in range(wide.shape[0]):
        wide_to[0, :, i * share: (i + 1) * share] = wide[i].astype(F32)


def finish(qkv, out, wide, shrink, local_exp, share):
    groups, rows, _ = wide.shape
    whole = (local_exp, rows, 2 * groups * share)
    if share % 128:
        wide = wide.reshape(groups, rows, local_exp // 2, 2, 2, share).transpose(2, 4, 1, 3, 0, 5)
        return qkv.astype(F32), out.astype(F32), wide.reshape(whole).astype(F32), shrink
    steps = 2 * local_exp
    cut = lambda a: pl.BlockSpec((a.shape[0] // steps, a.shape[1]), lambda i: (i, 0))
    outs = [jax.ShapeDtypeStruct(a.shape, F32) for a in (qkv, out)] + [
        jax.ShapeDtypeStruct(whole, F32), jax.ShapeDtypeStruct(shrink.shape, F32)]
    return pl.pallas_call(
        functools.partial(finish_kernel, share),
        grid=(steps,),
        out_shape=outs,
        in_specs=[cut(qkv), cut(out),
                  pl.BlockSpec((groups, rows, share), lambda i: (0, 0, i // 4 * 4 + i % 2 * 2 + i // 2 % 2)), cut(shrink)],
        out_specs=[cut(qkv), cut(out),
                   pl.BlockSpec((1, rows, groups * share), lambda i: (i // 2, 0, i % 2)), cut(shrink)],
        compiler_params=pltpu.CompilerParams(vmem_limit_bytes=40 * 2**20),
    )(qkv, out, wide, shrink)


class Backdrop:
    PACE = 2

    def __init__(self, groups, parts, part, out, acc, land_c, land_p, land_q, land_z, local, send, recv):
        self.core, self.first, self.third, self.fourth = lines(groups, parts)
        self.part, self.out, self.acc, self.lands = part, out, acc, (land_c, land_p, land_q)
        self.land_z = land_z
        self.local, self.send, self.recv = local, send, recv
        self.chunks = part.shape[0]
        self.levels = 3 + hop_count(self.third.size)
        self.lag = self.PACE * self.levels

    @staticmethod
    def scratch(chunks, width):
        major, minor, xn = mesh_sizes(lax.axis_size("grp"), lax.axis_size("ep"))
        legs = minor + xn - 1 + leg_count(major)
        return [
            pltpu.VMEM((chunks, xn, major, minor, ROWS, width), BF),
            pltpu.VMEM((4, 1, xn, major, minor, ROWS, width), BF),
            pltpu.VMEM((4, xn - 1, major, minor, ROWS, width), BF),
            pltpu.VMEM((4, minor - 1, major, ROWS, width), BF),
            pltpu.VMEM((chunks, leg_count(major), ROWS, width), BF),
            pltpu.SemaphoreType.DMA((chunks,)),
            pltpu.SemaphoreType.DMA((chunks, legs)),
            pltpu.SemaphoreType.DMA((chunks, legs)),
        ]

    def near(self):
        return [self.core, self.first, self.third, self.fourth]

    def own(self, k):
        return pltpu.make_async_copy(self.part.at[k, self.core.place], self.acc.at[k], self.local.at[k])

    def hop(self, k, level):
        p, q = self.first.place, self.fourth.place
        pn, qn = self.first.size, self.fourth.size
        if level >= 3:
            offset = pn + qn - 1
            land = self.land_z.at[k]
            return reduce_hops(self.third, lambda i: self.acc.at[k, p, i, q], lambda i: land.at[i], add,
                               lambda i: self.send.at[k, offset + i], lambda i: self.recv.at[k, offset + i])[level - 3]
        line, offset, source = [
            (self.core, 0, lambda i: self.part.at[k, i]),
            (self.first, 1, lambda i: self.acc.at[k, i]),
            (self.fourth, pn, lambda i: self.acc.at[k, p, :, i]),
        ][level]
        land = self.lands[level]
        return Swap(line, source, lambda j, i: land.at[lax.rem(k, 4), j],
                    lambda j: self.send.at[k, offset + j], lambda j: self.recv.at[k, offset + j])

    def end(self, k, level):
        p, q, z = self.first.place, self.fourth.place, self.third.place
        self.hop(k, level).finish()
        if level + 1 == self.levels:
            self.out[k] = self.acc[k, p, z, q]
            return
        after = self.hop(k, level + 1)
        if level == 0:
            self.own(k).wait()
            if self.first.size == 2:
                add(self.acc.at[k, 1 - p], self.lands[0].at[lax.rem(k, 4), 0, 1 - p])
                after.start()
                add(self.acc.at[k, p], self.lands[0].at[lax.rem(k, 4), 0, p])
                return
            add(self.acc.at[k], self.lands[0].at[lax.rem(k, 4), 0])
        elif level < 3:
            to = self.acc.at[k, p] if level == 1 else self.acc.at[k, p, :, q]
            for j in range(self.lands[level].shape[1]):
                add(to, self.lands[level].at[lax.rem(k, 4), j])
        after.start()

    def begin(self, k):
        self.hop(k, 0).start()
        self.own(k).start()

    def step(self, t):
        for level in reversed(range(self.levels)):
            k = t - self.PACE * (level + 1)

            @pl.when((k >= 0) & (k < self.chunks))
            def _(k=k, level=level):
                self.end(k, level)

        @pl.when((t >= 0) & (t < self.chunks))
        def _():
            self.begin(t)


class Sequence:
    def __init__(self, parts, block, micro):
        e = lax.axis_index("ep")
        self.xn, self.block, self.micro, self.e = parts // 2, block, micro, e
        self.x, self.c = lax.div(e, 2), lax.rem(e, 2)
        self.line = Line(parts, e, (0, 1))
        self.line_x = Line(self.xn, self.x, (0, 2))
        self.line_c = Line(2, self.c, (0, 1))

    def at(self, ref, m, x, c):
        return ref.at[m, pl.ds(pl.multiple_of((x * 2 + c) * self.block, self.block), self.block), :]

    def gather_x(self, ref, send, recv):
        legs = []
        for m in range(self.micro):
            legs += swap_legs(
                self.line_x, lambda i, m=m: self.at(ref, m, self.x, self.c), lambda j, i, m=m: self.at(ref, m, i, self.c),
                lambda j, m=m: send.at[m, j], lambda j, m=m: recv.at[m, j])
        return legs

    def gather_c(self, ref, send, recv):
        legs = []
        for m in range(self.micro):
            for x in range(self.xn):
                legs += swap_legs(
                    self.line_c, lambda i, m=m, x=x: self.at(ref, m, x, self.c), lambda j, i, m=m, x=x: self.at(ref, m, x, i),
                    lambda j, m=m, x=x: send.at[m, self.xn - 1 + x], lambda j, m=m, x=x: recv.at[m, self.xn - 1 + x])
        return legs

    def reduce_c(self, ref, land, send, recv):
        legs = []
        for m in range(self.micro):
            for x in range(self.xn):
                legs += swap_legs(
                    self.line_c, lambda i, m=m, x=x: self.at(ref, m, x, i), lambda j, i, m=m, x=x: land.at[m, x],
                    lambda j, m=m, x=x: send.at[m, self.xn - 1 + x], lambda j, m=m, x=x: recv.at[m, self.xn - 1 + x])
        return legs

    def reduce_x(self, ref, land, send, recv):
        legs = []
        for m in range(self.micro):
            legs += swap_legs(
                self.line_x, lambda i, m=m: self.at(ref, m, i, self.c), lambda j, i, m=m: land.at[m, j],
                lambda j, m=m: send.at[m, j], lambda j, m=m: recv.at[m, j])
        return legs

    def add_c(self, ref, land):
        for m in range(self.micro):
            for x in range(self.xn):
                add_rows(ref.at[m], (x * 2 + self.c) * self.block, land.at[m, x], self.block)

    def total_x(self, ref, land, out):
        for m in range(self.micro):
            @pl.loop(0, self.block // ROWS)
            def _(i, m=m):
                here = pl.ds(pl.multiple_of(i * ROWS, ROWS), ROWS)
                total = ref[m, pl.ds(pl.multiple_of(self.e * self.block + i * ROWS, ROWS), ROWS), :].astype(F32)
                for j in range(self.xn - 1):
                    total = total + land[m, j, here, :].astype(F32)
                out[m, here, :] = total


def sum_over_parts(seq, columns, sent, got, send, recv, meanwhile):
    flat = columns.T
    sent[...] = flat[:8]
    legs = swap_legs(seq.line, lambda i: sent, lambda j, i: got.at[j], lambda j: send.at[j], lambda j: recv.at[j])
    start_legs(legs)
    meanwhile()
    end_legs(legs)
    total = sent[...]
    for j in range(seq.line.size - 1):
        total = total + got[j]
    return jnp.concatenate([total] * 16, axis=0).T


def back_kernel(
    groups, parts, backed,
    branch, merge, triple, queries, keys, values, mixed, probs, hat, inv, gains_in, cos, sin, wide, part,
    d_proj, d_in, grad_heads, grad_out, wide_all, summed,
    gains, rows_all, merge_v, triple_v, q_v, k_v, v_v, mixed_v, probs_v, hat_v, d_mixed, d_qk, sums, partial, land_c, land_x, sent, got,
    load, g_send, g_recv, s_send, s_recv, t_send, t_recv, w_send, w_recv, *behind
):
    micro, block, width = branch.shape
    seq = Sequence(parts, block, micro)
    length = queries.shape[1]
    tokens = micro * length
    heads = queries.shape[2] // HD
    scale = 1.0 / math.sqrt(HD)
    loads = [pltpu.make_async_copy(a, b, load.at[i]) for i, (a, b) in enumerate((
        (merge, merge_v), (mixed, mixed_v), (queries, q_v), (keys, k_v), (values, v_v), (probs, probs_v), (hat, hat_v), (triple, triple_v)))]
    for copy in loads:
        copy.start()
    gains[...] = gains_in[...].astype(F32)
    over = Line(groups, lax.axis_index("grp"), (1, 0))
    if backed:
        back = Backdrop(groups, parts, part, summed, *behind)
        greet_lines([seq.line, over] + back.near())
        steps = back.chunks + back.lag
        behind_step = back.step
    else:
        greet_lines([seq.line, over])
        steps, behind_step = 0, lambda t: None
        summed[...] = jnp.zeros_like(summed)
    for m in range(micro):
        rows_all[m, pl.ds(pl.multiple_of(seq.e * block, block), block), :] = branch[m]
    gather_x = seq.gather_x(rows_all, g_send, g_recv)
    start_legs(gather_x)
    g = over.place
    own_wide = pltpu.make_async_copy(wide.at[g], wide_all.at[g], load.at[8])
    own_wide.start()
    turn = swap_legs(over, lambda i: wide.at[i], lambda j, i: wide_all.at[i], lambda j: w_send.at[j], lambda j: w_recv.at[j])
    pieces = CUTS * (groups - 1)
    tall = wide.shape[1] // CUTS

    def step(t):
        for u in range(PER_STEP):
            i = t * PER_STEP + u

            @pl.when((i >= 0) & (i < pieces))
            def _(i=i):
                j, cut = lax.rem(i, groups - 1), lax.div(i, groups - 1)
                to = lax.rem(g + 1 + j, groups)
                here = pl.ds(pl.multiple_of(cut * tall, ROWS), tall)
                remote(wide.at[to, here, :], wide_all.at[g, here, :], w_send.at[j], w_recv.at[j], over.at(to - g)).start()

        behind_step(t)

    step(0)
    step(1)
    step(2)
    end_legs(gather_x)
    gather_c = seq.gather_c(rows_all, g_send, g_recv)
    start_legs(gather_c)
    step(3)
    sums[...] = jnp.zeros_like(sums)
    grad_heads[...] = jnp.zeros_like(grad_heads)
    end_legs(gather_c)
    for copy in loads[:2]:
        copy.wait()
    for m in range(micro):
        d_mixed[m] = lax.dot_general(rows_all[m], merge_v[...], (((1,), (1,)), ((), ())), preferred_element_type=F32).astype(BF)
    step(4)

    @pl.loop(0, width // 512)
    def _(n):
        cols = pl.ds(pl.multiple_of(n * 512, 512), 512)
        total = lax.dot_general(mixed_v[0], rows_all[0, :, cols], (((0,), (0,)), ((), ())), preferred_element_type=F32)
        for m in range(1, micro):
            total = total + lax.dot_general(
                mixed_v[m], rows_all[m, :, cols], (((0,), (0,)), ((), ())), preferred_element_type=F32)
        grad_out[:, cols] = total.astype(BF)

    step(5)
    for copy in loads[2:7]:
        copy.wait()
    lane = lax.broadcasted_iota(jnp.int32, (1, 128), 1)

    def one_head(i):
        m, h = lax.div(i, heads), lax.rem(i, heads)
        cols = pl.ds(pl.multiple_of(h * HD, HD), HD)
        here = pl.ds(pl.multiple_of(m * length, length), length)
        d_m = d_mixed[m, :, cols]
        weights = probs_v[m, h]
        low = weights.astype(BF)
        d_proj[2, here, cols] = lax.dot_general(low, d_m, (((0,), (0,)), ((), ())), preferred_element_type=F32).astype(BF)
        d_w = lax.dot_general(d_m, v_v[m, :, cols], (((1,), (1,)), ((), ())), preferred_element_type=F32)
        d_s = (weights * (d_w - jnp.sum(weights * d_w, axis=-1, keepdims=True))).astype(BF)
        d_q = jnp.dot(d_s, k_v[m, :, cols], preferred_element_type=F32) * scale
        d_k = lax.dot_general(d_s, q_v[m, :, cols], (((0,), (0,)), ((), ())), preferred_element_type=F32) * scale
        marks = sums[here, :]
        for c, d in enumerate((d_q, d_k)):
            d = d * cos[...] - pltpu.roll(d, HD // 2, 1) * sin[...]
            d_qk[c, here, cols] = d
            product = d * hat_v[c, here, cols]
            grad_heads[c: c + 1, cols] += jnp.sum(product, axis=0, keepdims=True)
            marks = marks + jnp.where(lane == c, jnp.sum(product * gains[c: c + 1, cols], axis=-1, keepdims=True), 0.0)
        sums[here, :] = marks

    @pl.loop(0, micro * heads)
    def _(i):
        one_head(i)
        step(i + 6)

    done = 7 + micro * heads
    sums[...] = sum_over_parts(seq, sums[...], sent, got, t_send, t_recv, lambda: step(done - 1))

    @pl.loop(0, tokens // 64)
    def _(i):
        here = pl.ds(pl.multiple_of(i * 64, 64), 64)
        for c in range(2):
            inner = sums[here, c: c + 1] * (1.0 / width)
            d_proj[c, here, :] = (inv[here, c: c + 1] * (
                d_qk[c, here, :] * gains[c: c + 1, :] - hat_v[c, here, :] * inner)).astype(BF)

    loads[7].wait()

    @pl.loop(0, width // 512)
    def _(n):
        cols = pl.ds(pl.multiple_of(n * 512, 512), 512)
        for m in range(micro):
            here = pl.ds(m * length, length)
            total = lax.dot_general(d_proj[0, here, :], triple_v[0, cols, :], (((1,), (1,)), ((), ())), preferred_element_type=F32)
            for c in (1, 2):
                total = total + lax.dot_general(
                    d_proj[c, here, :], triple_v[c, cols, :], (((1,), (1,)), ((), ())), preferred_element_type=F32)
            partial[m, :, cols] = total.astype(BF)

    reduce_c = seq.reduce_c(partial, land_c, s_send, s_recv)
    start_legs(reduce_c)
    step(done)
    end_legs(reduce_c)
    seq.add_c(partial, land_c)
    reduce_x = seq.reduce_x(partial, land_x, s_send, s_recv)
    start_legs(reduce_x)
    step(done + 1)
    end_legs(reduce_x)
    seq.total_x(partial, land_x, d_in)
    for t in range(done + 2, max(steps, -(-pieces // PER_STEP))):
        step(t)
    end_legs(turn)
    own_wide.wait()


def attention_back(branch, merge, triple, queries, keys, values, mixed, probs, hat, inv, gains, cos, sin, wide, part, collective_id):
    groups, parts = lax.axis_size("grp"), lax.axis_size("ep")
    micro, block, width = branch.shape
    length, local_width = queries.shape[1:]
    tokens = micro * length
    backed = part is not None
    behind = Backdrop.scratch(part.shape[0], width) if backed else []
    summed = (part.shape[0], ROWS, width) if backed else (8, 128)
    vmem = pl.BlockSpec(memory_space=pltpu.VMEM)
    hbm = pl.BlockSpec(memory_space=pl.ANY)
    xn = parts // 2
    return pl.pallas_call(
        functools.partial(back_kernel, groups, parts, backed),
        out_shape=[
            jax.ShapeDtypeStruct((3, tokens, local_width), BF),
            jax.ShapeDtypeStruct((micro, block, width), F32),
            jax.ShapeDtypeStruct((8, local_width), F32),
            jax.ShapeDtypeStruct((local_width, width), BF),
            jax.ShapeDtypeStruct(wide.shape, BF),
            jax.ShapeDtypeStruct(summed, BF if backed else F32),
        ],
        in_specs=[vmem] + [hbm] * 8 + [vmem] * 4 + [hbm] * 2,
        out_specs=[vmem] * 4 + [hbm, vmem],
        scratch_shapes=[
            pltpu.VMEM(gains.shape, F32),
            pltpu.VMEM((micro, length, width), BF),
            pltpu.VMEM(merge.shape, BF),
            pltpu.VMEM(triple.shape, BF),
            pltpu.VMEM(queries.shape, BF),
            pltpu.VMEM(queries.shape, BF),
            pltpu.VMEM(queries.shape, BF),
            pltpu.VMEM(queries.shape, BF),
            pltpu.VMEM(probs.shape, F32),
            pltpu.VMEM(hat.shape, F32),
            pltpu.VMEM(queries.shape, BF),
            pltpu.VMEM((2, tokens, local_width), F32),
            pltpu.VMEM((tokens, 128), F32),
            pltpu.VMEM((micro, length, width), BF),
            pltpu.VMEM((micro, xn, block, width), BF),
            pltpu.VMEM((micro, xn - 1, block, width), BF),
            pltpu.VMEM((8, tokens), F32),
            pltpu.VMEM((parts - 1, 8, tokens), F32),
            pltpu.SemaphoreType.DMA((9,)),
            pltpu.SemaphoreType.DMA((micro, 2 * xn - 1)),
            pltpu.SemaphoreType.DMA((micro, 2 * xn - 1)),
            pltpu.SemaphoreType.DMA((micro, 2 * xn - 1)),
            pltpu.SemaphoreType.DMA((micro, 2 * xn - 1)),
            pltpu.SemaphoreType.DMA((parts - 1,)),
            pltpu.SemaphoreType.DMA((parts - 1,)),
            pltpu.SemaphoreType.DMA((groups - 1,)),
            pltpu.SemaphoreType.DMA((groups - 1,)),
        ] + behind,
        compiler_params=pltpu.CompilerParams(
            collective_id=collective_id, has_side_effects=True, vmem_limit_bytes=58 * 2**20
        ),
        cost_estimate=pl.CostEstimate(flops=10**10, bytes_accessed=40 * 2**20, transcendentals=0),
    )(branch, merge, triple, queries, keys, values, mixed, probs, hat, inv, gains, cos, sin, wide,
      part if backed else mixed)


class BackGather:
    PACE = 3

    def __init__(self, groups, parts, own, out, local, send, recv):
        self.lines = lines(groups, parts)
        self.own, self.out, self.local, self.send, self.recv = own, out, local, send, recv
        self.chunks = own.shape[0]
        self.levels = 4
        self.lag = self.PACE * self.levels

    @staticmethod
    def scratch(chunks):
        major, minor, xn = mesh_sizes(lax.axis_size("grp"), lax.axis_size("ep"))
        legs = minor + xn + major - 2
        return [
            pltpu.SemaphoreType.DMA((chunks,)),
            pltpu.SemaphoreType.DMA((chunks, legs)),
            pltpu.SemaphoreType.DMA((chunks, legs)),
        ]

    def near(self):
        return list(self.lines)

    def mine(self, k):
        return pltpu.make_async_copy(
            self.own.at[k], self.out.at[(k,) + tuple(line.place for line in self.lines)], self.local.at[k])

    def hop(self, k, level):
        core, first, third, fourth = self.lines
        c, p, q = core.place, first.place, fourth.place
        line, offset, at = [
            (third, 0, lambda i: self.out.at[k, c, p, i, q]),
            (fourth, third.size - 1, lambda i: self.out.at[k, c, p, :, i]),
            (first, third.size + fourth.size - 2, lambda i: self.out.at[k, c, i]),
            (core, third.size + fourth.size + first.size - 3, lambda i: self.out.at[k, i]),
        ][level]
        source = (lambda i: self.own.at[k]) if level == 0 else (lambda i: at(line.place))
        return Swap(line, source, lambda j, i: at(i),
                    lambda j: self.send.at[k, offset + j], lambda j: self.recv.at[k, offset + j])

    def step(self, t):
        for level in reversed(range(self.levels)):
            k = t - self.PACE * (level + 1)

            @pl.when((k >= 0) & (k < self.chunks))
            def _(k=k, level=level):
                self.hop(k, level).finish()
                if level == 0:
                    self.mine(k).wait()
                if level + 1 < self.levels:
                    self.hop(k, level + 1).start()

        @pl.when((t >= 0) & (t < self.chunks))
        def _():
            self.mine(t).start()
            self.hop(t, 0).start()


def forward_kernel(
    groups, parts, experts,
    x, dy, routes, quota, gains_in, head_gains_in, cos, sin, docs, dispatch_in, triple, merge,
    gathered, q_out, k_out, v_out, mixed, probs, hat, inv, hidden, ffn_in, router, dy_all,
    kept, gains, head_gains, docs_down, dispatch, triple_v, merge_v, sums, partial, land_c, land_x, sent, got,
    load, g_send, g_recv, s_send, s_recv, t_send, t_recv, *behind
):
    micro, block, width = x.shape
    seq = Sequence(parts, block, micro)
    length = gathered.shape[1]
    tokens = micro * length
    heads = q_out.shape[2] // HD
    scale = 1.0 / math.sqrt(HD)
    cuts = block // ROWS
    loads = [pltpu.make_async_copy(triple, triple_v, load.at[0]), pltpu.make_async_copy(merge, merge_v, load.at[1])]
    for copy in loads:
        copy.start()
    back = BackGather(groups, parts, dy, dy_all, *behind)
    step, steps = back.step, back.chunks + back.lag
    gains[...] = gains_in[...].astype(F32)
    head_gains[...] = head_gains_in[...].astype(F32)
    lane = lax.broadcasted_iota(jnp.int32, (1, 128), 1)
    earlier = (lax.broadcasted_iota(jnp.int32, (block, block), 1) < lax.broadcasted_iota(jnp.int32, (block, block), 0))
    for m in range(micro):
        @pl.loop(0, cuts)
        def _(r, m=m):
            here = pl.ds(pl.multiple_of(r * ROWS, ROWS), ROWS)
            v = x[m, here, :].astype(F32)
            v = v * lax.rsqrt(jnp.mean(v * v, axis=-1, keepdims=True) + EPS)
            gathered[m, pl.ds(pl.multiple_of(seq.e * block + r * ROWS, ROWS), ROWS), :] = (v * gains[0:1, :]).astype(BF)
    greet_lines([seq.line] + back.near())
    gather_x = seq.gather_x(gathered, g_send, g_recv)
    start_legs(gather_x)
    step(0)
    limits = jnp.concatenate([quota[...], jnp.zeros((1, 128 - experts), jnp.int32)], axis=1).astype(F32)
    dispatch[...] = jnp.zeros_like(dispatch)
    dispatch[:experts, :] = dispatch_in[...]
    for m in range(micro):
        chosen = jnp.zeros((128, block), F32)
        for j in range(TOP):
            chosen = chosen + jnp.where(routes[m, j: j + 1, :] == lax.broadcasted_iota(jnp.int32, (128, 1), 0), 1.0, 0.0)
        counts = chosen.T
        prior = jnp.dot(jnp.where(earlier, 1.0, 0.0).astype(BF), counts.astype(BF), preferred_element_type=F32)
        kept[m] = jnp.where((counts > 0.0) & (prior < limits), 1.0, 0.0)
        docs_down[m] = jnp.broadcast_to(docs[m: m + 1, :], (128, length)).astype(F32).T
    step(1)
    step(2)
    end_legs(gather_x)
    gather_c = seq.gather_c(gathered, g_send, g_recv)
    start_legs(gather_c)
    step(3)
    loads[0].wait()
    end_legs(gather_c)

    @pl.loop(0, micro)
    def _(m):
        here = pl.ds(pl.multiple_of(m * length, length), length)
        marks = jnp.zeros((length, 128), F32)
        for c in range(2):
            raw = jnp.dot(gathered[m], triple_v[c], preferred_element_type=F32)
            hat[c, here, :] = raw
            marks = marks + jnp.where(lane == c, jnp.sum(raw * raw, axis=-1, keepdims=True), 0.0)
        sums[here, :] = marks
        v_out[m] = jnp.dot(gathered[m], triple_v[2], preferred_element_type=F32).astype(BF)
        step(m + 4)

    done = micro + 5
    squares = sum_over_parts(seq, sums[...], sent, got, t_send, t_recv, lambda: step(done - 1))
    inv[...] = lax.rsqrt(squares * (1.0 / width) + EPS)
    loads[1].wait()

    @pl.loop(0, micro * heads)
    def _(i):
        m, h = lax.div(i, heads), lax.rem(i, heads)
        cols = pl.ds(pl.multiple_of(h * HD, HD), HD)
        here = pl.ds(pl.multiple_of(m * length, length), length)
        for c, to in enumerate((q_out, k_out)):
            v = hat[c, here, cols] * inv[here, c: c + 1]
            hat[c, here, cols] = v
            v = v * head_gains[c: c + 1, cols]
            to[m, :, cols] = (v * cos[...] + pltpu.roll(v, HD // 2, 1) * sin[...]).astype(BF)
        scores = lax.dot_general(
            q_out[m, :, cols], k_out[m, :, cols], (((1,), (1,)), ((), ())), preferred_element_type=F32) * scale
        allowed = (docs_down[m][:, :1] == docs[pl.ds(m, 1), :].astype(F32)) & (
            lax.broadcasted_iota(jnp.int32, (length, length), 1) <= lax.broadcasted_iota(jnp.int32, (length, length), 0))
        scores = jnp.where(allowed, scores, NEG)
        grown = jnp.exp(scores - jnp.max(scores, axis=-1, keepdims=True))
        weights = grown / jnp.sum(grown, axis=-1, keepdims=True)
        probs[m, h] = weights
        mixed[m, :, cols] = jnp.dot(weights.astype(BF), v_out[m, :, cols], preferred_element_type=F32).astype(BF)
        step(done + i)

    done = done + micro * heads

    @pl.loop(0, width // 512)
    def _(n):
        cols = pl.ds(pl.multiple_of(n * 512, 512), 512)
        for m in range(micro):
            partial[m, :, cols] = jnp.dot(mixed[m], merge_v[:, cols], preferred_element_type=F32).astype(BF)

    reduce_c = seq.reduce_c(partial, land_c, s_send, s_recv)
    start_legs(reduce_c)
    step(done)
    end_legs(reduce_c)
    seq.add_c(partial, land_c)
    reduce_x = seq.reduce_x(partial, land_x, s_send, s_recv)
    start_legs(reduce_x)
    step(done + 1)
    end_legs(reduce_x)
    seq.total_x(partial, land_x, hidden)
    for m in range(micro):
        @pl.loop(0, cuts)
        def _(r, m=m):
            here = pl.ds(pl.multiple_of(r * ROWS, ROWS), ROWS)
            v = hidden[m, here, :] + x[m, here, :].astype(F32)
            hidden[m, here, :] = v
            v = v * lax.rsqrt(jnp.mean(v * v, axis=-1, keepdims=True) + EPS)
            ffn_in[m, here, :width] = (v * gains[1:2, :]).astype(BF)
        logits = lax.dot_general(
            ffn_in[m, :, :width], dispatch[...], (((1,), (1,)), ((), ())), preferred_element_type=F32)
        logits = jnp.where(lane < experts, logits, NEG)
        grown = jnp.exp(logits - jnp.max(logits, axis=-1, keepdims=True))
        grown = grown / jnp.sum(grown, axis=-1, keepdims=True)
        gate = grown * kept[m]
        router[m] = grown + pltpu.roll(kept[m], experts, 1)
        head = gate.astype(BF).astype(F32)
        ffn_in[m, :, width:] = (head + pltpu.roll(gate - head, experts, 1)).astype(BF)
    for t in range(done + 2, steps):
        step(t)


def attention_forward(x, dy, routes, quota, gains, head_gains, cos, sin, docs, dispatch, triple, merge, collective_id):
    groups, parts = lax.axis_size("grp"), lax.axis_size("ep")
    major, minor, xn = mesh_sizes(groups, parts)
    micro, block, width = x.shape
    length = docs.shape[1]
    local_width = triple.shape[2]
    heads = local_width // HD
    tokens = micro * length
    chunks = micro * block // ROWS
    vmem = pl.BlockSpec(memory_space=pltpu.VMEM)
    hbm = pl.BlockSpec(memory_space=pl.ANY)
    low = jax.ShapeDtypeStruct((micro, length, local_width), BF)
    experts = dispatch.shape[1]
    return pl.pallas_call(
        functools.partial(forward_kernel, groups, parts, experts),
        out_shape=[
            jax.ShapeDtypeStruct((micro, length, width), BF),
            low, low, low, low,
            jax.ShapeDtypeStruct((micro, heads, length, length), F32),
            jax.ShapeDtypeStruct((2, tokens, local_width), F32),
            jax.ShapeDtypeStruct((tokens, 128), F32),
            jax.ShapeDtypeStruct((micro, block, width), F32),
            jax.ShapeDtypeStruct((micro, block, width + 128), BF),
            jax.ShapeDtypeStruct((micro, block, 128), F32),
            jax.ShapeDtypeStruct((chunks, 2, xn, major, minor, ROWS, width), BF),
        ],
        in_specs=[vmem] * 10 + [hbm] * 2,
        out_specs=[vmem] * 11 + [hbm],
        scratch_shapes=[
            pltpu.VMEM((micro, block, 128), F32),
            pltpu.VMEM(gains.shape, F32),
            pltpu.VMEM(head_gains.shape, F32),
            pltpu.VMEM((micro, length, 128), F32),
            pltpu.VMEM((128, width), BF),
            pltpu.VMEM(triple.shape, BF),
            pltpu.VMEM(merge.shape, BF),
            pltpu.VMEM((tokens, 128), F32),
            pltpu.VMEM((micro, length, width), BF),
            pltpu.VMEM((micro, xn, block, width), BF),
            pltpu.VMEM((micro, xn - 1, block, width), BF),
            pltpu.VMEM((8, tokens), F32),
            pltpu.VMEM((parts - 1, 8, tokens), F32),
            pltpu.SemaphoreType.DMA((2,)),
            pltpu.SemaphoreType.DMA((micro, 2 * xn - 1)),
            pltpu.SemaphoreType.DMA((micro, 2 * xn - 1)),
            pltpu.SemaphoreType.DMA((micro, 2 * xn - 1)),
            pltpu.SemaphoreType.DMA((micro, 2 * xn - 1)),
            pltpu.SemaphoreType.DMA((parts - 1,)),
            pltpu.SemaphoreType.DMA((parts - 1,)),
        ] + BackGather.scratch(chunks),
        compiler_params=pltpu.CompilerParams(
            collective_id=collective_id, has_side_effects=True, vmem_limit_bytes=56 * 2**20
        ),
        cost_estimate=pl.CostEstimate(flops=6 * 10**9, bytes_accessed=40 * 2**20, transcendentals=0),
    )(x, dy.reshape(chunks, ROWS, width), routes.transpose(0, 2, 1), quota.reshape(1, -1), gains, head_gains, cos, sin, docs,
      dispatch.T, triple, merge)


def per_device(
    block_entry_states,
    document_labels,
    token_assignments,
    worker_quota_tallies,
    rescale_factors_both,
    triple_projection_matrix,
    probe_lookup_scalers,
    heads_merge_matrix,
    dispatcher_matrix,
    specialist_widen_matrix,
    specialist_shrink_matrix,
    output_gradient,
):
    micro, local_rows, width = block_entry_states.shape
    groups, parts = lax.axis_size("grp"), lax.axis_size("ep")
    major, minor, xs = mesh_sizes(groups, parts)
    group = lax.axis_index("grp")
    part = lax.axis_index("ep")
    seq_len = document_labels.shape[1]
    experts = dispatcher_matrix.shape[1]
    local_exp = specialist_widen_matrix.shape[0]
    inner = specialist_shrink_matrix.shape[1]
    share = inner // groups
    local_width = triple_projection_matrix.shape[2]
    heads = local_width // HD
    scale = 1.0 / math.sqrt(HD)
    gains = rescale_factors_both.astype(F32)
    cos, signed_sin = rope_tables(seq_len, HD)
    triple = triple_projection_matrix.transpose(1, 0, 2)
    gathered, queries, keys, values, mixed, weights, qk_hat, qk_inv, hidden, ffn_ext, probs, dy_all = attention_forward(
        block_entry_states, output_gradient, token_assignments, worker_quota_tallies, rescale_factors_both,
        probe_lookup_scalers, cos, signed_sin,
        document_labels, dispatcher_matrix, triple, heads_merge_matrix, 0)
    ffn_in = ffn_ext[..., :width]

    fused = xs == minor and share % 128 == 0 and local_exp % 2 == 0 and 2 * xs * minor * major * ROWS <= 512
    chunk_shape = (micro * local_rows // ROWS, 2, xs, major, minor, ROWS)
    if fused:
        dx_sum, moe_part, grad_widen, grad_shrink = experts_together(
            ffn_ext, dy_all.reshape(dy_all.shape[0], -1, width), specialist_widen_matrix, specialist_shrink_matrix, experts, 1)
    else:
        dx_sum, moe_part, grad_widen, grad_shrink = experts_apart(
            ffn_ext, dy_all, specialist_widen_matrix, specialist_shrink_matrix, experts)
    dx_sum = dx_sum.astype(F32).reshape(micro, local_rows, width + 128)
    grad_widen = grad_widen.reshape(groups, width // groups, -1)

    inv_second = lax.rsqrt(jnp.mean(hidden * hidden, axis=-1, keepdims=True) + EPS)
    hat_second = hidden * inv_second
    probs, keep = probs[..., :experts], probs[..., experts: 2 * experts]
    d_probs = dx_sum[..., width: width + experts] * keep
    d_logits = probs * (d_probs - jnp.sum(probs * d_probs, axis=-1, keepdims=True))
    d_ffn = dx_sum[..., :width] + jnp.einsum("mte,de->mtd", d_logits, dispatcher_matrix.astype(F32), precision=HIGH)
    grad_router = jnp.einsum("mtd,mte->ed", ffn_in.astype(F32), d_logits, precision=HIGH)
    scaled = d_ffn * gains[1]
    adjoint = output_gradient.astype(F32)
    d_hidden = adjoint + inv_second * (scaled - hat_second * jnp.mean(scaled * hat_second, axis=-1, keepdims=True))
    grad_second = jnp.sum(d_ffn * hat_second, axis=(0, 1))

    d_proj, d_attn_in, grad_heads, grad_out, grad_widen, moe = attention_back(
        d_hidden.astype(BF), heads_merge_matrix, triple, queries, keys, values, mixed, weights,
        qk_hat, qk_inv, probe_lookup_scalers, cos, signed_sin, grad_widen,
        moe_part.reshape(chunk_shape + (width,)) if fused else None, 5)
    if not fused:
        moe = scatter_all(moe_part.reshape(chunk_shape + (width,)), 3)
    output = (hidden + moe.astype(F32).reshape(micro, local_rows, width)).astype(BF)
    skip = block_entry_states.astype(F32)
    inv_first = lax.rsqrt(jnp.mean(skip * skip, axis=-1, keepdims=True) + EPS)
    hat_first = skip * inv_first
    scaled = d_attn_in * gains[0]
    grad_input = d_hidden + inv_first * (scaled - hat_first * jnp.mean(scaled * hat_first, axis=-1, keepdims=True))
    grad_first = jnp.sum(d_attn_in * hat_first, axis=(0, 1))

    shared = jnp.concatenate([grad_first[None], grad_second[None], grad_router]).reshape(-1).astype(BF)
    own = grad_heads[:2].reshape(-1).astype(BF)
    gap, size = shared.shape[0], shared.shape[0] + own.shape[0]
    block = (groups, ROWS, -(-size // (groups * ROWS * 128)) * 128)
    room = math.prod(block)
    shared = jnp.pad(shared, (0, room - gap)).reshape(block)
    own = jnp.pad(own, (gap, room - size)).reshape(block)
    out_sum, qkv_sum, misc_sum = total_over_groups(
        gathered.reshape(-1, width), d_proj, grad_out, shared, own, 4)
    qkv_sum, out_sum, grad_widen, grad_shrink = finish(
        qkv_sum.reshape(-1, local_width), out_sum.reshape(-1, width), grad_widen, grad_shrink, local_exp, share)
    qkv_sum = qkv_sum.reshape(3, width, local_width).transpose(1, 0, 2)
    grad_shrink = grad_shrink.reshape(local_exp, share, width)
    misc_sum = misc_sum.reshape(-1)[:size].astype(F32)
    rows = misc_sum[: (2 + experts) * width].reshape(2 + experts, width)
    return (
        output,
        grad_input,
        rows[:2],
        qkv_sum,
        misc_sum[(2 + experts) * width:].reshape(2, local_width),
        out_sum,
        rows[2:].T,
        grad_widen,
        grad_shrink,
    )


def solution(mesh):
    return jax.shard_map(
        per_device,
        mesh=mesh,
        in_specs=(
            P(None, ALL, None),
            P(None, "grp"),
            P(None, ALL, None),
            P(),
            P(),
            P(None, None, "ep"),
            P(None, "ep"),
            P("ep", None),
            P(),
            P("ep", None, None),
            P("ep", None, None),
            P(None, ALL, None),
        ),
        out_specs=(
            P(None, ALL, None),
            P(None, ALL, None),
            P(),
            P(None, None, "ep"),
            P(None, "ep"),
            P("ep", None),
            P(),
            P("ep", "grp", None),
            P("ep", "grp", None),
        ),
        check_vma=False,
    )
```
